32 devices in a mesh: dp: 8 (over y, x, core), shard: 4 (over z).
Axes of the slice: x: 2, y: 2, z: 4, core: 2. Of those that a mesh axis runs over, the one named last changes fastest.
Arguments:
- tokens: bfloat16 [8192, 2048], P(('dp', 'shard')), may hold values from -6 to 6
- out_grad: bfloat16 [8192, 2048], P(('dp', 'shard')), may hold values from -6 to 6
- routes: int32 [8192, 2], P(('dp', 'shard')), may hold values from 0 to 3, all different within a row; in each aligned block of 256 rows (0 to 255, 256 to 511, ...) at most 170 rows name the same one
- gate_weights: float32 [8192, 2], P(('dp', 'shard')), may hold values from 0.2 to 1
- prefix: int32 [8], P('dp'), may hold values from 102 to 512
- query_weight: bfloat16 [2048, 2048], P(None, 'shard'), may hold values from -0.125 to 0.125
- key_weight: bfloat16 [2048, 2048], P(None, 'shard'), may hold values from -0.125 to 0.125
- value_weight: bfloat16 [2048, 2048], P(None, 'shard'), may hold values from -0.125 to 0.125
- output_weight: bfloat16 [2048, 2048], P(None, 'shard'), may hold values from -2 to 2
- norm_gains: bfloat16 [4, 2048], P(None, 'shard'), may hold values from 0.5 to 1.5
- expert_gate: bfloat16 [4, 2048, 1024], P(None, None, 'shard'), may hold values from -0.125 to 0.125
- expert_up: bfloat16 [4, 2048, 1024], P(None, None, 'shard'), may hold values from -0.125 to 0.125
- expert_down: bfloat16 [4, 1024, 2048], P(None, 'shard'), may hold values from -0.375 to 0.375
Outputs:
- layer_out: bfloat16 [8192, 2048], P(('dp', 'shard'))
- grad_tokens: float32 [8192, 2048], P(('dp', 'shard'))
- root_means: float32 [3, 8192], P(None, ('dp', 'shard'))
- grad_query: float32 [2048, 2048], P(None, 'shard')
- grad_key: float32 [2048, 2048], P(None, 'shard')
- grad_value: float32 [2048, 2048], P(None, 'shard')
- grad_output: float32 [2048, 2048], P(None, 'shard')
- grad_gains: float32 [4, 2048], P(None, 'shard')
- grad_gate: float32 [4, 2048, 1024], P(None, None, 'shard')
- grad_up: float32 [4, 2048, 1024], P(None, None, 'shard')
- grad_down: float32 [4, 1024, 2048], P(None, 'shard')
The draws below stay inside these ranges and needn't reach their ends.
Inputs may be any that keep to these rules, and one draw needn't show every extreme that they name: `routes`: each row names 2 different experts; among the rows of one device each expert is named by at most 170 rows, and on some devices one expert is named by exactly 170 rows.
All inputs are finite; a program needn't handle non-finite values.
Results may differ from the reference program's by a relative error of at most 0.023.
Values may be sent and summed in bfloat16 or wider, within the bound.
A program may use at most 384 MiB of HBM per device.

```python
import math
import jax
import jax.numpy as jnp
import numpy as np
from jax import lax

HEADS = 16
HEAD_DIM = 128
FF = 1024
EXPERTS = 4
TOPK = 2
TOK_DEV = 256
D = 2048
CAP = 170
SEQ_LEN = 1024
SEQS = 8
TOKENS = 8192


def with_ends(result, own_key, smallest, largest):
    spot = [jax.random.randint(jax.random.fold_in(own_key, axis), (), 0, length) for axis, length in enumerate(result.shape)]
    main_axis = result.shape.index(max(result.shape))
    beside = spot[:main_axis] + [(spot[main_axis] + 1) % result.shape[main_axis]] + spot[main_axis + 1:]
    return result.at[tuple(spot)].set(smallest).at[tuple(beside)].set(largest)


def block_scale(key, extent, cuts, smallest, largest):
    def one(position, parts):
        draws = jax.random.uniform(jax.random.fold_in(jax.random.fold_in(key, 6), position), (parts,), jnp.float32, smallest / len(cuts), largest / len(cuts))
        return jnp.repeat(jnp.exp(draws), extent[position] // parts).reshape((-1,) + (1,) * (len(extent) - position - 1))

    level = one(*cuts[0])
    for cut in cuts[1:]:
        level = level * one(*cut)
    return level


def deal_out(rng, own, number, rows, count, top, limit, skew):
    order = jax.random.permutation(rng, count)
    heavy_load, common = shares(count, rows * top, limit, skew, True), shares(count, rows * top, limit, skew, False)
    places = jnp.arange(count)

    def named(sizes, rotation):
        used = int((sizes > 0).sum())
        fixed = max(1, used // 4)
        passed = fixed + (places - fixed + rotation * (used - fixed)) % max(1, count - fixed)
        return jnp.zeros((count,), jnp.int32).at[order[jnp.where(places < fixed, places, passed)]].set(jnp.asarray(sizes, jnp.int32))

    sizes = jnp.where(number % 4 == 0, named(heavy_load, number // 4), named(common, number - number // 4 - 1))
    mixed = jax.random.permutation(jax.random.fold_in(own, 3), count)
    donor, receiver = mixed[0:count // 2 * 2:2], mixed[1:count // 2 * 2:2]
    room = jnp.minimum(sizes[donor] - 1, limit - sizes[receiver]) // 2
    room = jnp.where((donor == order[0]) | (receiver == order[0]) | (sizes[receiver] == 0), 0, jnp.maximum(room, 0))
    passed = jax.random.randint(jax.random.fold_in(own, 4), (count // 2,), 0, 1 << 20) % (room + 1)
    sizes = sizes.at[donor].add(-passed).at[receiver].add(passed)
    members = jnp.searchsorted(jnp.cumsum(sizes), jnp.arange(rows * top), side="right").astype(jnp.int32)
    listing = members.reshape(top, rows).T
    listing = listing[jax.random.permutation(jax.random.fold_in(own, 1), rows)]
    rotation = jax.random.randint(jax.random.fold_in(own, 2), (rows, 1), 0, top)
    return jnp.take_along_axis(listing, (jnp.arange(top)[None, :] + rotation) % top, axis=1)


def shares(amount, total, bound, lean, full):
    portions = [(1 << 20) // math.isqrt(rank ** lean) + 1 for rank in range(1, amount + 1)]
    largest = bound if full else min(bound, max(-(-total // amount), total * portions[0] // sum(portions)))
    least = 1 if total - largest >= amount - 1 else 0
    given, spare = [largest] + [least] * (amount - 1), total - largest - least * (amount - 1)
    while spare > 0:
        candidates = [i for i in range(1, amount) if given[i] < largest] or [i for i in range(1, amount) if given[i] < bound]
        mass, budget = sum([portions[i] for i in candidates]), spare
        for i in candidates:
            more = min(bound - given[i], max(1, budget * portions[i] // mass), spare)
            given[i] = given[i] + more
            spare = spare - more
    return np.array(given)


def normal_values(rng, extent, scale, limit, cuts=(), kind=jnp.bfloat16):
    result = scale * jax.random.normal(rng, extent, jnp.float32)
    if cuts:
        result = result * block_scale(rng, extent, cuts, -0.22, 0.18)
    return jnp.clip(result, -limit, limit).astype(kind)


def setup_inputs(seed: int = 0) -> dict:
    seeds = jax.random.split(jax.random.key(seed), 14)
    tokens = normal_values(seeds[0], (TOKENS, D), 1.0, 6.0, ((0, 32),))
    out_grad = normal_values(seeds[1], (TOKENS, D), 1.0, 6.0, ((0, 32),))
    routes_keys = jax.random.split(jax.random.fold_in(seeds[2], 1), TOKENS // TOK_DEV)
    routes_turns = jax.random.permutation(jax.random.fold_in(seeds[2], 3), TOKENS // TOK_DEV)
    routes = jax.vmap(lambda own, number: deal_out(jax.random.fold_in(seeds[2], 2), own, number, TOK_DEV, EXPERTS, TOPK, CAP, 1))(routes_keys, routes_turns).reshape((TOKENS, TOPK))
    gate_weights = jnp.clip(0.2 + 0.8 * jax.random.uniform(seeds[3], (TOKENS, TOPK), jnp.float32) ** block_scale(seeds[3], (TOKENS, TOPK), ((0, 32),), -0.2, 0.2), 0.2, 1.0)
    prefix = with_ends(jax.random.randint(seeds[4], (SEQS,), SEQ_LEN // 10, SEQ_LEN // 2 + 1), jax.random.fold_in(seeds[4], 1), SEQ_LEN // 10, (SEQ_LEN // 2 + 1) - 1).astype(jnp.int32)
    query_weight = normal_values(seeds[5], (D, D), D ** -0.5, 0.125, ((1, 4),))
    key_weight = normal_values(seeds[6], (D, D), D ** -0.5, 0.125, ((1, 4),))
    value_weight = normal_values(seeds[7], (D, D), D ** -0.5, 0.125, ((1, 4),))
    output_weight = normal_values(seeds[8], (D, D), (max(D // 256, 1)) ** -0.5, 2.0, ((1, 4),))
    norm_gains = jnp.clip(1.0 + 0.1 * jax.random.normal(seeds[9], (4, D), jnp.float32), 0.5, 1.5).astype(jnp.bfloat16)
    expert_gate = normal_values(seeds[10], (EXPERTS, D, FF), D ** -0.5, 0.125, ((2, 4),))
    expert_up = normal_values(seeds[11], (EXPERTS, D, FF), D ** -0.5, 0.125, ((2, 4),))
    expert_down = normal_values(seeds[12], (EXPERTS, FF, D), (FF // 4) ** -0.5, 0.375, ((1, 4),))
    return {"tokens": tokens, "out_grad": out_grad, "routes": routes, "gate_weights": gate_weights, "prefix": prefix, "query_weight": query_weight, "key_weight": key_weight, "value_weight": value_weight, "output_weight": output_weight, "norm_gains": norm_gains, "expert_gate": expert_gate, "expert_up": expert_up, "expert_down": expert_down}


EPSILON = 1e-05
ROPE_BASE = 10000.0
MASKED = -1e+30

@jax.custom_vjp
def low(v):
    return lax.optimization_barrier(v.astype(jnp.bfloat16)).astype(jnp.float32)

@jax.custom_vjp
def low_back(v):
    return v

def low_keep(v):
    return (low(v), None)

def low_pass(kept, grad):
    return (grad,)

def back_keep(v):
    return (v, None)

def back_low(kept, grad):
    return (low(grad),)
low.defvjp(low_keep, low_pass)
low_back.defvjp(back_keep, back_low)

def matmul_high(left, right):
    return jnp.dot(left, right, precision=lax.Precision.HIGHEST, preferred_element_type=jnp.float32)

def rms_norm(values, gain):
    return values * lax.rsqrt(lax.optimization_barrier(jnp.mean(values * values, axis=-1, keepdims=True)) + EPSILON) * gain

def root_mean(values):
    return jnp.sqrt(lax.optimization_barrier(jnp.mean(values * values, axis=-1)))

def rotary_tables(positions, half_dim):
    inverse = ROPE_BASE ** (-jnp.arange(half_dim, dtype=jnp.float32) / half_dim)
    angles = positions.astype(jnp.float32)[:, None] * inverse[None, :]
    return (jnp.cos(angles), jnp.sin(angles))

def rotate(values, cosine, sine):
    row_count = values.shape[0]
    half_dim = cosine.shape[1]
    halves = values.reshape(row_count, -1, 2, half_dim)
    leading = halves[:, :, 0, :]
    trailing = halves[:, :, 1, :]
    cos_wide = cosine[:, None, :]
    sin_wide = sine[:, None, :]
    turned = jnp.stack([leading * cos_wide - trailing * sin_wide, trailing * cos_wide + leading * sin_wide], axis=2)
    return turned.reshape(row_count, -1)

def split_heads(values):
    return values.reshape(values.shape[0], HEADS, HEAD_DIM).transpose(1, 0, 2)

def layer(inputs, query_weight, key_weight, value_weight, output_weight, norm_gains, expert_gate, expert_up, expert_down, routes, gate_weights, prefix):
    seq_rows = inputs.shape[0]
    positions = jnp.arange(seq_rows, dtype=jnp.int32)
    cosine, sine = rotary_tables(positions, HEAD_DIM // 2)
    normed = low(rms_norm(inputs, norm_gains[0]))
    query_raw = low_back(matmul_high(normed, query_weight))
    key_raw = low_back(matmul_high(normed, key_weight))
    value_raw = low_back(matmul_high(normed, value_weight))
    queries = low(rotate(rms_norm(query_raw, norm_gains[1]), cosine, sine))
    keys = low(rotate(rms_norm(key_raw, norm_gains[2]), cosine, sine))
    values = low(value_raw)
    visible = (positions[None, :] <= positions[:, None]) | (positions[None, :] < prefix)

    def one_head(head_parts):
        head_query, head_key, head_value = head_parts
        scores = low_back(matmul_high(head_query, head_key.T) * HEAD_DIM ** (-0.5))
        scores = jnp.where(visible, scores, MASKED)
        weights = low(jax.nn.softmax(scores, axis=-1))
        return matmul_high(weights, head_value)
    mixed = lax.map(jax.checkpoint(one_head), (split_heads(queries), split_heads(keys), split_heads(values)))
    mixed = low(low_back(mixed.transpose(1, 0, 2).reshape(seq_rows, -1)))
    attended = low_back(matmul_high(mixed, output_weight))
    residual = inputs + attended
    expert_in = low(rms_norm(residual, norm_gains[3]))
    expert_sum = jnp.zeros_like(inputs)
    for expert in range(EXPERTS):
        combine = lax.optimization_barrier(jnp.sum(jnp.where(routes == expert, gate_weights, 0.0), axis=1, keepdims=True))
        gate_part = low_back(matmul_high(expert_in, expert_gate[expert]))
        up_part = low_back(matmul_high(expert_in, expert_up[expert]))
        hidden_units = low(jax.nn.silu(gate_part) * up_part)
        expert_sum = expert_sum + combine * low_back(matmul_high(hidden_units, expert_down[expert]))
    layer_out = residual + expert_sum
    root_means = jnp.stack([root_mean(attended), root_mean(expert_sum), root_mean(layer_out)])
    return (layer_out, root_means)

def reference(tokens, out_grad, routes, gate_weights, prefix, query_weight, key_weight, value_weight, output_weight, norm_gains, expert_gate, expert_up, expert_down):
    params = tuple((weight.astype(jnp.float32) for weight in (query_weight, key_weight, value_weight, output_weight, norm_gains, expert_gate, expert_up, expert_down)))
    width = tokens.shape[1]
    inputs = tokens.astype(jnp.float32).reshape(SEQS, SEQ_LEN, width)
    cotangent = out_grad.astype(jnp.float32).reshape(SEQS, SEQ_LEN, width)
    route_rows = routes.reshape(SEQS, SEQ_LEN, TOPK)
    gate_rows = gate_weights.reshape(SEQS, SEQ_LEN, TOPK)

    def per_sequence(totals, items):
        seq_in, seq_cotangent, seq_routes, seq_gates, seq_prefix = items

        def run_layer(layer_in, *weights):
            return layer(layer_in, *weights, seq_routes, seq_gates, seq_prefix)
        layer_rows, pullback, root_means = jax.vjp(run_layer, seq_in, *params, has_aux=True)
        grads = pullback(seq_cotangent)
        totals = tuple((running + piece_grad for running, piece_grad in zip(totals, grads[1:])))
        return (totals, (layer_rows, grads[0], root_means))
    zeros_start = tuple((jnp.zeros_like(weight) for weight in params))
    totals, (layer_rows, grad_rows, mean_rows) = lax.scan(per_sequence, zeros_start, (inputs, cotangent, route_rows, gate_rows, prefix))
    return (layer_rows.reshape(TOKENS, width).astype(jnp.bfloat16), grad_rows.reshape(TOKENS, width), mean_rows.transpose(1, 0, 2).reshape(3, TOKENS), totals[0], totals[1], totals[2], totals[3], totals[4], totals[5], totals[6], totals[7])
```

```python
import jax
import jax.numpy as jnp
from jax import lax
from jax.sharding import PartitionSpec as P

HEAD_DIM = 128
EPSILON = 1e-05
ROPE_BASE = 10000.0
MASKED = -1e30

f32 = jnp.float32
bf16 = jnp.bfloat16


def rotary_tables(row_count):
    half_dim = HEAD_DIM // 2
    positions = jnp.arange(row_count, dtype=jnp.int32)
    inverse = ROPE_BASE ** (-jnp.arange(half_dim, dtype=f32) / half_dim)
    angles = positions.astype(f32)[:, None] * inverse[None, :]
    return (jnp.cos(angles), jnp.sin(angles))


def rotate(values, cosine, sine):
    row_count = values.shape[0]
    half_dim = cosine.shape[1]
    halves = values.reshape(row_count, -1, 2, half_dim)
    leading = halves[:, :, 0, :]
    trailing = halves[:, :, 1, :]
    cos_wide = cosine[:, None, :]
    sin_wide = sine[:, None, :]
    turned = jnp.stack(
        [leading * cos_wide - trailing * sin_wide, trailing * cos_wide + leading * sin_wide], axis=2
    )
    return turned.reshape(row_count, -1)


def row_factor(values):
    return lax.rsqrt(jnp.mean(values * values, axis=-1, keepdims=True) + EPSILON)


def norm_back(grad_unit, unit_rows, factor):
    return factor * (
        grad_unit - unit_rows * jnp.mean(grad_unit * unit_rows, axis=-1, keepdims=True)
    )


def root_mean(values):
    return jnp.sqrt(jnp.mean(values * values, axis=-1))


def dot(a, b):
    return jnp.dot(a, b, preferred_element_type=f32)


def dot_nt(a, b):
    return lax.dot_general(a, b, (((1,), (1,)), ((), ())), preferred_element_type=f32)


def dot_tn(a, b):
    return lax.dot_general(a, b, (((0,), (0,)), ((), ())), preferred_element_type=f32)


def per_device(
    tokens,
    out_grad,
    routes,
    gate_weights,
    prefix,
    query_weight,
    key_weight,
    value_weight,
    output_weight,
    norm_gains,
    expert_gate,
    expert_up,
    expert_down,
):
    rows, width = tokens.shape
    shards = lax.axis_size("shard")
    groups = lax.axis_size("dp")
    place = lax.axis_index("shard")
    group = lax.axis_index("dp")
    length = rows * shards
    local = width // shards
    heads = local // HEAD_DIM
    experts = expert_gate.shape[0]
    units = expert_gate.shape[2]
    scale = HEAD_DIM ** (-0.5)

    expert_ids = jnp.arange(experts, dtype=jnp.int32)
    weight_own = jnp.sum(
        jnp.where(routes[:, :, None] == expert_ids[None, None, :], gate_weights[:, :, None], 0.0),
        axis=1,
    )
    small = jnp.concatenate(
        [weight_own.reshape(-1), norm_gains[0].astype(f32), norm_gains[3].astype(f32)]
    )
    small_all = lax.all_gather(small, "shard", axis=0)
    combine = small_all[:, : rows * experts].reshape(length, experts)
    gain_in = small_all[:, rows * experts : rows * experts + local].reshape(width)
    gain_expert = small_all[:, rows * experts + local :].reshape(width)
    gain_query = norm_gains[1].astype(f32)
    gain_key = norm_gains[2].astype(f32)

    x_all_b = lax.all_gather(tokens, "shard", axis=0, tiled=True)
    slab = width // groups
    out_slab = lax.dynamic_slice_in_dim(output_weight, group * slab, slab, 0)
    out_slab = lax.all_gather(out_slab, "shard", axis=1, tiled=True)
    full_output = lax.all_gather(out_slab, "dp", axis=0, tiled=True)

    x_all = x_all_b.astype(f32)
    normed = (x_all * row_factor(x_all) * gain_in).astype(bf16)
    query_raw = dot(normed, query_weight)
    key_raw = dot(normed, key_weight)
    values = dot(normed, value_weight).astype(bf16)
    squares = jnp.stack([jnp.sum(query_raw * query_raw, -1), jnp.sum(key_raw * key_raw, -1)])
    squares = lax.psum(squares, "shard")
    factors = lax.rsqrt(squares / width + EPSILON)
    factor_query = factors[0][:, None]
    factor_key = factors[1][:, None]
    unit_query = query_raw * factor_query
    unit_key = key_raw * factor_key
    cosine, sine = rotary_tables(length)
    queries = rotate(unit_query * gain_query, cosine, sine).astype(bf16)
    keys = rotate(unit_key * gain_key, cosine, sine).astype(bf16)

    def split(v):
        return v.reshape(length, heads, HEAD_DIM).transpose(1, 0, 2)

    query_heads, key_heads, value_heads = split(queries), split(keys), split(values)
    positions = jnp.arange(length, dtype=jnp.int32)
    visible = (positions[None, :] <= positions[:, None]) | (positions[None, :] < prefix[0])
    scores = jnp.einsum("hqd,hkd->hqk", query_heads, key_heads, preferred_element_type=f32) * scale
    scores = jnp.where(visible[None], scores, MASKED)
    top = jnp.max(scores, axis=-1, keepdims=True)
    expd = jnp.exp(scores - top)
    total = jnp.sum(expd, axis=-1, keepdims=True)
    probs = expd / total
    mixed = jnp.einsum(
        "hqk,hkd->hqd", probs.astype(bf16), value_heads, preferred_element_type=f32
    )
    mixed_own = mixed.transpose(1, 0, 2).reshape(length, local).astype(bf16)
    mixed_all = lax.all_gather(mixed_own, "shard", axis=1, tiled=True)

    attended = dot(mixed_all, full_output)
    residual = x_all + attended
    factor_res = row_factor(residual)
    expert_in = (residual * factor_res * gain_expert).astype(bf16)

    g_all = lax.all_gather(out_grad, "shard", axis=0, tiled=True)
    gate_flat = expert_gate.transpose(1, 0, 2).reshape(width, experts * units)
    up_flat = expert_up.transpose(1, 0, 2).reshape(width, experts * units)
    down_flat = expert_down.reshape(experts * units, width)
    gate_part = dot(expert_in, gate_flat)
    up_part = dot(expert_in, up_flat)
    sig = jax.nn.sigmoid(gate_part)
    wide = jnp.repeat(combine, units, axis=1)
    hidden = (gate_part * sig * up_part * wide).astype(bf16)
    sum_part = dot(hidden, down_flat)
    expert_sum = lax.psum_scatter(
        sum_part.astype(bf16), "shard", scatter_dimension=0, tiled=True
    ).astype(f32)

    hidden_grad = dot_nt(g_all, down_flat) * wide
    up_grad = (hidden_grad * gate_part * sig).astype(bf16)
    gate_grad = (hidden_grad * up_part * sig * (1.0 + gate_part * (1.0 - sig))).astype(bf16)
    in_part = dot_nt(gate_grad, gate_flat) + dot_nt(up_grad, up_flat)
    in_grad = lax.psum_scatter(
        in_part.astype(bf16), "shard", scatter_dimension=0, tiled=True
    ).astype(f32)
    grad_down = dot_tn(hidden, g_all).reshape(experts, units, width)
    grad_gate = dot_tn(expert_in, gate_grad).reshape(width, experts, units).transpose(1, 0, 2)
    grad_up = dot_tn(expert_in, up_grad).reshape(width, experts, units).transpose(1, 0, 2)

    def own_rows(v):
        return lax.dynamic_slice_in_dim(v, place * rows, rows, 0)

    x_own = tokens.astype(f32)
    g_own = out_grad.astype(f32)
    attended_own = own_rows(attended)
    residual_own = x_own + attended_own
    output = residual_own + expert_sum
    root_means = jnp.stack([root_mean(attended_own), root_mean(expert_sum), root_mean(output)])
    factor_own = own_rows(factor_res)
    unit_res = residual_own * factor_own
    gain_grad_res = jnp.sum(in_grad * unit_res, axis=0)
    residual_grad = g_own + norm_back(in_grad * gain_expert, unit_res, factor_own)
    attended_grad = lax.all_gather(residual_grad.astype(bf16), "shard", axis=0, tiled=True)

    grad_output = dot_tn(
        mixed_all, lax.dynamic_slice_in_dim(attended_grad, place * local, local, 1)
    )
    mixed_grad = dot_nt(
        attended_grad, lax.dynamic_slice_in_dim(full_output, place * local, local, 0)
    ).astype(bf16)
    grad_heads = split(mixed_grad)
    delta = jnp.sum(grad_heads.astype(f32) * mixed, axis=-1, keepdims=True)
    prob_grad = jnp.einsum("hqd,hkd->hqk", grad_heads, value_heads, preferred_element_type=f32)
    score_grad = (probs * (prob_grad - delta)).astype(bf16)
    query_acc = jnp.einsum("hqk,hkd->hqd", score_grad, key_heads, preferred_element_type=f32)
    key_acc = jnp.einsum("hqk,hqd->hkd", score_grad, query_heads, preferred_element_type=f32)
    value_acc = jnp.einsum(
        "hqk,hqd->hkd", probs.astype(bf16), grad_heads, preferred_element_type=f32
    )

    def merge(v):
        return v.transpose(1, 0, 2).reshape(length, local)

    query_norm_grad = rotate(merge(query_acc) * scale, cosine, -sine)
    key_norm_grad = rotate(merge(key_acc) * scale, cosine, -sine)
    value_raw_grad = merge(value_acc).astype(bf16)
    gain_grad_query = jnp.sum(query_norm_grad * unit_query, axis=0)
    gain_grad_key = jnp.sum(key_norm_grad * unit_key, axis=0)
    query_norm_grad = query_norm_grad * gain_query
    key_norm_grad = key_norm_grad * gain_key
    inner = jnp.stack(
        [jnp.sum(query_norm_grad * unit_query, -1), jnp.sum(key_norm_grad * unit_key, -1)]
    )
    inner = lax.psum(inner, "shard") / width
    query_raw_grad = (factor_query * (query_norm_grad - unit_query * inner[0][:, None])).astype(
        bf16
    )
    key_raw_grad = (factor_key * (key_norm_grad - unit_key * inner[1][:, None])).astype(bf16)
    normed_part = (
        dot_nt(query_raw_grad, query_weight)
        + dot_nt(key_raw_grad, key_weight)
        + dot_nt(value_raw_grad, value_weight)
    )
    normed_grad = lax.psum_scatter(
        normed_part.astype(bf16), "shard", scatter_dimension=0, tiled=True
    ).astype(f32)
    grad_query = dot_tn(normed, query_raw_grad)
    grad_key = dot_tn(normed, key_raw_grad)
    grad_value = dot_tn(normed, value_raw_grad)

    factor_x = row_factor(x_own)
    unit_x = x_own * factor_x
    gain_grad_x = jnp.sum(normed_grad * unit_x, axis=0)
    grad_tokens = residual_grad + norm_back(normed_grad * gain_in, unit_x, factor_x)

    gain_rows = lax.psum_scatter(
        jnp.stack([gain_grad_x, gain_grad_res]), "shard", scatter_dimension=1, tiled=True
    )
    grad_gains = jnp.stack([gain_rows[0], gain_grad_query, gain_grad_key, gain_rows[1]])

    def over_groups(v):
        return lax.psum(v.astype(bf16), "dp").astype(f32)

    return (
        output.astype(bf16),
        grad_tokens,
        root_means,
        over_groups(grad_query),
        over_groups(grad_key),
        over_groups(grad_value),
        over_groups(grad_output),
        lax.psum(grad_gains, "dp"),
        over_groups(grad_gate),
        over_groups(grad_up),
        over_groups(grad_down),
    )


def solution(mesh):
    placed = (
        P(("dp", "shard"), None),
        P(("dp", "shard"), None),
        P(("dp", "shard"), None),
        P(("dp", "shard"), None),
        P("dp"),
        P(None, "shard"),
        P(None, "shard"),
        P(None, "shard"),
        P(None, "shard"),
        P(None, "shard"),
        P(None, None, "shard"),
        P(None, None, "shard"),
        P(None, "shard", None),
    )
    return jax.shard_map(
        per_device,
        mesh=mesh,
        in_specs=placed,
        out_specs=(
            P(("dp", "shard"), None),
            P(("dp", "shard"), None),
            P(None, ("dp", "shard")),
            P(None, "shard"),
            P(None, "shard"),
            P(None, "shard"),
            P(None, "shard"),
            P(None, "shard"),
            P(None, None, "shard"),
            P(None, None, "shard"),
            P(None, "shard", None),
        ),
        check_vma=False,
    )
```

```python
import functools

import jax
import jax.numpy as jnp
from jax import lax
from jax.experimental import pallas as pl
from jax.experimental.pallas import tpu as pltpu
from jax.sharding import PartitionSpec as P

HEAD_DIM = 128
EPSILON = 1e-05
ROPE_BASE = 10000.0
MASKED = -1e30
VMEM_LIMIT = 60 * 2**20

f32 = jnp.float32
bf16 = jnp.bfloat16


def rotary_tables(row_count):
    half_dim = HEAD_DIM // 2
    positions = jnp.arange(row_count, dtype=jnp.int32)
    inverse = ROPE_BASE ** (-jnp.arange(half_dim, dtype=f32) / half_dim)
    angles = positions.astype(f32)[:, None] * inverse[None, :]
    cosine, sine = jnp.cos(angles), jnp.sin(angles)
    return jnp.concatenate([cosine, cosine], 1), jnp.concatenate([-sine, sine], 1)


def row_factor(values):
    return lax.rsqrt(jnp.mean(values * values, axis=-1, keepdims=True) + EPSILON)


def norm_back(grad_unit, unit_rows, factor):
    return factor * (
        grad_unit - unit_rows * jnp.mean(grad_unit * unit_rows, axis=-1, keepdims=True)
    )


def root_mean(values):
    return jnp.sqrt(jnp.mean(values * values, axis=-1))


def dot(a, b):
    return jnp.dot(a, b, preferred_element_type=f32)


def dot_nt(a, b):
    return lax.dot_general(a, b, (((1,), (1,)), ((), ())), preferred_element_type=f32)


def dot_tn(a, b):
    return lax.dot_general(a, b, (((0,), (0,)), ((), ())), preferred_element_type=f32)


MESH = pl.DeviceIdType.MESH


def greet(peers):
    barrier = pltpu.get_barrier_semaphore()
    for peer in peers:
        pl.semaphore_signal(barrier, inc=1, device_id=peer, device_id_type=MESH)
    pl.semaphore_wait(barrier, len(peers))


def others(n):
    d, z = lax.axis_index("dp"), lax.axis_index("shard")
    return d, z, [(d, lax.rem(z + p, n)) for p in range(1, n)]


def gather_project_kernel(
    n, x_hbm, small_ref, wq_hbm, wk_hbm, wv_hbm,
    x_out, normed_out, q_out, k_out, v_out, small_out, sq_out,
    xs, nb, qb, kb, vb, wq, wk, wv, sq_all, small_all,
    load_sem, out_sem, up_sem, down_sem, recv_sem, small_send, small_recv, sq_send, sq_recv,
):
    T, D = xs.shape[1:]
    C = qb.shape[2]
    d, z, peers = others(n)
    own_load = pltpu.make_async_copy(x_hbm, xs.at[z], load_sem.at[0])
    own_load.start()
    loads = [
        pltpu.make_async_copy(src, dst, load_sem.at[i + 1])
        for i, (src, dst) in enumerate(((wq_hbm, wq), (wk_hbm, wk), (wv_hbm, wv)))
    ]
    for load in loads:
        load.start()
    greet(peers)

    def send_up(o):
        return pltpu.make_async_remote_copy(
            src_ref=xs.at[o], dst_ref=xs.at[o], send_sem=up_sem.at[o], recv_sem=recv_sem.at[o],
            device_id=(d, lax.rem(z + 1, n)), device_id_type=MESH,
        )

    def send_down(o):
        return pltpu.make_async_remote_copy(
            src_ref=xs.at[o], dst_ref=xs.at[o], send_sem=down_sem.at[o], recv_sem=recv_sem.at[o],
            device_id=(d, lax.rem(z + n - 1, n)), device_id_type=MESH,
        )

    own_load.wait()
    small_copies = []
    for p, peer in enumerate(peers):
        copy = pltpu.make_async_remote_copy(
            src_ref=small_ref, dst_ref=small_all.at[z], send_sem=small_send.at[p],
            recv_sem=small_recv.at[z], device_id=peer, device_id_type=MESH,
        )
        copy.start()
        small_copies.append(copy)

    @pl.when(z < n - 1)
    def _():
        send_up(z).start()

    @pl.when(z > 0)
    def _():
        send_down(z).start()

    small_all[z] = small_ref[...]
    for load in loads:
        load.wait()
    for p in range(1, n):
        o = lax.rem(z + n - p, n)
        pltpu.make_async_remote_copy(
            src_ref=small_ref, dst_ref=small_all.at[o], send_sem=small_send.at[p - 1],
            recv_sem=small_recv.at[o], device_id=(d, o), device_id_type=MESH,
        ).wait_recv()

    lanes = lax.broadcasted_iota(jnp.int32, (T, 128), 1)
    step_rows = 32

    def outs(o):
        return [
            pltpu.make_async_copy(src.at[o], dst.at[o], out_sem.at[i, o])
            for i, (src, dst) in enumerate(
                ((xs, x_out), (nb, normed_out), (qb, q_out), (kb, k_out), (vb, v_out))
            )
        ]

    def compute(o):
        gain = jnp.concatenate([small_all[s, 0:1, T:] for s in range(n)], axis=1)

        def norm_rows(i, carry):
            r = pl.ds(pl.multiple_of(i * step_rows, step_rows), step_rows)
            x = xs[o, r, :].astype(f32)
            factor = lax.rsqrt(jnp.sum(x * x, axis=1, keepdims=True) / D + EPSILON)
            nb[o, r, :] = (x * factor * gain).astype(bf16)
            return carry

        lax.fori_loop(0, T // step_rows, norm_rows, 0)
        q = jnp.dot(nb[o], wq[...], preferred_element_type=f32)
        qb[o] = q
        q_sum = jnp.sum(q * q, axis=1, keepdims=True)
        k = jnp.dot(nb[o], wk[...], preferred_element_type=f32)
        kb[o] = k
        k_sum = jnp.sum(k * k, axis=1, keepdims=True)
        vb[o] = jnp.dot(nb[o], wv[...], preferred_element_type=f32).astype(bf16)
        both = jnp.where(lanes == 0, q_sum, jnp.where(lanes == 1, k_sum, 0.0))
        sq_all[z, o] = both.T[0:8]
        for copy in outs(o):
            copy.start()

    def step(s, carry):
        below, above = z - s, z + s

        @pl.when((s > 0) & (below >= 0))
        def _():
            send_up(below).wait_recv()

            @pl.when(z < n - 1)
            def _():
                send_up(below).start()

        @pl.when((s > 0) & (above < n))
        def _():
            send_down(above).wait_recv()

            @pl.when(z > 0)
            def _():
                send_down(above).start()

        def side(j, inner):
            o = z - s + 2 * s * j

            @pl.when((o >= 0) & (o < n) & ((s > 0) | (j == 0)))
            def _():
                compute(o)

            return inner

        lax.fori_loop(0, 2, side, 0)
        return carry

    lax.fori_loop(0, n, step, 0)

    sq_copies = []
    for p, peer in enumerate(peers):
        copy = pltpu.make_async_remote_copy(
            src_ref=sq_all.at[z], dst_ref=sq_all.at[z], send_sem=sq_send.at[p],
            recv_sem=sq_recv.at[z], device_id=peer, device_id_type=MESH,
        )
        copy.start()
        sq_copies.append(copy)
    small_out[...] = small_all[...]

    def finish(o, carry):
        for copy in outs(o):
            copy.wait()

        @pl.when((z < n - 1) & (o <= z))
        def _():
            send_up(o).wait_send()

        @pl.when((z > 0) & (o >= z))
        def _():
            send_down(o).wait_send()

        return carry

    lax.fori_loop(0, n, finish, 0)
    for p in range(1, n):
        o = lax.rem(z + n - p, n)
        pltpu.make_async_remote_copy(
            src_ref=sq_all.at[o], dst_ref=sq_all.at[o], send_sem=sq_send.at[p - 1],
            recv_sem=sq_recv.at[o], device_id=(d, o), device_id_type=MESH,
        ).wait_recv()
    total = sq_all[0]
    for s in range(1, n):
        total = total + sq_all[s]
    sq_out[...] = total
    for copy in small_copies + sq_copies:
        copy.wait_send()


def gather_project(n, tokens, small, wq, wk, wv):
    T, D = tokens.shape
    C = wq.shape[1]
    hbm = pl.BlockSpec(memory_space=pl.ANY)
    vmem = pl.BlockSpec(memory_space=pltpu.VMEM)
    dma = pltpu.SemaphoreType.DMA
    return pl.pallas_call(
        functools.partial(gather_project_kernel, n),
        out_shape=[
            jax.ShapeDtypeStruct((n, T, D), bf16),
            jax.ShapeDtypeStruct((n, T, D), bf16),
            jax.ShapeDtypeStruct((n, T, C), f32),
            jax.ShapeDtypeStruct((n, T, C), f32),
            jax.ShapeDtypeStruct((n, T, C), bf16),
            jax.ShapeDtypeStruct((n,) + small.shape, f32),
            jax.ShapeDtypeStruct((n, 8, T), f32),
        ],
        in_specs=[hbm, vmem, hbm, hbm, hbm],
        out_specs=[hbm] * 5 + [vmem] * 2,
        scratch_shapes=[
            pltpu.VMEM((n, T, D), bf16),
            pltpu.VMEM((n, T, D), bf16),
            pltpu.VMEM((n, T, C), f32),
            pltpu.VMEM((n, T, C), f32),
            pltpu.VMEM((n, T, C), bf16),
            pltpu.VMEM((D, C), bf16),
            pltpu.VMEM((D, C), bf16),
            pltpu.VMEM((D, C), bf16),
            pltpu.VMEM((n, n, 8, T), f32),
            pltpu.VMEM((n,) + small.shape, f32),
            dma((4,)),
            dma((5, n)),
            dma((n,)),
            dma((n,)),
            dma((n,)),
            dma((n,)),
            dma((n,)),
            dma((n,)),
            dma((n,)),
        ],
        compiler_params=pltpu.CompilerParams(
            collective_id=0, has_side_effects=True, vmem_limit_bytes=VMEM_LIMIT
        ),
        name="gather_project",
    )(tokens, small, wq, wk, wv)


def rope(v, cosine, sine):
    return v * cosine + pltpu.roll(v, HEAD_DIM // 2, 1) * sine


def key_span(i, block, length):
    return min(length, max((i + 1) * block, length // 2))


def block_scores(q, k, i, block, limit):
    s = dot_nt(q, k) * (HEAD_DIM**-0.5)
    row = lax.broadcasted_iota(jnp.int32, s.shape, 0) + i * block
    col = lax.broadcasted_iota(jnp.int32, s.shape, 1)
    return jnp.where((col <= row) | (col < limit), s, MASKED)


def attention_kernel(prefix, q_raw, k_raw, v_ref, factors, cosine, sine, gains, q_out, k_out, mixed):
    length = q_raw.shape[0]
    block = 256
    limit = prefix[0]

    def turn(raw, out, column, gain):
        def part(i, carry):
            r = pl.ds(pl.multiple_of(i * block, block), block)
            v = raw[r, :] * factors[r, column : column + 1] * gain
            out[r, :] = rope(v, cosine[r, :], sine[r, :]).astype(bf16)
            return carry

        lax.fori_loop(0, length // block, part, 0)

    turn(q_raw, q_out, 0, gains[0:1, :])
    turn(k_raw, k_out, 1, gains[1:2, :])
    for i in range(length // block):
        span = key_span(i, block, length)
        r = pl.ds(i * block, block)
        s = block_scores(q_out[r, :], k_out[0:span, :], i, block, limit)
        e = jnp.exp(s - jnp.max(s, axis=1, keepdims=True))
        total = jnp.sum(e, axis=1, keepdims=True)
        mixed[r, :] = (dot(e.astype(bf16), v_ref[0:span, :]) / total).astype(bf16)


def attention(prefix, q_raw, k_raw, values, factors, cosine, sine, gains):
    length, local = q_raw.shape
    heads = local // HEAD_DIM
    head = pl.BlockSpec((length, HEAD_DIM), lambda h, p: (0, h))
    whole = lambda a: pl.BlockSpec(a.shape, lambda h, p: (0, 0))
    out = jax.ShapeDtypeStruct((length, local), bf16)
    return pl.pallas_call(
        attention_kernel,
        out_shape=[out] * 3,
        grid_spec=pltpu.PrefetchScalarGridSpec(
            num_scalar_prefetch=1,
            grid=(heads,),
            in_specs=[
                head, head, head, whole(factors), whole(cosine), whole(sine),
                pl.BlockSpec((2, HEAD_DIM), lambda h, p: (0, h)),
            ],
            out_specs=[head] * 3,
        ),
        compiler_params=pltpu.CompilerParams(vmem_limit_bytes=VMEM_LIMIT),
        name="attention",
    )(prefix, q_raw, k_raw, values, factors, cosine, sine, gains)


def attention_back_kernel(
    prefix, q_ref, k_ref, v_ref, g_ref, q_raw, k_raw, factors, cosine, sine, gains,
    dq_out, dk_out, dv_out, gain_out, inner_out, k_acc, v_acc, inner_acc,
):
    length = q_ref.shape[0]
    block = 256
    limit = prefix[0]
    scale = HEAD_DIM**-0.5
    h = pl.program_id(0)
    k_acc[...] = jnp.zeros_like(k_acc)
    v_acc[...] = jnp.zeros_like(v_acc)

    @pl.when(h == 0)
    def _():
        inner_acc[...] = jnp.zeros_like(inner_acc)

    for i in range(length // block):
        span = key_span(i, block, length)
        r = pl.ds(i * block, block)
        q, g = q_ref[r, :], g_ref[r, :]
        s = block_scores(q, k_ref[0:span, :], i, block, limit)
        e = jnp.exp(s - jnp.max(s, axis=1, keepdims=True))
        p = e * (1.0 / jnp.sum(e, axis=1, keepdims=True))
        pg = dot_nt(g, v_ref[0:span, :])
        t = p * pg
        ds = (t - p * jnp.sum(t, axis=1, keepdims=True)).astype(bf16)
        dq_out[r, :] = dot(ds, k_ref[0:span, :]) * scale
        k_acc[0:span, :] += dot_tn(ds, q) * scale
        v_acc[0:span, :] += dot_tn(p.astype(bf16), g)
    dv_out[...] = v_acc[...].astype(bf16)
    lanes = lax.broadcasted_iota(jnp.int32, (block, 128), 1)

    def back(i, carry):
        gq, gk = carry
        r = pl.ds(pl.multiple_of(i * block, block), block)
        c, s = cosine[r, :], sine[r, :]
        dq = rope(dq_out[r, :], c, -s)
        dk = rope(k_acc[r, :], c, -s)
        uq = q_raw[r, :] * factors[r, 0:1]
        uk = k_raw[r, :] * factors[r, 1:2]
        gq = gq + jnp.sum(dq * uq, axis=0, keepdims=True)
        gk = gk + jnp.sum(dk * uk, axis=0, keepdims=True)
        dq = dq * gains[0:1, :]
        dk = dk * gains[1:2, :]
        dq_out[r, :] = dq
        dk_out[r, :] = dk
        inner_q = jnp.sum(dq * uq, axis=1, keepdims=True)
        inner_k = jnp.sum(dk * uk, axis=1, keepdims=True)
        both = jnp.where(lanes == 0, inner_q, jnp.where(lanes == 1, inner_k, 0.0))
        inner_acc[i] += both.T[0:8]
        return gq, gk

    zero = jnp.zeros((1, HEAD_DIM), f32)
    gq, gk = lax.fori_loop(0, length // block, back, (zero, zero))
    gain_out[0:1, :] = gq
    gain_out[1:2, :] = gk

    @pl.when(h == pl.num_programs(0) - 1)
    def _():
        inner_out[...] = inner_acc[...]


def attention_back(prefix, q, k, v, g, q_raw, k_raw, factors, cosine, sine, gains):
    length, local = q.shape
    heads = local // HEAD_DIM
    head = pl.BlockSpec((length, HEAD_DIM), lambda h, p: (0, h))
    pair = pl.BlockSpec((2, HEAD_DIM), lambda h, p: (0, h))
    whole = lambda a: pl.BlockSpec(a.shape, lambda h, p: (0, 0))
    wide = jax.ShapeDtypeStruct((length, local), f32)
    inner = (length // 256, 8, 256)
    return pl.pallas_call(
        attention_back_kernel,
        out_shape=[
            wide, wide, jax.ShapeDtypeStruct((length, local), bf16),
            jax.ShapeDtypeStruct((2, local), f32), jax.ShapeDtypeStruct(inner, f32),
        ],
        grid_spec=pltpu.PrefetchScalarGridSpec(
            num_scalar_prefetch=1,
            grid=(heads,),
            in_specs=[head] * 6 + [whole(factors), whole(cosine), whole(sine), pair],
            out_specs=[head, head, head, pair, pl.BlockSpec(inner, lambda h, p: (0, 0, 0))],
            scratch_shapes=[
                pltpu.VMEM((length, HEAD_DIM), f32),
                pltpu.VMEM((length, HEAD_DIM), f32),
                pltpu.VMEM(inner, f32),
            ],
        ),
        compiler_params=pltpu.CompilerParams(vmem_limit_bytes=VMEM_LIMIT),
        name="attention_back",
    )(prefix, q, k, v, g, q_raw, k_raw, factors, cosine, sine, gains)


def per_device(
    tokens,
    out_grad,
    routes,
    gate_weights,
    prefix,
    query_weight,
    key_weight,
    value_weight,
    output_weight,
    norm_gains,
    expert_gate,
    expert_up,
    expert_down,
):
    rows, width = tokens.shape
    shards = lax.axis_size("shard")
    groups = lax.axis_size("dp")
    place = lax.axis_index("shard")
    group = lax.axis_index("dp")
    length = rows * shards
    local = width // shards
    experts = expert_gate.shape[0]
    units = expert_gate.shape[2]

    expert_ids = jnp.arange(experts, dtype=jnp.int32)
    weight_own = jnp.sum(
        jnp.where(routes[:, :, None] == expert_ids[None, None, :], gate_weights[:, :, None], 0.0),
        axis=1,
    )
    own_gains = norm_gains.astype(f32)
    small = jnp.concatenate(
        [
            jnp.pad(weight_own.T, ((0, 8 - experts), (0, 0))),
            jnp.pad(jnp.stack([own_gains[0], own_gains[3]]), ((0, 6), (0, 0))),
        ],
        axis=1,
    )
    x_all_b, normed, query_raw, key_raw, values, small_all, squares = gather_project(
        shards, tokens, small, query_weight, key_weight, value_weight
    )
    x_all_b = x_all_b.reshape(length, width)
    normed = normed.reshape(length, width)
    query_raw = query_raw.reshape(length, local)
    key_raw = key_raw.reshape(length, local)
    values = values.reshape(length, local)
    combine = small_all[:, :experts, :rows].transpose(0, 2, 1).reshape(length, experts)
    gain_in = small_all[:, 0, rows:].reshape(width)
    gain_expert = small_all[:, 1, rows:].reshape(width)
    head_gains = own_gains[1:3]
    slab = width // groups
    output_weight, out_grad_b, squares = lax.optimization_barrier(
        (output_weight, out_grad, squares)
    )
    out_slab = lax.dynamic_slice_in_dim(output_weight, group * slab, slab, 0)
    out_slab = lax.all_gather(out_slab, "shard", axis=1, tiled=True)
    full_output = lax.all_gather(out_slab, "dp", axis=0, tiled=True)

    x_all = x_all_b.astype(f32)
    factors = lax.rsqrt(squares[:, :2].transpose(0, 2, 1).reshape(length, 2) / width + EPSILON)
    cosine, sine = rotary_tables(length)
    queries, keys, mixed_own = attention(
        prefix, query_raw, key_raw, values, factors, cosine, sine, head_gains
    )
    mixed_all = lax.all_gather(mixed_own, "shard", axis=1, tiled=True)

    attended = dot(mixed_all, full_output)
    residual = x_all + attended
    factor_res = row_factor(residual)
    expert_in = (residual * factor_res * gain_expert).astype(bf16)

    g_all = lax.all_gather(out_grad_b, "shard", axis=0, tiled=True)
    gate_flat = expert_gate.transpose(1, 0, 2).reshape(width, experts * units)
    up_flat = expert_up.transpose(1, 0, 2).reshape(width, experts * units)
    down_flat = expert_down.reshape(experts * units, width)
    gate_part = dot(expert_in, gate_flat)
    up_part = dot(expert_in, up_flat)
    sig = jax.nn.sigmoid(gate_part)
    wide = jnp.repeat(combine, units, axis=1)
    hidden = (gate_part * sig * up_part * wide).astype(bf16)
    sum_part = dot(hidden, down_flat)
    expert_sum = lax.psum_scatter(
        sum_part.astype(bf16), "shard", scatter_dimension=0, tiled=True
    ).astype(f32)

    hidden_grad = dot_nt(g_all, down_flat) * wide
    up_grad = (hidden_grad * gate_part * sig).astype(bf16)
    gate_grad = (hidden_grad * up_part * sig * (1.0 + gate_part * (1.0 - sig))).astype(bf16)
    in_part = dot_nt(gate_grad, gate_flat) + dot_nt(up_grad, up_flat)
    in_grad = lax.psum_scatter(
        in_part.astype(bf16), "shard", scatter_dimension=0, tiled=True
    ).astype(f32)
    grad_down = dot_tn(hidden, g_all).reshape(experts, units, width)
    grad_gate = dot_tn(expert_in, gate_grad).reshape(width, experts, units).transpose(1, 0, 2)
    grad_up = dot_tn(expert_in, up_grad).reshape(width, experts, units).transpose(1, 0, 2)

    grad_gate, grad_up, grad_down = lax.psum(
        (grad_gate.astype(bf16), grad_up.astype(bf16), grad_down.astype(bf16)), "dp"
    )

    def own_rows(v):
        return lax.dynamic_slice_in_dim(v, place * rows, rows, 0)

    x_own = tokens.astype(f32)
    g_own = out_grad.astype(f32)
    attended_own = own_rows(attended)
    residual_own = x_own + attended_own
    output = residual_own + expert_sum
    root_means = jnp.stack([root_mean(attended_own), root_mean(expert_sum), root_mean(output)])
    factor_own = own_rows(factor_res)
    unit_res = residual_own * factor_own
    gain_grad_res = jnp.sum(in_grad * unit_res, axis=0)
    residual_grad = g_own + norm_back(in_grad * gain_expert, unit_res, factor_own)
    attended_grad = lax.all_gather(residual_grad.astype(bf16), "shard", axis=0, tiled=True)

    grad_output = dot_tn(
        mixed_all, lax.dynamic_slice_in_dim(attended_grad, place * local, local, 1)
    )
    mixed_grad = dot_nt(
        attended_grad, lax.dynamic_slice_in_dim(full_output, place * local, local, 0)
    ).astype(bf16)
    query_norm_grad, key_norm_grad, value_raw_grad, gain_grad_heads, inner = attention_back(
        prefix, queries, keys, values, mixed_grad, query_raw, key_raw, factors, cosine, sine,
        head_gains,
    )
    inner = lax.psum(inner[:, :2], "shard") / width
    inner = inner.transpose(0, 2, 1).reshape(length, 2)
    factor_query, factor_key = factors[:, 0:1], factors[:, 1:2]
    query_raw_grad = (
        factor_query * (query_norm_grad - query_raw * factor_query * inner[:, 0:1])
    ).astype(bf16)
    key_raw_grad = (factor_key * (key_norm_grad - key_raw * factor_key * inner[:, 1:2])).astype(
        bf16
    )
    normed_part = (
        dot_nt(query_raw_grad, query_weight)
        + dot_nt(key_raw_grad, key_weight)
        + dot_nt(value_raw_grad, value_weight)
    )
    normed_grad = lax.psum_scatter(
        normed_part.astype(bf16), "shard", scatter_dimension=0, tiled=True
    ).astype(f32)
    grad_query = dot_tn(normed, query_raw_grad)
    grad_key = dot_tn(normed, key_raw_grad)
    grad_value = dot_tn(normed, value_raw_grad)

    factor_x = row_factor(x_own)
    unit_x = x_own * factor_x
    gain_grad_x = jnp.sum(normed_grad * unit_x, axis=0)
    grad_tokens = residual_grad + norm_back(normed_grad * gain_in, unit_x, factor_x)

    gain_rows = lax.psum_scatter(
        jnp.stack([gain_grad_x, gain_grad_res]), "shard", scatter_dimension=1, tiled=True
    )
    grad_gains = jnp.stack([gain_rows[0], gain_grad_heads[0], gain_grad_heads[1], gain_rows[1]])

    (grad_query, grad_key, grad_value, grad_output), grad_gate, grad_up, grad_down = (
        lax.optimization_barrier(
            (
                tuple(v.astype(bf16) for v in (grad_query, grad_key, grad_value, grad_output)),
                grad_gate,
                grad_up,
                grad_down,
            )
        )
    )
    grad_query, grad_key, grad_value, grad_output = lax.psum(
        (grad_query, grad_key, grad_value, grad_output), "dp"
    )

    return (
        output.astype(bf16),
        grad_tokens,
        root_means,
        grad_query.astype(f32),
        grad_key.astype(f32),
        grad_value.astype(f32),
        grad_output.astype(f32),
        lax.psum(grad_gains, "dp"),
        grad_gate.astype(f32),
        grad_up.astype(f32),
        grad_down.astype(f32),
    )


def solution(mesh):
    placed = (
        P(("dp", "shard"), None),
        P(("dp", "shard"), None),
        P(("dp", "shard"), None),
        P(("dp", "shard"), None),
        P("dp"),
        P(None, "shard"),
        P(None, "shard"),
        P(None, "shard"),
        P(None, "shard"),
        P(None, "shard"),
        P(None, None, "shard"),
        P(None, None, "shard"),
        P(None, "shard", None),
    )
    return jax.shard_map(
        per_device,
        mesh=mesh,
        in_specs=placed,
        out_specs=(
            P(("dp", "shard"), None),
            P(("dp", "shard"), None),
            P(None, ("dp", "shard")),
            P(None, "shard"),
            P(None, "shard"),
            P(None, "shard"),
            P(None, "shard"),
            P(None, "shard"),
            P(None, None, "shard"),
            P(None, None, "shard"),
            P(None, "shard", None),
        ),
        check_vma=False,
    )
```

```python
import functools

import jax
import jax.numpy as jnp
from jax import lax
from jax.experimental import pallas as pl
from jax.experimental.pallas import tpu as pltpu
from jax.sharding import PartitionSpec as P

HEAD_DIM = 128
EPSILON = 1e-05
ROPE_BASE = 10000.0
MASKED = -1e30
VMEM_LIMIT = 60 * 2**20

f32 = jnp.float32
bf16 = jnp.bfloat16


def rotary_tables(row_count):
    half_dim = HEAD_DIM // 2
    positions = jnp.arange(row_count, dtype=jnp.int32)
    inverse = ROPE_BASE ** (-jnp.arange(half_dim, dtype=f32) / half_dim)
    angles = positions.astype(f32)[:, None] * inverse[None, :]
    cosine, sine = jnp.cos(angles), jnp.sin(angles)
    return jnp.concatenate([cosine, cosine], 1), jnp.concatenate([-sine, sine], 1)


def row_factor(values):
    return lax.rsqrt(jnp.mean(values * values, axis=-1, keepdims=True) + EPSILON)


def norm_back(grad_unit, unit_rows, factor):
    return factor * (
        grad_unit - unit_rows * jnp.mean(grad_unit * unit_rows, axis=-1, keepdims=True)
    )


def root_mean(values):
    return jnp.sqrt(jnp.mean(values * values, axis=-1))


def dot(a, b):
    return jnp.dot(a, b, preferred_element_type=f32)


def dot_nt(a, b):
    return lax.dot_general(a, b, (((1,), (1,)), ((), ())), preferred_element_type=f32)


def dot_tn(a, b):
    return lax.dot_general(a, b, (((0,), (0,)), ((), ())), preferred_element_type=f32)


MESH = pl.DeviceIdType.MESH


def greet(peers):
    barrier = pltpu.get_barrier_semaphore()
    for peer in peers:
        pl.semaphore_signal(barrier, inc=1, device_id=peer, device_id_type=MESH)
    pl.semaphore_wait(barrier, len(peers))


def others(n):
    d, z = lax.axis_index("dp"), lax.axis_index("shard")
    return d, z, [(d, lax.rem(z + p, n)) for p in range(1, n)]


def gather_project_kernel(
    n, x_hbm, small_ref, wq_hbm, wk_hbm, wv_hbm,
    x_out, normed_out, q_out, k_out, v_out, small_out, sq_out,
    xs, nb, qb, kb, vb, wq, wk, wv, sq_all, small_all,
    load_sem, out_sem, up_sem, down_sem, recv_sem, small_send, small_recv, sq_send, sq_recv,
):
    T, D = xs.shape[1:]
    C = qb.shape[2]
    d, z, peers = others(n)
    own_load = pltpu.make_async_copy(x_hbm, xs.at[z], load_sem.at[0])
    own_load.start()
    loads = [
        pltpu.make_async_copy(src, dst, load_sem.at[i + 1])
        for i, (src, dst) in enumerate(((wq_hbm, wq), (wk_hbm, wk), (wv_hbm, wv)))
    ]
    for load in loads:
        load.start()
    greet(peers)

    def send_up(o):
        return pltpu.make_async_remote_copy(
            src_ref=xs.at[o], dst_ref=xs.at[o], send_sem=up_sem.at[o], recv_sem=recv_sem.at[o],
            device_id=(d, lax.rem(z + 1, n)), device_id_type=MESH,
        )

    def send_down(o):
        return pltpu.make_async_remote_copy(
            src_ref=xs.at[o], dst_ref=xs.at[o], send_sem=down_sem.at[o], recv_sem=recv_sem.at[o],
            device_id=(d, lax.rem(z + n - 1, n)), device_id_type=MESH,
        )

    own_load.wait()
    small_copies = []
    for p, peer in enumerate(peers):
        copy = pltpu.make_async_remote_copy(
            src_ref=small_ref, dst_ref=small_all.at[z], send_sem=small_send.at[p],
            recv_sem=small_recv.at[z], device_id=peer, device_id_type=MESH,
        )
        copy.start()
        small_copies.append(copy)

    @pl.when(z < n - 1)
    def _():
        send_up(z).start()

    @pl.when(z > 0)
    def _():
        send_down(z).start()

    small_all[z] = small_ref[...]
    for load in loads:
        load.wait()
    for p in range(1, n):
        o = lax.rem(z + n - p, n)
        pltpu.make_async_remote_copy(
            src_ref=small_ref, dst_ref=small_all.at[o], send_sem=small_send.at[p - 1],
            recv_sem=small_recv.at[o], device_id=(d, o), device_id_type=MESH,
        ).wait_recv()

    lanes = lax.broadcasted_iota(jnp.int32, (T, 128), 1)
    step_rows = 32

    def outs(o):
        return [
            pltpu.make_async_copy(src.at[o], dst.at[o], out_sem.at[i, o])
            for i, (src, dst) in enumerate(
                ((xs, x_out), (nb, normed_out), (qb, q_out), (kb, k_out), (vb, v_out))
            )
        ]

    def compute(o):
        gain = jnp.concatenate([small_all[s, 0:1, T:] for s in range(n)], axis=1)

        def norm_rows(i, carry):
            r = pl.ds(pl.multiple_of(i * step_rows, step_rows), step_rows)
            x = xs[o, r, :].astype(f32)
            factor = lax.rsqrt(jnp.sum(x * x, axis=1, keepdims=True) / D + EPSILON)
            nb[o, r, :] = (x * factor * gain).astype(bf16)
            return carry

        lax.fori_loop(0, T // step_rows, norm_rows, 0)
        q = jnp.dot(nb[o], wq[...], preferred_element_type=f32)
        qb[o] = q
        q_sum = jnp.sum(q * q, axis=1, keepdims=True)
        k = jnp.dot(nb[o], wk[...], preferred_element_type=f32)
        kb[o] = k
        k_sum = jnp.sum(k * k, axis=1, keepdims=True)
        vb[o] = jnp.dot(nb[o], wv[...], preferred_element_type=f32).astype(bf16)
        both = jnp.where(lanes == 0, q_sum, jnp.where(lanes == 1, k_sum, 0.0))
        sq_all[z, o] = both.T[0:8]
        for copy in outs(o):
            copy.start()

    def step(s, carry):
        below, above = z - s, z + s

        @pl.when((s > 0) & (below >= 0))
        def _():
            send_up(below).wait_recv()

            @pl.when(z < n - 1)
            def _():
                send_up(below).start()

        @pl.when((s > 0) & (above < n))
        def _():
            send_down(above).wait_recv()

            @pl.when(z > 0)
            def _():
                send_down(above).start()

        def side(j, inner):
            o = z - s + 2 * s * j

            @pl.when((o >= 0) & (o < n) & ((s > 0) | (j == 0)))
            def _():
                compute(o)

            return inner

        lax.fori_loop(0, 2, side, 0)
        return carry

    lax.fori_loop(0, n, step, 0)

    sq_copies = []
    for p, peer in enumerate(peers):
        copy = pltpu.make_async_remote_copy(
            src_ref=sq_all.at[z], dst_ref=sq_all.at[z], send_sem=sq_send.at[p],
            recv_sem=sq_recv.at[z], device_id=peer, device_id_type=MESH,
        )
        copy.start()
        sq_copies.append(copy)
    small_out[...] = small_all[...]

    def finish(o, carry):
        for copy in outs(o):
            copy.wait()

        @pl.when((z < n - 1) & (o <= z))
        def _():
            send_up(o).wait_send()

        @pl.when((z > 0) & (o >= z))
        def _():
            send_down(o).wait_send()

        return carry

    lax.fori_loop(0, n, finish, 0)
    for p in range(1, n):
        o = lax.rem(z + n - p, n)
        pltpu.make_async_remote_copy(
            src_ref=sq_all.at[o], dst_ref=sq_all.at[o], send_sem=sq_send.at[p - 1],
            recv_sem=sq_recv.at[o], device_id=(d, o), device_id_type=MESH,
        ).wait_recv()
    total = sq_all[0]
    for s in range(1, n):
        total = total + sq_all[s]
    sq_out[...] = total
    for copy in small_copies + sq_copies:
        copy.wait_send()


def gather_project(n, tokens, small, wq, wk, wv):
    T, D = tokens.shape
    C = wq.shape[1]
    hbm = pl.BlockSpec(memory_space=pl.ANY)
    vmem = pl.BlockSpec(memory_space=pltpu.VMEM)
    dma = pltpu.SemaphoreType.DMA
    return pl.pallas_call(
        functools.partial(gather_project_kernel, n),
        out_shape=[
            jax.ShapeDtypeStruct((n, T, D), bf16),
            jax.ShapeDtypeStruct((n, T, D), bf16),
            jax.ShapeDtypeStruct((n, T, C), f32),
            jax.ShapeDtypeStruct((n, T, C), f32),
            jax.ShapeDtypeStruct((n, T, C), bf16),
            jax.ShapeDtypeStruct((n,) + small.shape, f32),
            jax.ShapeDtypeStruct((n, 8, T), f32),
        ],
        in_specs=[hbm, vmem, hbm, hbm, hbm],
        out_specs=[hbm] * 5 + [vmem] * 2,
        scratch_shapes=[
            pltpu.VMEM((n, T, D), bf16),
            pltpu.VMEM((n, T, D), bf16),
            pltpu.VMEM((n, T, C), f32),
            pltpu.VMEM((n, T, C), f32),
            pltpu.VMEM((n, T, C), bf16),
            pltpu.VMEM((D, C), bf16),
            pltpu.VMEM((D, C), bf16),
            pltpu.VMEM((D, C), bf16),
            pltpu.VMEM((n, n, 8, T), f32),
            pltpu.VMEM((n,) + small.shape, f32),
            dma((4,)),
            dma((5, n)),
            dma((n,)),
            dma((n,)),
            dma((n,)),
            dma((n,)),
            dma((n,)),
            dma((n,)),
            dma((n,)),
        ],
        compiler_params=pltpu.CompilerParams(
            collective_id=0, has_side_effects=True, vmem_limit_bytes=VMEM_LIMIT
        ),
        cost_estimate=pl.CostEstimate(flops=80 * 10**9, bytes_accessed=32 * 2**20, transcendentals=0),
        name="gather_project",
    )(tokens, small, wq, wk, wv)


def rope(v, cosine, sine):
    return v * cosine + pltpu.roll(v, HEAD_DIM // 2, 1) * sine


def key_span(i, block, length):
    return min(length, max((i + 1) * block, length // 2))


def block_scores(q, k, i, block, limit):
    s = dot_nt(q, k) * (HEAD_DIM**-0.5)
    row = lax.broadcasted_iota(jnp.int32, s.shape, 0) + i * block
    col = lax.broadcasted_iota(jnp.int32, s.shape, 1)
    return jnp.where((col <= row) | (col < limit), s, MASKED)


def attention_kernel(prefix, q_raw, k_raw, v_ref, factors, cosine, sine, gains, q_out, k_out, mixed):
    length = q_raw.shape[0]
    block = 256
    limit = prefix[0]

    def turn(raw, out, column, gain):
        def part(i, carry):
            r = pl.ds(pl.multiple_of(i * block, block), block)
            v = raw[r, :] * factors[r, column : column + 1] * gain
            out[r, :] = rope(v, cosine[r, :], sine[r, :]).astype(bf16)
            return carry

        lax.fori_loop(0, length // block, part, 0)

    turn(q_raw, q_out, 0, gains[0:1, :])
    turn(k_raw, k_out, 1, gains[1:2, :])
    for i in range(length // block):
        span = key_span(i, block, length)
        r = pl.ds(i * block, block)
        s = block_scores(q_out[r, :], k_out[0:span, :], i, block, limit)
        e = jnp.exp(s - jnp.max(s, axis=1, keepdims=True))
        total = jnp.sum(e, axis=1, keepdims=True)
        mixed[r, :] = (dot(e.astype(bf16), v_ref[0:span, :]) / total).astype(bf16)


def attention(prefix, q_raw, k_raw, values, factors, cosine, sine, gains):
    length, local = q_raw.shape
    heads = local // HEAD_DIM
    head = pl.BlockSpec((length, HEAD_DIM), lambda h, p: (0, h))
    whole = lambda a: pl.BlockSpec(a.shape, lambda h, p: (0, 0))
    out = jax.ShapeDtypeStruct((length, local), bf16)
    return pl.pallas_call(
        attention_kernel,
        out_shape=[out] * 3,
        grid_spec=pltpu.PrefetchScalarGridSpec(
            num_scalar_prefetch=1,
            grid=(heads,),
            in_specs=[
                head, head, head, whole(factors), whole(cosine), whole(sine),
                pl.BlockSpec((2, HEAD_DIM), lambda h, p: (0, h)),
            ],
            out_specs=[head] * 3,
        ),
        compiler_params=pltpu.CompilerParams(vmem_limit_bytes=VMEM_LIMIT),
        cost_estimate=pl.CostEstimate(flops=14 * 10**9, bytes_accessed=16 * 2**20, transcendentals=0),
        name="attention",
    )(prefix, q_raw, k_raw, values, factors, cosine, sine, gains)


def attention_back_kernel(
    prefix, q_ref, k_ref, v_ref, g_ref, q_raw, k_raw, factors, cosine, sine, gains,
    dq_out, dk_out, dv_out, gain_out, inner_out, k_acc, v_acc, inner_acc,
):
    length = q_ref.shape[0]
    block = 256
    limit = prefix[0]
    scale = HEAD_DIM**-0.5
    h = pl.program_id(0)
    k_acc[...] = jnp.zeros_like(k_acc)
    v_acc[...] = jnp.zeros_like(v_acc)

    @pl.when(h == 0)
    def _():
        inner_acc[...] = jnp.zeros_like(inner_acc)

    for i in range(length // block):
        span = key_span(i, block, length)
        r = pl.ds(i * block, block)
        q, g = q_ref[r, :], g_ref[r, :]
        s = block_scores(q, k_ref[0:span, :], i, block, limit)
        e = jnp.exp(s - jnp.max(s, axis=1, keepdims=True))
        p = e * (1.0 / jnp.sum(e, axis=1, keepdims=True))
        pg = dot_nt(g, v_ref[0:span, :])
        t = p * pg
        ds = (t - p * jnp.sum(t, axis=1, keepdims=True)).astype(bf16)
        dq_out[r, :] = dot(ds, k_ref[0:span, :]) * scale
        k_acc[0:span, :] += dot_tn(ds, q) * scale
        v_acc[0:span, :] += dot_tn(p.astype(bf16), g)
    dv_out[...] = v_acc[...].astype(bf16)
    lanes = lax.broadcasted_iota(jnp.int32, (block, 128), 1)

    def back(i, carry):
        gq, gk = carry
        r = pl.ds(pl.multiple_of(i * block, block), block)
        c, s = cosine[r, :], sine[r, :]
        dq = rope(dq_out[r, :], c, -s)
        dk = rope(k_acc[r, :], c, -s)
        uq = q_raw[r, :] * factors[r, 0:1]
        uk = k_raw[r, :] * factors[r, 1:2]
        gq = gq + jnp.sum(dq * uq, axis=0, keepdims=True)
        gk = gk + jnp.sum(dk * uk, axis=0, keepdims=True)
        dq = dq * gains[0:1, :]
        dk = dk * gains[1:2, :]
        dq_out[r, :] = dq
        dk_out[r, :] = dk
        inner_q = jnp.sum(dq * uq, axis=1, keepdims=True)
        inner_k = jnp.sum(dk * uk, axis=1, keepdims=True)
        both = jnp.where(lanes == 0, inner_q, jnp.where(lanes == 1, inner_k, 0.0))
        inner_acc[i] += both.T[0:8]
        return gq, gk

    zero = jnp.zeros((1, HEAD_DIM), f32)
    gq, gk = lax.fori_loop(0, length // block, back, (zero, zero))
    gain_out[0:1, :] = gq
    gain_out[1:2, :] = gk

    @pl.when(h == pl.num_programs(0) - 1)
    def _():
        inner_out[...] = inner_acc[...]


def attention_back(prefix, q, k, v, g, q_raw, k_raw, factors, cosine, sine, gains):
    length, local = q.shape
    heads = local // HEAD_DIM
    head = pl.BlockSpec((length, HEAD_DIM), lambda h, p: (0, h))
    pair = pl.BlockSpec((2, HEAD_DIM), lambda h, p: (0, h))
    whole = lambda a: pl.BlockSpec(a.shape, lambda h, p: (0, 0))
    wide = jax.ShapeDtypeStruct((length, local), f32)
    inner = (length // 256, 8, 256)
    return pl.pallas_call(
        attention_back_kernel,
        out_shape=[
            wide, wide, jax.ShapeDtypeStruct((length, local), bf16),
            jax.ShapeDtypeStruct((2, local), f32), jax.ShapeDtypeStruct(inner, f32),
        ],
        grid_spec=pltpu.PrefetchScalarGridSpec(
            num_scalar_prefetch=1,
            grid=(heads,),
            in_specs=[head] * 6 + [whole(factors), whole(cosine), whole(sine), pair],
            out_specs=[head, head, head, pair, pl.BlockSpec(inner, lambda h, p: (0, 0, 0))],
            scratch_shapes=[
                pltpu.VMEM((length, HEAD_DIM), f32),
                pltpu.VMEM((length, HEAD_DIM), f32),
                pltpu.VMEM(inner, f32),
            ],
        ),
        compiler_params=pltpu.CompilerParams(vmem_limit_bytes=VMEM_LIMIT),
        cost_estimate=pl.CostEstimate(flops=2 * 10**9, bytes_accessed=2**20, transcendentals=0),
        name="attention_back",
    )(prefix, q, k, v, g, q_raw, k_raw, factors, cosine, sine, gains)


def scatter_norm_kernel(n, steps, gather, plain, *refs):
    part, refs = refs[0], refs[1:]
    if not plain:
        base, addend, gain = refs[:3]
        refs = refs[3:]
    if gather:
        out, all_out, gain_out = refs[:3]
        refs = refs[3:]
        alls, ag_up, ag_down, ag_recv, all_sem = refs[:5]
        refs = refs[5:]
    elif plain:
        out, refs = refs[0], refs[1:]
    else:
        out, gain_out = refs[:2]
        refs = refs[2:]
    from_below, from_above, gain_acc, up_send, up_recv, down_send, down_recv = refs
    R, D = part.shape[2:]
    d, z, peers = others(n)
    upper, lower = (d, lax.rem(z + 1, n)), (d, lax.rem(z + n - 1, n))
    greet(peers)
    gain_acc[...] = jnp.zeros_like(gain_acc)

    def move_up(src, o, k):
        return pltpu.make_async_remote_copy(
            src_ref=src.at[o, k], dst_ref=from_below.at[o, k], send_sem=up_send.at[o, k],
            recv_sem=up_recv.at[o, k], device_id=upper, device_id_type=MESH,
        )

    def move_down(src, o, k):
        return pltpu.make_async_remote_copy(
            src_ref=src.at[o, k], dst_ref=from_above.at[o, k], send_sem=down_send.at[o, k],
            recv_sem=down_recv.at[o, k], device_id=lower, device_id_type=MESH,
        )

    def all_up(o, k):
        return pltpu.make_async_remote_copy(
            src_ref=alls.at[o, k], dst_ref=alls.at[o, k], send_sem=ag_up.at[o, k],
            recv_sem=ag_recv.at[o, k], device_id=upper, device_id_type=MESH,
        )

    def all_down(o, k):
        return pltpu.make_async_remote_copy(
            src_ref=alls.at[o, k], dst_ref=alls.at[o, k], send_sem=ag_down.at[o, k],
            recv_sem=ag_recv.at[o, k], device_id=lower, device_id_type=MESH,
        )

    def pass_up(k):
        def far(i, carry):
            o = z + n - 1 - i

            @pl.when(o < n)
            def _():
                @pl.when(z == 0)
                def _():
                    move_up(part, o, k).start()

                @pl.when(z > 0)
                def _():
                    move_up(part, o, k).wait_recv()
                    both = from_below[o, k].astype(f32) + part[o, k].astype(f32)
                    from_below[o, k] = both.astype(bf16)
                    move_up(from_below, o, k).start()

            return carry

        lax.fori_loop(0, n - 1, far, 0)

    def pass_down(k):
        def far(i, carry):
            o = z - n + 1 + i

            @pl.when(o >= 0)
            def _():
                @pl.when(z == n - 1)
                def _():
                    move_down(part, o, k).start()

                @pl.when(z < n - 1)
                def _():
                    move_down(part, o, k).wait_recv()
                    both = from_above[o, k].astype(f32) + part[o, k].astype(f32)
                    from_above[o, k] = both.astype(bf16)
                    move_down(from_above, o, k).start()

            return carry

        lax.fori_loop(0, n - 1, far, 0)

    def own(k):
        @pl.when(z > 0)
        def _():
            move_up(part, z, k).wait_recv()

        @pl.when(z == 0)
        def _():
            from_below[z, k] = jnp.zeros((R, D), bf16)

        @pl.when(z < n - 1)
        def _():
            move_down(part, z, k).wait_recv()

        @pl.when(z == n - 1)
        def _():
            from_above[z, k] = jnp.zeros((R, D), bf16)

        total = (
            part[z, k].astype(f32) + from_below[z, k].astype(f32) + from_above[z, k].astype(f32)
        )
        if plain:
            out[k] = total
            return
        rows = base[k].astype(f32)
        factor = lax.rsqrt(jnp.sum(rows * rows, axis=1, keepdims=True) / D + EPSILON)
        unit = rows * factor
        along = total * unit
        gain_acc[...] += jnp.sum(along.reshape(R // 8, 8, D), axis=0)
        weighted = along * gain[...]
        mean = jnp.sum(weighted, axis=1, keepdims=True) / D
        result = addend[k].astype(f32) + factor * (total * gain[...] - unit * mean)
        out[k] = result
        if gather:
            alls[z, k] = result.astype(bf16)

            @pl.when(z < n - 1)
            def _():
                all_up(z, k).start()

            @pl.when(z > 0)
            def _():
                all_down(z, k).start()

    def forward(own_k):
        def hop(s, carry):
            below, above, k = z - s, z + s, own_k - s
            live = (k >= 0) & (k < steps)

            @pl.when(live & (below >= 0))
            def _():
                all_up(below, k).wait_recv()

                @pl.when(z < n - 1)
                def _():
                    all_up(below, k).start()

            @pl.when(live & (above < n))
            def _():
                all_down(above, k).wait_recv()

                @pl.when(z > 0)
                def _():
                    all_down(above, k).start()

            return carry

        lax.fori_loop(1, n, hop, 0)

    def turn(t, carry):
        up_k, down_k, own_k = t - z, t - (n - 1 - z), t - (n - 1)

        @pl.when((up_k >= 0) & (up_k < steps))
        def _():
            pass_up(up_k)

        @pl.when((down_k >= 0) & (down_k < steps))
        def _():
            pass_down(down_k)

        @pl.when((own_k >= 0) & (own_k < steps))
        def _():
            own(own_k)

        if gather:
            forward(own_k)

        return carry

    lax.fori_loop(0, steps + (2 * n - 2 if gather else n - 1), turn, 0)
    if not plain:
        gain_out[...] = gain_acc[...]

    def drain(i, carry):
        o, k = i // steps, i % steps

        @pl.when(o > z)
        def _():
            move_up(part, o, k).wait_send()

        @pl.when(o < z)
        def _():
            move_down(part, o, k).wait_send()

        if gather:

            @pl.when((z < n - 1) & (o <= z))
            def _():
                all_up(o, k).wait_send()

            @pl.when((z > 0) & (o >= z))
            def _():
                all_down(o, k).wait_send()

        return carry

    lax.fori_loop(0, n * steps, drain, 0)
    if gather:
        copies = [pltpu.make_async_copy(alls.at[o], all_out.at[o], all_sem.at[o]) for o in range(n)]
        for copy in copies:
            copy.start()
        for copy in copies:
            copy.wait()


def scatter_norm(n, steps, gather, part, base, addend, gain, collective_id, plain=False):
    T, D = part.shape[0] // n, part.shape[1]
    R = T // steps
    hbm = pl.BlockSpec(memory_space=pl.ANY)
    vmem = pl.BlockSpec(memory_space=pltpu.VMEM)
    dma = pltpu.SemaphoreType.DMA
    slots = pltpu.VMEM((n, steps, R, D), bf16)
    rows = jax.ShapeDtypeStruct((steps, R, D), f32)
    gains = jax.ShapeDtypeStruct((8, D), f32)
    sems = dma((n, steps))
    results = pl.pallas_call(
        functools.partial(scatter_norm_kernel, n, steps, gather, plain),
        out_shape=[rows]
        + ([jax.ShapeDtypeStruct((n, steps, R, D), bf16)] if gather else [])
        + ([] if plain else [gains]),
        in_specs=[vmem] * (1 if plain else 4),
        out_specs=[vmem] + ([hbm] if gather else []) + ([] if plain else [vmem]),
        scratch_shapes=([slots, sems, sems, sems, dma((n,))] if gather else [])
        + [slots, slots, pltpu.VMEM((8, D), f32), sems, sems, sems, sems],
        compiler_params=pltpu.CompilerParams(
            collective_id=collective_id, has_side_effects=True, vmem_limit_bytes=VMEM_LIMIT
        ),
        cost_estimate=pl.CostEstimate(
            flops=10**9, bytes_accessed=2**20, transcendentals=0
        ),
        name="scatter_norm_gather" if gather else "scatter_norm",
    )(
        part.reshape(n, steps, R, D),
        *(
            ()
            if plain
            else (base.reshape(steps, R, D), addend.reshape(steps, R, D), gain)
        ),
    )
    if plain:
        return results[0].reshape(T, D)
    if gather:
        out, alls, gains = results
        return out.reshape(T, D), alls.reshape(n * T, D), gains
    out, gains = results
    return out.reshape(T, D), gains


def gather_mix_kernel(
    n, mixed_hbm, weight_hbm, x_ref, gain, mixed_out, in_out, own_out,
    ms, acc, weight, load_sem, up_sem, down_sem, recv_sem, out_sem,
):
    L, C = ms.shape[1:]
    D = weight.shape[1]
    T = own_out.shape[0]
    d, z, peers = others(n)
    own_load = pltpu.make_async_copy(mixed_hbm, ms.at[z], load_sem.at[0])
    own_load.start()
    weight_load = pltpu.make_async_copy(weight_hbm, weight, load_sem.at[1])
    weight_load.start()
    greet(peers)

    def send_up(o):
        return pltpu.make_async_remote_copy(
            src_ref=ms.at[o], dst_ref=ms.at[o], send_sem=up_sem.at[o], recv_sem=recv_sem.at[o],
            device_id=(d, lax.rem(z + 1, n)), device_id_type=MESH,
        )

    def send_down(o):
        return pltpu.make_async_remote_copy(
            src_ref=ms.at[o], dst_ref=ms.at[o], send_sem=down_sem.at[o], recv_sem=recv_sem.at[o],
            device_id=(d, lax.rem(z + n - 1, n)), device_id_type=MESH,
        )

    own_load.wait()

    @pl.when(z < n - 1)
    def _():
        send_up(z).start()

    @pl.when(z > 0)
    def _():
        send_down(z).start()

    weight_load.wait()
    block = 256

    def add(o, first):
        w = weight[pl.ds(pl.multiple_of(o * C, C), C), :]

        def rows(i, carry):
            r = pl.ds(pl.multiple_of(i * block, block), block)
            new = jnp.dot(ms[o, r, :], w, preferred_element_type=f32)
            acc[r, :] = new if first else acc[r, :] + new
            return carry

        lax.fori_loop(0, L // block, rows, 0)

    def save(o):
        return pltpu.make_async_copy(ms.at[o], mixed_out.at[o], out_sem.at[o])

    add(z, True)
    save(z).start()

    def step(s, carry):
        below, above = z - s, z + s

        @pl.when(below >= 0)
        def _():
            send_up(below).wait_recv()

            @pl.when(z < n - 1)
            def _():
                send_up(below).start()

        @pl.when(above < n)
        def _():
            send_down(above).wait_recv()

            @pl.when(z > 0)
            def _():
                send_down(above).start()

        def side(j, inner):
            o = z - s + 2 * s * j

            @pl.when((o >= 0) & (o < n))
            def _():
                add(o, False)
                save(o).start()

            return inner

        lax.fori_loop(0, 2, side, 0)
        return carry

    lax.fori_loop(1, n, step, 0)
    own_rows = pl.ds(pl.multiple_of(z * T, T), T)
    own_out[...] = acc[own_rows, :]
    part = 32

    def norm_rows(i, carry):
        r = pl.ds(pl.multiple_of(i * part, part), part)
        v = acc[r, :] + x_ref[r, :].astype(f32)
        factor = lax.rsqrt(jnp.sum(v * v, axis=1, keepdims=True) / D + EPSILON)
        in_out[r, :] = (v * factor * gain[...]).astype(bf16)
        return carry

    lax.fori_loop(0, L // part, norm_rows, 0)

    def finish(o, carry):
        save(o).wait()

        @pl.when((z < n - 1) & (o <= z))
        def _():
            send_up(o).wait_send()

        @pl.when((z > 0) & (o >= z))
        def _():
            send_down(o).wait_send()

        return carry

    lax.fori_loop(0, n, finish, 0)


def gather_mix(n, mixed, weight, x_all, gain, rows):
    L, C = mixed.shape
    D = weight.shape[1]
    hbm = pl.BlockSpec(memory_space=pl.ANY)
    vmem = pl.BlockSpec(memory_space=pltpu.VMEM)
    dma = pltpu.SemaphoreType.DMA
    return pl.pallas_call(
        functools.partial(gather_mix_kernel, n),
        out_shape=[
            jax.ShapeDtypeStruct((n, L, C), bf16),
            jax.ShapeDtypeStruct((L, D), bf16),
            jax.ShapeDtypeStruct((rows, D), f32),
        ],
        in_specs=[hbm, hbm, vmem, vmem],
        out_specs=[hbm, vmem, vmem],
        scratch_shapes=[
            pltpu.VMEM((n, L, C), bf16),
            pltpu.VMEM((L, D), f32),
            pltpu.VMEM((D, D), bf16),
            dma((2,)),
            dma((n,)),
            dma((n,)),
            dma((n,)),
            dma((n,)),
        ],
        compiler_params=pltpu.CompilerParams(
            collective_id=1, has_side_effects=True, vmem_limit_bytes=VMEM_LIMIT
        ),
        cost_estimate=pl.CostEstimate(flops=100 * 10**9, bytes_accessed=32 * 2**20, transcendentals=0),
        name="gather_mix",
    )(mixed, weight, x_all, gain)


def experts_kernel(
    x_ref, g_ref, combine, gate_w, up_w, down_w,
    sum_out, in_out, hidden_out, gate_out, up_out, sum_acc, in_acc,
):
    e = pl.program_id(1)
    last = pl.num_programs(1) - 1
    x, g = x_ref[...], g_ref[...]
    gate_m, up_m, down_m = gate_w[0], up_w[0], down_w[0]
    lane = lax.broadcasted_iota(jnp.int32, combine.shape, 1)
    weight = jnp.sum(jnp.where(lane == e, combine[...], 0.0), axis=1, keepdims=True)
    gate_part = dot(x, gate_m)
    up_part = dot(x, up_m)
    hidden_grad = dot_nt(g, down_m) * weight
    sig = jax.nn.sigmoid(gate_part)
    silu = gate_part * sig
    hidden = (silu * up_part * weight).astype(bf16)
    hidden_out[...] = hidden
    up_grad = (hidden_grad * silu).astype(bf16)
    up_out[...] = up_grad
    gate_grad = (hidden_grad * up_part * sig * (1.0 + gate_part * (1.0 - sig))).astype(bf16)
    gate_out[...] = gate_grad
    made = dot(hidden, down_m)
    back = dot_nt(gate_grad, gate_m) + dot_nt(up_grad, up_m)

    @pl.when(e == 0)
    def _():
        sum_acc[...] = made
        in_acc[...] = back

    @pl.when((e > 0) & (e < last))
    def _():
        sum_acc[...] += made
        in_acc[...] += back

    @pl.when((e > 0) & (e == last))
    def _():
        sum_out[...] = (sum_acc[...] + made).astype(bf16)
        in_out[...] = (in_acc[...] + back).astype(bf16)

    @pl.when((e == 0) & (e == last))
    def _():
        sum_out[...] = made.astype(bf16)
        in_out[...] = back.astype(bf16)


def experts_pass(x, g, combine, gate_w, up_w, down_w):
    L, D = x.shape
    E, _, F = gate_w.shape
    block = min(512, L)
    rows = pl.BlockSpec((block, D), lambda i, e: (i, 0))
    units = pl.BlockSpec((block, F), lambda i, e: (i, e))
    column = pl.BlockSpec((1, D, F), lambda i, e: (e, 0, 0))
    wide = jax.ShapeDtypeStruct((L, D), bf16)
    narrow = jax.ShapeDtypeStruct((L, E * F), bf16)
    return pl.pallas_call(
        experts_kernel,
        out_shape=[wide, wide, narrow, narrow, narrow],
        grid=(L // block, E),
        in_specs=[
            rows, rows, pl.BlockSpec((block, combine.shape[1]), lambda i, e: (i, 0)),
            column, column, pl.BlockSpec((1, F, D), lambda i, e: (e, 0, 0)),
        ],
        out_specs=[rows, rows, units, units, units],
        scratch_shapes=[pltpu.VMEM((block, D), f32), pltpu.VMEM((block, D), f32)],
        compiler_params=pltpu.CompilerParams(vmem_limit_bytes=VMEM_LIMIT),
        cost_estimate=pl.CostEstimate(
            flops=12 * L * D * E * F, bytes_accessed=40 * 2**20, transcendentals=L * E * F
        ),
        name="experts_pass",
    )(x, g, combine, gate_w, up_w, down_w)


def expert_grads_kernel(x_ref, g_ref, hidden, gate_grad, up_grad, gate_out, up_out, down_out, xt):
    @pl.when(pl.program_id(0) == 0)
    def _():
        xt[...] = x_ref[...].T

    gate_out[0] = dot(xt[...], gate_grad[...]).astype(bf16)
    up_out[0] = dot(xt[...], up_grad[...]).astype(bf16)
    down_out[0] = dot_tn(hidden[...], g_ref[...]).astype(bf16)


def expert_grads(x, g, hidden, gate_grad, up_grad, experts):
    L, D = x.shape
    F = hidden.shape[1] // experts
    whole = pl.BlockSpec((L, D), lambda e: (0, 0))
    units = pl.BlockSpec((L, F), lambda e: (0, e))
    column = pl.BlockSpec((1, D, F), lambda e: (e, 0, 0))
    grad = jax.ShapeDtypeStruct((experts, D, F), bf16)
    return pl.pallas_call(
        expert_grads_kernel,
        out_shape=[grad, grad, jax.ShapeDtypeStruct((experts, F, D), bf16)],
        grid=(experts,),
        in_specs=[whole, whole, units, units, units],
        out_specs=[column, column, pl.BlockSpec((1, F, D), lambda e: (e, 0, 0))],
        scratch_shapes=[pltpu.VMEM((D, L), bf16)],
        compiler_params=pltpu.CompilerParams(vmem_limit_bytes=VMEM_LIMIT),
        cost_estimate=pl.CostEstimate(
            flops=6 * L * D * experts * F, bytes_accessed=26 * 2**20, transcendentals=0
        ),
        name="expert_grads",
    )(x, g, hidden, gate_grad, up_grad)


def gather_line_kernel(n, v_hbm, out, slots, load_sem, up_sem, down_sem, recv_sem, out_sem):
    d, z, peers = others(n)
    own_load = pltpu.make_async_copy(v_hbm, slots.at[z], load_sem.at[0])
    own_load.start()
    greet(peers)

    def send_up(o):
        return pltpu.make_async_remote_copy(
            src_ref=slots.at[o], dst_ref=slots.at[o], send_sem=up_sem.at[o],
            recv_sem=recv_sem.at[o], device_id=(d, lax.rem(z + 1, n)), device_id_type=MESH,
        )

    def send_down(o):
        return pltpu.make_async_remote_copy(
            src_ref=slots.at[o], dst_ref=slots.at[o], send_sem=down_sem.at[o],
            recv_sem=recv_sem.at[o], device_id=(d, lax.rem(z + n - 1, n)), device_id_type=MESH,
        )

    own_load.wait()

    @pl.when(z < n - 1)
    def _():
        send_up(z).start()

    @pl.when(z > 0)
    def _():
        send_down(z).start()

    def save(o):
        return pltpu.make_async_copy(slots.at[o], out.at[o], out_sem.at[o])

    save(z).start()

    def step(s, carry):
        below, above = z - s, z + s

        @pl.when(below >= 0)
        def _():
            send_up(below).wait_recv()

            @pl.when(z < n - 1)
            def _():
                send_up(below).start()

            save(below).start()

        @pl.when(above < n)
        def _():
            send_down(above).wait_recv()

            @pl.when(z > 0)
            def _():
                send_down(above).start()

            save(above).start()

        return carry

    lax.fori_loop(1, n, step, 0)

    def finish(o, carry):
        save(o).wait()

        @pl.when((z < n - 1) & (o <= z))
        def _():
            send_up(o).wait_send()

        @pl.when((z > 0) & (o >= z))
        def _():
            send_down(o).wait_send()

        return carry

    lax.fori_loop(0, n, finish, 0)


def gather_line(n, v, collective_id):
    hbm = pl.BlockSpec(memory_space=pl.ANY)
    dma = pltpu.SemaphoreType.DMA
    return pl.pallas_call(
        functools.partial(gather_line_kernel, n),
        out_shape=jax.ShapeDtypeStruct((n,) + v.shape, v.dtype),
        in_specs=[hbm],
        out_specs=hbm,
        scratch_shapes=[
            pltpu.VMEM((n,) + v.shape, v.dtype), dma((1,)), dma((n,)), dma((n,)), dma((n,)),
            dma((n,)),
        ],
        compiler_params=pltpu.CompilerParams(
            collective_id=collective_id, has_side_effects=True, vmem_limit_bytes=VMEM_LIMIT
        ),
        cost_estimate=pl.CostEstimate(flops=20 * 10**9, bytes_accessed=2 * 2**20, transcendentals=0),
        name="gather_line",
    )(v)


def per_device(
    tokens,
    out_grad,
    routes,
    gate_weights,
    prefix,
    query_weight,
    key_weight,
    value_weight,
    output_weight,
    norm_gains,
    expert_gate,
    expert_up,
    expert_down,
):
    rows, width = tokens.shape
    shards = lax.axis_size("shard")
    groups = lax.axis_size("dp")
    place = lax.axis_index("shard")
    group = lax.axis_index("dp")
    length = rows * shards
    local = width // shards
    experts = expert_gate.shape[0]
    units = expert_gate.shape[2]

    expert_ids = jnp.arange(experts, dtype=jnp.int32)
    weight_own = jnp.sum(
        jnp.where(routes[:, :, None] == expert_ids[None, None, :], gate_weights[:, :, None], 0.0),
        axis=1,
    )
    own_gains = norm_gains.astype(f32)
    small = jnp.concatenate(
        [
            jnp.pad(weight_own.T, ((0, 8 - experts), (0, 0))),
            jnp.pad(jnp.stack([own_gains[0], own_gains[3]]), ((0, 6), (0, 0))),
        ],
        axis=1,
    )
    x_all_b, normed, query_raw, key_raw, values, small_all, squares = gather_project(
        shards, tokens, small, query_weight, key_weight, value_weight
    )
    x_all_b = x_all_b.reshape(length, width)
    normed = normed.reshape(length, width)
    query_raw = query_raw.reshape(length, local)
    key_raw = key_raw.reshape(length, local)
    values = values.reshape(length, local)
    combine = small_all[:, :experts, :rows].transpose(0, 2, 1).reshape(length, experts)
    gain_in = small_all[:, 0, rows:].reshape(width)
    gain_expert = small_all[:, 1, rows:].reshape(width)
    head_gains = own_gains[1:3]
    slab = width // groups
    out_grad_b, squares = lax.optimization_barrier((out_grad, squares))
    out_slab = lax.dynamic_slice_in_dim(output_weight, group * slab, slab, 0)
    out_slab = gather_line(shards, out_slab, 4).transpose(1, 0, 2).reshape(slab, width)
    full_output = lax.all_gather(out_slab, "dp", axis=0, tiled=True)

    factors = lax.rsqrt(squares[:, :2].transpose(0, 2, 1).reshape(length, 2) / width + EPSILON)
    cosine, sine = rotary_tables(length)
    queries, keys, mixed_own = attention(
        prefix, query_raw, key_raw, values, factors, cosine, sine, head_gains
    )
    mixed_all, expert_in, attended_own = gather_mix(
        shards, mixed_own, full_output, x_all_b, gain_expert[None, :], rows
    )

    g_all = lax.all_gather(out_grad_b, "shard", axis=0, tiled=True)
    sum_part, in_part, hidden, gate_grad, up_grad = experts_pass(
        expert_in, g_all, combine, expert_gate, expert_up, expert_down
    )
    grad_gate, grad_up, grad_down = expert_grads(
        expert_in, g_all, hidden, gate_grad, up_grad, experts
    )
    in_part, grad_gate, grad_up, grad_down = lax.optimization_barrier(
        (in_part, grad_gate, grad_up, grad_down)
    )
    grad_gate, grad_up, grad_down = lax.psum((grad_gate, grad_up, grad_down), "dp")

    x_own = tokens.astype(f32)
    residual_own = x_own + attended_own
    residual_grad, attended_grad, gain_grad_res = scatter_norm(
        shards, 16, True, in_part, residual_own, out_grad, gain_expert[None, :], 2
    )

    own_columns = lax.dynamic_slice_in_dim(attended_grad, place * local, local, 1)
    grad_output = jnp.concatenate([dot_tn(mixed_all[s], own_columns) for s in range(shards)], 0)
    mixed_grad = dot_nt(
        attended_grad, lax.dynamic_slice_in_dim(full_output, place * local, local, 0)
    ).astype(bf16)
    query_norm_grad, key_norm_grad, value_raw_grad, gain_grad_heads, inner = attention_back(
        prefix, queries, keys, values, mixed_grad, query_raw, key_raw, factors, cosine, sine,
        head_gains,
    )
    inner, grad_gate, grad_up, grad_down = lax.optimization_barrier(
        (inner, grad_gate, grad_up, grad_down)
    )
    inner = lax.psum(inner[:, :2], "shard") / width
    inner = inner.transpose(0, 2, 1).reshape(length, 2)
    factor_query, factor_key = factors[:, 0:1], factors[:, 1:2]
    query_raw_grad = (
        factor_query * (query_norm_grad - query_raw * factor_query * inner[:, 0:1])
    ).astype(bf16)
    key_raw_grad = (factor_key * (key_norm_grad - key_raw * factor_key * inner[:, 1:2])).astype(
        bf16
    )
    normed_part = (
        dot_nt(query_raw_grad, query_weight)
        + dot_nt(key_raw_grad, key_weight)
        + dot_nt(value_raw_grad, value_weight)
    )
    grad_query = dot_tn(normed, query_raw_grad)
    grad_key = dot_tn(normed, key_raw_grad)
    grad_value = dot_tn(normed, value_raw_grad)

    attention_grads, normed_part = lax.optimization_barrier(
        (
            tuple(v.astype(bf16) for v in (grad_query, grad_key, grad_value, grad_output)),
            normed_part.astype(bf16),
        )
    )
    grad_query, grad_key, grad_value, grad_output = lax.psum(attention_grads, "dp")
    grad_tokens, gain_grad_x = scatter_norm(
        shards, 8, False, normed_part, tokens, residual_grad, gain_in[None, :], 3
    )
    sum_part, grad_tokens = lax.optimization_barrier((sum_part, grad_tokens))
    expert_sum = scatter_norm(shards, 8, False, sum_part, None, None, None, 5, plain=True)
    output = residual_own + expert_sum
    root_means = jnp.stack([root_mean(attended_own), root_mean(expert_sum), root_mean(output)])
    placed = lax.dynamic_update_slice(
        jnp.zeros((2, width), f32), gain_grad_heads, (jnp.int32(0), place * local)
    )
    gain_rows = lax.psum(
        jnp.concatenate([gain_grad_x.sum(0)[None], placed, gain_grad_res.sum(0)[None]], 0),
        ("dp", "shard"),
    )
    grad_gains = lax.dynamic_slice_in_dim(gain_rows, place * local, local, 1)

    return (
        output.astype(bf16),
        grad_tokens,
        root_means,
        grad_query.astype(f32),
        grad_key.astype(f32),
        grad_value.astype(f32),
        grad_output.astype(f32),
        grad_gains,
        grad_gate.astype(f32),
        grad_up.astype(f32),
        grad_down.astype(f32),
    )


def solution(mesh):
    placed = (
        P(("dp", "shard"), None),
        P(("dp", "shard"), None),
        P(("dp", "shard"), None),
        P(("dp", "shard"), None),
        P("dp"),
        P(None, "shard"),
        P(None, "shard"),
        P(None, "shard"),
        P(None, "shard"),
        P(None, "shard"),
        P(None, None, "shard"),
        P(None, None, "shard"),
        P(None, "shard", None),
    )
    return jax.shard_map(
        per_device,
        mesh=mesh,
        in_specs=placed,
        out_specs=(
            P(("dp", "shard"), None),
            P(("dp", "shard"), None),
            P(None, ("dp", "shard")),
            P(None, "shard"),
            P(None, "shard"),
            P(None, "shard"),
            P(None, "shard"),
            P(None, "shard"),
            P(None, None, "shard"),
            P(None, None, "shard"),
            P(None, "shard", None),
        ),
        check_vma=False,
    )
```

```python
import functools

import jax
import jax.numpy as jnp
from jax import lax
from jax.experimental import pallas as pl
from jax.experimental.pallas import tpu as pltpu
from jax.sharding import PartitionSpec as P

HEAD_DIM = 128
EPSILON = 1e-05
ROPE_BASE = 10000.0
MASKED = -1e30
VMEM_LIMIT = 60 * 2**20

f32 = jnp.float32
bf16 = jnp.bfloat16


def rotary_tables(row_count):
    half_dim = HEAD_DIM // 2
    positions = jnp.arange(row_count, dtype=jnp.int32)
    inverse = ROPE_BASE ** (-jnp.arange(half_dim, dtype=f32) / half_dim)
    angles = positions.astype(f32)[:, None] * inverse[None, :]
    cosine, sine = jnp.cos(angles), jnp.sin(angles)
    return jnp.concatenate([cosine, cosine], 1), jnp.concatenate([-sine, sine], 1)


def row_factor(values):
    return lax.rsqrt(jnp.mean(values * values, axis=-1, keepdims=True) + EPSILON)


def norm_back(grad_unit, unit_rows, factor):
    return factor * (
        grad_unit - unit_rows * jnp.mean(grad_unit * unit_rows, axis=-1, keepdims=True)
    )


def root_mean(values):
    return jnp.sqrt(jnp.mean(values * values, axis=-1))


def dot(a, b):
    return jnp.dot(a, b, preferred_element_type=f32)


def dot_nt(a, b):
    return lax.dot_general(a, b, (((1,), (1,)), ((), ())), preferred_element_type=f32)


def dot_tn(a, b):
    return lax.dot_general(a, b, (((0,), (0,)), ((), ())), preferred_element_type=f32)


MESH = pl.DeviceIdType.MESH


def greet(peers):
    barrier = pltpu.get_barrier_semaphore()
    for peer in peers:
        pl.semaphore_signal(barrier, inc=1, device_id=peer, device_id_type=MESH)
    pl.semaphore_wait(barrier, len(peers))


def others(n):
    d, z = lax.axis_index("dp"), lax.axis_index("shard")
    return d, z, [(d, lax.rem(z + p, n)) for p in range(1, n)]


def gather_project_kernel(
    n, x_hbm, small_ref, wq_hbm, wk_hbm, wv_hbm,
    x_out, normed_out, q_out, k_out, v_out, small_out, sq_out,
    xs, nb, qb, kb, vb, wq, wk, wv, sq_all, small_all,
    load_sem, out_sem, up_sem, down_sem, recv_sem, small_send, small_recv, sq_send, sq_recv,
):
    T, D = xs.shape[1:]
    C = qb.shape[2]
    d, z, peers = others(n)
    own_load = pltpu.make_async_copy(x_hbm, xs.at[z], load_sem.at[0])
    own_load.start()
    loads = [
        pltpu.make_async_copy(src, dst, load_sem.at[i + 1])
        for i, (src, dst) in enumerate(((wq_hbm, wq), (wk_hbm, wk), (wv_hbm, wv)))
    ]
    for load in loads:
        load.start()
    greet(peers)

    def send_up(o):
        return pltpu.make_async_remote_copy(
            src_ref=xs.at[o], dst_ref=xs.at[o], send_sem=up_sem.at[o], recv_sem=recv_sem.at[o],
            device_id=(d, lax.rem(z + 1, n)), device_id_type=MESH,
        )

    def send_down(o):
        return pltpu.make_async_remote_copy(
            src_ref=xs.at[o], dst_ref=xs.at[o], send_sem=down_sem.at[o], recv_sem=recv_sem.at[o],
            device_id=(d, lax.rem(z + n - 1, n)), device_id_type=MESH,
        )

    own_load.wait()
    small_copies = []
    for p, peer in enumerate(peers):
        copy = pltpu.make_async_remote_copy(
            src_ref=small_ref, dst_ref=small_all.at[z], send_sem=small_send.at[p],
            recv_sem=small_recv.at[z], device_id=peer, device_id_type=MESH,
        )
        copy.start()
        small_copies.append(copy)

    @pl.when(z < n - 1)
    def _():
        send_up(z).start()

    @pl.when(z > 0)
    def _():
        send_down(z).start()

    small_all[z] = small_ref[...]
    for load in loads:
        load.wait()
    for p in range(1, n):
        o = lax.rem(z + n - p, n)
        pltpu.make_async_remote_copy(
            src_ref=small_ref, dst_ref=small_all.at[o], send_sem=small_send.at[p - 1],
            recv_sem=small_recv.at[o], device_id=(d, o), device_id_type=MESH,
        ).wait_recv()

    lanes = lax.broadcasted_iota(jnp.int32, (T, 128), 1)
    step_rows = 32

    def outs(o):
        return [
            pltpu.make_async_copy(src.at[o], dst.at[o], out_sem.at[i, o])
            for i, (src, dst) in enumerate(
                ((xs, x_out), (nb, normed_out), (qb, q_out), (kb, k_out), (vb, v_out))
            )
        ]

    def compute(o):
        gain = jnp.concatenate([small_all[s, 0:1, T:] for s in range(n)], axis=1)

        def norm_rows(i, carry):
            r = pl.ds(pl.multiple_of(i * step_rows, step_rows), step_rows)
            x = xs[o, r, :].astype(f32)
            factor = lax.rsqrt(jnp.sum(x * x, axis=1, keepdims=True) / D + EPSILON)
            nb[o, r, :] = (x * factor * gain).astype(bf16)
            return carry

        lax.fori_loop(0, T // step_rows, norm_rows, 0)
        q = jnp.dot(nb[o], wq[...], preferred_element_type=f32)
        qb[o] = q
        q_sum = jnp.sum(q * q, axis=1, keepdims=True)
        k = jnp.dot(nb[o], wk[...], preferred_element_type=f32)
        kb[o] = k
        k_sum = jnp.sum(k * k, axis=1, keepdims=True)
        vb[o] = jnp.dot(nb[o], wv[...], preferred_element_type=f32).astype(bf16)
        both = jnp.where(lanes == 0, q_sum, jnp.where(lanes == 1, k_sum, 0.0))
        sq_all[z, o] = both.T[0:8]
        for copy in outs(o):
            copy.start()

    def step(s, carry):
        below, above = z - s, z + s

        @pl.when((s > 0) & (below >= 0))
        def _():
            send_up(below).wait_recv()

            @pl.when(z < n - 1)
            def _():
                send_up(below).start()

        @pl.when((s > 0) & (above < n))
        def _():
            send_down(above).wait_recv()

            @pl.when(z > 0)
            def _():
                send_down(above).start()

        def side(j, inner):
            o = z - s + 2 * s * j

            @pl.when((o >= 0) & (o < n) & ((s > 0) | (j == 0)))
            def _():
                compute(o)

            return inner

        lax.fori_loop(0, 2, side, 0)
        return carry

    lax.fori_loop(0, n, step, 0)

    sq_copies = []
    for p, peer in enumerate(peers):
        copy = pltpu.make_async_remote_copy(
            src_ref=sq_all.at[z], dst_ref=sq_all.at[z], send_sem=sq_send.at[p],
            recv_sem=sq_recv.at[z], device_id=peer, device_id_type=MESH,
        )
        copy.start()
        sq_copies.append(copy)
    small_out[...] = small_all[...]

    def finish(o, carry):
        for copy in outs(o):
            copy.wait()

        @pl.when((z < n - 1) & (o <= z))
        def _():
            send_up(o).wait_send()

        @pl.when((z > 0) & (o >= z))
        def _():
            send_down(o).wait_send()

        return carry

    lax.fori_loop(0, n, finish, 0)
    for p in range(1, n):
        o = lax.rem(z + n - p, n)
        pltpu.make_async_remote_copy(
            src_ref=sq_all.at[o], dst_ref=sq_all.at[o], send_sem=sq_send.at[p - 1],
            recv_sem=sq_recv.at[o], device_id=(d, o), device_id_type=MESH,
        ).wait_recv()
    total = sq_all[0]
    for s in range(1, n):
        total = total + sq_all[s]
    sq_out[...] = total
    for copy in small_copies + sq_copies:
        copy.wait_send()


def gather_project(n, tokens, small, wq, wk, wv):
    T, D = tokens.shape
    C = wq.shape[1]
    hbm = pl.BlockSpec(memory_space=pl.ANY)
    vmem = pl.BlockSpec(memory_space=pltpu.VMEM)
    dma = pltpu.SemaphoreType.DMA
    return pl.pallas_call(
        functools.partial(gather_project_kernel, n),
        out_shape=[
            jax.ShapeDtypeStruct((n, T, D), bf16),
            jax.ShapeDtypeStruct((n, T, D), bf16),
            jax.ShapeDtypeStruct((n, T, C), f32),
            jax.ShapeDtypeStruct((n, T, C), f32),
            jax.ShapeDtypeStruct((n, T, C), bf16),
            jax.ShapeDtypeStruct((n,) + small.shape, f32),
            jax.ShapeDtypeStruct((n, 8, T), f32),
        ],
        in_specs=[hbm, vmem, hbm, hbm, hbm],
        out_specs=[hbm] * 5 + [vmem] * 2,
        scratch_shapes=[
            pltpu.VMEM((n, T, D), bf16),
            pltpu.VMEM((n, T, D), bf16),
            pltpu.VMEM((n, T, C), f32),
            pltpu.VMEM((n, T, C), f32),
            pltpu.VMEM((n, T, C), bf16),
            pltpu.VMEM((D, C), bf16),
            pltpu.VMEM((D, C), bf16),
            pltpu.VMEM((D, C), bf16),
            pltpu.VMEM((n, n, 8, T), f32),
            pltpu.VMEM((n,) + small.shape, f32),
            dma((4,)),
            dma((5, n)),
            dma((n,)),
            dma((n,)),
            dma((n,)),
            dma((n,)),
            dma((n,)),
            dma((n,)),
            dma((n,)),
        ],
        compiler_params=pltpu.CompilerParams(
            collective_id=0, has_side_effects=True, vmem_limit_bytes=VMEM_LIMIT
        ),
        cost_estimate=pl.CostEstimate(flops=80 * 10**9, bytes_accessed=32 * 2**20, transcendentals=0),
        name="gather_project",
    )(tokens, small, wq, wk, wv)


def rope(v, cosine, sine):
    return v * cosine + pltpu.roll(v, HEAD_DIM // 2, 1) * sine


def key_span(i, block, length):
    return min(length, max((i + 1) * block, length // 2))


def block_scores(q, k, i, block, limit):
    s = dot_nt(q, k) * (HEAD_DIM**-0.5)
    row = lax.broadcasted_iota(jnp.int32, s.shape, 0) + i * block
    col = lax.broadcasted_iota(jnp.int32, s.shape, 1)
    return jnp.where((col <= row) | (col < limit), s, MASKED)


def attention_kernel(prefix, q_raw, k_raw, v_ref, factors, cosine, sine, gains, q_out, k_out, mixed):
    length = q_raw.shape[0]
    block = 256
    limit = prefix[0]

    def turn(raw, out, column, gain):
        def part(i, carry):
            r = pl.ds(pl.multiple_of(i * block, block), block)
            v = raw[r, :] * factors[r, column : column + 1] * gain
            out[r, :] = rope(v, cosine[r, :], sine[r, :]).astype(bf16)
            return carry

        lax.fori_loop(0, length // block, part, 0)

    turn(q_raw, q_out, 0, gains[0:1, :])
    turn(k_raw, k_out, 1, gains[1:2, :])
    for i in range(length // block):
        span = key_span(i, block, length)
        r = pl.ds(i * block, block)
        s = block_scores(q_out[r, :], k_out[0:span, :], i, block, limit)
        e = jnp.exp(s - jnp.max(s, axis=1, keepdims=True))
        total = jnp.sum(e, axis=1, keepdims=True)
        mixed[r, :] = (dot(e.astype(bf16), v_ref[0:span, :]) / total).astype(bf16)


def attention(prefix, q_raw, k_raw, values, factors, cosine, sine, gains):
    length, local = q_raw.shape
    heads = local // HEAD_DIM
    head = pl.BlockSpec((length, HEAD_DIM), lambda h, p: (0, h))
    whole = lambda a: pl.BlockSpec(a.shape, lambda h, p: (0, 0))
    out = jax.ShapeDtypeStruct((length, local), bf16)
    return pl.pallas_call(
        attention_kernel,
        out_shape=[out] * 3,
        grid_spec=pltpu.PrefetchScalarGridSpec(
            num_scalar_prefetch=1,
            grid=(heads,),
            in_specs=[
                head, head, head, whole(factors), whole(cosine), whole(sine),
                pl.BlockSpec((2, HEAD_DIM), lambda h, p: (0, h)),
            ],
            out_specs=[head] * 3,
        ),
        compiler_params=pltpu.CompilerParams(vmem_limit_bytes=VMEM_LIMIT),
        cost_estimate=pl.CostEstimate(flops=14 * 10**9, bytes_accessed=16 * 2**20, transcendentals=0),
        name="attention",
    )(prefix, q_raw, k_raw, values, factors, cosine, sine, gains)


def attention_back_kernel(
    n, steps, width, limit_ref, q_ref, k_ref, v_ref, g_ref, q_raw, k_raw, factors, cosine, sine,
    gains, sum_hbm, q_grad, k_grad, v_grad, gain_out, own_sum,
    dq_acc, dk_acc, k_acc, v_acc, inner_all, inner_send, inner_recv, part, *line,
):
    length, local = q_ref.shape
    heads = local // HEAD_DIM
    block = 256
    blocks = length // block
    scale = HEAD_DIM**-0.5
    load_sem = line[-1]
    turn, drain = line_sum(n, steps, part, own_sum, *line[:-1])
    load = pltpu.make_async_copy(sum_hbm.at[:, 1], part, load_sem.at[0])
    load.start()
    d, z, peers = others(n)
    greet(peers)
    load.wait()
    slots = -(-(steps + n - 1) // heads)
    limit = limit_ref[0:1, 0:1]
    lanes = lax.broadcasted_iota(jnp.int32, (block, 128), 1)

    def clear(i, carry):
        inner_all[z, i] = jnp.zeros((8, block), f32)
        return carry

    lax.fori_loop(0, blocks, clear, 0)

    def head(h, carry):
        c = pl.ds(pl.multiple_of(h * HEAD_DIM, HEAD_DIM), HEAD_DIM)
        k_acc[...] = jnp.zeros_like(k_acc)
        v_acc[...] = jnp.zeros_like(v_acc)
        for i in range(blocks):
            for j in range(i * slots // blocks, (i + 1) * slots // blocks):
                turn(h * slots + j)
            span = key_span(i, block, length)
            r = pl.ds(i * block, block)
            q, g, k, v = q_ref[r, c], g_ref[r, c], k_ref[0:span, c], v_ref[0:span, c]
            s = block_scores(q, k, i, block, limit)
            e = jnp.exp(s - jnp.max(s, axis=1, keepdims=True))
            p = e * (1.0 / jnp.sum(e, axis=1, keepdims=True))
            t = p * dot_nt(g, v)
            ds = (t - p * jnp.sum(t, axis=1, keepdims=True)).astype(bf16)
            dq_acc[r, c] = dot(ds, k) * scale
            k_acc[0:span, :] += dot_tn(ds, q) * scale
            v_acc[0:span, :] += dot_tn(p.astype(bf16), g)
        v_grad[:, c] = v_acc[...].astype(bf16)
        gain_q, gain_k = gains[0:1, c], gains[1:2, c]

        def back(i, carry):
            gq, gk = carry
            r = pl.ds(pl.multiple_of(i * block, block), block)
            cos, sin = cosine[r, :], sine[r, :]
            dq = rope(dq_acc[r, c], cos, -sin)
            dk = rope(k_acc[r, :], cos, -sin)
            uq = q_raw[r, c] * factors[r, 0:1]
            uk = k_raw[r, c] * factors[r, 1:2]
            gq = gq + jnp.sum(dq * uq, axis=0, keepdims=True)
            gk = gk + jnp.sum(dk * uk, axis=0, keepdims=True)
            dq = dq * gain_q
            dk = dk * gain_k
            dq_acc[r, c] = dq
            dk_acc[r, c] = dk
            inner_q = jnp.sum(dq * uq, axis=1, keepdims=True)
            inner_k = jnp.sum(dk * uk, axis=1, keepdims=True)
            both = jnp.where(lanes == 0, inner_q, jnp.where(lanes == 1, inner_k, 0.0))
            inner_all[z, i] += both.T[0:8]
            return gq, gk

        zero = jnp.zeros((1, HEAD_DIM), f32)
        gq, gk = lax.fori_loop(0, blocks, back, (zero, zero))
        gain_out[0:1, c] = gq
        gain_out[1:2, c] = gk
        return carry

    lax.fori_loop(0, heads, head, 0)

    copies = []
    for p, peer in enumerate(peers):
        copy = pltpu.make_async_remote_copy(
            src_ref=inner_all.at[z], dst_ref=inner_all.at[z], send_sem=inner_send.at[p],
            recv_sem=inner_recv.at[z], device_id=peer, device_id_type=MESH,
        )
        copy.start()
        copies.append(copy)
    drain()
    for p in range(1, n):
        o = lax.rem(z + n - p, n)
        pltpu.make_async_remote_copy(
            src_ref=inner_all.at[o], dst_ref=inner_all.at[o], send_sem=inner_send.at[p - 1],
            recv_sem=inner_recv.at[o], device_id=(d, o), device_id_type=MESH,
        ).wait_recv()

    def raw(i, carry):
        r = pl.ds(pl.multiple_of(i * block, block), block)
        total = inner_all[0, i]
        for s in range(1, n):
            total = total + inner_all[s, i]
        total = jnp.concatenate([total, jnp.zeros((120, block), f32)], axis=0).T
        fq, fk = factors[r, 0:1], factors[r, 1:2]
        mean_q, mean_k = total[:, 0:1] / width, total[:, 1:2] / width
        q_grad[r, :] = (fq * (dq_acc[r, :] - q_raw[r, :] * (fq * mean_q))).astype(bf16)
        k_grad[r, :] = (fk * (dk_acc[r, :] - k_raw[r, :] * (fk * mean_k))).astype(bf16)
        return carry

    lax.fori_loop(0, blocks, raw, 0)
    for copy in copies:
        copy.wait_send()


def attention_back(
    n, width, limit, q, k, v, g, q_raw, k_raw, factors, cosine, sine, gains, sum_halves
):
    length, local = q.shape
    _, _, steps, R, D = sum_halves.shape
    vmem = pl.BlockSpec(memory_space=pltpu.VMEM)
    dma = pltpu.SemaphoreType.DMA
    grad = jax.ShapeDtypeStruct((length, local), bf16)
    return pl.pallas_call(
        functools.partial(attention_back_kernel, n, steps, width),
        out_shape=[
            grad, grad, grad, jax.ShapeDtypeStruct((2, local), f32),
            jax.ShapeDtypeStruct((steps, R, D), f32),
        ],
        in_specs=[vmem] * 11 + [pl.BlockSpec(memory_space=pl.ANY)],
        out_specs=[vmem] * 5,
        scratch_shapes=[
            pltpu.VMEM((length, local), f32),
            pltpu.VMEM((length, local), f32),
            pltpu.VMEM((length, HEAD_DIM), f32),
            pltpu.VMEM((length, HEAD_DIM), f32),
            pltpu.VMEM((n, length // 256, 8, 256), f32),
            dma((n,)),
            dma((n,)),
        ]
        + line_scratch(n, steps, R, D),
        compiler_params=pltpu.CompilerParams(
            collective_id=6, has_side_effects=True, vmem_limit_bytes=VMEM_LIMIT
        ),
        cost_estimate=pl.CostEstimate(
            flops=2 * 10**9, bytes_accessed=2**20, transcendentals=0
        ),
        name="attention_back",
    )(limit, q, k, v, g, q_raw, k_raw, factors, cosine, sine, gains, sum_halves)


def scatter_norm_kernel(n, groups, steps, gather, *refs):
    part, base, addend, gain = refs[:4]
    refs = refs[4:]
    if gather:
        out, all_out, gain_out = refs[:3]
        alls, ag_up, ag_down, ag_recv, all_sem = refs[3:8]
        refs = refs[8:]
    else:
        expert_gains, head_gains, out, gain_out = refs[:4]
        pieces, landed, sums, piece_send, piece_recv, sum_send, sum_recv = refs[4:11]
        refs = refs[11:]
    from_below, from_above, gain_acc, up_send, up_recv, down_send, down_recv = refs
    R, D = part.shape[2:]
    d, z, peers = others(n)
    upper, lower = (d, lax.rem(z + 1, n)), (d, lax.rem(z + n - 1, n))
    alike = [] if gather else [(lax.rem(d + p, groups), z) for p in range(1, groups)]
    greet(peers + alike)
    gain_acc[...] = jnp.zeros_like(gain_acc)

    def move_up(src, o, k):
        return pltpu.make_async_remote_copy(
            src_ref=src.at[o, k], dst_ref=from_below.at[o, k], send_sem=up_send.at[o, k],
            recv_sem=up_recv.at[o, k], device_id=upper, device_id_type=MESH,
        )

    def move_down(src, o, k):
        return pltpu.make_async_remote_copy(
            src_ref=src.at[o, k], dst_ref=from_above.at[o, k], send_sem=down_send.at[o, k],
            recv_sem=down_recv.at[o, k], device_id=lower, device_id_type=MESH,
        )

    def all_up(o, k):
        return pltpu.make_async_remote_copy(
            src_ref=alls.at[o, k], dst_ref=alls.at[o, k], send_sem=ag_up.at[o, k],
            recv_sem=ag_recv.at[o, k], device_id=upper, device_id_type=MESH,
        )

    def all_down(o, k):
        return pltpu.make_async_remote_copy(
            src_ref=alls.at[o, k], dst_ref=alls.at[o, k], send_sem=ag_down.at[o, k],
            recv_sem=ag_recv.at[o, k], device_id=lower, device_id_type=MESH,
        )

    def pass_up(k):
        def far(i, carry):
            o = z + n - 1 - i

            @pl.when(o < n)
            def _():
                @pl.when(z == 0)
                def _():
                    move_up(part, o, k).start()

                @pl.when(z > 0)
                def _():
                    move_up(part, o, k).wait_recv()
                    both = from_below[o, k].astype(f32) + part[o, k].astype(f32)
                    from_below[o, k] = both.astype(bf16)
                    move_up(from_below, o, k).start()

            return carry

        lax.fori_loop(0, n - 1, far, 0)

    def pass_down(k):
        def far(i, carry):
            o = z - n + 1 + i

            @pl.when(o >= 0)
            def _():
                @pl.when(z == n - 1)
                def _():
                    move_down(part, o, k).start()

                @pl.when(z < n - 1)
                def _():
                    move_down(part, o, k).wait_recv()
                    both = from_above[o, k].astype(f32) + part[o, k].astype(f32)
                    from_above[o, k] = both.astype(bf16)
                    move_down(from_above, o, k).start()

            return carry

        lax.fori_loop(0, n - 1, far, 0)

    def own(k):
        @pl.when(z > 0)
        def _():
            move_up(part, z, k).wait_recv()

        @pl.when(z == 0)
        def _():
            from_below[z, k] = jnp.zeros((R, D), bf16)

        @pl.when(z < n - 1)
        def _():
            move_down(part, z, k).wait_recv()

        @pl.when(z == n - 1)
        def _():
            from_above[z, k] = jnp.zeros((R, D), bf16)

        total = (
            part[z, k].astype(f32) + from_below[z, k].astype(f32) + from_above[z, k].astype(f32)
        )
        rows = base[k].astype(f32)
        factor = lax.rsqrt(jnp.sum(rows * rows, axis=1, keepdims=True) / D + EPSILON)
        unit = rows * factor
        along = total * unit
        gain_acc[...] += jnp.sum(along.reshape(R // 8, 8, D), axis=0)
        weighted = along * gain[...]
        mean = jnp.sum(weighted, axis=1, keepdims=True) / D
        result = addend[k].astype(f32) + factor * (total * gain[...] - unit * mean)
        out[k] = result
        if gather:
            alls[z, k] = result.astype(bf16)

            @pl.when(z < n - 1)
            def _():
                all_up(z, k).start()

            @pl.when(z > 0)
            def _():
                all_down(z, k).start()

    def forward(own_k):
        def hop(s, carry):
            below, above, k = z - s, z + s, own_k - s
            live = (k >= 0) & (k < steps)

            @pl.when(live & (below >= 0))
            def _():
                all_up(below, k).wait_recv()

                @pl.when(z < n - 1)
                def _():
                    all_up(below, k).start()

            @pl.when(live & (above < n))
            def _():
                all_down(above, k).wait_recv()

                @pl.when(z > 0)
                def _():
                    all_down(above, k).start()

            return carry

        lax.fori_loop(1, n, hop, 0)

    def turn(t, carry):
        up_k, down_k, own_k = t - z, t - (n - 1 - z), t - (n - 1)

        @pl.when((up_k >= 0) & (up_k < steps))
        def _():
            pass_up(up_k)

        @pl.when((down_k >= 0) & (down_k < steps))
        def _():
            pass_down(down_k)

        @pl.when((own_k >= 0) & (own_k < steps))
        def _():
            own(own_k)

        if gather:
            forward(own_k)

        return carry

    lax.fori_loop(0, steps + (2 * n - 2 if gather else n - 1), turn, 0)
    if gather:
        gain_out[...] = gain_acc[...]
    else:
        C = D // n
        for s in range(n):
            c = slice(s * C, (s + 1) * C)
            pieces[s, 0:1] = jnp.sum(gain_acc[:, c], axis=0, keepdims=True)
            pieces[s, 1:2] = jnp.sum(expert_gains[:, c], axis=0, keepdims=True)
            pieces[s, 2:8] = jnp.zeros((6, C), f32)

        def piece(p):
            o = lax.rem(z + p, n)
            return pltpu.make_async_remote_copy(
                src_ref=pieces.at[o], dst_ref=landed.at[z], send_sem=piece_send.at[p - 1],
                recv_sem=piece_recv.at[z], device_id=(d, o), device_id_type=MESH,
            )

        for p in range(1, n):
            piece(p).start()
        landed[z] = pieces[z]
        for p in range(1, n):
            o = lax.rem(z + n - p, n)
            pltpu.make_async_remote_copy(
                src_ref=pieces.at[o], dst_ref=landed.at[o], send_sem=piece_send.at[p - 1],
                recv_sem=piece_recv.at[o], device_id=(d, o), device_id_type=MESH,
            ).wait_recv()
        two = landed[0]
        for s in range(1, n):
            two = two + landed[s]
        sums[d, 0:1] = two[0:1]
        sums[d, 1:3] = head_gains[...]
        sums[d, 3:4] = two[1:2]
        sums[d, 4:8] = jnp.zeros((4, C), f32)
        for p in range(1, groups):
            pltpu.make_async_remote_copy(
                src_ref=sums.at[d], dst_ref=sums.at[d], send_sem=sum_send.at[p - 1],
                recv_sem=sum_recv.at[d], device_id=alike[p - 1], device_id_type=MESH,
            ).start()
        for p in range(1, groups):
            o = lax.rem(d + groups - p, groups)
            pltpu.make_async_remote_copy(
                src_ref=sums.at[o], dst_ref=sums.at[o], send_sem=sum_send.at[p - 1],
                recv_sem=sum_recv.at[o], device_id=(o, z), device_id_type=MESH,
            ).wait_recv()
        total = sums[0]
        for s in range(1, groups):
            total = total + sums[s]
        gain_out[...] = total
        for p in range(1, n):
            piece(p).wait_send()
        for p in range(1, groups):
            pltpu.make_async_remote_copy(
                src_ref=sums.at[d], dst_ref=sums.at[d], send_sem=sum_send.at[p - 1],
                recv_sem=sum_recv.at[d], device_id=alike[p - 1], device_id_type=MESH,
            ).wait_send()

    def drain(i, carry):
        o, k = i // steps, i % steps

        @pl.when(o > z)
        def _():
            move_up(part, o, k).wait_send()

        @pl.when(o < z)
        def _():
            move_down(part, o, k).wait_send()

        if gather:

            @pl.when((z < n - 1) & (o <= z))
            def _():
                all_up(o, k).wait_send()

            @pl.when((z > 0) & (o >= z))
            def _():
                all_down(o, k).wait_send()

        return carry

    lax.fori_loop(0, n * steps, drain, 0)
    if gather:
        copies = [pltpu.make_async_copy(alls.at[o], all_out.at[o], all_sem.at[o]) for o in range(n)]
        for copy in copies:
            copy.start()
        for copy in copies:
            copy.wait()


def scatter_norm(n, groups, steps, part, base, addend, gain, other_gains=None):
    gather = other_gains is None
    T, D = base.shape
    R = T // steps
    C = D // n
    hbm = pl.BlockSpec(memory_space=pl.ANY)
    vmem = pl.BlockSpec(memory_space=pltpu.VMEM)
    dma = pltpu.SemaphoreType.DMA
    slots = pltpu.VMEM((n, steps, R, D), bf16)
    rows = jax.ShapeDtypeStruct((steps, R, D), f32)
    sems = dma((n, steps))
    if gather:
        own = [slots, sems, sems, sems, dma((n,))]
        outs = [rows, jax.ShapeDtypeStruct((n, steps, R, D), bf16)]
        outs += [jax.ShapeDtypeStruct((8, D), f32)]
    else:
        own = [
            pltpu.VMEM((n, 8, C), f32), pltpu.VMEM((n, 8, C), f32),
            pltpu.VMEM((groups, 8, C), f32), dma((n,)), dma((n,)), dma((groups,)), dma((groups,)),
        ]
        outs = [rows, jax.ShapeDtypeStruct((8, C), f32)]
    return pl.pallas_call(
        functools.partial(scatter_norm_kernel, n, groups, steps, gather),
        out_shape=outs,
        in_specs=[vmem] * (4 if gather else 6),
        out_specs=[vmem, hbm, vmem] if gather else [vmem, vmem],
        scratch_shapes=own + [slots, slots, pltpu.VMEM((8, D), f32), sems, sems, sems, sems],
        compiler_params=pltpu.CompilerParams(
            collective_id=2 if gather else 3, has_side_effects=True, vmem_limit_bytes=VMEM_LIMIT
        ),
        cost_estimate=pl.CostEstimate(
            flops=10**9, bytes_accessed=2**20, transcendentals=0
        ),
        name="scatter_norm_gather" if gather else "scatter_norm",
    )(
        part.reshape(n, steps, R, D),
        base.reshape(steps, R, D),
        addend.reshape(steps, R, D),
        gain,
        *(() if gather else other_gains),
    )


def gather_mix_kernel(
    n, mixed_hbm, weight_hbm, x_ref, gain, mixed_out, in_out, own_out,
    ms, acc, weight, load_sem, up_sem, down_sem, recv_sem, out_sem,
):
    L, C = ms.shape[1:]
    D = weight.shape[1]
    T = own_out.shape[0]
    d, z, peers = others(n)
    own_load = pltpu.make_async_copy(mixed_hbm, ms.at[z], load_sem.at[0])
    own_load.start()
    weight_load = pltpu.make_async_copy(weight_hbm, weight, load_sem.at[1])
    weight_load.start()
    greet(peers)

    def send_up(o):
        return pltpu.make_async_remote_copy(
            src_ref=ms.at[o], dst_ref=ms.at[o], send_sem=up_sem.at[o], recv_sem=recv_sem.at[o],
            device_id=(d, lax.rem(z + 1, n)), device_id_type=MESH,
        )

    def send_down(o):
        return pltpu.make_async_remote_copy(
            src_ref=ms.at[o], dst_ref=ms.at[o], send_sem=down_sem.at[o], recv_sem=recv_sem.at[o],
            device_id=(d, lax.rem(z + n - 1, n)), device_id_type=MESH,
        )

    own_load.wait()

    @pl.when(z < n - 1)
    def _():
        send_up(z).start()

    @pl.when(z > 0)
    def _():
        send_down(z).start()

    weight_load.wait()
    block = 256

    def add(o, first):
        w = weight[pl.ds(pl.multiple_of(o * C, C), C), :]

        def rows(i, carry):
            r = pl.ds(pl.multiple_of(i * block, block), block)
            new = jnp.dot(ms[o, r, :], w, preferred_element_type=f32)
            acc[r, :] = new if first else acc[r, :] + new
            return carry

        lax.fori_loop(0, L // block, rows, 0)

    def save(o):
        return pltpu.make_async_copy(ms.at[o], mixed_out.at[o], out_sem.at[o])

    add(z, True)
    save(z).start()

    def step(s, carry):
        below, above = z - s, z + s

        @pl.when(below >= 0)
        def _():
            send_up(below).wait_recv()

            @pl.when(z < n - 1)
            def _():
                send_up(below).start()

        @pl.when(above < n)
        def _():
            send_down(above).wait_recv()

            @pl.when(z > 0)
            def _():
                send_down(above).start()

        def side(j, inner):
            o = z - s + 2 * s * j

            @pl.when((o >= 0) & (o < n))
            def _():
                add(o, False)
                save(o).start()

            return inner

        lax.fori_loop(0, 2, side, 0)
        return carry

    lax.fori_loop(1, n, step, 0)
    own_rows = pl.ds(pl.multiple_of(z * T, T), T)
    own_out[...] = acc[own_rows, :]
    part = 32

    def norm_rows(i, carry):
        r = pl.ds(pl.multiple_of(i * part, part), part)
        v = acc[r, :] + x_ref[r, :].astype(f32)
        factor = lax.rsqrt(jnp.sum(v * v, axis=1, keepdims=True) / D + EPSILON)
        in_out[r, :] = (v * factor * gain[...]).astype(bf16)
        return carry

    lax.fori_loop(0, L // part, norm_rows, 0)

    def finish(o, carry):
        save(o).wait()

        @pl.when((z < n - 1) & (o <= z))
        def _():
            send_up(o).wait_send()

        @pl.when((z > 0) & (o >= z))
        def _():
            send_down(o).wait_send()

        return carry

    lax.fori_loop(0, n, finish, 0)


def gather_mix(n, mixed, weight, x_all, gain, rows):
    L, C = mixed.shape
    D = weight.shape[1]
    hbm = pl.BlockSpec(memory_space=pl.ANY)
    vmem = pl.BlockSpec(memory_space=pltpu.VMEM)
    dma = pltpu.SemaphoreType.DMA
    return pl.pallas_call(
        functools.partial(gather_mix_kernel, n),
        out_shape=[
            jax.ShapeDtypeStruct((n, L, C), bf16),
            jax.ShapeDtypeStruct((L, D), bf16),
            jax.ShapeDtypeStruct((rows, D), f32),
        ],
        in_specs=[hbm, hbm, vmem, vmem],
        out_specs=[hbm, vmem, vmem],
        scratch_shapes=[
            pltpu.VMEM((n, L, C), bf16),
            pltpu.VMEM((L, D), f32),
            pltpu.VMEM((D, D), bf16),
            dma((2,)),
            dma((n,)),
            dma((n,)),
            dma((n,)),
            dma((n,)),
        ],
        compiler_params=pltpu.CompilerParams(
            collective_id=1, has_side_effects=True, vmem_limit_bytes=VMEM_LIMIT
        ),
        cost_estimate=pl.CostEstimate(flops=100 * 10**9, bytes_accessed=32 * 2**20, transcendentals=0),
        name="gather_mix",
    )(mixed, weight, x_all, gain)


def experts_kernel(
    x_ref, g_ref, combine, gate_w, up_w, down_w,
    sum_out, in_out, hidden_out, gate_out, up_out, sum_acc, in_acc,
):
    e = pl.program_id(1)
    last = pl.num_programs(1) - 1
    x, g = x_ref[...], g_ref[...]
    gate_m, up_m, down_m = gate_w[0], up_w[0], down_w[0]
    lane = lax.broadcasted_iota(jnp.int32, combine.shape, 1)
    weight = jnp.sum(jnp.where(lane == e, combine[...], 0.0), axis=1, keepdims=True)
    gate_part = dot(x, gate_m)
    up_part = dot(x, up_m)
    hidden_grad = dot_nt(g, down_m) * weight
    sig = jax.nn.sigmoid(gate_part)
    silu = gate_part * sig
    hidden = (silu * up_part * weight).astype(bf16)
    hidden_out[...] = hidden
    up_grad = (hidden_grad * silu).astype(bf16)
    up_out[...] = up_grad
    gate_grad = (hidden_grad * up_part * sig * (1.0 + gate_part * (1.0 - sig))).astype(bf16)
    gate_out[...] = gate_grad
    made = dot(hidden, down_m)
    back = dot_nt(gate_grad, gate_m) + dot_nt(up_grad, up_m)

    @pl.when(e == 0)
    def _():
        sum_acc[...] = made
        in_acc[...] = back

    @pl.when((e > 0) & (e < last))
    def _():
        sum_acc[...] += made
        in_acc[...] += back

    @pl.when((e > 0) & (e == last))
    def _():
        sum_out[...] = (sum_acc[...] + made).astype(bf16)
        in_out[...] = (in_acc[...] + back).astype(bf16)

    @pl.when((e == 0) & (e == last))
    def _():
        sum_out[...] = made.astype(bf16)
        in_out[...] = back.astype(bf16)


def experts_pass(x, g, combine, gate_w, up_w, down_w):
    L, D = x.shape
    E, _, F = gate_w.shape
    block = min(512, L)
    rows = pl.BlockSpec((block, D), lambda i, e: (i, 0))
    units = pl.BlockSpec((block, F), lambda i, e: (i, e))
    column = pl.BlockSpec((1, D, F), lambda i, e: (e, 0, 0))
    wide = jax.ShapeDtypeStruct((L, D), bf16)
    narrow = jax.ShapeDtypeStruct((L, E * F), bf16)
    return pl.pallas_call(
        experts_kernel,
        out_shape=[wide, wide, narrow, narrow, narrow],
        grid=(L // block, E),
        in_specs=[
            rows, rows, pl.BlockSpec((block, combine.shape[1]), lambda i, e: (i, 0)),
            column, column, pl.BlockSpec((1, F, D), lambda i, e: (e, 0, 0)),
        ],
        out_specs=[rows, rows, units, units, units],
        scratch_shapes=[pltpu.VMEM((block, D), f32), pltpu.VMEM((block, D), f32)],
        compiler_params=pltpu.CompilerParams(vmem_limit_bytes=VMEM_LIMIT),
        cost_estimate=pl.CostEstimate(
            flops=12 * L * D * E * F, bytes_accessed=40 * 2**20, transcendentals=L * E * F
        ),
        name="experts_pass",
    )(x, g, combine, gate_w, up_w, down_w)


def line_sum(n, steps, part, out, from_below, from_above, up_send, up_recv, down_send, down_recv):
    d, z = lax.axis_index("dp"), lax.axis_index("shard")
    upper, lower = (d, lax.rem(z + 1, n)), (d, lax.rem(z + n - 1, n))

    def move_up(src, o, k):
        return pltpu.make_async_remote_copy(
            src_ref=src.at[o, k], dst_ref=from_below.at[o, k], send_sem=up_send.at[o, k],
            recv_sem=up_recv.at[o, k], device_id=upper, device_id_type=MESH,
        )

    def move_down(src, o, k):
        return pltpu.make_async_remote_copy(
            src_ref=src.at[o, k], dst_ref=from_above.at[o, k], send_sem=down_send.at[o, k],
            recv_sem=down_recv.at[o, k], device_id=lower, device_id_type=MESH,
        )

    def passing(move, landed, first, owner):
        def run(k):
            def far(i, carry):
                o = owner(i)

                @pl.when((o >= 0) & (o < n))
                def _():
                    @pl.when(z == first)
                    def _():
                        move(part, o, k).start()

                    @pl.when(z != first)
                    def _():
                        move(part, o, k).wait_recv()
                        both = landed[o, k].astype(f32) + part[o, k].astype(f32)
                        landed[o, k] = both.astype(bf16)
                        move(landed, o, k).start()

                return carry

            lax.fori_loop(0, n - 1, far, 0)

        return run

    pass_up = passing(move_up, from_below, 0, lambda i: z + n - 1 - i)
    pass_down = passing(move_down, from_above, n - 1, lambda i: z - n + 1 + i)

    def own(k):
        @pl.when(z > 0)
        def _():
            move_up(part, z, k).wait_recv()

        @pl.when(z == 0)
        def _():
            from_below[z, k] = jnp.zeros(part.shape[2:], bf16)

        @pl.when(z < n - 1)
        def _():
            move_down(part, z, k).wait_recv()

        @pl.when(z == n - 1)
        def _():
            from_above[z, k] = jnp.zeros(part.shape[2:], bf16)

        out[k] = (
            part[z, k].astype(f32) + from_below[z, k].astype(f32) + from_above[z, k].astype(f32)
        )

    def turn(t):
        up_k, down_k, own_k = t - z, t - (n - 1 - z), t - (n - 1)

        @pl.when((up_k >= 0) & (up_k < steps))
        def _():
            pass_up(up_k)

        @pl.when((down_k >= 0) & (down_k < steps))
        def _():
            pass_down(down_k)

        @pl.when((own_k >= 0) & (own_k < steps))
        def _():
            own(own_k)

    def drain():
        def one(i, carry):
            o, k = i // steps, i % steps

            @pl.when(o > z)
            def _():
                move_up(part, o, k).wait_send()

            @pl.when(o < z)
            def _():
                move_down(part, o, k).wait_send()

            return carry

        lax.fori_loop(0, n * steps, one, 0)

    return turn, drain


def line_scratch(n, steps, R, D):
    dma = pltpu.SemaphoreType.DMA
    return [pltpu.VMEM((n, steps, R, D), bf16)] * 3 + [dma((n, steps))] * 4 + [dma((1,))]


def expert_grads_kernel(x_ref, g_ref, hidden, gate_grad, up_grad, gate_out, up_out, down_out, xt):
    @pl.when(pl.program_id(0) == 0)
    def _():
        xt[...] = x_ref[...].T

    gate_out[0] = dot(xt[...], gate_grad[...]).astype(bf16)
    up_out[0] = dot(xt[...], up_grad[...]).astype(bf16)
    down_out[0] = dot_tn(hidden[...], g_ref[...]).astype(bf16)


def expert_grads(x, g, hidden, gate_grad, up_grad, experts):
    L, D = x.shape
    F = hidden.shape[1] // experts
    whole = pl.BlockSpec((L, D), lambda e: (0, 0))
    units = pl.BlockSpec((L, F), lambda e: (0, e))
    column = pl.BlockSpec((1, D, F), lambda e: (e, 0, 0))
    grad = jax.ShapeDtypeStruct((experts, D, F), bf16)
    return pl.pallas_call(
        expert_grads_kernel,
        out_shape=[grad, grad, jax.ShapeDtypeStruct((experts, F, D), bf16)],
        grid=(experts,),
        in_specs=[whole, whole, units, units, units],
        out_specs=[column, column, pl.BlockSpec((1, F, D), lambda e: (e, 0, 0))],
        scratch_shapes=[pltpu.VMEM((D, L), bf16)],
        compiler_params=pltpu.CompilerParams(vmem_limit_bytes=VMEM_LIMIT),
        cost_estimate=pl.CostEstimate(
            flops=6 * L * D * experts * F, bytes_accessed=26 * 2**20, transcendentals=0
        ),
        name="expert_grads",
    )(x, g, hidden, gate_grad, up_grad)


def line_sum_kernel(n, half, sum_hbm, own_sum, part, *line):
    steps = part.shape[1]
    load_sem = line[-1]
    load = pltpu.make_async_copy(sum_hbm.at[:, half], part, load_sem.at[0])
    load.start()
    _, _, peers = others(n)
    greet(peers)
    load.wait()
    turn, drain = line_sum(n, steps, part, own_sum, *line[:-1])

    def one(t, carry):
        turn(t)
        return carry

    lax.fori_loop(0, steps + n - 1, one, 0)
    drain()


def line_sum_alone(n, half, sum_halves):
    _, _, steps, R, D = sum_halves.shape
    return pl.pallas_call(
        functools.partial(line_sum_kernel, n, half),
        out_shape=jax.ShapeDtypeStruct((steps, R, D), f32),
        in_specs=[pl.BlockSpec(memory_space=pl.ANY)],
        out_specs=pl.BlockSpec(memory_space=pltpu.VMEM),
        scratch_shapes=line_scratch(n, steps, R, D),
        compiler_params=pltpu.CompilerParams(
            collective_id=5, has_side_effects=True, vmem_limit_bytes=VMEM_LIMIT
        ),
        cost_estimate=pl.CostEstimate(flops=10**9, bytes_accessed=2**20, transcendentals=0),
        name="line_sum",
    )(sum_halves)


def gather_line_kernel(n, v_hbm, out, slots, load_sem, up_sem, down_sem, recv_sem, out_sem):
    d, z, peers = others(n)
    own_load = pltpu.make_async_copy(v_hbm, slots.at[z], load_sem.at[0])
    own_load.start()
    greet(peers)

    def send_up(o):
        return pltpu.make_async_remote_copy(
            src_ref=slots.at[o], dst_ref=slots.at[o], send_sem=up_sem.at[o],
            recv_sem=recv_sem.at[o], device_id=(d, lax.rem(z + 1, n)), device_id_type=MESH,
        )

    def send_down(o):
        return pltpu.make_async_remote_copy(
            src_ref=slots.at[o], dst_ref=slots.at[o], send_sem=down_sem.at[o],
            recv_sem=recv_sem.at[o], device_id=(d, lax.rem(z + n - 1, n)), device_id_type=MESH,
        )

    own_load.wait()

    @pl.when(z < n - 1)
    def _():
        send_up(z).start()

    @pl.when(z > 0)
    def _():
        send_down(z).start()

    def save(o):
        return pltpu.make_async_copy(slots.at[o], out.at[o], out_sem.at[o])

    save(z).start()

    def step(s, carry):
        below, above = z - s, z + s

        @pl.when(below >= 0)
        def _():
            send_up(below).wait_recv()

            @pl.when(z < n - 1)
            def _():
                send_up(below).start()

            save(below).start()

        @pl.when(above < n)
        def _():
            send_down(above).wait_recv()

            @pl.when(z > 0)
            def _():
                send_down(above).start()

            save(above).start()

        return carry

    lax.fori_loop(1, n, step, 0)

    def finish(o, carry):
        save(o).wait()

        @pl.when((z < n - 1) & (o <= z))
        def _():
            send_up(o).wait_send()

        @pl.when((z > 0) & (o >= z))
        def _():
            send_down(o).wait_send()

        return carry

    lax.fori_loop(0, n, finish, 0)


def gather_line(n, v, collective_id):
    hbm = pl.BlockSpec(memory_space=pl.ANY)
    dma = pltpu.SemaphoreType.DMA
    return pl.pallas_call(
        functools.partial(gather_line_kernel, n),
        out_shape=jax.ShapeDtypeStruct((n,) + v.shape, v.dtype),
        in_specs=[hbm],
        out_specs=hbm,
        scratch_shapes=[
            pltpu.VMEM((n,) + v.shape, v.dtype), dma((1,)), dma((n,)), dma((n,)), dma((n,)),
            dma((n,)),
        ],
        compiler_params=pltpu.CompilerParams(
            collective_id=collective_id, has_side_effects=True, vmem_limit_bytes=VMEM_LIMIT
        ),
        cost_estimate=pl.CostEstimate(flops=20 * 10**9, bytes_accessed=2 * 2**20, transcendentals=0),
        name="gather_line",
    )(v)


def per_device(
    tokens,
    out_grad,
    routes,
    gate_weights,
    prefix,
    query_weight,
    key_weight,
    value_weight,
    output_weight,
    norm_gains,
    expert_gate,
    expert_up,
    expert_down,
):
    rows, width = tokens.shape
    shards = lax.axis_size("shard")
    groups = lax.axis_size("dp")
    place = lax.axis_index("shard")
    group = lax.axis_index("dp")
    length = rows * shards
    local = width // shards
    experts = expert_gate.shape[0]
    units = expert_gate.shape[2]

    expert_ids = jnp.arange(experts, dtype=jnp.int32)
    weight_own = jnp.sum(
        jnp.where(routes[:, :, None] == expert_ids[None, None, :], gate_weights[:, :, None], 0.0),
        axis=1,
    )
    own_gains = norm_gains.astype(f32)
    small = jnp.concatenate(
        [
            jnp.pad(weight_own.T, ((0, 8 - experts), (0, 0))),
            jnp.pad(jnp.stack([own_gains[0], own_gains[3]]), ((0, 6), (0, 0))),
        ],
        axis=1,
    )
    x_all_b, normed, query_raw, key_raw, values, small_all, squares = gather_project(
        shards, tokens, small, query_weight, key_weight, value_weight
    )
    x_all_b = x_all_b.reshape(length, width)
    normed = normed.reshape(length, width)
    query_raw = query_raw.reshape(length, local)
    key_raw = key_raw.reshape(length, local)
    values = values.reshape(length, local)
    combine = small_all[:, :experts, :rows].transpose(0, 2, 1).reshape(length, experts)
    gain_in = small_all[:, 0, rows:].reshape(width)
    gain_expert = small_all[:, 1, rows:].reshape(width)
    head_gains = own_gains[1:3]
    slab = width // groups
    out_grad_b, squares = lax.optimization_barrier((out_grad, squares))
    out_slab = lax.dynamic_slice_in_dim(output_weight, group * slab, slab, 0)
    out_slab = gather_line(shards, out_slab, 4).transpose(1, 0, 2).reshape(slab, width)
    full_output = lax.all_gather(out_slab, "dp", axis=0, tiled=True)

    factors = lax.rsqrt(squares[:, :2].transpose(0, 2, 1).reshape(length, 2) / width + EPSILON)
    cosine, sine = rotary_tables(length)
    queries, keys, mixed_own = attention(
        prefix, query_raw, key_raw, values, factors, cosine, sine, head_gains
    )
    mixed_all, expert_in, attended_own = gather_mix(
        shards, mixed_own, full_output, x_all_b, gain_expert[None, :], rows
    )

    g_all = lax.all_gather(out_grad_b, "shard", axis=0, tiled=True)
    sum_part, in_part, hidden, gate_grad, up_grad = experts_pass(
        expert_in, g_all, combine, expert_gate, expert_up, expert_down
    )
    sum_halves = sum_part.reshape(shards, 2, 8, rows // 16, width)
    grad_gate, grad_up, grad_down = expert_grads(
        expert_in, g_all, hidden, gate_grad, up_grad, experts
    )
    in_part, grad_gate, grad_up, grad_down = lax.optimization_barrier(
        (in_part, grad_gate, grad_up, grad_down)
    )
    grad_gate, grad_up, grad_down = lax.psum((grad_gate, grad_up, grad_down), "dp")

    x_own = tokens.astype(f32)
    residual_own = x_own + attended_own
    residual_grad, attended_grad, gain_grad_res = scatter_norm(
        shards, groups, 16, in_part, residual_own, out_grad, gain_expert[None, :]
    )
    residual_grad = residual_grad.reshape(rows, width)
    attended_grad = attended_grad.reshape(length, width)

    own_columns = lax.dynamic_slice_in_dim(attended_grad, place * local, local, 1)
    grad_output = jnp.concatenate([dot_tn(mixed_all[s], own_columns) for s in range(shards)], 0)
    mixed_grad = dot_nt(
        attended_grad, lax.dynamic_slice_in_dim(full_output, place * local, local, 0)
    ).astype(bf16)
    limit = jnp.broadcast_to(prefix.reshape(1, 1), (8, 128))
    query_raw_grad, key_raw_grad, value_raw_grad, gain_grad_heads, sum_second = attention_back(
        shards, width, limit, queries, keys, values, mixed_grad, query_raw, key_raw, factors,
        cosine, sine, head_gains, sum_halves,
    )
    query_raw_grad, key_raw_grad, grad_gate, grad_up, grad_down = lax.optimization_barrier(
        (query_raw_grad, key_raw_grad, grad_gate, grad_up, grad_down)
    )
    normed_part = (
        dot_nt(query_raw_grad, query_weight)
        + dot_nt(key_raw_grad, key_weight)
        + dot_nt(value_raw_grad, value_weight)
    )
    grad_query = dot_tn(normed, query_raw_grad)
    grad_key = dot_tn(normed, key_raw_grad)
    grad_value = dot_tn(normed, value_raw_grad)

    attention_grads, normed_part = lax.optimization_barrier(
        (
            tuple(v.astype(bf16) for v in (grad_query, grad_key, grad_value, grad_output)),
            normed_part.astype(bf16),
        )
    )
    grad_query, grad_key, grad_value, grad_output = lax.psum(attention_grads, "dp")
    grad_tokens, grad_gains = scatter_norm(
        shards, groups, 8, normed_part, tokens, residual_grad, gain_in[None, :],
        (gain_grad_res, gain_grad_heads),
    )
    grad_tokens = grad_tokens.reshape(rows, width)
    grad_gains = grad_gains[:4]
    sum_halves, grad_tokens = lax.optimization_barrier((sum_halves, grad_tokens))
    sum_first = line_sum_alone(shards, 0, sum_halves)
    expert_sum = jnp.concatenate(
        [sum_first.reshape(rows // 2, width), sum_second.reshape(rows // 2, width)], 0
    )
    output = residual_own + expert_sum
    root_means = jnp.stack([root_mean(attended_own), root_mean(expert_sum), root_mean(output)])
    return (
        output.astype(bf16),
        grad_tokens,
        root_means,
        grad_query.astype(f32),
        grad_key.astype(f32),
        grad_value.astype(f32),
        grad_output.astype(f32),
        grad_gains,
        grad_gate.astype(f32),
        grad_up.astype(f32),
        grad_down.astype(f32),
    )


def solution(mesh):
    placed = (
        P(("dp", "shard"), None),
        P(("dp", "shard"), None),
        P(("dp", "shard"), None),
        P(("dp", "shard"), None),
        P("dp"),
        P(None, "shard"),
        P(None, "shard"),
        P(None, "shard"),
        P(None, "shard"),
        P(None, "shard"),
        P(None, None, "shard"),
        P(None, None, "shard"),
        P(None, "shard", None),
    )
    return jax.shard_map(
        per_device,
        mesh=mesh,
        in_specs=placed,
        out_specs=(
            P(("dp", "shard"), None),
            P(("dp", "shard"), None),
            P(None, ("dp", "shard")),
            P(None, "shard"),
            P(None, "shard"),
            P(None, "shard"),
            P(None, "shard"),
            P(None, "shard"),
            P(None, None, "shard"),
            P(None, None, "shard"),
            P(None, "shard", None),
        ),
        check_vma=False,
    )
```

```python
import functools

import jax
import jax.numpy as jnp
from jax import lax
from jax.experimental import pallas as pl
from jax.experimental.pallas import tpu as pltpu
from jax.sharding import PartitionSpec as P

HEAD_DIM = 128
EPSILON = 1e-05
ROPE_BASE = 10000.0
MASKED = -1e30
VMEM_LIMIT = 60 * 2**20

f32 = jnp.float32
bf16 = jnp.bfloat16


def rotary_tables(row_count):
    half_dim = HEAD_DIM // 2
    positions = jnp.arange(row_count, dtype=jnp.int32)
    inverse = ROPE_BASE ** (-jnp.arange(half_dim, dtype=f32) / half_dim)
    angles = positions.astype(f32)[:, None] * inverse[None, :]
    cosine, sine = jnp.cos(angles), jnp.sin(angles)
    return jnp.concatenate([cosine, cosine], 1), jnp.concatenate([-sine, sine], 1)


def row_factor(values):
    return lax.rsqrt(jnp.mean(values * values, axis=-1, keepdims=True) + EPSILON)


def norm_back(grad_unit, unit_rows, factor):
    return factor * (
        grad_unit - unit_rows * jnp.mean(grad_unit * unit_rows, axis=-1, keepdims=True)
    )


def root_mean(values):
    return jnp.sqrt(jnp.mean(values * values, axis=-1))


def dot(a, b):
    return jnp.dot(a, b, preferred_element_type=f32)


def dot_nt(a, b):
    return lax.dot_general(a, b, (((1,), (1,)), ((), ())), preferred_element_type=f32)


def dot_tn(a, b):
    return lax.dot_general(a, b, (((0,), (0,)), ((), ())), preferred_element_type=f32)


MESH = pl.DeviceIdType.MESH


def greet(peers):
    barrier = pltpu.get_barrier_semaphore()
    for peer in peers:
        pl.semaphore_signal(barrier, inc=1, device_id=peer, device_id_type=MESH)
    pl.semaphore_wait(barrier, len(peers))


def others(n):
    d, z = lax.axis_index("dp"), lax.axis_index("shard")
    return d, z, [(d, lax.rem(z + p, n)) for p in range(1, n)]


def gather_project_kernel(
    n, x_hbm, small_ref, wq_hbm, wk_hbm, wv_hbm,
    x_out, normed_out, q_out, k_out, v_out, small_out, sq_out,
    xs, nb, qb, kb, vb, wq, wk, wv, sq_all, small_all,
    load_sem, out_sem, up_sem, down_sem, recv_sem, small_send, small_recv, sq_send, sq_recv,
):
    T, D = xs.shape[1:]
    C = qb.shape[2]
    d, z, peers = others(n)
    own_load = pltpu.make_async_copy(x_hbm, xs.at[z], load_sem.at[0])
    own_load.start()
    loads = [
        pltpu.make_async_copy(src, dst, load_sem.at[i + 1])
        for i, (src, dst) in enumerate(((wq_hbm, wq), (wk_hbm, wk), (wv_hbm, wv)))
    ]
    for load in loads:
        load.start()
    greet(peers)

    def send_up(o):
        return pltpu.make_async_remote_copy(
            src_ref=xs.at[o], dst_ref=xs.at[o], send_sem=up_sem.at[o], recv_sem=recv_sem.at[o],
            device_id=(d, lax.rem(z + 1, n)), device_id_type=MESH,
        )

    def send_down(o):
        return pltpu.make_async_remote_copy(
            src_ref=xs.at[o], dst_ref=xs.at[o], send_sem=down_sem.at[o], recv_sem=recv_sem.at[o],
            device_id=(d, lax.rem(z + n - 1, n)), device_id_type=MESH,
        )

    own_load.wait()
    small_copies = []
    for p, peer in enumerate(peers):
        copy = pltpu.make_async_remote_copy(
            src_ref=small_ref, dst_ref=small_all.at[z], send_sem=small_send.at[p],
            recv_sem=small_recv.at[z], device_id=peer, device_id_type=MESH,
        )
        copy.start()
        small_copies.append(copy)

    @pl.when(z < n - 1)
    def _():
        send_up(z).start()

    @pl.when(z > 0)
    def _():
        send_down(z).start()

    small_all[z] = small_ref[...]
    for load in loads:
        load.wait()
    for p in range(1, n):
        o = lax.rem(z + n - p, n)
        pltpu.make_async_remote_copy(
            src_ref=small_ref, dst_ref=small_all.at[o], send_sem=small_send.at[p - 1],
            recv_sem=small_recv.at[o], device_id=(d, o), device_id_type=MESH,
        ).wait_recv()

    lanes = lax.broadcasted_iota(jnp.int32, (T, 128), 1)
    step_rows = 32

    def outs(o):
        return [
            pltpu.make_async_copy(src.at[o], dst.at[o], out_sem.at[i, o])
            for i, (src, dst) in enumerate(
                ((xs, x_out), (nb, normed_out), (qb, q_out), (kb, k_out), (vb, v_out))
            )
        ]

    def compute(o):
        gain = jnp.concatenate([small_all[s, 0:1, T:] for s in range(n)], axis=1)

        def norm_rows(i, carry):
            r = pl.ds(pl.multiple_of(i * step_rows, step_rows), step_rows)
            x = xs[o, r, :].astype(f32)
            factor = lax.rsqrt(jnp.sum(x * x, axis=1, keepdims=True) / D + EPSILON)
            nb[o, r, :] = (x * factor * gain).astype(bf16)
            return carry

        lax.fori_loop(0, T // step_rows, norm_rows, 0)
        q = jnp.dot(nb[o], wq[...], preferred_element_type=f32)
        qb[o] = q
        q_sum = jnp.sum(q * q, axis=1, keepdims=True)
        k = jnp.dot(nb[o], wk[...], preferred_element_type=f32)
        kb[o] = k
        k_sum = jnp.sum(k * k, axis=1, keepdims=True)
        vb[o] = jnp.dot(nb[o], wv[...], preferred_element_type=f32).astype(bf16)
        both = jnp.where(lanes == 0, q_sum, jnp.where(lanes == 1, k_sum, 0.0))
        sq_all[z, o] = both.T[0:8]
        for copy in outs(o):
            copy.start()

    def step(s, carry):
        below, above = z - s, z + s

        @pl.when((s > 0) & (below >= 0))
        def _():
            send_up(below).wait_recv()

            @pl.when(z < n - 1)
            def _():
                send_up(below).start()

        @pl.when((s > 0) & (above < n))
        def _():
            send_down(above).wait_recv()

            @pl.when(z > 0)
            def _():
                send_down(above).start()

        def side(j, inner):
            o = z - s + 2 * s * j

            @pl.when((o >= 0) & (o < n) & ((s > 0) | (j == 0)))
            def _():
                compute(o)

            return inner

        lax.fori_loop(0, 2, side, 0)
        return carry

    lax.fori_loop(0, n, step, 0)

    sq_copies = []
    for p, peer in enumerate(peers):
        copy = pltpu.make_async_remote_copy(
            src_ref=sq_all.at[z], dst_ref=sq_all.at[z], send_sem=sq_send.at[p],
            recv_sem=sq_recv.at[z], device_id=peer, device_id_type=MESH,
        )
        copy.start()
        sq_copies.append(copy)
    small_out[...] = small_all[...]

    def finish(o, carry):
        for copy in outs(o):
            copy.wait()

        @pl.when((z < n - 1) & (o <= z))
        def _():
            send_up(o).wait_send()

        @pl.when((z > 0) & (o >= z))
        def _():
            send_down(o).wait_send()

        return carry

    lax.fori_loop(0, n, finish, 0)
    for p in range(1, n):
        o = lax.rem(z + n - p, n)
        pltpu.make_async_remote_copy(
            src_ref=sq_all.at[o], dst_ref=sq_all.at[o], send_sem=sq_send.at[p - 1],
            recv_sem=sq_recv.at[o], device_id=(d, o), device_id_type=MESH,
        ).wait_recv()
    total = sq_all[0]
    for s in range(1, n):
        total = total + sq_all[s]
    sq_out[...] = total
    for copy in small_copies + sq_copies:
        copy.wait_send()


def gather_project(n, tokens, small, wq, wk, wv):
    T, D = tokens.shape
    C = wq.shape[1]
    hbm = pl.BlockSpec(memory_space=pl.ANY)
    vmem = pl.BlockSpec(memory_space=pltpu.VMEM)
    dma = pltpu.SemaphoreType.DMA
    return pl.pallas_call(
        functools.partial(gather_project_kernel, n),
        out_shape=[
            jax.ShapeDtypeStruct((n, T, D), bf16),
            jax.ShapeDtypeStruct((n, T, D), bf16),
            jax.ShapeDtypeStruct((n, T, C), f32),
            jax.ShapeDtypeStruct((n, T, C), f32),
            jax.ShapeDtypeStruct((n, T, C), bf16),
            jax.ShapeDtypeStruct((n,) + small.shape, f32),
            jax.ShapeDtypeStruct((n, 8, T), f32),
        ],
        in_specs=[hbm, vmem, hbm, hbm, hbm],
        out_specs=[hbm] * 5 + [vmem] * 2,
        scratch_shapes=[
            pltpu.VMEM((n, T, D), bf16),
            pltpu.VMEM((n, T, D), bf16),
            pltpu.VMEM((n, T, C), f32),
            pltpu.VMEM((n, T, C), f32),
            pltpu.VMEM((n, T, C), bf16),
            pltpu.VMEM((D, C), bf16),
            pltpu.VMEM((D, C), bf16),
            pltpu.VMEM((D, C), bf16),
            pltpu.VMEM((n, n, 8, T), f32),
            pltpu.VMEM((n,) + small.shape, f32),
            dma((4,)),
            dma((5, n)),
            dma((n,)),
            dma((n,)),
            dma((n,)),
            dma((n,)),
            dma((n,)),
            dma((n,)),
            dma((n,)),
        ],
        compiler_params=pltpu.CompilerParams(
            collective_id=0, has_side_effects=True, vmem_limit_bytes=VMEM_LIMIT
        ),
        cost_estimate=pl.CostEstimate(flops=80 * 10**9, bytes_accessed=32 * 2**20, transcendentals=0),
        name="gather_project",
    )(tokens, small, wq, wk, wv)


def rope(v, cosine, sine):
    return v * cosine + pltpu.roll(v, HEAD_DIM // 2, 1) * sine


def key_span(i, block, length):
    return min(length, max((i + 1) * block, length // 2))


def block_scores(q, k, i, block, limit):
    s = dot_nt(q, k) * (HEAD_DIM**-0.5)
    row = lax.broadcasted_iota(jnp.int32, s.shape, 0) + i * block
    col = lax.broadcasted_iota(jnp.int32, s.shape, 1)
    return jnp.where((col <= row) | (col < limit), s, MASKED)


def attention_kernel(prefix, q_raw, k_raw, v_ref, factors, cosine, sine, gains, q_out, k_out, mixed):
    length = q_raw.shape[0]
    block = 256
    limit = prefix[0]

    def turn(raw, out, column, gain):
        def part(i, carry):
            r = pl.ds(pl.multiple_of(i * block, block), block)
            v = raw[r, :] * factors[r, column : column + 1] * gain
            out[r, :] = rope(v, cosine[r, :], sine[r, :]).astype(bf16)
            return carry

        lax.fori_loop(0, length // block, part, 0)

    turn(q_raw, q_out, 0, gains[0:1, :])
    turn(k_raw, k_out, 1, gains[1:2, :])
    for i in range(length // block):
        span = key_span(i, block, length)
        r = pl.ds(i * block, block)
        s = block_scores(q_out[r, :], k_out[0:span, :], i, block, limit)
        e = jnp.exp(s - jnp.max(s, axis=1, keepdims=True))
        total = jnp.sum(e, axis=1, keepdims=True)
        mixed[r, :] = (dot(e.astype(bf16), v_ref[0:span, :]) / total).astype(bf16)


def attention(prefix, q_raw, k_raw, values, factors, cosine, sine, gains):
    length, local = q_raw.shape
    heads = local // HEAD_DIM
    head = pl.BlockSpec((length, HEAD_DIM), lambda h, p: (0, h))
    whole = lambda a: pl.BlockSpec(a.shape, lambda h, p: (0, 0))
    out = jax.ShapeDtypeStruct((length, local), bf16)
    return pl.pallas_call(
        attention_kernel,
        out_shape=[out] * 3,
        grid_spec=pltpu.PrefetchScalarGridSpec(
            num_scalar_prefetch=1,
            grid=(heads,),
            in_specs=[
                head, head, head, whole(factors), whole(cosine), whole(sine),
                pl.BlockSpec((2, HEAD_DIM), lambda h, p: (0, h)),
            ],
            out_specs=[head] * 3,
        ),
        compiler_params=pltpu.CompilerParams(vmem_limit_bytes=VMEM_LIMIT),
        cost_estimate=pl.CostEstimate(flops=14 * 10**9, bytes_accessed=16 * 2**20, transcendentals=0),
        name="attention",
    )(prefix, q_raw, k_raw, values, factors, cosine, sine, gains)


def attention_back_kernel(
    n, steps, width, limit_ref, q_ref, k_ref, v_ref, g_ref, q_raw, k_raw, factors, cosine, sine,
    gains, wq, wk, wv, normed_hbm, sum_hbm, gq_out, gk_out, gv_out, normed_out, gain_out, own_sum,
    dq_acc, dk_acc, k_acc, v_acc, q_grad, k_grad, v_grad, columns, turned, staged,
    inner_all, inner_send, inner_recv, column_sem, staged_sem, part, *line,
):
    length, local = q_ref.shape
    strips = width // local
    heads = local // HEAD_DIM
    block = 256
    blocks = length // block
    scale = HEAD_DIM**-0.5
    load_sem = line[-1]
    turn, drain = line_sum(n, steps, part, own_sum, *line[:-1])
    load = pltpu.make_async_copy(sum_hbm, part, load_sem.at[0])
    load.start()
    d, z, peers = others(n)
    greet(peers)

    def strip(b):
        c = pl.ds(pl.multiple_of(b * local, local), local)
        return pltpu.make_async_copy(
            normed_hbm.at[:, c], columns.at[lax.rem(b, 2)], column_sem.at[lax.rem(b, 2)]
        )

    strip(0).start()
    load.wait()
    turns = steps + n - 1
    in_heads, in_parts = 8 * turns // 19, 4 * turns // 19
    slots = -(-in_heads // heads)
    in_strips = turns - heads * slots - in_parts - 2

    def take(first, count, i, of):
        def one(t, carry):
            turn(first + t)
            return carry

        lax.fori_loop(i * count // of, (i + 1) * count // of, one, 0)
    limit = limit_ref[0:1, 0:1]
    lanes = lax.broadcasted_iota(jnp.int32, (block, 128), 1)

    def clear(i, carry):
        inner_all[z, i] = jnp.zeros((8, block), f32)
        return carry

    lax.fori_loop(0, blocks, clear, 0)

    def head(h, carry):
        c = pl.ds(pl.multiple_of(h * HEAD_DIM, HEAD_DIM), HEAD_DIM)
        k_acc[...] = jnp.zeros_like(k_acc)
        v_acc[...] = jnp.zeros_like(v_acc)
        for i in range(blocks):
            for j in range(i * slots // blocks, (i + 1) * slots // blocks):
                turn(h * slots + j)
            span = key_span(i, block, length)
            r = pl.ds(i * block, block)
            q, g, k, v = q_ref[r, c], g_ref[r, c], k_ref[0:span, c], v_ref[0:span, c]
            s = block_scores(q, k, i, block, limit)
            e = jnp.exp(s - jnp.max(s, axis=1, keepdims=True))
            p = e * (1.0 / jnp.sum(e, axis=1, keepdims=True))
            t = p * dot_nt(g, v)
            ds = (t - p * jnp.sum(t, axis=1, keepdims=True)).astype(bf16)
            dq_acc[r, c] = dot(ds, k) * scale
            k_acc[0:span, :] += dot_tn(ds, q) * scale
            v_acc[0:span, :] += dot_tn(p.astype(bf16), g)
        v_grad[:, c] = v_acc[...].astype(bf16)
        gain_q, gain_k = gains[0:1, c], gains[1:2, c]

        def back(i, carry):
            gq, gk = carry
            r = pl.ds(pl.multiple_of(i * block, block), block)
            cos, sin = cosine[r, :], sine[r, :]
            dq = rope(dq_acc[r, c], cos, -sin)
            dk = rope(k_acc[r, :], cos, -sin)
            uq = q_raw[r, c] * factors[r, 0:1]
            uk = k_raw[r, c] * factors[r, 1:2]
            gq = gq + jnp.sum(dq * uq, axis=0, keepdims=True)
            gk = gk + jnp.sum(dk * uk, axis=0, keepdims=True)
            dq = dq * gain_q
            dk = dk * gain_k
            dq_acc[r, c] = dq
            dk_acc[r, c] = dk
            inner_q = jnp.sum(dq * uq, axis=1, keepdims=True)
            inner_k = jnp.sum(dk * uk, axis=1, keepdims=True)
            both = jnp.where(lanes == 0, inner_q, jnp.where(lanes == 1, inner_k, 0.0))
            inner_all[z, i] += both.T[0:8]
            return gq, gk

        zero = jnp.zeros((1, HEAD_DIM), f32)
        gq, gk = lax.fori_loop(0, blocks, back, (zero, zero))
        gain_out[0:1, c] = gq
        gain_out[1:2, c] = gk
        return carry

    lax.fori_loop(0, heads, head, 0)

    copies = []
    for p, peer in enumerate(peers):
        copy = pltpu.make_async_remote_copy(
            src_ref=inner_all.at[z], dst_ref=inner_all.at[z], send_sem=inner_send.at[p],
            recv_sem=inner_recv.at[z], device_id=peer, device_id_type=MESH,
        )
        copy.start()
        copies.append(copy)
    turn(heads * slots)
    for p in range(1, n):
        o = lax.rem(z + n - p, n)
        pltpu.make_async_remote_copy(
            src_ref=inner_all.at[o], dst_ref=inner_all.at[o], send_sem=inner_send.at[p - 1],
            recv_sem=inner_recv.at[o], device_id=(d, o), device_id_type=MESH,
        ).wait_recv()

    def raw(i, carry):
        r = pl.ds(pl.multiple_of(i * block, block), block)
        total = inner_all[0, i]
        for s in range(1, n):
            total = total + inner_all[s, i]
        total = jnp.concatenate([total, jnp.zeros((120, block), f32)], axis=0).T
        fq, fk = factors[r, 0:1], factors[r, 1:2]
        mean_q, mean_k = total[:, 0:1] / width, total[:, 1:2] / width
        q_grad[r, :] = (fq * (dq_acc[r, :] - q_raw[r, :] * (fq * mean_q))).astype(bf16)
        k_grad[r, :] = (fk * (dk_acc[r, :] - k_raw[r, :] * (fk * mean_k))).astype(bf16)
        return carry

    lax.fori_loop(0, blocks, raw, 0)
    turn(heads * slots + 1)

    def save(i):
        r = pl.ds(pl.multiple_of(i * block, block), block)
        return pltpu.make_async_copy(
            staged.at[lax.rem(i, 2)], normed_out.at[r, :], staged_sem.at[lax.rem(i, 2)]
        )

    def rows_back(i, carry):
        r = pl.ds(pl.multiple_of(i * block, block), block)

        @pl.when(i >= 2)
        def _():
            save(i - 2).wait()

        staged[lax.rem(i, 2)] = (
            dot_nt(q_grad[r, :], wq[...])
            + dot_nt(k_grad[r, :], wk[...])
            + dot_nt(v_grad[r, :], wv[...])
        ).astype(bf16)
        save(i).start()
        take(heads * slots + 2, in_parts, i, blocks)
        return carry

    lax.fori_loop(0, blocks, rows_back, 0)

    def strip_grads(b, carry):
        strip(b).wait()

        @pl.when(b + 1 < strips)
        def _():
            strip(b + 1).start()

        turned[...] = columns[lax.rem(b, 2)].T
        c = pl.ds(pl.multiple_of(b * local, local), local)
        gq_out[c, :] = dot(turned[...], q_grad[...]).astype(bf16)
        gk_out[c, :] = dot(turned[...], k_grad[...]).astype(bf16)
        gv_out[c, :] = dot(turned[...], v_grad[...]).astype(bf16)
        take(heads * slots + 2 + in_parts, in_strips, b, strips)
        return carry

    lax.fori_loop(0, strips, strip_grads, 0)
    drain()
    for i in range(max(blocks - 2, 0), blocks):
        save(i).wait()
    for copy in copies:
        copy.wait_send()


def attention_back(
    n, width, limit, q, k, v, g, q_raw, k_raw, factors, cosine, sine, gains, wq, wk, wv, normed,
    sum_parts,
):
    length, local = q.shape
    _, steps, R, D = sum_parts.shape
    hbm = pl.BlockSpec(memory_space=pl.ANY)
    vmem = pl.BlockSpec(memory_space=pltpu.VMEM)
    dma = pltpu.SemaphoreType.DMA
    weight = jax.ShapeDtypeStruct((D, local), bf16)
    raw = pltpu.VMEM((length, local), bf16)
    return pl.pallas_call(
        functools.partial(attention_back_kernel, n, steps, width),
        out_shape=[
            weight, weight, weight, jax.ShapeDtypeStruct((length, D), bf16),
            jax.ShapeDtypeStruct((2, local), f32),
            jax.ShapeDtypeStruct((steps, R, D), f32),
        ],
        in_specs=[vmem] * 14 + [hbm, hbm],
        out_specs=[vmem, vmem, vmem, hbm, vmem, vmem],
        scratch_shapes=[
            pltpu.VMEM((length, local), f32),
            pltpu.VMEM((length, local), f32),
            pltpu.VMEM((length, HEAD_DIM), f32),
            pltpu.VMEM((length, HEAD_DIM), f32),
            raw,
            raw,
            raw,
            pltpu.VMEM((2, length, local), bf16),
            pltpu.VMEM((local, length), bf16),
            pltpu.VMEM((2, 256, D), bf16),
            pltpu.VMEM((n, length // 256, 8, 256), f32),
            dma((n,)),
            dma((n,)),
            dma((2,)),
            dma((2,)),
        ]
        + line_scratch(n, steps, R, D),
        compiler_params=pltpu.CompilerParams(
            collective_id=6, has_side_effects=True, vmem_limit_bytes=VMEM_LIMIT
        ),
        cost_estimate=pl.CostEstimate(
            flops=2 * 10**9, bytes_accessed=2**20, transcendentals=0
        ),
        name="attention_back",
    )(
        limit, q, k, v, g, q_raw, k_raw, factors, cosine, sine, gains, wq, wk, wv, normed, sum_parts
    )


def scatter_norm_kernel(n, groups, steps, gather, *refs):
    part, base, addend, gain = refs[:4]
    refs = refs[4:]
    if gather:
        out, all_out, gain_out = refs[:3]
        alls, ag_up, ag_down, ag_recv, all_sem = refs[3:8]
        refs = refs[8:]
    else:
        expert_gains, head_gains, out, gain_out = refs[:4]
        pieces, landed, sums, piece_send, piece_recv, sum_send, sum_recv = refs[4:11]
        refs = refs[11:]
    from_below, from_above, gain_acc, up_send, up_recv, down_send, down_recv = refs
    R, D = part.shape[2:]
    d, z, peers = others(n)
    upper, lower = (d, lax.rem(z + 1, n)), (d, lax.rem(z + n - 1, n))
    alike = [] if gather else [(lax.rem(d + p, groups), z) for p in range(1, groups)]
    greet(peers + alike)
    gain_acc[...] = jnp.zeros_like(gain_acc)

    def move_up(src, o, k):
        return pltpu.make_async_remote_copy(
            src_ref=src.at[o, k], dst_ref=from_below.at[o, k], send_sem=up_send.at[o, k],
            recv_sem=up_recv.at[o, k], device_id=upper, device_id_type=MESH,
        )

    def move_down(src, o, k):
        return pltpu.make_async_remote_copy(
            src_ref=src.at[o, k], dst_ref=from_above.at[o, k], send_sem=down_send.at[o, k],
            recv_sem=down_recv.at[o, k], device_id=lower, device_id_type=MESH,
        )

    def all_up(o, k):
        return pltpu.make_async_remote_copy(
            src_ref=alls.at[o, k], dst_ref=alls.at[o, k], send_sem=ag_up.at[o, k],
            recv_sem=ag_recv.at[o, k], device_id=upper, device_id_type=MESH,
        )

    def all_down(o, k):
        return pltpu.make_async_remote_copy(
            src_ref=alls.at[o, k], dst_ref=alls.at[o, k], send_sem=ag_down.at[o, k],
            recv_sem=ag_recv.at[o, k], device_id=lower, device_id_type=MESH,
        )

    def pass_up(k):
        def far(i, carry):
            o = z + n - 1 - i

            @pl.when(o < n)
            def _():
                @pl.when(z == 0)
                def _():
                    move_up(part, o, k).start()

                @pl.when(z > 0)
                def _():
                    move_up(part, o, k).wait_recv()
                    both = from_below[o, k].astype(f32) + part[o, k].astype(f32)
                    from_below[o, k] = both.astype(bf16)
                    move_up(from_below, o, k).start()

            return carry

        lax.fori_loop(0, n - 1, far, 0)

    def pass_down(k):
        def far(i, carry):
            o = z - n + 1 + i

            @pl.when(o >= 0)
            def _():
                @pl.when(z == n - 1)
                def _():
                    move_down(part, o, k).start()

                @pl.when(z < n - 1)
                def _():
                    move_down(part, o, k).wait_recv()
                    both = from_above[o, k].astype(f32) + part[o, k].astype(f32)
                    from_above[o, k] = both.astype(bf16)
                    move_down(from_above, o, k).start()

            return carry

        lax.fori_loop(0, n - 1, far, 0)

    def own(k):
        @pl.when(z > 0)
        def _():
            move_up(part, z, k).wait_recv()

        @pl.when(z == 0)
        def _():
            from_below[z, k] = jnp.zeros((R, D), bf16)

        @pl.when(z < n - 1)
        def _():
            move_down(part, z, k).wait_recv()

        @pl.when(z == n - 1)
        def _():
            from_above[z, k] = jnp.zeros((R, D), bf16)

        total = (
            part[z, k].astype(f32) + from_below[z, k].astype(f32) + from_above[z, k].astype(f32)
        )
        rows = base[k].astype(f32)
        factor = lax.rsqrt(jnp.sum(rows * rows, axis=1, keepdims=True) / D + EPSILON)
        unit = rows * factor
        along = total * unit
        gain_acc[...] += jnp.sum(along.reshape(R // 8, 8, D), axis=0)
        weighted = along * gain[...]
        mean = jnp.sum(weighted, axis=1, keepdims=True) / D
        result = addend[k].astype(f32) + factor * (total * gain[...] - unit * mean)
        out[k] = result
        if gather:
            alls[z, k] = result.astype(bf16)

            @pl.when(z < n - 1)
            def _():
                all_up(z, k).start()

            @pl.when(z > 0)
            def _():
                all_down(z, k).start()

    def forward(own_k):
        def hop(s, carry):
            below, above, k = z - s, z + s, own_k - s
            live = (k >= 0) & (k < steps)

            @pl.when(live & (below >= 0))
            def _():
                all_up(below, k).wait_recv()

                @pl.when(z < n - 1)
                def _():
                    all_up(below, k).start()

            @pl.when(live & (above < n))
            def _():
                all_down(above, k).wait_recv()

                @pl.when(z > 0)
                def _():
                    all_down(above, k).start()

            return carry

        lax.fori_loop(1, n, hop, 0)

    def turn(t, carry):
        up_k, down_k, own_k = t - z, t - (n - 1 - z), t - (n - 1)

        @pl.when((up_k >= 0) & (up_k < steps))
        def _():
            pass_up(up_k)

        @pl.when((down_k >= 0) & (down_k < steps))
        def _():
            pass_down(down_k)

        @pl.when((own_k >= 0) & (own_k < steps))
        def _():
            own(own_k)

        if gather:
            forward(own_k)

        return carry

    lax.fori_loop(0, steps + (2 * n - 2 if gather else n - 1), turn, 0)
    if gather:
        gain_out[...] = gain_acc[...]
    else:
        C = D // n
        for s in range(n):
            c = slice(s * C, (s + 1) * C)
            pieces[s, 0:1] = jnp.sum(gain_acc[:, c], axis=0, keepdims=True)
            pieces[s, 1:2] = jnp.sum(expert_gains[:, c], axis=0, keepdims=True)
            pieces[s, 2:8] = jnp.zeros((6, C), f32)

        def piece(p):
            o = lax.rem(z + p, n)
            return pltpu.make_async_remote_copy(
                src_ref=pieces.at[o], dst_ref=landed.at[z], send_sem=piece_send.at[p - 1],
                recv_sem=piece_recv.at[z], device_id=(d, o), device_id_type=MESH,
            )

        for p in range(1, n):
            piece(p).start()
        landed[z] = pieces[z]
        for p in range(1, n):
            o = lax.rem(z + n - p, n)
            pltpu.make_async_remote_copy(
                src_ref=pieces.at[o], dst_ref=landed.at[o], send_sem=piece_send.at[p - 1],
                recv_sem=piece_recv.at[o], device_id=(d, o), device_id_type=MESH,
            ).wait_recv()
        two = landed[0]
        for s in range(1, n):
            two = two + landed[s]
        sums[d, 0:1] = two[0:1]
        sums[d, 1:3] = head_gains[...]
        sums[d, 3:4] = two[1:2]
        sums[d, 4:8] = jnp.zeros((4, C), f32)
        for p in range(1, groups):
            pltpu.make_async_remote_copy(
                src_ref=sums.at[d], dst_ref=sums.at[d], send_sem=sum_send.at[p - 1],
                recv_sem=sum_recv.at[d], device_id=alike[p - 1], device_id_type=MESH,
            ).start()
        for p in range(1, groups):
            o = lax.rem(d + groups - p, groups)
            pltpu.make_async_remote_copy(
                src_ref=sums.at[o], dst_ref=sums.at[o], send_sem=sum_send.at[p - 1],
                recv_sem=sum_recv.at[o], device_id=(o, z), device_id_type=MESH,
            ).wait_recv()
        total = sums[0]
        for s in range(1, groups):
            total = total + sums[s]
        gain_out[...] = total
        for p in range(1, n):
            piece(p).wait_send()
        for p in range(1, groups):
            pltpu.make_async_remote_copy(
                src_ref=sums.at[d], dst_ref=sums.at[d], send_sem=sum_send.at[p - 1],
                recv_sem=sum_recv.at[d], device_id=alike[p - 1], device_id_type=MESH,
            ).wait_send()

    def drain(i, carry):
        o, k = i // steps, i % steps

        @pl.when(o > z)
        def _():
            move_up(part, o, k).wait_send()

        @pl.when(o < z)
        def _():
            move_down(part, o, k).wait_send()

        if gather:

            @pl.when((z < n - 1) & (o <= z))
            def _():
                all_up(o, k).wait_send()

            @pl.when((z > 0) & (o >= z))
            def _():
                all_down(o, k).wait_send()

        return carry

    lax.fori_loop(0, n * steps, drain, 0)
    if gather:
        copies = [pltpu.make_async_copy(alls.at[o], all_out.at[o], all_sem.at[o]) for o in range(n)]
        for copy in copies:
            copy.start()
        for copy in copies:
            copy.wait()


def scatter_norm(n, groups, steps, part, base, addend, gain, other_gains=None):
    gather = other_gains is None
    T, D = base.shape
    R = T // steps
    C = D // n
    hbm = pl.BlockSpec(memory_space=pl.ANY)
    vmem = pl.BlockSpec(memory_space=pltpu.VMEM)
    dma = pltpu.SemaphoreType.DMA
    slots = pltpu.VMEM((n, steps, R, D), bf16)
    rows = jax.ShapeDtypeStruct((steps, R, D), f32)
    sems = dma((n, steps))
    if gather:
        own = [slots, sems, sems, sems, dma((n,))]
        outs = [rows, jax.ShapeDtypeStruct((n, steps, R, D), bf16)]
        outs += [jax.ShapeDtypeStruct((8, D), f32)]
    else:
        own = [
            pltpu.VMEM((n, 8, C), f32), pltpu.VMEM((n, 8, C), f32),
            pltpu.VMEM((groups, 8, C), f32), dma((n,)), dma((n,)), dma((groups,)), dma((groups,)),
        ]
        outs = [rows, jax.ShapeDtypeStruct((8, C), f32)]
    return pl.pallas_call(
        functools.partial(scatter_norm_kernel, n, groups, steps, gather),
        out_shape=outs,
        in_specs=[vmem] * (4 if gather else 6),
        out_specs=[vmem, hbm, vmem] if gather else [vmem, vmem],
        scratch_shapes=own + [slots, slots, pltpu.VMEM((8, D), f32), sems, sems, sems, sems],
        compiler_params=pltpu.CompilerParams(
            collective_id=2 if gather else 3, has_side_effects=True, vmem_limit_bytes=VMEM_LIMIT
        ),
        cost_estimate=pl.CostEstimate(
            flops=10**9, bytes_accessed=2**20, transcendentals=0
        ),
        name="scatter_norm_gather" if gather else "scatter_norm",
    )(
        part.reshape(n, steps, R, D),
        base.reshape(steps, R, D),
        addend.reshape(steps, R, D),
        gain,
        *(() if gather else other_gains),
    )


def gather_mix_kernel(
    n, mixed_hbm, weight_hbm, x_ref, gain, mixed_out, in_out, own_out,
    ms, acc, weight, load_sem, up_sem, down_sem, recv_sem, out_sem,
):
    L, C = ms.shape[1:]
    D = weight.shape[1]
    T = own_out.shape[0]
    d, z, peers = others(n)
    own_load = pltpu.make_async_copy(mixed_hbm, ms.at[z], load_sem.at[0])
    own_load.start()
    weight_load = pltpu.make_async_copy(weight_hbm, weight, load_sem.at[1])
    weight_load.start()
    greet(peers)

    def send_up(o):
        return pltpu.make_async_remote_copy(
            src_ref=ms.at[o], dst_ref=ms.at[o], send_sem=up_sem.at[o], recv_sem=recv_sem.at[o],
            device_id=(d, lax.rem(z + 1, n)), device_id_type=MESH,
        )

    def send_down(o):
        return pltpu.make_async_remote_copy(
            src_ref=ms.at[o], dst_ref=ms.at[o], send_sem=down_sem.at[o], recv_sem=recv_sem.at[o],
            device_id=(d, lax.rem(z + n - 1, n)), device_id_type=MESH,
        )

    own_load.wait()

    @pl.when(z < n - 1)
    def _():
        send_up(z).start()

    @pl.when(z > 0)
    def _():
        send_down(z).start()

    weight_load.wait()
    block = 256

    def add(o, first):
        w = weight[pl.ds(pl.multiple_of(o * C, C), C), :]

        def rows(i, carry):
            r = pl.ds(pl.multiple_of(i * block, block), block)
            new = jnp.dot(ms[o, r, :], w, preferred_element_type=f32)
            acc[r, :] = new if first else acc[r, :] + new
            return carry

        lax.fori_loop(0, L // block, rows, 0)

    def save(o):
        return pltpu.make_async_copy(ms.at[o], mixed_out.at[o], out_sem.at[o])

    add(z, True)
    save(z).start()

    def step(s, carry):
        below, above = z - s, z + s

        @pl.when(below >= 0)
        def _():
            send_up(below).wait_recv()

            @pl.when(z < n - 1)
            def _():
                send_up(below).start()

        @pl.when(above < n)
        def _():
            send_down(above).wait_recv()

            @pl.when(z > 0)
            def _():
                send_down(above).start()

        def side(j, inner):
            o = z - s + 2 * s * j

            @pl.when((o >= 0) & (o < n))
            def _():
                add(o, False)
                save(o).start()

            return inner

        lax.fori_loop(0, 2, side, 0)
        return carry

    lax.fori_loop(1, n, step, 0)
    own_rows = pl.ds(pl.multiple_of(z * T, T), T)
    own_out[...] = acc[own_rows, :]
    part = 32

    def norm_rows(i, carry):
        r = pl.ds(pl.multiple_of(i * part, part), part)
        v = acc[r, :] + x_ref[r, :].astype(f32)
        factor = lax.rsqrt(jnp.sum(v * v, axis=1, keepdims=True) / D + EPSILON)
        in_out[r, :] = (v * factor * gain[...]).astype(bf16)
        return carry

    lax.fori_loop(0, L // part, norm_rows, 0)

    def finish(o, carry):
        save(o).wait()

        @pl.when((z < n - 1) & (o <= z))
        def _():
            send_up(o).wait_send()

        @pl.when((z > 0) & (o >= z))
        def _():
            send_down(o).wait_send()

        return carry

    lax.fori_loop(0, n, finish, 0)


def gather_mix(n, mixed, weight, x_all, gain, rows):
    L, C = mixed.shape
    D = weight.shape[1]
    hbm = pl.BlockSpec(memory_space=pl.ANY)
    vmem = pl.BlockSpec(memory_space=pltpu.VMEM)
    dma = pltpu.SemaphoreType.DMA
    return pl.pallas_call(
        functools.partial(gather_mix_kernel, n),
        out_shape=[
            jax.ShapeDtypeStruct((n, L, C), bf16),
            jax.ShapeDtypeStruct((L, D), bf16),
            jax.ShapeDtypeStruct((rows, D), f32),
        ],
        in_specs=[hbm, hbm, vmem, vmem],
        out_specs=[hbm, vmem, vmem],
        scratch_shapes=[
            pltpu.VMEM((n, L, C), bf16),
            pltpu.VMEM((L, D), f32),
            pltpu.VMEM((D, D), bf16),
            dma((2,)),
            dma((n,)),
            dma((n,)),
            dma((n,)),
            dma((n,)),
        ],
        compiler_params=pltpu.CompilerParams(
            collective_id=1, has_side_effects=True, vmem_limit_bytes=VMEM_LIMIT
        ),
        cost_estimate=pl.CostEstimate(flops=100 * 10**9, bytes_accessed=32 * 2**20, transcendentals=0),
        name="gather_mix",
    )(mixed, weight, x_all, gain)


def experts_kernel(
    x_ref, g_ref, combine, gate_w, up_w, down_w,
    sum_out, in_out, hidden_out, gate_out, up_out, sum_acc, in_acc,
):
    e = pl.program_id(1)
    last = pl.num_programs(1) - 1
    x, g = x_ref[...], g_ref[...]
    gate_m, up_m, down_m = gate_w[0], up_w[0], down_w[0]
    lane = lax.broadcasted_iota(jnp.int32, combine.shape, 1)
    weight = jnp.sum(jnp.where(lane == e, combine[...], 0.0), axis=1, keepdims=True)
    gate_part = dot(x, gate_m)
    up_part = dot(x, up_m)
    hidden_grad = dot_nt(g, down_m) * weight
    sig = jax.nn.sigmoid(gate_part)
    silu = gate_part * sig
    hidden = (silu * up_part * weight).astype(bf16)
    hidden_out[...] = hidden
    up_grad = (hidden_grad * silu).astype(bf16)
    up_out[...] = up_grad
    gate_grad = (hidden_grad * up_part * sig * (1.0 + gate_part * (1.0 - sig))).astype(bf16)
    gate_out[...] = gate_grad
    made = dot(hidden, down_m)
    back = dot_nt(gate_grad, gate_m) + dot_nt(up_grad, up_m)

    @pl.when(e == 0)
    def _():
        sum_acc[...] = made
        in_acc[...] = back

    @pl.when((e > 0) & (e < last))
    def _():
        sum_acc[...] += made
        in_acc[...] += back

    @pl.when((e > 0) & (e == last))
    def _():
        sum_out[...] = (sum_acc[...] + made).astype(bf16)
        in_out[...] = (in_acc[...] + back).astype(bf16)

    @pl.when((e == 0) & (e == last))
    def _():
        sum_out[...] = made.astype(bf16)
        in_out[...] = back.astype(bf16)


def experts_pass(x, g, combine, gate_w, up_w, down_w):
    L, D = x.shape
    E, _, F = gate_w.shape
    block = min(512, L)
    rows = pl.BlockSpec((block, D), lambda i, e: (i, 0))
    units = pl.BlockSpec((block, F), lambda i, e: (i, e))
    column = pl.BlockSpec((1, D, F), lambda i, e: (e, 0, 0))
    wide = jax.ShapeDtypeStruct((L, D), bf16)
    narrow = jax.ShapeDtypeStruct((L, E * F), bf16)
    return pl.pallas_call(
        experts_kernel,
        out_shape=[wide, wide, narrow, narrow, narrow],
        grid=(L // block, E),
        in_specs=[
            rows, rows, pl.BlockSpec((block, combine.shape[1]), lambda i, e: (i, 0)),
            column, column, pl.BlockSpec((1, F, D), lambda i, e: (e, 0, 0)),
        ],
        out_specs=[rows, rows, units, units, units],
        scratch_shapes=[pltpu.VMEM((block, D), f32), pltpu.VMEM((block, D), f32)],
        compiler_params=pltpu.CompilerParams(vmem_limit_bytes=VMEM_LIMIT),
        cost_estimate=pl.CostEstimate(
            flops=12 * L * D * E * F, bytes_accessed=40 * 2**20, transcendentals=L * E * F
        ),
        name="experts_pass",
    )(x, g, combine, gate_w, up_w, down_w)


def line_sum(n, steps, part, out, landed, up_send, up_recv, down_send, down_recv):
    d, z = lax.axis_index("dp"), lax.axis_index("shard")
    upper, lower = (d, lax.rem(z + 1, n)), (d, lax.rem(z + n - 1, n))

    def move_up(src, o, k):
        return pltpu.make_async_remote_copy(
            src_ref=src.at[o, k], dst_ref=landed.at[o, k], send_sem=up_send.at[o, k],
            recv_sem=up_recv.at[o, k], device_id=upper, device_id_type=MESH,
        )

    def move_down(src, o, k):
        slot = jnp.where(o == z - 1, n, o)
        return pltpu.make_async_remote_copy(
            src_ref=src.at[o, k], dst_ref=landed.at[slot, k], send_sem=down_send.at[o, k],
            recv_sem=down_recv.at[o, k], device_id=lower, device_id_type=MESH,
        )

    def passing(move, first, owner):
        def run(k):
            def far(i, carry):
                o = owner(i)

                @pl.when((o >= 0) & (o < n))
                def _():
                    @pl.when(z == first)
                    def _():
                        move(part, o, k).start()

                    @pl.when(z != first)
                    def _():
                        move(part, o, k).wait_recv()
                        both = landed[o, k].astype(f32) + part[o, k].astype(f32)
                        landed[o, k] = both.astype(bf16)
                        move(landed, o, k).start()

                return carry

            lax.fori_loop(0, n - 1, far, 0)

        return run

    pass_up = passing(move_up, 0, lambda i: z + n - 1 - i)
    pass_down = passing(move_down, n - 1, lambda i: z - n + 1 + i)

    def own(k):
        @pl.when(z > 0)
        def _():
            move_up(part, z, k).wait_recv()

        @pl.when(z == 0)
        def _():
            landed[z, k] = jnp.zeros(part.shape[2:], bf16)

        @pl.when(z < n - 1)
        def _():
            move_down(part, z, k).wait_recv()

        @pl.when(z == n - 1)
        def _():
            landed[n, k] = jnp.zeros(part.shape[2:], bf16)

        out[k] = part[z, k].astype(f32) + landed[z, k].astype(f32) + landed[n, k].astype(f32)

    def turn(t):
        up_k, down_k, own_k = t - z, t - (n - 1 - z), t - (n - 1)

        @pl.when((up_k >= 0) & (up_k < steps))
        def _():
            pass_up(up_k)

        @pl.when((down_k >= 0) & (down_k < steps))
        def _():
            pass_down(down_k)

        @pl.when((own_k >= 0) & (own_k < steps))
        def _():
            own(own_k)

    def drain():
        def one(i, carry):
            o, k = i // steps, i % steps

            @pl.when(o > z)
            def _():
                move_up(part, o, k).wait_send()

            @pl.when(o < z)
            def _():
                move_down(part, o, k).wait_send()

            return carry

        lax.fori_loop(0, n * steps, one, 0)

    return turn, drain


def line_scratch(n, steps, R, D):
    dma = pltpu.SemaphoreType.DMA
    slots = [pltpu.VMEM((n, steps, R, D), bf16), pltpu.VMEM((n + 1, steps, R, D), bf16)]
    return slots + [dma((n, steps))] * 4 + [dma((1,))]


def expert_grads_kernel(x_ref, g_ref, hidden, gate_grad, up_grad, gate_out, up_out, down_out, xt):
    @pl.when(pl.program_id(0) == 0)
    def _():
        xt[...] = x_ref[...].T

    gate_out[0] = dot(xt[...], gate_grad[...]).astype(bf16)
    up_out[0] = dot(xt[...], up_grad[...]).astype(bf16)
    down_out[0] = dot_tn(hidden[...], g_ref[...]).astype(bf16)


def expert_grads(x, g, hidden, gate_grad, up_grad, experts):
    L, D = x.shape
    F = hidden.shape[1] // experts
    whole = pl.BlockSpec((L, D), lambda e: (0, 0))
    units = pl.BlockSpec((L, F), lambda e: (0, e))
    column = pl.BlockSpec((1, D, F), lambda e: (e, 0, 0))
    grad = jax.ShapeDtypeStruct((experts, D, F), bf16)
    return pl.pallas_call(
        expert_grads_kernel,
        out_shape=[grad, grad, jax.ShapeDtypeStruct((experts, F, D), bf16)],
        grid=(experts,),
        in_specs=[whole, whole, units, units, units],
        out_specs=[column, column, pl.BlockSpec((1, F, D), lambda e: (e, 0, 0))],
        scratch_shapes=[pltpu.VMEM((D, L), bf16)],
        compiler_params=pltpu.CompilerParams(vmem_limit_bytes=VMEM_LIMIT),
        cost_estimate=pl.CostEstimate(
            flops=6 * L * D * experts * F, bytes_accessed=26 * 2**20, transcendentals=0
        ),
        name="expert_grads",
    )(x, g, hidden, gate_grad, up_grad)


def widen_kernel(count, *refs):
    for src, dst in zip(refs[:count], refs[count:]):
        dst[...] = src[...].astype(f32)


def widen(*arrays):
    flat = [v.reshape(-1, v.shape[-1]) for v in arrays]
    steps = 8
    specs = [
        pl.BlockSpec((v.shape[0] // steps, v.shape[1]), lambda i: (i, 0)) for v in flat
    ]
    out = pl.pallas_call(
        functools.partial(widen_kernel, len(flat)),
        out_shape=[jax.ShapeDtypeStruct(v.shape, f32) for v in flat],
        grid=(steps,),
        in_specs=specs,
        out_specs=specs,
        compiler_params=pltpu.CompilerParams(vmem_limit_bytes=VMEM_LIMIT),
        cost_estimate=pl.CostEstimate(
            flops=0, bytes_accessed=sum(6 * v.size for v in flat), transcendentals=0
        ),
        name="widen",
    )(*flat)
    return tuple(v.reshape(w.shape) for v, w in zip(out, arrays))


def gather_line_kernel(n, v_hbm, out, slots, load_sem, up_sem, down_sem, recv_sem, out_sem):
    d, z, peers = others(n)
    own_load = pltpu.make_async_copy(v_hbm, slots.at[z], load_sem.at[0])
    own_load.start()
    greet(peers)

    def send_up(o):
        return pltpu.make_async_remote_copy(
            src_ref=slots.at[o], dst_ref=slots.at[o], send_sem=up_sem.at[o],
            recv_sem=recv_sem.at[o], device_id=(d, lax.rem(z + 1, n)), device_id_type=MESH,
        )

    def send_down(o):
        return pltpu.make_async_remote_copy(
            src_ref=slots.at[o], dst_ref=slots.at[o], send_sem=down_sem.at[o],
            recv_sem=recv_sem.at[o], device_id=(d, lax.rem(z + n - 1, n)), device_id_type=MESH,
        )

    own_load.wait()

    @pl.when(z < n - 1)
    def _():
        send_up(z).start()

    @pl.when(z > 0)
    def _():
        send_down(z).start()

    def save(o):
        return pltpu.make_async_copy(slots.at[o], out.at[o], out_sem.at[o])

    save(z).start()

    def step(s, carry):
        below, above = z - s, z + s

        @pl.when(below >= 0)
        def _():
            send_up(below).wait_recv()

            @pl.when(z < n - 1)
            def _():
                send_up(below).start()

            save(below).start()

        @pl.when(above < n)
        def _():
            send_down(above).wait_recv()

            @pl.when(z > 0)
            def _():
                send_down(above).start()

            save(above).start()

        return carry

    lax.fori_loop(1, n, step, 0)

    def finish(o, carry):
        save(o).wait()

        @pl.when((z < n - 1) & (o <= z))
        def _():
            send_up(o).wait_send()

        @pl.when((z > 0) & (o >= z))
        def _():
            send_down(o).wait_send()

        return carry

    lax.fori_loop(0, n, finish, 0)


def gather_line(n, v, collective_id):
    hbm = pl.BlockSpec(memory_space=pl.ANY)
    dma = pltpu.SemaphoreType.DMA
    return pl.pallas_call(
        functools.partial(gather_line_kernel, n),
        out_shape=jax.ShapeDtypeStruct((n,) + v.shape, v.dtype),
        in_specs=[hbm],
        out_specs=hbm,
        scratch_shapes=[
            pltpu.VMEM((n,) + v.shape, v.dtype), dma((1,)), dma((n,)), dma((n,)), dma((n,)),
            dma((n,)),
        ],
        compiler_params=pltpu.CompilerParams(
            collective_id=collective_id, has_side_effects=True, vmem_limit_bytes=VMEM_LIMIT
        ),
        cost_estimate=pl.CostEstimate(flops=20 * 10**9, bytes_accessed=2 * 2**20, transcendentals=0),
        name="gather_line",
    )(v)


def per_device(
    tokens,
    out_grad,
    routes,
    gate_weights,
    prefix,
    query_weight,
    key_weight,
    value_weight,
    output_weight,
    norm_gains,
    expert_gate,
    expert_up,
    expert_down,
):
    rows, width = tokens.shape
    shards = lax.axis_size("shard")
    groups = lax.axis_size("dp")
    place = lax.axis_index("shard")
    group = lax.axis_index("dp")
    length = rows * shards
    local = width // shards
    experts = expert_gate.shape[0]
    units = expert_gate.shape[2]

    expert_ids = jnp.arange(experts, dtype=jnp.int32)
    weight_own = jnp.sum(
        jnp.where(routes[:, :, None] == expert_ids[None, None, :], gate_weights[:, :, None], 0.0),
        axis=1,
    )
    own_gains = norm_gains.astype(f32)
    small = jnp.concatenate(
        [
            jnp.pad(weight_own.T, ((0, 8 - experts), (0, 0))),
            jnp.pad(jnp.stack([own_gains[0], own_gains[3]]), ((0, 6), (0, 0))),
        ],
        axis=1,
    )
    x_all_b, normed, query_raw, key_raw, values, small_all, squares = gather_project(
        shards, tokens, small, query_weight, key_weight, value_weight
    )
    x_all_b = x_all_b.reshape(length, width)
    normed = normed.reshape(length, width)
    query_raw = query_raw.reshape(length, local)
    key_raw = key_raw.reshape(length, local)
    values = values.reshape(length, local)
    combine = small_all[:, :experts, :rows].transpose(0, 2, 1).reshape(length, experts)
    gain_in = small_all[:, 0, rows:].reshape(width)
    gain_expert = small_all[:, 1, rows:].reshape(width)
    head_gains = own_gains[1:3]
    slab = width // groups
    out_grad_b, squares = lax.optimization_barrier((out_grad, squares))
    out_slab = lax.dynamic_slice_in_dim(output_weight, group * slab, slab, 0)
    out_slab = gather_line(shards, out_slab, 4).transpose(1, 0, 2).reshape(slab, width)
    full_output = lax.all_gather(out_slab, "dp", axis=0, tiled=True)

    factors = lax.rsqrt(squares[:, :2].transpose(0, 2, 1).reshape(length, 2) / width + EPSILON)
    cosine, sine = rotary_tables(length)
    queries, keys, mixed_own = attention(
        prefix, query_raw, key_raw, values, factors, cosine, sine, head_gains
    )
    mixed_all, expert_in, attended_own = gather_mix(
        shards, mixed_own, full_output, x_all_b, gain_expert[None, :], rows
    )

    g_all = lax.all_gather(out_grad_b, "shard", axis=0, tiled=True)
    sum_part, in_part, hidden, gate_grad, up_grad = experts_pass(
        expert_in, g_all, combine, expert_gate, expert_up, expert_down
    )
    sum_parts = sum_part.reshape(shards, 16, rows // 16, width)
    grad_gate, grad_up, grad_down = expert_grads(
        expert_in, g_all, hidden, gate_grad, up_grad, experts
    )
    in_part, grad_gate, grad_up, grad_down = lax.optimization_barrier(
        (in_part, grad_gate, grad_up, grad_down)
    )
    grad_gate, grad_up, grad_down = lax.psum((grad_gate, grad_up, grad_down), "dp")

    x_own = tokens.astype(f32)
    residual_own = x_own + attended_own
    residual_grad, attended_grad, gain_grad_res = scatter_norm(
        shards, groups, 16, in_part, residual_own, out_grad, gain_expert[None, :]
    )
    residual_grad = residual_grad.reshape(rows, width)
    attended_grad = attended_grad.reshape(length, width)

    own_columns = lax.dynamic_slice_in_dim(attended_grad, place * local, local, 1)
    grad_output = lax.dot_general(
        mixed_all, own_columns, (((1,), (0,)), ((), ())), preferred_element_type=f32
    ).reshape(width, local)
    mixed_grad = dot_nt(
        attended_grad, lax.dynamic_slice_in_dim(full_output, place * local, local, 0)
    ).astype(bf16)
    limit = jnp.broadcast_to(prefix.reshape(1, 1), (8, 128))
    grad_query, grad_key, grad_value, normed_part, gain_grad_heads, expert_sum = attention_back(
        shards, width, limit, queries, keys, values, mixed_grad, query_raw, key_raw, factors,
        cosine, sine, head_gains, query_weight, key_weight, value_weight, normed, sum_parts,
    )
    expert_sum = expert_sum.reshape(rows, width)
    attention_grads, normed_part, grad_gate, grad_up, grad_down = lax.optimization_barrier(
        (
            (grad_query, grad_key, grad_value, grad_output.astype(bf16)),
            normed_part,
            grad_gate,
            grad_up,
            grad_down,
        )
    )
    grad_query, grad_key, grad_value, grad_output = lax.psum(attention_grads, "dp")
    grad_tokens, grad_gains = scatter_norm(
        shards, groups, 8, normed_part, tokens, residual_grad, gain_in[None, :],
        (gain_grad_res, gain_grad_heads),
    )
    grad_tokens = grad_tokens.reshape(rows, width)
    grad_gains = grad_gains[:4]
    output = residual_own + expert_sum
    root_means = jnp.stack([root_mean(attended_own), root_mean(expert_sum), root_mean(output)])
    grad_gate, grad_up, grad_down = widen(grad_gate, grad_up, grad_down)
    grad_query, grad_key, grad_value, grad_output = widen(
        grad_query, grad_key, grad_value, grad_output
    )

    return (
        output.astype(bf16),
        grad_tokens,
        root_means,
        grad_query,
        grad_key,
        grad_value,
        grad_output,
        grad_gains,
        grad_gate,
        grad_up,
        grad_down,
    )


def solution(mesh):
    placed = (
        P(("dp", "shard"), None),
        P(("dp", "shard"), None),
        P(("dp", "shard"), None),
        P(("dp", "shard"), None),
        P("dp"),
        P(None, "shard"),
        P(None, "shard"),
        P(None, "shard"),
        P(None, "shard"),
        P(None, "shard"),
        P(None, None, "shard"),
        P(None, None, "shard"),
        P(None, "shard", None),
    )
    return jax.shard_map(
        per_device,
        mesh=mesh,
        in_specs=placed,
        out_specs=(
            P(("dp", "shard"), None),
            P(("dp", "shard"), None),
            P(None, ("dp", "shard")),
            P(None, "shard"),
            P(None, "shard"),
            P(None, "shard"),
            P(None, "shard"),
            P(None, "shard"),
            P(None, None, "shard"),
            P(None, None, "shard"),
            P(None, "shard", None),
        ),
        check_vma=False,
    )
```

```python
import functools

import jax
import jax.numpy as jnp
import numpy as np
from jax import lax
from jax.experimental import pallas as pl
from jax.experimental.pallas import tpu as pltpu
from jax.sharding import PartitionSpec as P

HEAD_DIM = 128
EPSILON = 1e-05
ROPE_BASE = 10000.0
MASKED = -1e30
VMEM_LIMIT = 60 * 2**20

f32 = jnp.float32
bf16 = jnp.bfloat16


def rotary_tables(row_count):
    half_dim = HEAD_DIM // 2
    inverse = ROPE_BASE ** (-np.arange(half_dim) / half_dim)
    angles = np.arange(row_count)[:, None] * inverse.astype(np.float32).astype(np.float64)[None, :]
    angles = angles.astype(np.float32).astype(np.float64)
    cosine, sine = np.cos(angles), np.sin(angles)
    return (
        jnp.asarray(np.concatenate([cosine, cosine], 1), f32),
        jnp.asarray(np.concatenate([-sine, sine], 1), f32),
    )


def row_factor(values):
    return lax.rsqrt(jnp.mean(values * values, axis=-1, keepdims=True) + EPSILON)


def norm_back(grad_unit, unit_rows, factor):
    return factor * (
        grad_unit - unit_rows * jnp.mean(grad_unit * unit_rows, axis=-1, keepdims=True)
    )


def root_mean(values):
    return jnp.sqrt(jnp.mean(values * values, axis=-1))


def dot(a, b):
    return jnp.dot(a, b, preferred_element_type=f32)


def dot_nt(a, b):
    return lax.dot_general(a, b, (((1,), (1,)), ((), ())), preferred_element_type=f32)


def dot_tn(a, b):
    return lax.dot_general(a, b, (((0,), (0,)), ((), ())), preferred_element_type=f32)


MESH = pl.DeviceIdType.MESH


def greet(peers):
    barrier = pltpu.get_barrier_semaphore()
    for peer in peers:
        pl.semaphore_signal(barrier, inc=1, device_id=peer, device_id_type=MESH)
    pl.semaphore_wait(barrier, len(peers))


def others(n):
    d, z = lax.axis_index("dp"), lax.axis_index("shard")
    return d, z, [(d, lax.rem(z + p, n)) for p in range(1, n)]


def line_gather(n, slots, up_sem, down_sem, recv_sem):
    d, z = lax.axis_index("dp"), lax.axis_index("shard")

    def send_up(o):
        return pltpu.make_async_remote_copy(
            src_ref=slots.at[o], dst_ref=slots.at[o], send_sem=up_sem.at[o],
            recv_sem=recv_sem.at[o], device_id=(d, lax.rem(z + 1, n)), device_id_type=MESH,
        )

    def send_down(o):
        return pltpu.make_async_remote_copy(
            src_ref=slots.at[o], dst_ref=slots.at[o], send_sem=down_sem.at[o],
            recv_sem=recv_sem.at[o], device_id=(d, lax.rem(z + n - 1, n)), device_id_type=MESH,
        )

    def begin():
        @pl.when(z < n - 1)
        def _():
            send_up(z).start()

        @pl.when(z > 0)
        def _():
            send_down(z).start()

    def hop(s, landed):
        below, above = z - s, z + s

        @pl.when((s > 0) & (below >= 0))
        def _():
            send_up(below).wait_recv()

            @pl.when(z < n - 1)
            def _():
                send_up(below).start()

            landed(below)

        @pl.when((s > 0) & (above < n))
        def _():
            send_down(above).wait_recv()

            @pl.when(z > 0)
            def _():
                send_down(above).start()

            landed(above)

    def drain():
        def one(o, carry):
            @pl.when((z < n - 1) & (o <= z))
            def _():
                send_up(o).wait_send()

            @pl.when((z > 0) & (o >= z))
            def _():
                send_down(o).wait_send()

            return carry

        lax.fori_loop(0, n, one, 0)

    return begin, hop, drain


def gather_project_kernel(
    n, x_hbm, small_ref, slab_hbm, wq_hbm, wk_hbm, wv_hbm,
    x_out, normed_out, q_out, k_out, v_out, slab_out, small_out, sq_out,
    slabs, xs, nb, qb, kb, vb, wq, wk, wv, sq_all, small_all,
    load_sem, out_sem, up_sem, down_sem, recv_sem, small_send, small_recv, sq_send, sq_recv,
    slab_up, slab_down, slab_recv, slab_sem,
):
    T, D = xs.shape[1:]
    C = qb.shape[2]
    d, z, peers = others(n)
    slab_load = pltpu.make_async_copy(slab_hbm, slabs.at[z], load_sem.at[4])
    slab_load.start()
    own_load = pltpu.make_async_copy(x_hbm, xs.at[z], load_sem.at[0])
    own_load.start()
    slab_begin, slab_hop, slab_drain = line_gather(n, slabs, slab_up, slab_down, slab_recv)

    def slab_save(o):
        c = pl.ds(pl.multiple_of(o * C, C), C)
        return pltpu.make_async_copy(slabs.at[o], slab_out.at[:, c], slab_sem.at[o])

    loads = [
        pltpu.make_async_copy(src, dst, load_sem.at[i + 1])
        for i, (src, dst) in enumerate(((wq_hbm, wq), (wk_hbm, wk), (wv_hbm, wv)))
    ]
    for load in loads:
        load.start()
    greet(peers)

    def send_up(o):
        return pltpu.make_async_remote_copy(
            src_ref=xs.at[o], dst_ref=xs.at[o], send_sem=up_sem.at[o], recv_sem=recv_sem.at[o],
            device_id=(d, lax.rem(z + 1, n)), device_id_type=MESH,
        )

    def send_down(o):
        return pltpu.make_async_remote_copy(
            src_ref=xs.at[o], dst_ref=xs.at[o], send_sem=down_sem.at[o], recv_sem=recv_sem.at[o],
            device_id=(d, lax.rem(z + n - 1, n)), device_id_type=MESH,
        )

    slab_load.wait()
    slab_begin()
    slab_save(z).start()
    own_load.wait()
    small_copies = []
    for p, peer in enumerate(peers):
        copy = pltpu.make_async_remote_copy(
            src_ref=small_ref, dst_ref=small_all.at[z], send_sem=small_send.at[p],
            recv_sem=small_recv.at[z], device_id=peer, device_id_type=MESH,
        )
        copy.start()
        small_copies.append(copy)

    @pl.when(z < n - 1)
    def _():
        send_up(z).start()

    @pl.when(z > 0)
    def _():
        send_down(z).start()

    small_all[z] = small_ref[...]
    for load in loads:
        load.wait()
    for p in range(1, n):
        o = lax.rem(z + n - p, n)
        pltpu.make_async_remote_copy(
            src_ref=small_ref, dst_ref=small_all.at[o], send_sem=small_send.at[p - 1],
            recv_sem=small_recv.at[o], device_id=(d, o), device_id_type=MESH,
        ).wait_recv()

    lanes = lax.broadcasted_iota(jnp.int32, (T, 128), 1)
    step_rows = 32

    def outs(o):
        return [
            pltpu.make_async_copy(src.at[o], dst.at[o], out_sem.at[i, o])
            for i, (src, dst) in enumerate(
                ((xs, x_out), (nb, normed_out), (qb, q_out), (kb, k_out), (vb, v_out))
            )
        ]

    def compute(o):
        gain = jnp.concatenate([small_all[s, 0:1, T:] for s in range(n)], axis=1)

        def norm_rows(i, carry):
            r = pl.ds(pl.multiple_of(i * step_rows, step_rows), step_rows)
            x = xs[o, r, :].astype(f32)
            factor = lax.rsqrt(jnp.sum(x * x, axis=1, keepdims=True) / D + EPSILON)
            nb[o, r, :] = (x * factor * gain).astype(bf16)
            return carry

        lax.fori_loop(0, T // step_rows, norm_rows, 0)
        q = jnp.dot(nb[o], wq[...], preferred_element_type=f32)
        qb[o] = q
        q_sum = jnp.sum(q * q, axis=1, keepdims=True)
        k = jnp.dot(nb[o], wk[...], preferred_element_type=f32)
        kb[o] = k
        k_sum = jnp.sum(k * k, axis=1, keepdims=True)
        vb[o] = jnp.dot(nb[o], wv[...], preferred_element_type=f32).astype(bf16)
        both = jnp.where(lanes == 0, q_sum, jnp.where(lanes == 1, k_sum, 0.0))
        sq_all[z, o] = both.T[0:8]
        for copy in outs(o):
            copy.start()

    def step(s, carry):
        below, above = z - s, z + s
        slab_hop(s, lambda o: slab_save(o).start())

        @pl.when((s > 0) & (below >= 0))
        def _():
            send_up(below).wait_recv()

            @pl.when(z < n - 1)
            def _():
                send_up(below).start()

        @pl.when((s > 0) & (above < n))
        def _():
            send_down(above).wait_recv()

            @pl.when(z > 0)
            def _():
                send_down(above).start()

        def side(j, inner):
            o = z - s + 2 * s * j

            @pl.when((o >= 0) & (o < n) & ((s > 0) | (j == 0)))
            def _():
                compute(o)

            return inner

        lax.fori_loop(0, 2, side, 0)
        return carry

    lax.fori_loop(0, n, step, 0)

    sq_copies = []
    for p, peer in enumerate(peers):
        copy = pltpu.make_async_remote_copy(
            src_ref=sq_all.at[z], dst_ref=sq_all.at[z], send_sem=sq_send.at[p],
            recv_sem=sq_recv.at[z], device_id=peer, device_id_type=MESH,
        )
        copy.start()
        sq_copies.append(copy)
    small_out[...] = small_all[...]

    def finish(o, carry):
        for copy in outs(o):
            copy.wait()
        slab_save(o).wait()

        @pl.when((z < n - 1) & (o <= z))
        def _():
            send_up(o).wait_send()

        @pl.when((z > 0) & (o >= z))
        def _():
            send_down(o).wait_send()

        return carry

    lax.fori_loop(0, n, finish, 0)
    slab_drain()
    for p in range(1, n):
        o = lax.rem(z + n - p, n)
        pltpu.make_async_remote_copy(
            src_ref=sq_all.at[o], dst_ref=sq_all.at[o], send_sem=sq_send.at[p - 1],
            recv_sem=sq_recv.at[o], device_id=(d, o), device_id_type=MESH,
        ).wait_recv()
    def turn_factors(i, carry):
        total = sq_all[0, i]
        for s in range(1, n):
            total = total + sq_all[s, i]
        total = jnp.concatenate([total, jnp.zeros((120, T), f32)], axis=0).T
        r = pl.ds(pl.multiple_of(i * T, T), T)
        sq_out[r, :] = lax.rsqrt(total / D + EPSILON)
        return carry

    lax.fori_loop(0, n, turn_factors, 0)
    for copy in small_copies + sq_copies:
        copy.wait_send()


def gather_project(n, tokens, small, slab, wq, wk, wv):
    T, D = tokens.shape
    C = wq.shape[1]
    hbm = pl.BlockSpec(memory_space=pl.ANY)
    vmem = pl.BlockSpec(memory_space=pltpu.VMEM)
    dma = pltpu.SemaphoreType.DMA
    return pl.pallas_call(
        functools.partial(gather_project_kernel, n),
        out_shape=[
            jax.ShapeDtypeStruct((n, T, D), bf16),
            jax.ShapeDtypeStruct((n, T, D), bf16),
            jax.ShapeDtypeStruct((n, T, C), f32),
            jax.ShapeDtypeStruct((n, T, C), f32),
            jax.ShapeDtypeStruct((n, T, C), bf16),
            jax.ShapeDtypeStruct((slab.shape[0], D), bf16),
            jax.ShapeDtypeStruct((n,) + small.shape, f32),
            jax.ShapeDtypeStruct((n * T, 128), f32),
        ],
        in_specs=[hbm, vmem, hbm, hbm, hbm, hbm],
        out_specs=[hbm] * 6 + [vmem] * 2,
        scratch_shapes=[
            pltpu.VMEM((n,) + slab.shape, bf16),
            pltpu.VMEM((n, T, D), bf16),
            pltpu.VMEM((n, T, D), bf16),
            pltpu.VMEM((n, T, C), f32),
            pltpu.VMEM((n, T, C), f32),
            pltpu.VMEM((n, T, C), bf16),
            pltpu.VMEM((D, C), bf16),
            pltpu.VMEM((D, C), bf16),
            pltpu.VMEM((D, C), bf16),
            pltpu.VMEM((n, n, 8, T), f32),
            pltpu.VMEM((n,) + small.shape, f32),
            dma((5,)),
            dma((5, n)),
            dma((n,)),
            dma((n,)),
            dma((n,)),
            dma((n,)),
            dma((n,)),
            dma((n,)),
            dma((n,)),
            dma((n,)),
            dma((n,)),
            dma((n,)),
            dma((n,)),
        ],
        compiler_params=pltpu.CompilerParams(
            collective_id=0, has_side_effects=True, vmem_limit_bytes=VMEM_LIMIT
        ),
        cost_estimate=pl.CostEstimate(flops=80 * 10**9, bytes_accessed=32 * 2**20, transcendentals=0),
        name="gather_project",
    )(tokens, small, slab, wq, wk, wv)


def rope(v, cosine, sine):
    return v * cosine + pltpu.roll(v, HEAD_DIM // 2, 1) * sine


def key_span(i, block, length):
    return min(length, max((i + 1) * block, length // 2))


def block_scores(q, k, i, block, limit):
    s = dot_nt(q, k) * (HEAD_DIM**-0.5)
    row = lax.broadcasted_iota(jnp.int32, s.shape, 0) + i * block
    col = lax.broadcasted_iota(jnp.int32, s.shape, 1)
    return jnp.where((col <= row) | (col < limit), s, MASKED)


def attention_kernel(
    n, limit_ref, q_raw, k_raw, v_ref, factors, cosine, sine, gains, first_hbm,
    q_out, k_out, mixed, first_out, slots, load_sem, up_sem, down_sem, recv_sem, out_sem,
):
    length = q_raw.shape[0]
    block = 256
    limit = limit_ref[0:1, 0:1]
    h, heads = pl.program_id(0), pl.num_programs(0)
    begin, hop, drain = line_gather(n, slots, up_sem, down_sem, recv_sem)
    z = lax.axis_index("shard")

    def save(o):
        return pltpu.make_async_copy(slots.at[o], first_out.at[o], out_sem.at[o])

    @pl.when(h == 0)
    def _():
        load = pltpu.make_async_copy(first_hbm, slots.at[z], load_sem.at[0])
        load.start()
        _, _, peers = others(n)
        greet(peers)
        load.wait()
        begin()
        save(z).start()

    def turn(raw, out, column, gain):
        def part(i, carry):
            r = pl.ds(pl.multiple_of(i * block, block), block)
            v = raw[r, :] * factors[r, column : column + 1] * gain
            out[r, :] = rope(v, cosine[r, :], sine[r, :]).astype(bf16)
            return carry

        lax.fori_loop(0, length // block, part, 0)

    turn(q_raw, q_out, 0, gains[0:1, :])
    turn(k_raw, k_out, 1, gains[1:2, :])
    for i in range(length // block):
        span = key_span(i, block, length)
        r = pl.ds(i * block, block)
        s = block_scores(q_out[r, :], k_out[0:span, :], i, block, limit)
        e = jnp.exp(s - jnp.max(s, axis=1, keepdims=True))
        total = jnp.sum(e, axis=1, keepdims=True)
        mixed[r, :] = (dot(e.astype(bf16), v_ref[0:span, :]) / total).astype(bf16)

    def hops(s, carry):
        hop(s, lambda o: save(o).start())
        return carry

    lax.fori_loop(1 + h * (n - 1) // heads, 1 + (h + 1) * (n - 1) // heads, hops, 0)

    @pl.when(h == heads - 1)
    def _():
        drain()

        def finish(o, carry):
            save(o).wait()
            return carry

        lax.fori_loop(0, n, finish, 0)


def attention(n, limit, q_raw, k_raw, values, factors, cosine, sine, gains, first):
    length, local = q_raw.shape
    heads = local // HEAD_DIM
    head = pl.BlockSpec((length, HEAD_DIM), lambda h: (0, h))
    whole = lambda a: pl.BlockSpec(a.shape, lambda h: (0, 0))
    hbm = pl.BlockSpec(memory_space=pl.ANY)
    out = jax.ShapeDtypeStruct((length, local), bf16)
    dma = pltpu.SemaphoreType.DMA
    return pl.pallas_call(
        functools.partial(attention_kernel, n),
        out_shape=[out] * 3 + [jax.ShapeDtypeStruct((n,) + first.shape, bf16)],
        grid=(heads,),
        in_specs=[
            whole(limit), head, head, head, whole(factors), whole(cosine), whole(sine),
            pl.BlockSpec((2, HEAD_DIM), lambda h: (0, h)), hbm,
        ],
        out_specs=[head] * 3 + [hbm],
        scratch_shapes=[pltpu.VMEM((n,) + first.shape, bf16), dma((1,))] + [dma((n,))] * 4,
        compiler_params=pltpu.CompilerParams(
            collective_id=7, has_side_effects=True, vmem_limit_bytes=VMEM_LIMIT
        ),
        cost_estimate=pl.CostEstimate(
            flops=20 * 10**9, bytes_accessed=16 * 2**20, transcendentals=0
        ),
        name="attention",
    )(limit, q_raw, k_raw, values, factors, cosine, sine, gains, first)


def attention_back_kernel(
    n, steps, width, limit_ref, q_ref, k_ref, v_ref, q_raw, k_raw, factors, cosine, sine,
    gains, wq, wk, wv, normed_hbm, sum_hbm, grad_hbm, output_hbm, gq_out, gk_out, gv_out, normed_out, gain_out, own_sum,
    g_ref, output, dq_acc, dk_acc, k_acc, v_acc, q_grad, k_grad, v_grad, columns, turned, staged,
    inner_all, inner_send, inner_recv, column_sem, staged_sem, grad_sem, part, *line,
):
    length, local = q_ref.shape
    strips = width // local
    heads = local // HEAD_DIM
    block = 256
    blocks = length // block
    scale = HEAD_DIM**-0.5
    load_sem = line[-1]
    turn, drain = line_sum(n, steps, part, own_sum, *line[:-1])
    d, z, peers = others(n)
    load = pltpu.make_async_copy(sum_hbm, part, load_sem.at[0])
    load.start()

    def grad_rows(i):
        r = pl.ds(pl.multiple_of(i * block, block), block)
        return pltpu.make_async_copy(
            grad_hbm.at[r, :], staged.at[lax.rem(i, 2)], grad_sem.at[lax.rem(i, 2)]
        )

    own_rows = pl.ds(pl.multiple_of(z * local, local), local)
    output_load = pltpu.make_async_copy(output_hbm.at[own_rows, :], output, grad_sem.at[2])
    output_load.start()
    grad_rows(0).start()
    greet(peers)

    def strip(b):
        c = pl.ds(pl.multiple_of(b * local, local), local)
        return pltpu.make_async_copy(
            normed_hbm.at[:, c], columns.at[lax.rem(b, 2)], column_sem.at[lax.rem(b, 2)]
        )

    strip(0).start()
    load.wait()
    turns = steps + n - 1
    in_heads, in_parts = 8 * turns // 19, 4 * turns // 19
    slots = -(-in_heads // heads)
    past = 1 + heads * slots
    in_strips = turns - past - in_parts - 2

    def take(first, count, i, of):
        def one(t, carry):
            turn(first + t)
            return carry

        lax.fori_loop(i * count // of, (i + 1) * count // of, one, 0)
    limit = limit_ref[0:1, 0:1]
    lanes = lax.broadcasted_iota(jnp.int32, (block, 128), 1)

    def clear(i, carry):
        inner_all[z, i] = jnp.zeros((8, block), f32)
        return carry

    lax.fori_loop(0, blocks, clear, 0)

    turn(0)
    output_load.wait()

    def mixed_rows(i, carry):
        r = pl.ds(pl.multiple_of(i * block, block), block)
        grad_rows(i).wait()

        @pl.when(i + 1 < blocks)
        def _():
            grad_rows(i + 1).start()

        g_ref[r, :] = dot_nt(staged[lax.rem(i, 2)], output[...]).astype(bf16)
        return carry

    lax.fori_loop(0, blocks, mixed_rows, 0)

    def head(h, carry):
        c = pl.ds(pl.multiple_of(h * HEAD_DIM, HEAD_DIM), HEAD_DIM)
        k_acc[...] = jnp.zeros_like(k_acc)
        v_acc[...] = jnp.zeros_like(v_acc)
        for i in range(blocks):
            for j in range(i * slots // blocks, (i + 1) * slots // blocks):
                turn(1 + h * slots + j)
            span = key_span(i, block, length)
            r = pl.ds(i * block, block)
            q, g, k, v = q_ref[r, c], g_ref[r, c], k_ref[0:span, c], v_ref[0:span, c]
            s = block_scores(q, k, i, block, limit)
            e = jnp.exp(s - jnp.max(s, axis=1, keepdims=True))
            p = e * (1.0 / jnp.sum(e, axis=1, keepdims=True))
            t = p * dot_nt(g, v)
            ds = (t - p * jnp.sum(t, axis=1, keepdims=True)).astype(bf16)
            dq_acc[r, c] = dot(ds, k) * scale
            k_acc[0:span, :] += dot_tn(ds, q) * scale
            v_acc[0:span, :] += dot_tn(p.astype(bf16), g)
        v_grad[:, c] = v_acc[...].astype(bf16)
        gain_q, gain_k = gains[0:1, c], gains[1:2, c]

        def back(i, carry):
            gq, gk = carry
            r = pl.ds(pl.multiple_of(i * block, block), block)
            cos, sin = cosine[r, :], sine[r, :]
            dq = rope(dq_acc[r, c], cos, -sin)
            dk = rope(k_acc[r, :], cos, -sin)
            uq = q_raw[r, c] * factors[r, 0:1]
            uk = k_raw[r, c] * factors[r, 1:2]
            gq = gq + jnp.sum(dq * uq, axis=0, keepdims=True)
            gk = gk + jnp.sum(dk * uk, axis=0, keepdims=True)
            dq = dq * gain_q
            dk = dk * gain_k
            dq_acc[r, c] = dq
            dk_acc[r, c] = dk
            inner_q = jnp.sum(dq * uq, axis=1, keepdims=True)
            inner_k = jnp.sum(dk * uk, axis=1, keepdims=True)
            both = jnp.where(lanes == 0, inner_q, jnp.where(lanes == 1, inner_k, 0.0))
            inner_all[z, i] += both.T[0:8]
            return gq, gk

        zero = jnp.zeros((1, HEAD_DIM), f32)
        gq, gk = lax.fori_loop(0, blocks, back, (zero, zero))
        gain_out[0:1, c] = gq
        gain_out[1:2, c] = gk
        return carry

    lax.fori_loop(0, heads, head, 0)

    copies = []
    for p, peer in enumerate(peers):
        copy = pltpu.make_async_remote_copy(
            src_ref=inner_all.at[z], dst_ref=inner_all.at[z], send_sem=inner_send.at[p],
            recv_sem=inner_recv.at[z], device_id=peer, device_id_type=MESH,
        )
        copy.start()
        copies.append(copy)
    turn(past)
    for p in range(1, n):
        o = lax.rem(z + n - p, n)
        pltpu.make_async_remote_copy(
            src_ref=inner_all.at[o], dst_ref=inner_all.at[o], send_sem=inner_send.at[p - 1],
            recv_sem=inner_recv.at[o], device_id=(d, o), device_id_type=MESH,
        ).wait_recv()

    def raw(i, carry):
        r = pl.ds(pl.multiple_of(i * block, block), block)
        total = inner_all[0, i]
        for s in range(1, n):
            total = total + inner_all[s, i]
        total = jnp.concatenate([total, jnp.zeros((120, block), f32)], axis=0).T
        fq, fk = factors[r, 0:1], factors[r, 1:2]
        mean_q, mean_k = total[:, 0:1] / width, total[:, 1:2] / width
        q_grad[r, :] = (fq * (dq_acc[r, :] - q_raw[r, :] * (fq * mean_q))).astype(bf16)
        k_grad[r, :] = (fk * (dk_acc[r, :] - k_raw[r, :] * (fk * mean_k))).astype(bf16)
        return carry

    lax.fori_loop(0, blocks, raw, 0)
    turn(past + 1)

    def save(i):
        r = pl.ds(pl.multiple_of(i * block, block), block)
        return pltpu.make_async_copy(
            staged.at[lax.rem(i, 2)], normed_out.at[r, :], staged_sem.at[lax.rem(i, 2)]
        )

    def rows_back(i, carry):
        r = pl.ds(pl.multiple_of(i * block, block), block)

        @pl.when(i >= 2)
        def _():
            save(i - 2).wait()

        staged[lax.rem(i, 2)] = (
            dot_nt(q_grad[r, :], wq[...])
            + dot_nt(k_grad[r, :], wk[...])
            + dot_nt(v_grad[r, :], wv[...])
        ).astype(bf16)
        save(i).start()
        take(past + 2, in_parts, i, blocks)
        return carry

    lax.fori_loop(0, blocks, rows_back, 0)

    def strip_grads(b, carry):
        strip(b).wait()

        @pl.when(b + 1 < strips)
        def _():
            strip(b + 1).start()

        turned[...] = columns[lax.rem(b, 2)].T
        c = pl.ds(pl.multiple_of(b * local, local), local)
        gq_out[c, :] = dot(turned[...], q_grad[...]).astype(bf16)
        gk_out[c, :] = dot(turned[...], k_grad[...]).astype(bf16)
        gv_out[c, :] = dot(turned[...], v_grad[...]).astype(bf16)
        take(past + 2 + in_parts, in_strips, b, strips)
        return carry

    lax.fori_loop(0, strips, strip_grads, 0)
    drain()
    for i in range(max(blocks - 2, 0), blocks):
        save(i).wait()
    for copy in copies:
        copy.wait_send()


def attention_back(
    n, width, limit, q, k, v, q_raw, k_raw, factors, cosine, sine, gains, wq, wk, wv, normed,
    sum_parts, attended_grad, full_output,
):
    length, local = q.shape
    _, steps, R, D = sum_parts.shape
    hbm = pl.BlockSpec(memory_space=pl.ANY)
    vmem = pl.BlockSpec(memory_space=pltpu.VMEM)
    dma = pltpu.SemaphoreType.DMA
    weight = jax.ShapeDtypeStruct((D, local), bf16)
    raw = pltpu.VMEM((length, local), bf16)
    return pl.pallas_call(
        functools.partial(attention_back_kernel, n, steps, width),
        out_shape=[
            weight, weight, weight, jax.ShapeDtypeStruct((length, D), bf16),
            jax.ShapeDtypeStruct((2, local), f32),
            jax.ShapeDtypeStruct((steps, R, D), f32),
        ],
        in_specs=[vmem] * 13 + [hbm] * 4,
        out_specs=[vmem, vmem, vmem, hbm, vmem, vmem],
        scratch_shapes=[
            raw,
            pltpu.VMEM((local, D), bf16),
            pltpu.VMEM((length, local), f32),
            pltpu.VMEM((length, local), f32),
            pltpu.VMEM((length, HEAD_DIM), f32),
            pltpu.VMEM((length, HEAD_DIM), f32),
            raw,
            raw,
            raw,
            pltpu.VMEM((2, length, local), bf16),
            pltpu.VMEM((local, length), bf16),
            pltpu.VMEM((2, 256, D), bf16),
            pltpu.VMEM((n, length // 256, 8, 256), f32),
            dma((n,)),
            dma((n,)),
            dma((2,)),
            dma((2,)),
            dma((3,)),
        ]
        + line_scratch(n, steps, R, D),
        compiler_params=pltpu.CompilerParams(
            collective_id=6, has_side_effects=True, vmem_limit_bytes=VMEM_LIMIT
        ),
        cost_estimate=pl.CostEstimate(
            flops=2 * 10**9, bytes_accessed=2**20, transcendentals=0
        ),
        name="attention_back",
    )(
        limit, q, k, v, q_raw, k_raw, factors, cosine, sine, gains, wq, wk, wv, normed, sum_parts,
        attended_grad, full_output,
    )


def scatter_norm_kernel(n, groups, steps, gather, *refs):
    part, base, gain = refs[:3]
    refs = refs[3:]
    if gather:
        addend, attended_hbm, hidden, g_all = refs[:4]
        out, all_out, gain_out, down_out = refs[4:8]
        alls, ag_up, ag_down, ag_recv, all_sem, attended, load_sem = refs[8:15]
        refs = refs[15:]
    else:
        expert_gains, head_gains, out, gain_out = refs[:4]
        pieces, landed, sums, piece_send, piece_recv, sum_send, sum_recv = refs[4:11]
        refs = refs[11:]
    from_below, from_above, gain_acc, up_send, up_recv, down_send, down_recv = refs
    R, D = part.shape[2:]
    d, z, peers = others(n)
    upper, lower = (d, lax.rem(z + 1, n)), (d, lax.rem(z + n - 1, n))
    alike = [] if gather else [(lax.rem(d + p, groups), z) for p in range(1, groups)]
    if gather:
        load = pltpu.make_async_copy(attended_hbm.at[z], attended, load_sem.at[0])
        load.start()
    greet(peers + alike)
    if gather:
        load.wait()
    gain_acc[...] = jnp.zeros_like(gain_acc)

    def move_up(src, o, k):
        return pltpu.make_async_remote_copy(
            src_ref=src.at[o, k], dst_ref=from_below.at[o, k], send_sem=up_send.at[o, k],
            recv_sem=up_recv.at[o, k], device_id=upper, device_id_type=MESH,
        )

    def move_down(src, o, k):
        return pltpu.make_async_remote_copy(
            src_ref=src.at[o, k], dst_ref=from_above.at[o, k], send_sem=down_send.at[o, k],
            recv_sem=down_recv.at[o, k], device_id=lower, device_id_type=MESH,
        )

    def all_up(o, k):
        return pltpu.make_async_remote_copy(
            src_ref=alls.at[o, k], dst_ref=alls.at[o, k], send_sem=ag_up.at[o, k],
            recv_sem=ag_recv.at[o, k], device_id=upper, device_id_type=MESH,
        )

    def all_down(o, k):
        return pltpu.make_async_remote_copy(
            src_ref=alls.at[o, k], dst_ref=alls.at[o, k], send_sem=ag_down.at[o, k],
            recv_sem=ag_recv.at[o, k], device_id=lower, device_id_type=MESH,
        )

    def pass_up(k):
        def far(i, carry):
            o = z + n - 1 - i

            @pl.when(o < n)
            def _():
                @pl.when(z == 0)
                def _():
                    move_up(part, o, k).start()

                @pl.when(z > 0)
                def _():
                    move_up(part, o, k).wait_recv()
                    both = from_below[o, k].astype(f32) + part[o, k].astype(f32)
                    from_below[o, k] = both.astype(bf16)
                    move_up(from_below, o, k).start()

            return carry

        lax.fori_loop(0, n - 1, far, 0)

    def pass_down(k):
        def far(i, carry):
            o = z - n + 1 + i

            @pl.when(o >= 0)
            def _():
                @pl.when(z == n - 1)
                def _():
                    move_down(part, o, k).start()

                @pl.when(z < n - 1)
                def _():
                    move_down(part, o, k).wait_recv()
                    both = from_above[o, k].astype(f32) + part[o, k].astype(f32)
                    from_above[o, k] = both.astype(bf16)
                    move_down(from_above, o, k).start()

            return carry

        lax.fori_loop(0, n - 1, far, 0)

    def own(k):
        @pl.when(z > 0)
        def _():
            move_up(part, z, k).wait_recv()

        @pl.when(z == 0)
        def _():
            from_below[z, k] = jnp.zeros((R, D), bf16)

        @pl.when(z < n - 1)
        def _():
            move_down(part, z, k).wait_recv()

        @pl.when(z == n - 1)
        def _():
            from_above[z, k] = jnp.zeros((R, D), bf16)

        total = (
            part[z, k].astype(f32) + from_below[z, k].astype(f32) + from_above[z, k].astype(f32)
        )
        rows = base[k].astype(f32)
        if gather:
            rows = rows + attended[k]
        factor = lax.rsqrt(jnp.sum(rows * rows, axis=1, keepdims=True) / D + EPSILON)
        unit = rows * factor
        along = total * unit
        gain_acc[...] += jnp.sum(along.reshape(R // 8, 8, D), axis=0)
        weighted = along * gain[...]
        mean = jnp.sum(weighted, axis=1, keepdims=True) / D
        result = factor * (total * gain[...] - unit * mean)
        if gather:
            result = result + addend[k].astype(f32)
        out[k] = result
        if gather:
            alls[z, k] = result.astype(bf16)

            @pl.when(z < n - 1)
            def _():
                all_up(z, k).start()

            @pl.when(z > 0)
            def _():
                all_down(z, k).start()

    def forward(own_k):
        def hop(s, carry):
            below, above, k = z - s, z + s, own_k - s
            live = (k >= 0) & (k < steps)

            @pl.when(live & (below >= 0))
            def _():
                all_up(below, k).wait_recv()

                @pl.when(z < n - 1)
                def _():
                    all_up(below, k).start()

            @pl.when(live & (above < n))
            def _():
                all_down(above, k).wait_recv()

                @pl.when(z > 0)
                def _():
                    all_down(above, k).start()

            return carry

        lax.fori_loop(1, n, hop, 0)

    def turn(t, carry):
        up_k, down_k, own_k = t - z, t - (n - 1 - z), t - (n - 1)

        @pl.when((up_k >= 0) & (up_k < steps))
        def _():
            pass_up(up_k)

        @pl.when((down_k >= 0) & (down_k < steps))
        def _():
            pass_down(down_k)

        @pl.when((own_k >= 0) & (own_k < steps))
        def _():
            own(own_k)

        if gather:
            forward(own_k)
            experts, units = down_out.shape[:2]
            e = t - n

            @pl.when((e >= 0) & (e < experts))
            def _():
                c = pl.ds(pl.multiple_of(e * units, units), units)
                down_out[e] = dot_tn(hidden[:, c], g_all[...]).astype(bf16)

        return carry

    lax.fori_loop(0, steps + (2 * n - 2 if gather else n - 1), turn, 0)
    if gather:
        gain_out[...] = gain_acc[...]
    else:
        C = D // n
        for s in range(n):
            c = slice(s * C, (s + 1) * C)
            pieces[s, 0:1] = jnp.sum(gain_acc[:, c], axis=0, keepdims=True)
            pieces[s, 1:2] = jnp.sum(expert_gains[:, c], axis=0, keepdims=True)
            pieces[s, 2:8] = jnp.zeros((6, C), f32)

        def piece(p):
            o = lax.rem(z + p, n)
            return pltpu.make_async_remote_copy(
                src_ref=pieces.at[o], dst_ref=landed.at[z], send_sem=piece_send.at[p - 1],
                recv_sem=piece_recv.at[z], device_id=(d, o), device_id_type=MESH,
            )

        for p in range(1, n):
            piece(p).start()
        landed[z] = pieces[z]
        for p in range(1, n):
            o = lax.rem(z + n - p, n)
            pltpu.make_async_remote_copy(
                src_ref=pieces.at[o], dst_ref=landed.at[o], send_sem=piece_send.at[p - 1],
                recv_sem=piece_recv.at[o], device_id=(d, o), device_id_type=MESH,
            ).wait_recv()
        two = landed[0]
        for s in range(1, n):
            two = two + landed[s]
        sums[d, 0:1] = two[0:1]
        sums[d, 1:3] = head_gains[...]
        sums[d, 3:4] = two[1:2]
        sums[d, 4:8] = jnp.zeros((4, C), f32)
        for p in range(1, groups):
            pltpu.make_async_remote_copy(
                src_ref=sums.at[d], dst_ref=sums.at[d], send_sem=sum_send.at[p - 1],
                recv_sem=sum_recv.at[d], device_id=alike[p - 1], device_id_type=MESH,
            ).start()
        for p in range(1, groups):
            o = lax.rem(d + groups - p, groups)
            pltpu.make_async_remote_copy(
                src_ref=sums.at[o], dst_ref=sums.at[o], send_sem=sum_send.at[p - 1],
                recv_sem=sum_recv.at[o], device_id=(o, z), device_id_type=MESH,
            ).wait_recv()
        total = sums[0]
        for s in range(1, groups):
            total = total + sums[s]
        gain_out[...] = total
        for p in range(1, n):
            piece(p).wait_send()
        for p in range(1, groups):
            pltpu.make_async_remote_copy(
                src_ref=sums.at[d], dst_ref=sums.at[d], send_sem=sum_send.at[p - 1],
                recv_sem=sum_recv.at[d], device_id=alike[p - 1], device_id_type=MESH,
            ).wait_send()

    def drain(i, carry):
        o, k = i // steps, i % steps

        @pl.when(o > z)
        def _():
            move_up(part, o, k).wait_send()

        @pl.when(o < z)
        def _():
            move_down(part, o, k).wait_send()

        if gather:

            @pl.when((z < n - 1) & (o <= z))
            def _():
                all_up(o, k).wait_send()

            @pl.when((z > 0) & (o >= z))
            def _():
                all_down(o, k).wait_send()

        return carry

    lax.fori_loop(0, n * steps, drain, 0)
    if gather:
        copies = [pltpu.make_async_copy(alls.at[o], all_out.at[o], all_sem.at[o]) for o in range(n)]
        for copy in copies:
            copy.start()
        for copy in copies:
            copy.wait()


def scatter_norm(n, groups, steps, part, base, gain, more=None, other_gains=None):
    gather = more is not None
    T, D = base.shape
    R = T // steps
    C = D // n
    hbm = pl.BlockSpec(memory_space=pl.ANY)
    vmem = pl.BlockSpec(memory_space=pltpu.VMEM)
    dma = pltpu.SemaphoreType.DMA
    slots = pltpu.VMEM((n, steps, R, D), bf16)
    rows = jax.ShapeDtypeStruct((steps, R, D), f32)
    sems = dma((n, steps))
    if gather:
        addend, attended, hidden, g_all, experts = more
        units = hidden.shape[1] // experts
        more = (
            addend.reshape(steps, R, D), attended.reshape(n, steps, R, D), hidden, g_all,
        )
        own = [slots, sems, sems, sems, dma((n,)), pltpu.VMEM((steps, R, D), f32), dma((1,))]
        outs = [rows, jax.ShapeDtypeStruct((n, steps, R, D), bf16)]
        outs += [jax.ShapeDtypeStruct((8, D), f32)]
        outs += [jax.ShapeDtypeStruct((experts, units, D), bf16)]
    else:
        own = [
            pltpu.VMEM((n, 8, C), f32), pltpu.VMEM((n, 8, C), f32),
            pltpu.VMEM((groups, 8, C), f32), dma((n,)), dma((n,)), dma((groups,)), dma((groups,)),
        ]
        outs = [rows, jax.ShapeDtypeStruct((8, C), f32)]
    return pl.pallas_call(
        functools.partial(scatter_norm_kernel, n, groups, steps, gather),
        out_shape=outs,
        in_specs=[vmem] * 4 + [hbm, vmem, vmem] if gather else [vmem] * 5,
        out_specs=[vmem, hbm, vmem, vmem] if gather else [vmem, vmem],
        scratch_shapes=own + [slots, slots, pltpu.VMEM((8, D), f32), sems, sems, sems, sems],
        compiler_params=pltpu.CompilerParams(
            collective_id=2 if gather else 3, has_side_effects=True, vmem_limit_bytes=VMEM_LIMIT
        ),
        cost_estimate=pl.CostEstimate(
            flops=10**9, bytes_accessed=2**20, transcendentals=0
        ),
        name="scatter_norm_gather" if gather else "scatter_norm",
    )(
        part.reshape(n, steps, R, D),
        base.reshape(steps, R, D),
        gain,
        *(more if gather else other_gains),
    )


def forward_kernel(
    mixed, weight, x_ref, gain, combine, gate_w, up_w, down_w,
    attended_out, in_out, gate_out, up_out, hidden_out, sum_out, gate_t, up_t, down_t,
    sum_acc,
):
    e = pl.program_id(1)
    last = pl.num_programs(1) - 1
    D = in_out.shape[1]
    C = mixed.shape[2]

    @pl.when(e == 0)
    def _():
        total = dot(mixed[0], weight[0:C, :])
        for s in range(1, mixed.shape[0]):
            total = total + dot(mixed[s], weight[s * C : (s + 1) * C, :])
        attended_out[...] = total
        part = 32

        def rows(i, carry):
            r = pl.ds(pl.multiple_of(i * part, part), part)
            v = attended_out[r, :] + x_ref[r, :].astype(f32)
            factor = lax.rsqrt(jnp.sum(v * v, axis=1, keepdims=True) / D + EPSILON)
            in_out[r, :] = (v * factor * gain[...]).astype(bf16)
            return carry

        lax.fori_loop(0, in_out.shape[0] // part, rows, 0)

    lane = lax.broadcasted_iota(jnp.int32, combine.shape, 1)
    share = jnp.sum(jnp.where(lane == e, combine[...], 0.0), axis=1, keepdims=True)
    @pl.when(pl.program_id(0) == 0)
    def _():
        gate_t[0] = gate_w[0].T
        up_t[0] = up_w[0].T
        down_t[0] = down_w[0].T

    gate_part = dot(in_out[...], gate_w[0])
    up_part = dot(in_out[...], up_w[0])
    sig = jax.nn.sigmoid(gate_part)
    silu = gate_part * sig * share
    gate_out[...] = up_part * sig * (1.0 + gate_part * (1.0 - sig)) * share
    up_out[...] = silu
    hidden = (silu * up_part).astype(bf16)
    hidden_out[...] = hidden
    made = dot(hidden, down_w[0])

    @pl.when(e == 0)
    def _():
        sum_acc[...] = made

    @pl.when(e > 0)
    def _():
        sum_acc[...] += made

    @pl.when(e == last)
    def _():
        sum_out[...] = sum_acc[...].astype(bf16)


def forward_pass(mixed, weight, x, gain, combine, gate_w, up_w, down_w):
    n, L, C = mixed.shape
    D = x.shape[1]
    E, _, F = gate_w.shape
    block = min(512, L)
    rows = pl.BlockSpec((block, D), lambda i, e: (i, 0))
    units = pl.BlockSpec((block, F), lambda i, e: (i, e))
    column = pl.BlockSpec((1, D, F), lambda i, e: (e, 0, 0))
    once = pl.Buffered(1)
    turned = pl.BlockSpec((1, F, D), lambda i, e: (jnp.where(i == 0, e, E - 1), 0, 0))
    turned_down = pl.BlockSpec((1, D, F), lambda i, e: (jnp.where(i == 0, e, E - 1), 0, 0))
    return pl.pallas_call(
        forward_kernel,
        out_shape=[
            jax.ShapeDtypeStruct((L, D), f32),
            jax.ShapeDtypeStruct((L, D), bf16),
            jax.ShapeDtypeStruct((L, E * F), f32),
            jax.ShapeDtypeStruct((L, E * F), f32),
            jax.ShapeDtypeStruct((L, E * F), bf16),
            jax.ShapeDtypeStruct((L, D), bf16),
            jax.ShapeDtypeStruct((E, F, D), bf16),
            jax.ShapeDtypeStruct((E, F, D), bf16),
            jax.ShapeDtypeStruct((E, D, F), bf16),
        ],
        grid=(L // block, E),
        in_specs=[
            pl.BlockSpec((n, block, C), lambda i, e: (0, i, 0)),
            pl.BlockSpec((D, D), lambda i, e: (0, 0), pipeline_mode=once),
            rows,
            pl.BlockSpec((1, D), lambda i, e: (0, 0)),
            pl.BlockSpec((block, combine.shape[1]), lambda i, e: (i, 0)),
            column, column, pl.BlockSpec((1, F, D), lambda i, e: (e, 0, 0)),
        ],
        out_specs=[rows, rows, units, units, units, rows, turned, turned, turned_down],
        scratch_shapes=[pltpu.VMEM((block, D), f32)],
        compiler_params=pltpu.CompilerParams(vmem_limit_bytes=VMEM_LIMIT),
        cost_estimate=pl.CostEstimate(
            flops=6 * L * D * E * F + 2 * L * D * D, bytes_accessed=50 * 2**20,
            transcendentals=L * E * F,
        ),
        name="forward_pass",
    )(mixed, weight, x, gain, combine, gate_w, up_w, down_w)


def backward_kernel(
    first, rest, gate_ref, up_ref, gate_hbm, up_hbm, down_t,
    g_out, in_out, gate_out, up_out, both, turned, load_sem,
):
    i, e = pl.program_id(0), pl.program_id(1)
    last = pl.num_programs(1) - 1
    F = gate_out.shape[1]
    half = turned.shape[0] // 2
    loads = [
        pltpu.make_async_copy(gate_hbm, turned.at[0:half], load_sem.at[0]),
        pltpu.make_async_copy(up_hbm, turned.at[half : 2 * half], load_sem.at[1]),
    ]

    @pl.when((i == 0) & (e == 0))
    def _():
        for load in loads:
            load.start()

    @pl.when(e == 0)
    def _():
        few, many = first.shape[1], rest.shape[1]
        for j in range(first.shape[0]):
            top = j * (few + many)
            g_out[top : top + few, :] = first[j]
            g_out[top + few : top + few + many, :] = rest[j]

    hidden_grad = dot(g_out[...], down_t[0])
    gate_grad = (hidden_grad * gate_ref[...]).astype(bf16)
    gate_out[...] = gate_grad
    both[:, pl.ds(pl.multiple_of(e * F, F), F)] = gate_grad
    up_grad = (hidden_grad * up_ref[...]).astype(bf16)
    up_out[...] = up_grad
    both[:, pl.ds(pl.multiple_of(half + e * F, F), F)] = up_grad

    @pl.when((i == 0) & (e == last))
    def _():
        for load in loads:
            load.wait()

    @pl.when(e == last)
    def _():
        in_out[...] = dot(both[...], turned[...]).astype(bf16)


def backward_pass(first, rest, gate_by, up_by, gate_t, up_t, down_t):
    n, few, D = first.shape
    T = few + rest.shape[1]
    L = n * T
    E, F, _ = gate_t.shape
    block = max(T, min(512, L))
    owners = block // T
    rows = pl.BlockSpec((block, D), lambda i, e: (i, 0))
    units = pl.BlockSpec((block, F), lambda i, e: (i, e))
    hbm = pl.BlockSpec(memory_space=pl.ANY)
    wide = jax.ShapeDtypeStruct((L, D), bf16)
    narrow = jax.ShapeDtypeStruct((L, E * F), bf16)
    return pl.pallas_call(
        backward_kernel,
        out_shape=[wide, wide, narrow, narrow],
        grid=(L // block, E),
        in_specs=[
            pl.BlockSpec((owners, few, D), lambda i, e: (i, 0, 0)),
            pl.BlockSpec((owners, T - few, D), lambda i, e: (i, 0, 0)),
            units, units, hbm, hbm, pl.BlockSpec((1, D, F), lambda i, e: (e, 0, 0)),
        ],
        out_specs=[rows, rows, units, units],
        scratch_shapes=[
            pltpu.VMEM((block, 2 * E * F), bf16),
            pltpu.VMEM((2 * E * F, D), bf16),
            pltpu.SemaphoreType.DMA((2,)),
        ],
        compiler_params=pltpu.CompilerParams(vmem_limit_bytes=VMEM_LIMIT),
        cost_estimate=pl.CostEstimate(
            flops=6 * L * D * E * F, bytes_accessed=40 * 2**20, transcendentals=0
        ),
        name="backward_pass",
    )(first, rest, gate_by, up_by, gate_t.reshape(E * F, D), up_t.reshape(E * F, D), down_t)


def line_sum(n, steps, part, out, landed, up_send, up_recv, down_send, down_recv):
    d, z = lax.axis_index("dp"), lax.axis_index("shard")
    upper, lower = (d, lax.rem(z + 1, n)), (d, lax.rem(z + n - 1, n))

    def move_up(src, o, k):
        return pltpu.make_async_remote_copy(
            src_ref=src.at[o, k], dst_ref=landed.at[o, k], send_sem=up_send.at[o, k],
            recv_sem=up_recv.at[o, k], device_id=upper, device_id_type=MESH,
        )

    def move_down(src, o, k):
        slot = jnp.where(o == z - 1, n, o)
        return pltpu.make_async_remote_copy(
            src_ref=src.at[o, k], dst_ref=landed.at[slot, k], send_sem=down_send.at[o, k],
            recv_sem=down_recv.at[o, k], device_id=lower, device_id_type=MESH,
        )

    def passing(move, first, owner):
        def run(k):
            def far(i, carry):
                o = owner(i)

                @pl.when((o >= 0) & (o < n))
                def _():
                    @pl.when(z == first)
                    def _():
                        move(part, o, k).start()

                    @pl.when(z != first)
                    def _():
                        move(part, o, k).wait_recv()
                        both = landed[o, k].astype(f32) + part[o, k].astype(f32)
                        landed[o, k] = both.astype(bf16)
                        move(landed, o, k).start()

                return carry

            lax.fori_loop(0, n - 1, far, 0)

        return run

    pass_up = passing(move_up, 0, lambda i: z + n - 1 - i)
    pass_down = passing(move_down, n - 1, lambda i: z - n + 1 + i)

    def own(k):
        @pl.when(z > 0)
        def _():
            move_up(part, z, k).wait_recv()

        @pl.when(z == 0)
        def _():
            landed[z, k] = jnp.zeros(part.shape[2:], bf16)

        @pl.when(z < n - 1)
        def _():
            move_down(part, z, k).wait_recv()

        @pl.when(z == n - 1)
        def _():
            landed[n, k] = jnp.zeros(part.shape[2:], bf16)

        out[k] = part[z, k].astype(f32) + landed[z, k].astype(f32) + landed[n, k].astype(f32)

    def turn(t):
        up_k, down_k, own_k = t - z, t - (n - 1 - z), t - (n - 1)

        @pl.when((up_k >= 0) & (up_k < steps))
        def _():
            pass_up(up_k)

        @pl.when((down_k >= 0) & (down_k < steps))
        def _():
            pass_down(down_k)

        @pl.when((own_k >= 0) & (own_k < steps))
        def _():
            own(own_k)

    def drain():
        def one(i, carry):
            o, k = i // steps, i % steps

            @pl.when(o > z)
            def _():
                move_up(part, o, k).wait_send()

            @pl.when(o < z)
            def _():
                move_down(part, o, k).wait_send()

            return carry

        lax.fori_loop(0, n * steps, one, 0)

    return turn, drain


def line_scratch(n, steps, R, D):
    dma = pltpu.SemaphoreType.DMA
    slots = [pltpu.VMEM((n, steps, R, D), bf16), pltpu.VMEM((n + 1, steps, R, D), bf16)]
    return slots + [dma((n, steps))] * 4 + [dma((1,))]


def expert_grads_kernel(x_ref, gate_grad, up_grad, gate_out, up_out, xt):
    @pl.when(pl.program_id(0) == 0)
    def _():
        xt[...] = x_ref[...].T

    gate_out[0] = dot(xt[...], gate_grad[...]).astype(bf16)
    up_out[0] = dot(xt[...], up_grad[...]).astype(bf16)


def expert_grads(x, gate_grad, up_grad, experts):
    L, D = x.shape
    F = gate_grad.shape[1] // experts
    whole = pl.BlockSpec((L, D), lambda e: (0, 0))
    units = pl.BlockSpec((L, F), lambda e: (0, e))
    column = pl.BlockSpec((1, D, F), lambda e: (e, 0, 0))
    grad = jax.ShapeDtypeStruct((experts, D, F), bf16)
    return pl.pallas_call(
        expert_grads_kernel,
        out_shape=[grad, grad],
        grid=(experts,),
        in_specs=[whole, units, units],
        out_specs=[column, column],
        scratch_shapes=[pltpu.VMEM((D, L), bf16)],
        compiler_params=pltpu.CompilerParams(vmem_limit_bytes=VMEM_LIMIT),
        cost_estimate=pl.CostEstimate(
            flops=4 * L * D * experts * F, bytes_accessed=16 * 2**20, transcendentals=0
        ),
        name="expert_grads",
    )(x, gate_grad, up_grad)


def widen_kernel(count, *refs):
    for src, dst in zip(refs[:count], refs[count:]):
        dst[...] = src[...].astype(f32)


def widen(*arrays):
    flat = [v.reshape(-1, v.shape[-1]) for v in arrays]
    steps = 8
    specs = [
        pl.BlockSpec((v.shape[0] // steps, v.shape[1]), lambda i: (i, 0)) for v in flat
    ]
    out = pl.pallas_call(
        functools.partial(widen_kernel, len(flat)),
        out_shape=[jax.ShapeDtypeStruct(v.shape, f32) for v in flat],
        grid=(steps,),
        in_specs=specs,
        out_specs=specs,
        compiler_params=pltpu.CompilerParams(vmem_limit_bytes=VMEM_LIMIT),
        cost_estimate=pl.CostEstimate(
            flops=0, bytes_accessed=sum(6 * v.size for v in flat), transcendentals=0
        ),
        name="widen",
    )(*flat)
    return tuple(v.reshape(w.shape) for v, w in zip(out, arrays))


def gather_line_kernel(n, v_hbm, out, slots, load_sem, up_sem, down_sem, recv_sem, out_sem):
    d, z, peers = others(n)
    own_load = pltpu.make_async_copy(v_hbm, slots.at[z], load_sem.at[0])
    own_load.start()
    greet(peers)

    def send_up(o):
        return pltpu.make_async_remote_copy(
            src_ref=slots.at[o], dst_ref=slots.at[o], send_sem=up_sem.at[o],
            recv_sem=recv_sem.at[o], device_id=(d, lax.rem(z + 1, n)), device_id_type=MESH,
        )

    def send_down(o):
        return pltpu.make_async_remote_copy(
            src_ref=slots.at[o], dst_ref=slots.at[o], send_sem=down_sem.at[o],
            recv_sem=recv_sem.at[o], device_id=(d, lax.rem(z + n - 1, n)), device_id_type=MESH,
        )

    own_load.wait()

    @pl.when(z < n - 1)
    def _():
        send_up(z).start()

    @pl.when(z > 0)
    def _():
        send_down(z).start()

    def save(o):
        return pltpu.make_async_copy(slots.at[o], out.at[o], out_sem.at[o])

    save(z).start()

    def step(s, carry):
        below, above = z - s, z + s

        @pl.when(below >= 0)
        def _():
            send_up(below).wait_recv()

            @pl.when(z < n - 1)
            def _():
                send_up(below).start()

            save(below).start()

        @pl.when(above < n)
        def _():
            send_down(above).wait_recv()

            @pl.when(z > 0)
            def _():
                send_down(above).start()

            save(above).start()

        return carry

    lax.fori_loop(1, n, step, 0)

    def finish(o, carry):
        save(o).wait()

        @pl.when((z < n - 1) & (o <= z))
        def _():
            send_up(o).wait_send()

        @pl.when((z > 0) & (o >= z))
        def _():
            send_down(o).wait_send()

        return carry

    lax.fori_loop(0, n, finish, 0)


def gather_line(n, v, collective_id):
    hbm = pl.BlockSpec(memory_space=pl.ANY)
    dma = pltpu.SemaphoreType.DMA
    return pl.pallas_call(
        functools.partial(gather_line_kernel, n),
        out_shape=jax.ShapeDtypeStruct((n,) + v.shape, v.dtype),
        in_specs=[hbm],
        out_specs=hbm,
        scratch_shapes=[
            pltpu.VMEM((n,) + v.shape, v.dtype), dma((1,)), dma((n,)), dma((n,)), dma((n,)),
            dma((n,)),
        ],
        compiler_params=pltpu.CompilerParams(
            collective_id=collective_id, has_side_effects=True, vmem_limit_bytes=VMEM_LIMIT
        ),
        cost_estimate=pl.CostEstimate(flops=70 * 10**9, bytes_accessed=8 * 2**20, transcendentals=0),
        name="gather_line",
    )(v)


def per_device(
    tokens,
    out_grad,
    routes,
    gate_weights,
    prefix,
    query_weight,
    key_weight,
    value_weight,
    output_weight,
    norm_gains,
    expert_gate,
    expert_up,
    expert_down,
):
    rows, width = tokens.shape
    shards = lax.axis_size("shard")
    groups = lax.axis_size("dp")
    place = lax.axis_index("shard")
    group = lax.axis_index("dp")
    length = rows * shards
    local = width // shards
    experts = expert_gate.shape[0]
    units = expert_gate.shape[2]

    expert_ids = jnp.arange(experts, dtype=jnp.int32)
    weight_own = jnp.sum(
        jnp.where(routes[:, :, None] == expert_ids[None, None, :], gate_weights[:, :, None], 0.0),
        axis=1,
    )
    own_gains = norm_gains.astype(f32)
    small = jnp.concatenate(
        [
            jnp.pad(weight_own.T, ((0, 8 - experts), (0, 0))),
            jnp.pad(jnp.stack([own_gains[0], own_gains[3]]), ((0, 6), (0, 0))),
        ],
        axis=1,
    )
    slab = width // groups
    out_slab = lax.dynamic_slice_in_dim(output_weight, group * slab, slab, 0)
    x_all_b, normed, query_raw, key_raw, values, out_slab, small_all, factors = gather_project(
        shards, tokens, small, out_slab, query_weight, key_weight, value_weight
    )
    full_output = lax.all_gather(out_slab, "dp", axis=0, tiled=True)
    x_all_b = x_all_b.reshape(length, width)
    normed = normed.reshape(length, width)
    query_raw = query_raw.reshape(length, local)
    key_raw = key_raw.reshape(length, local)
    values = values.reshape(length, local)
    gain_in = small_all[:, 0, rows:].reshape(width)
    head_gains = own_gains[1:3]
    cosine, sine = rotary_tables(length)
    limit = jnp.broadcast_to(prefix.reshape(1, 1), (8, 128))
    few = rows // 4
    queries, keys, mixed_own, grad_first = attention(
        shards, limit, query_raw, key_raw, values, factors, cosine, sine, head_gains,
        out_grad[:few],
    )
    mixed_all = gather_line(shards, mixed_own, 1)
    grad_rest, mixed_all, combine, gain_expert = lax.optimization_barrier(
        (out_grad[few:], mixed_all, small_all[:, :experts, :rows], small_all[:, 1, rows:])
    )
    combine = combine.transpose(0, 2, 1).reshape(length, experts)
    gain_expert = gain_expert.reshape(width)
    grad_rest = lax.all_gather(grad_rest, "shard", axis=0)
    attended, expert_in, gate_by, up_by, hidden, sum_part, gate_t, up_t, down_t = forward_pass(
        mixed_all, full_output, x_all_b, gain_expert[None, :], combine, expert_gate, expert_up,
        expert_down,
    )
    attended_own = lax.dynamic_slice_in_dim(attended, place * rows, rows, 0)
    g_all, in_part, gate_grad, up_grad = backward_pass(
        grad_first, grad_rest, gate_by, up_by, gate_t, up_t, down_t
    )
    sum_parts = sum_part.reshape(shards, 16, rows // 16, width)
    grad_gate, grad_up = expert_grads(expert_in, gate_grad, up_grad, experts)
    in_part, grad_gate, grad_up = lax.optimization_barrier((in_part, grad_gate, grad_up))
    grad_gate, grad_up = lax.psum((grad_gate, grad_up), "dp")

    x_own = tokens.astype(f32)
    residual_own = x_own + attended_own
    residual_grad, attended_grad, gain_grad_res, grad_down = scatter_norm(
        shards, groups, 16, in_part, tokens, gain_expert[None, :],
        more=(out_grad, attended, hidden, g_all, experts),
    )
    residual_grad = residual_grad.reshape(rows, width)
    attended_grad = attended_grad.reshape(length, width)

    own_columns = lax.dynamic_slice_in_dim(attended_grad, place * local, local, 1)
    grad_output = lax.dot_general(
        mixed_all, own_columns, (((1,), (0,)), ((), ())), preferred_element_type=f32
    ).reshape(width, local)
    grad_output, grad_down, grad_gate, grad_up, attended_grad = lax.optimization_barrier(
        (grad_output.astype(bf16), grad_down, grad_gate, grad_up, attended_grad)
    )
    grad_output, grad_down = lax.psum((grad_output, grad_down), "dp")
    grad_query, grad_key, grad_value, normed_part, gain_grad_heads, expert_sum = attention_back(
        shards, width, limit, queries, keys, values, query_raw, key_raw, factors, cosine, sine,
        head_gains, query_weight, key_weight, value_weight, normed, sum_parts, attended_grad,
        full_output,
    )
    expert_sum = expert_sum.reshape(rows, width)
    expert_sum, grad_gate, grad_up = lax.optimization_barrier((expert_sum, grad_gate, grad_up))
    grad_gate, grad_up = widen(grad_gate, grad_up)
    (
        grad_query, grad_key, grad_value, normed_part, grad_output, grad_down, grad_gate, grad_up,
    ) = lax.optimization_barrier(
        (
            grad_query, grad_key, grad_value, normed_part, grad_output, grad_down, grad_gate,
            grad_up,
        )
    )
    grad_query, grad_key, grad_value = lax.psum((grad_query, grad_key, grad_value), "dp")
    through_norm, grad_gains = scatter_norm(
        shards, groups, 16, normed_part, tokens, gain_in[None, :],
        other_gains=(gain_grad_res, gain_grad_heads),
    )
    through_norm, expert_sum = lax.optimization_barrier((through_norm, expert_sum))
    grad_tokens = residual_grad + through_norm.reshape(rows, width)
    grad_gains = grad_gains[:4]
    output = residual_own + expert_sum
    root_means = jnp.stack([root_mean(attended_own), root_mean(expert_sum), root_mean(output)])
    grad_down, grad_output = widen(grad_down, grad_output)
    grad_query, grad_key, grad_value = widen(grad_query, grad_key, grad_value)

    return (
        output.astype(bf16),
        grad_tokens,
        root_means,
        grad_query,
        grad_key,
        grad_value,
        grad_output,
        grad_gains,
        grad_gate,
        grad_up,
        grad_down,
    )


def solution(mesh):
    placed = (
        P(("dp", "shard"), None),
        P(("dp", "shard"), None),
        P(("dp", "shard"), None),
        P(("dp", "shard"), None),
        P("dp"),
        P(None, "shard"),
        P(None, "shard"),
        P(None, "shard"),
        P(None, "shard"),
        P(None, "shard"),
        P(None, None, "shard"),
        P(None, None, "shard"),
        P(None, "shard", None),
    )
    return jax.shard_map(
        per_device,
        mesh=mesh,
        in_specs=placed,
        out_specs=(
            P(("dp", "shard"), None),
            P(("dp", "shard"), None),
            P(None, ("dp", "shard")),
            P(None, "shard"),
            P(None, "shard"),
            P(None, "shard"),
            P(None, "shard"),
            P(None, "shard"),
            P(None, None, "shard"),
            P(None, None, "shard"),
            P(None, "shard", None),
        ),
        check_vma=False,
    )
```

```python
import functools

import jax
import jax.numpy as jnp
import numpy as np
from jax import lax
from jax.experimental import pallas as pl
from jax.experimental.pallas import tpu as pltpu
from jax.sharding import PartitionSpec as P

HEAD_DIM = 128
EPSILON = 1e-05
ROPE_BASE = 10000.0
MASKED = -1e30
VMEM_LIMIT = 60 * 2**20

f32 = jnp.float32
bf16 = jnp.bfloat16


def rotary_tables(row_count):
    half_dim = HEAD_DIM // 2
    inverse = ROPE_BASE ** (-np.arange(half_dim) / half_dim)
    angles = np.arange(row_count)[:, None] * inverse.astype(np.float32).astype(np.float64)[None, :]
    angles = angles.astype(np.float32).astype(np.float64)
    cosine, sine = np.cos(angles), np.sin(angles)
    return (
        jnp.asarray(np.concatenate([cosine, cosine], 1), f32),
        jnp.asarray(np.concatenate([-sine, sine], 1), f32),
    )


def row_factor(values):
    return lax.rsqrt(jnp.mean(values * values, axis=-1, keepdims=True) + EPSILON)


def norm_back(grad_unit, unit_rows, factor):
    return factor * (
        grad_unit - unit_rows * jnp.mean(grad_unit * unit_rows, axis=-1, keepdims=True)
    )


def root_mean(values):
    return jnp.sqrt(jnp.mean(values * values, axis=-1))


def dot(a, b):
    return jnp.dot(a, b, preferred_element_type=f32)


def dot_nt(a, b):
    return lax.dot_general(a, b, (((1,), (1,)), ((), ())), preferred_element_type=f32)


def dot_tn(a, b):
    return lax.dot_general(a, b, (((0,), (0,)), ((), ())), preferred_element_type=f32)


MESH = pl.DeviceIdType.MESH


def greet(peers):
    barrier = pltpu.get_barrier_semaphore()
    for peer in peers:
        pl.semaphore_signal(barrier, inc=1, device_id=peer, device_id_type=MESH)
    pl.semaphore_wait(barrier, len(peers))


def others(n):
    d, z = lax.axis_index("dp"), lax.axis_index("shard")
    return d, z, [(d, lax.rem(z + p, n)) for p in range(1, n)]


def line_gather(n, slots, up_sem, down_sem, recv_sem):
    d, z = lax.axis_index("dp"), lax.axis_index("shard")

    def send_up(o):
        return pltpu.make_async_remote_copy(
            src_ref=slots.at[o], dst_ref=slots.at[o], send_sem=up_sem.at[o],
            recv_sem=recv_sem.at[o], device_id=(d, lax.rem(z + 1, n)), device_id_type=MESH,
        )

    def send_down(o):
        return pltpu.make_async_remote_copy(
            src_ref=slots.at[o], dst_ref=slots.at[o], send_sem=down_sem.at[o],
            recv_sem=recv_sem.at[o], device_id=(d, lax.rem(z + n - 1, n)), device_id_type=MESH,
        )

    def begin():
        @pl.when(z < n - 1)
        def _():
            send_up(z).start()

        @pl.when(z > 0)
        def _():
            send_down(z).start()

    def hop(s, landed):
        below, above = z - s, z + s

        @pl.when((s > 0) & (below >= 0))
        def _():
            send_up(below).wait_recv()

            @pl.when(z < n - 1)
            def _():
                send_up(below).start()

            landed(below)

        @pl.when((s > 0) & (above < n))
        def _():
            send_down(above).wait_recv()

            @pl.when(z > 0)
            def _():
                send_down(above).start()

            landed(above)

    def drain():
        def one(o, carry):
            @pl.when((z < n - 1) & (o <= z))
            def _():
                send_up(o).wait_send()

            @pl.when((z > 0) & (o >= z))
            def _():
                send_down(o).wait_send()

            return carry

        lax.fori_loop(0, n, one, 0)

    return begin, hop, drain


def gather_project_kernel(
    n, x_hbm, small_ref, slab_hbm, wq_hbm, wk_hbm, wv_hbm,
    x_out, normed_out, q_out, k_out, v_out, slab_out, combine_out, gains_out, sq_out,
    slabs, xs, nb, qb, kb, vb, wq, wk, wv, sq_all, small_all,
    load_sem, out_sem, up_sem, down_sem, recv_sem, small_send, small_recv, sq_send, sq_recv,
    slab_up, slab_down, slab_recv, slab_sem,
):
    T, D = xs.shape[1:]
    C = qb.shape[2]
    d, z, peers = others(n)
    S = slabs.shape[1]
    slab_rows = pl.ds(pl.multiple_of(d * S, S), S)
    slab_load = pltpu.make_async_copy(slab_hbm.at[slab_rows, :], slabs.at[z], load_sem.at[4])
    slab_load.start()
    own_load = pltpu.make_async_copy(x_hbm, xs.at[z], load_sem.at[0])
    own_load.start()
    slab_begin, slab_hop, slab_drain = line_gather(n, slabs, slab_up, slab_down, slab_recv)

    def slab_save(o):
        c = pl.ds(pl.multiple_of(o * C, C), C)
        return pltpu.make_async_copy(slabs.at[o], slab_out.at[:, c], slab_sem.at[o])

    loads = [
        pltpu.make_async_copy(src, dst, load_sem.at[i + 1])
        for i, (src, dst) in enumerate(((wq_hbm, wq), (wk_hbm, wk), (wv_hbm, wv)))
    ]
    for load in loads:
        load.start()
    greet(peers)

    def send_up(o):
        return pltpu.make_async_remote_copy(
            src_ref=xs.at[o], dst_ref=xs.at[o], send_sem=up_sem.at[o], recv_sem=recv_sem.at[o],
            device_id=(d, lax.rem(z + 1, n)), device_id_type=MESH,
        )

    def send_down(o):
        return pltpu.make_async_remote_copy(
            src_ref=xs.at[o], dst_ref=xs.at[o], send_sem=down_sem.at[o], recv_sem=recv_sem.at[o],
            device_id=(d, lax.rem(z + n - 1, n)), device_id_type=MESH,
        )

    slab_load.wait()
    slab_begin()
    slab_save(z).start()
    own_load.wait()
    small_copies = []
    for p, peer in enumerate(peers):
        copy = pltpu.make_async_remote_copy(
            src_ref=small_ref, dst_ref=small_all.at[z], send_sem=small_send.at[p],
            recv_sem=small_recv.at[z], device_id=peer, device_id_type=MESH,
        )
        copy.start()
        small_copies.append(copy)

    @pl.when(z < n - 1)
    def _():
        send_up(z).start()

    @pl.when(z > 0)
    def _():
        send_down(z).start()

    small_all[z] = small_ref[...]
    for load in loads:
        load.wait()
    for p in range(1, n):
        o = lax.rem(z + n - p, n)
        pltpu.make_async_remote_copy(
            src_ref=small_ref, dst_ref=small_all.at[o], send_sem=small_send.at[p - 1],
            recv_sem=small_recv.at[o], device_id=(d, o), device_id_type=MESH,
        ).wait_recv()

    lanes = lax.broadcasted_iota(jnp.int32, (T, 128), 1)
    step_rows = 32

    def outs(o):
        return [
            pltpu.make_async_copy(src.at[o], dst.at[o], out_sem.at[i, o])
            for i, (src, dst) in enumerate(
                ((xs, x_out), (nb, normed_out), (qb, q_out), (kb, k_out), (vb, v_out))
            )
        ]

    def compute(o):
        gain = jnp.concatenate([small_all[s, 0:1, T:] for s in range(n)], axis=1)

        def norm_rows(i, carry):
            r = pl.ds(pl.multiple_of(i * step_rows, step_rows), step_rows)
            x = xs[o, r, :].astype(f32)
            factor = lax.rsqrt(jnp.sum(x * x, axis=1, keepdims=True) / D + EPSILON)
            nb[o, r, :] = (x * factor * gain).astype(bf16)
            return carry

        lax.fori_loop(0, T // step_rows, norm_rows, 0)
        q = jnp.dot(nb[o], wq[...], preferred_element_type=f32)
        qb[o] = q
        q_sum = jnp.sum(q * q, axis=1, keepdims=True)
        k = jnp.dot(nb[o], wk[...], preferred_element_type=f32)
        kb[o] = k
        k_sum = jnp.sum(k * k, axis=1, keepdims=True)
        vb[o] = jnp.dot(nb[o], wv[...], preferred_element_type=f32).astype(bf16)
        both = jnp.where(lanes == 0, q_sum, jnp.where(lanes == 1, k_sum, 0.0))
        sq_all[z, o] = both.T[0:8]
        for copy in outs(o):
            copy.start()

    def step(s, carry):
        below, above = z - s, z + s
        slab_hop(s, lambda o: slab_save(o).start())

        @pl.when((s > 0) & (below >= 0))
        def _():
            send_up(below).wait_recv()

            @pl.when(z < n - 1)
            def _():
                send_up(below).start()

        @pl.when((s > 0) & (above < n))
        def _():
            send_down(above).wait_recv()

            @pl.when(z > 0)
            def _():
                send_down(above).start()

        def side(j, inner):
            o = z - s + 2 * s * j

            @pl.when((o >= 0) & (o < n) & ((s > 0) | (j == 0)))
            def _():
                compute(o)

            return inner

        lax.fori_loop(0, 2, side, 0)
        return carry

    lax.fori_loop(0, n, step, 0)

    sq_copies = []
    for p, peer in enumerate(peers):
        copy = pltpu.make_async_remote_copy(
            src_ref=sq_all.at[z], dst_ref=sq_all.at[z], send_sem=sq_send.at[p],
            recv_sem=sq_recv.at[z], device_id=peer, device_id_type=MESH,
        )
        copy.start()
        sq_copies.append(copy)

    def spread(o, carry):
        r = pl.ds(pl.multiple_of(o * T, T), T)
        tall = jnp.concatenate([small_all[o, :, 0:T], jnp.zeros((120, T), f32)], axis=0)
        combine_out[r, :] = tall.T
        return carry

    lax.fori_loop(0, n, spread, 0)
    for s in range(n):
        gains_out[:, s * C : (s + 1) * C] = small_all[s, :, T:]

    def finish(o, carry):
        for copy in outs(o):
            copy.wait()
        slab_save(o).wait()

        @pl.when((z < n - 1) & (o <= z))
        def _():
            send_up(o).wait_send()

        @pl.when((z > 0) & (o >= z))
        def _():
            send_down(o).wait_send()

        return carry

    lax.fori_loop(0, n, finish, 0)
    slab_drain()
    for p in range(1, n):
        o = lax.rem(z + n - p, n)
        pltpu.make_async_remote_copy(
            src_ref=sq_all.at[o], dst_ref=sq_all.at[o], send_sem=sq_send.at[p - 1],
            recv_sem=sq_recv.at[o], device_id=(d, o), device_id_type=MESH,
        ).wait_recv()
    def turn_factors(i, carry):
        total = sq_all[0, i]
        for s in range(1, n):
            total = total + sq_all[s, i]
        total = jnp.concatenate([total, jnp.zeros((120, T), f32)], axis=0).T
        r = pl.ds(pl.multiple_of(i * T, T), T)
        sq_out[r, :] = lax.rsqrt(total / D + EPSILON)
        return carry

    lax.fori_loop(0, n, turn_factors, 0)
    for copy in small_copies + sq_copies:
        copy.wait_send()


def gather_project(n, groups, tokens, small, wo, wq, wk, wv):
    T, D = tokens.shape
    C = wq.shape[1]
    S = D // groups
    hbm = pl.BlockSpec(memory_space=pl.ANY)
    vmem = pl.BlockSpec(memory_space=pltpu.VMEM)
    dma = pltpu.SemaphoreType.DMA
    return pl.pallas_call(
        functools.partial(gather_project_kernel, n),
        out_shape=[
            jax.ShapeDtypeStruct((n, T, D), bf16),
            jax.ShapeDtypeStruct((n, T, D), bf16),
            jax.ShapeDtypeStruct((n, T, C), f32),
            jax.ShapeDtypeStruct((n, T, C), f32),
            jax.ShapeDtypeStruct((n, T, C), bf16),
            jax.ShapeDtypeStruct((S, D), bf16),
            jax.ShapeDtypeStruct((n * T, 128), f32),
            jax.ShapeDtypeStruct((8, D), f32),
            jax.ShapeDtypeStruct((n * T, 128), f32),
        ],
        in_specs=[hbm, vmem, hbm, hbm, hbm, hbm],
        out_specs=[hbm] * 6 + [vmem] * 3,
        scratch_shapes=[
            pltpu.VMEM((n, S, C), bf16),
            pltpu.VMEM((n, T, D), bf16),
            pltpu.VMEM((n, T, D), bf16),
            pltpu.VMEM((n, T, C), f32),
            pltpu.VMEM((n, T, C), f32),
            pltpu.VMEM((n, T, C), bf16),
            pltpu.VMEM((D, C), bf16),
            pltpu.VMEM((D, C), bf16),
            pltpu.VMEM((D, C), bf16),
            pltpu.VMEM((n, n, 8, T), f32),
            pltpu.VMEM((n,) + small.shape, f32),
            dma((5,)),
            dma((5, n)),
            dma((n,)),
            dma((n,)),
            dma((n,)),
            dma((n,)),
            dma((n,)),
            dma((n,)),
            dma((n,)),
            dma((n,)),
            dma((n,)),
            dma((n,)),
            dma((n,)),
        ],
        compiler_params=pltpu.CompilerParams(
            collective_id=0, has_side_effects=True, vmem_limit_bytes=VMEM_LIMIT
        ),
        cost_estimate=pl.CostEstimate(flops=80 * 10**9, bytes_accessed=32 * 2**20, transcendentals=0),
        name="gather_project",
    )(tokens, small, wo, wq, wk, wv)


def rope(v, cosine, sine):
    return v * cosine + pltpu.roll(v, HEAD_DIM // 2, 1) * sine


def key_span(i, block, length):
    return min(length, max((i + 1) * block, length // 2))


def block_scores(q, k, i, block, limit):
    s = dot_nt(q, k) * (HEAD_DIM**-0.5)
    row = lax.broadcasted_iota(jnp.int32, s.shape, 0) + i * block
    col = lax.broadcasted_iota(jnp.int32, s.shape, 1)
    return jnp.where((col <= row) | (col < limit), s, MASKED)


def attention_kernel(
    n, limit_ref, q_raw, k_raw, v_ref, factors, cosine, sine, gains, grad_hbm,
    q_out, k_out, mixed, first_out, slots, load_sem, up_sem, down_sem, recv_sem, out_sem,
):
    length = q_raw.shape[0]
    block = 256
    limit = limit_ref[0:1, 0:1]
    h, heads = pl.program_id(0), pl.num_programs(0)
    begin, hop, drain = line_gather(n, slots, up_sem, down_sem, recv_sem)
    z = lax.axis_index("shard")

    def save(o):
        return pltpu.make_async_copy(slots.at[o], first_out.at[o], out_sem.at[o])

    few = slots.shape[1]

    @pl.when(h == 0)
    def _():
        load = pltpu.make_async_copy(grad_hbm.at[0:few], slots.at[z], load_sem.at[0])
        load.start()
        _, _, peers = others(n)
        greet(peers)
        load.wait()
        begin()
        save(z).start()

    def turn(raw, out, column, gain):
        def part(i, carry):
            r = pl.ds(pl.multiple_of(i * block, block), block)
            v = raw[r, :] * factors[r, column : column + 1] * gain
            out[r, :] = rope(v, cosine[r, :], sine[r, :]).astype(bf16)
            return carry

        lax.fori_loop(0, length // block, part, 0)

    turn(q_raw, q_out, 0, gains[1:2, :])
    turn(k_raw, k_out, 1, gains[2:3, :])
    for i in range(length // block):
        span = key_span(i, block, length)
        r = pl.ds(i * block, block)
        s = block_scores(q_out[r, :], k_out[0:span, :], i, block, limit)
        e = jnp.exp(s - jnp.max(s, axis=1, keepdims=True))
        total = jnp.sum(e, axis=1, keepdims=True)
        mixed[r, :] = (dot(e.astype(bf16), v_ref[0:span, :]) / total).astype(bf16)

    def hops(s, carry):
        hop(s, lambda o: save(o).start())
        return carry

    lax.fori_loop(1 + h * (n - 1) // heads, 1 + (h + 1) * (n - 1) // heads, hops, 0)

    @pl.when(h == heads - 1)
    def _():
        drain()

        def finish(o, carry):
            save(o).wait()
            return carry

        lax.fori_loop(0, n, finish, 0)


def attention(n, limit, q_raw, k_raw, values, factors, cosine, sine, gains, grad, few):
    length, local = q_raw.shape
    heads = local // HEAD_DIM
    head = pl.BlockSpec((length, HEAD_DIM), lambda h: (0, h))
    whole = lambda a: pl.BlockSpec(a.shape, lambda h: (0, 0))
    hbm = pl.BlockSpec(memory_space=pl.ANY)
    out = jax.ShapeDtypeStruct((length, local), bf16)
    dma = pltpu.SemaphoreType.DMA
    return pl.pallas_call(
        functools.partial(attention_kernel, n),
        out_shape=[out] * 3
        + [jax.ShapeDtypeStruct((n, few, grad.shape[1]), bf16)],
        grid=(heads,),
        in_specs=[
            whole(limit), head, head, head, whole(factors), whole(cosine), whole(sine),
            pl.BlockSpec((gains.shape[0], HEAD_DIM), lambda h: (0, h)), hbm,
        ],
        out_specs=[head] * 3 + [hbm],
        scratch_shapes=[pltpu.VMEM((n, few, grad.shape[1]), bf16), dma((1,))] + [dma((n,))] * 4,
        compiler_params=pltpu.CompilerParams(
            collective_id=7, has_side_effects=True, vmem_limit_bytes=VMEM_LIMIT
        ),
        cost_estimate=pl.CostEstimate(
            flops=20 * 10**9, bytes_accessed=16 * 2**20, transcendentals=0
        ),
        name="attention",
    )(limit, q_raw, k_raw, values, factors, cosine, sine, gains, grad)


def attention_back_kernel(
    n, steps, width, limit_ref, q_ref, k_ref, v_ref, q_raw, k_raw, factors, cosine, sine,
    gains, wq, wk, wv, normed_hbm, sum_hbm, grad_hbm, output_hbm, gq_out, gk_out, gv_out, normed_out, gain_out, own_sum,
    g_ref, output, dq_acc, dk_acc, k_acc, v_acc, q_grad, k_grad, v_grad, columns, turned, staged,
    inner_all, inner_send, inner_recv, column_sem, staged_sem, grad_sem, part, *line,
):
    length, local = q_ref.shape
    strips = width // local
    heads = local // HEAD_DIM
    block = 256
    blocks = length // block
    scale = HEAD_DIM**-0.5
    load_sem = line[-1]
    turn, drain = line_sum(n, steps, part, own_sum, *line[:-1])
    d, z, peers = others(n)
    load = pltpu.make_async_copy(sum_hbm, part, load_sem.at[0])
    load.start()

    def grad_rows(i):
        r = pl.ds(pl.multiple_of(i * block, block), block)
        return pltpu.make_async_copy(
            grad_hbm.at[r, :], staged.at[lax.rem(i, 2)], grad_sem.at[lax.rem(i, 2)]
        )

    own_rows = pl.ds(pl.multiple_of(z * local, local), local)
    output_load = pltpu.make_async_copy(output_hbm.at[own_rows, :], output, grad_sem.at[2])
    output_load.start()
    grad_rows(0).start()
    greet(peers)

    def strip(b):
        c = pl.ds(pl.multiple_of(b * local, local), local)
        return pltpu.make_async_copy(
            normed_hbm.at[:, c], columns.at[lax.rem(b, 2)], column_sem.at[lax.rem(b, 2)]
        )

    strip(0).start()
    load.wait()
    turns = steps + n - 1
    in_heads, in_parts = 8 * turns // 19, 4 * turns // 19
    slots = -(-in_heads // heads)
    past = 1 + heads * slots
    in_strips = turns - past - in_parts - 2

    def take(first, count, i, of):
        def one(t, carry):
            turn(first + t)
            return carry

        lax.fori_loop(i * count // of, (i + 1) * count // of, one, 0)
    limit = limit_ref[0:1, 0:1]
    lanes = lax.broadcasted_iota(jnp.int32, (block, 128), 1)

    def clear(i, carry):
        inner_all[z, i] = jnp.zeros((8, block), f32)
        return carry

    lax.fori_loop(0, blocks, clear, 0)

    turn(0)
    output_load.wait()

    def mixed_rows(i, carry):
        r = pl.ds(pl.multiple_of(i * block, block), block)
        grad_rows(i).wait()

        @pl.when(i + 1 < blocks)
        def _():
            grad_rows(i + 1).start()

        g_ref[r, :] = dot_nt(staged[lax.rem(i, 2)], output[...]).astype(bf16)
        return carry

    lax.fori_loop(0, blocks, mixed_rows, 0)

    def head(h, carry):
        c = pl.ds(pl.multiple_of(h * HEAD_DIM, HEAD_DIM), HEAD_DIM)
        k_acc[...] = jnp.zeros_like(k_acc)
        v_acc[...] = jnp.zeros_like(v_acc)
        for i in range(blocks):
            for j in range(i * slots // blocks, (i + 1) * slots // blocks):
                turn(1 + h * slots + j)
            span = key_span(i, block, length)
            r = pl.ds(i * block, block)
            q, g, k, v = q_ref[r, c], g_ref[r, c], k_ref[0:span, c], v_ref[0:span, c]
            s = block_scores(q, k, i, block, limit)
            e = jnp.exp(s - jnp.max(s, axis=1, keepdims=True))
            p = e * (1.0 / jnp.sum(e, axis=1, keepdims=True))
            t = p * dot_nt(g, v)
            ds = (t - p * jnp.sum(t, axis=1, keepdims=True)).astype(bf16)
            dq_acc[r, c] = dot(ds, k) * scale
            k_acc[0:span, :] += dot_tn(ds, q) * scale
            v_acc[0:span, :] += dot_tn(p.astype(bf16), g)
        v_grad[:, c] = v_acc[...].astype(bf16)
        gain_q, gain_k = gains[1:2, c], gains[2:3, c]

        def back(i, carry):
            gq, gk = carry
            r = pl.ds(pl.multiple_of(i * block, block), block)
            cos, sin = cosine[r, :], sine[r, :]
            dq = rope(dq_acc[r, c], cos, -sin)
            dk = rope(k_acc[r, :], cos, -sin)
            uq = q_raw[r, c] * factors[r, 0:1]
            uk = k_raw[r, c] * factors[r, 1:2]
            gq = gq + jnp.sum(dq * uq, axis=0, keepdims=True)
            gk = gk + jnp.sum(dk * uk, axis=0, keepdims=True)
            dq = dq * gain_q
            dk = dk * gain_k
            dq_acc[r, c] = dq
            dk_acc[r, c] = dk
            inner_q = jnp.sum(dq * uq, axis=1, keepdims=True)
            inner_k = jnp.sum(dk * uk, axis=1, keepdims=True)
            both = jnp.where(lanes == 0, inner_q, jnp.where(lanes == 1, inner_k, 0.0))
            inner_all[z, i] += both.T[0:8]
            return gq, gk

        zero = jnp.zeros((1, HEAD_DIM), f32)
        gq, gk = lax.fori_loop(0, blocks, back, (zero, zero))
        gain_out[0:1, c] = gq
        gain_out[1:2, c] = gk
        return carry

    lax.fori_loop(0, heads, head, 0)

    copies = []
    for p, peer in enumerate(peers):
        copy = pltpu.make_async_remote_copy(
            src_ref=inner_all.at[z], dst_ref=inner_all.at[z], send_sem=inner_send.at[p],
            recv_sem=inner_recv.at[z], device_id=peer, device_id_type=MESH,
        )
        copy.start()
        copies.append(copy)
    turn(past)
    for p in range(1, n):
        o = lax.rem(z + n - p, n)
        pltpu.make_async_remote_copy(
            src_ref=inner_all.at[o], dst_ref=inner_all.at[o], send_sem=inner_send.at[p - 1],
            recv_sem=inner_recv.at[o], device_id=(d, o), device_id_type=MESH,
        ).wait_recv()

    def raw(i, carry):
        r = pl.ds(pl.multiple_of(i * block, block), block)
        total = inner_all[0, i]
        for s in range(1, n):
            total = total + inner_all[s, i]
        total = jnp.concatenate([total, jnp.zeros((120, block), f32)], axis=0).T
        fq, fk = factors[r, 0:1], factors[r, 1:2]
        mean_q, mean_k = total[:, 0:1] / width, total[:, 1:2] / width
        q_grad[r, :] = (fq * (dq_acc[r, :] - q_raw[r, :] * (fq * mean_q))).astype(bf16)
        k_grad[r, :] = (fk * (dk_acc[r, :] - k_raw[r, :] * (fk * mean_k))).astype(bf16)
        return carry

    lax.fori_loop(0, blocks, raw, 0)
    turn(past + 1)

    def save(i):
        r = pl.ds(pl.multiple_of(i * block, block), block)
        return pltpu.make_async_copy(
            staged.at[lax.rem(i, 2)], normed_out.at[r, :], staged_sem.at[lax.rem(i, 2)]
        )

    def rows_back(i, carry):
        r = pl.ds(pl.multiple_of(i * block, block), block)

        @pl.when(i >= 2)
        def _():
            save(i - 2).wait()

        staged[lax.rem(i, 2)] = (
            dot_nt(q_grad[r, :], wq[...])
            + dot_nt(k_grad[r, :], wk[...])
            + dot_nt(v_grad[r, :], wv[...])
        ).astype(bf16)
        save(i).start()
        take(past + 2, in_parts, i, blocks)
        return carry

    lax.fori_loop(0, blocks, rows_back, 0)

    def strip_grads(b, carry):
        strip(b).wait()

        @pl.when(b + 1 < strips)
        def _():
            strip(b + 1).start()

        turned[...] = columns[lax.rem(b, 2)].T
        c = pl.ds(pl.multiple_of(b * local, local), local)
        gq_out[c, :] = dot(turned[...], q_grad[...]).astype(bf16)
        gk_out[c, :] = dot(turned[...], k_grad[...]).astype(bf16)
        gv_out[c, :] = dot(turned[...], v_grad[...]).astype(bf16)
        take(past + 2 + in_parts, in_strips, b, strips)
        return carry

    lax.fori_loop(0, strips, strip_grads, 0)
    drain()
    for i in range(max(blocks - 2, 0), blocks):
        save(i).wait()
    for copy in copies:
        copy.wait_send()


def attention_back(
    n, width, limit, q, k, v, q_raw, k_raw, factors, cosine, sine, gains, wq, wk, wv, normed,
    sum_parts, attended_grad, full_output,
):
    length, local = q.shape
    _, steps, R, D = sum_parts.shape
    hbm = pl.BlockSpec(memory_space=pl.ANY)
    vmem = pl.BlockSpec(memory_space=pltpu.VMEM)
    dma = pltpu.SemaphoreType.DMA
    weight = jax.ShapeDtypeStruct((D, local), bf16)
    raw = pltpu.VMEM((length, local), bf16)
    return pl.pallas_call(
        functools.partial(attention_back_kernel, n, steps, width),
        out_shape=[
            weight, weight, weight, jax.ShapeDtypeStruct((length, D), bf16),
            jax.ShapeDtypeStruct((2, local), f32),
            jax.ShapeDtypeStruct((steps, R, D), f32),
        ],
        in_specs=[vmem] * 13 + [hbm] * 4,
        out_specs=[vmem, vmem, vmem, hbm, vmem, vmem],
        scratch_shapes=[
            raw,
            pltpu.VMEM((local, D), bf16),
            pltpu.VMEM((length, local), f32),
            pltpu.VMEM((length, local), f32),
            pltpu.VMEM((length, HEAD_DIM), f32),
            pltpu.VMEM((length, HEAD_DIM), f32),
            raw,
            raw,
            raw,
            pltpu.VMEM((2, length, local), bf16),
            pltpu.VMEM((local, length), bf16),
            pltpu.VMEM((2, 256, D), bf16),
            pltpu.VMEM((n, length // 256, 8, 256), f32),
            dma((n,)),
            dma((n,)),
            dma((2,)),
            dma((2,)),
            dma((3,)),
        ]
        + line_scratch(n, steps, R, D),
        compiler_params=pltpu.CompilerParams(
            collective_id=6, has_side_effects=True, vmem_limit_bytes=VMEM_LIMIT
        ),
        cost_estimate=pl.CostEstimate(
            flops=2 * 10**9, bytes_accessed=2**20, transcendentals=0
        ),
        name="attention_back",
    )(
        limit, q, k, v, q_raw, k_raw, factors, cosine, sine, gains, wq, wk, wv, normed, sum_parts,
        attended_grad, full_output,
    )


def scatter_norm_kernel(n, groups, steps, gather, *refs):
    part, base, gain = refs[:3]
    refs = refs[3:]
    if gather:
        addend, attended_hbm, hidden, g_all = refs[:4]
        out, all_out, columns_out, gain_out, down_out = refs[4:9]
        alls, ag_up, ag_down, ag_recv, all_sem, attended, load_sem = refs[9:16]
        refs = refs[16:]
    else:
        expert_gains, head_gains, out, gain_out = refs[:4]
        pieces, landed, sums, piece_send, piece_recv, sum_send, sum_recv = refs[4:11]
        refs = refs[11:]
    from_below, from_above, gain_acc, up_send, up_recv, down_send, down_recv = refs
    R, D = part.shape[2:]
    d, z, peers = others(n)
    upper, lower = (d, lax.rem(z + 1, n)), (d, lax.rem(z + n - 1, n))
    alike = [] if gather else [(lax.rem(d + p, groups), z) for p in range(1, groups)]
    if gather:
        load = pltpu.make_async_copy(attended_hbm.at[z], attended, load_sem.at[0])
        load.start()
    greet(peers + alike)
    if gather:
        load.wait()
    gain_acc[...] = jnp.zeros_like(gain_acc)

    def move_up(src, o, k):
        return pltpu.make_async_remote_copy(
            src_ref=src.at[o, k], dst_ref=from_below.at[o, k], send_sem=up_send.at[o, k],
            recv_sem=up_recv.at[o, k], device_id=upper, device_id_type=MESH,
        )

    def move_down(src, o, k):
        return pltpu.make_async_remote_copy(
            src_ref=src.at[o, k], dst_ref=from_above.at[o, k], send_sem=down_send.at[o, k],
            recv_sem=down_recv.at[o, k], device_id=lower, device_id_type=MESH,
        )

    def all_up(o, k):
        return pltpu.make_async_remote_copy(
            src_ref=alls.at[o, k], dst_ref=alls.at[o, k], send_sem=ag_up.at[o, k],
            recv_sem=ag_recv.at[o, k], device_id=upper, device_id_type=MESH,
        )

    def all_down(o, k):
        return pltpu.make_async_remote_copy(
            src_ref=alls.at[o, k], dst_ref=alls.at[o, k], send_sem=ag_down.at[o, k],
            recv_sem=ag_recv.at[o, k], device_id=lower, device_id_type=MESH,
        )

    def pass_up(k):
        def far(i, carry):
            o = z + n - 1 - i

            @pl.when(o < n)
            def _():
                @pl.when(z == 0)
                def _():
                    move_up(part, o, k).start()

                @pl.when(z > 0)
                def _():
                    move_up(part, o, k).wait_recv()
                    both = from_below[o, k].astype(f32) + part[o, k].astype(f32)
                    from_below[o, k] = both.astype(bf16)
                    move_up(from_below, o, k).start()

            return carry

        lax.fori_loop(0, n - 1, far, 0)

    def pass_down(k):
        def far(i, carry):
            o = z - n + 1 + i

            @pl.when(o >= 0)
            def _():
                @pl.when(z == n - 1)
                def _():
                    move_down(part, o, k).start()

                @pl.when(z < n - 1)
                def _():
                    move_down(part, o, k).wait_recv()
                    both = from_above[o, k].astype(f32) + part[o, k].astype(f32)
                    from_above[o, k] = both.astype(bf16)
                    move_down(from_above, o, k).start()

            return carry

        lax.fori_loop(0, n - 1, far, 0)

    def own(k):
        @pl.when(z > 0)
        def _():
            move_up(part, z, k).wait_recv()

        @pl.when(z == 0)
        def _():
            from_below[z, k] = jnp.zeros((R, D), bf16)

        @pl.when(z < n - 1)
        def _():
            move_down(part, z, k).wait_recv()

        @pl.when(z == n - 1)
        def _():
            from_above[z, k] = jnp.zeros((R, D), bf16)

        total = (
            part[z, k].astype(f32) + from_below[z, k].astype(f32) + from_above[z, k].astype(f32)
        )
        rows = base[k].astype(f32)
        if gather:
            rows = rows + attended[k]
        factor = lax.rsqrt(jnp.sum(rows * rows, axis=1, keepdims=True) / D + EPSILON)
        unit = rows * factor
        along = total * unit
        gain_acc[...] += jnp.sum(along.reshape(R // 8, 8, D), axis=0)
        weights = gain[1:2, :] if gather else gain[0:1, :]
        weighted = along * weights
        mean = jnp.sum(weighted, axis=1, keepdims=True) / D
        result = factor * (total * weights - unit * mean)
        if gather:
            result = result + addend[k].astype(f32)
        out[k] = result
        if gather:
            alls[z, k] = result.astype(bf16)

            @pl.when(z < n - 1)
            def _():
                all_up(z, k).start()

            @pl.when(z > 0)
            def _():
                all_down(z, k).start()

    def forward(own_k):
        def hop(s, carry):
            below, above, k = z - s, z + s, own_k - s
            live = (k >= 0) & (k < steps)

            @pl.when(live & (below >= 0))
            def _():
                all_up(below, k).wait_recv()

                @pl.when(z < n - 1)
                def _():
                    all_up(below, k).start()

            @pl.when(live & (above < n))
            def _():
                all_down(above, k).wait_recv()

                @pl.when(z > 0)
                def _():
                    all_down(above, k).start()

            return carry

        lax.fori_loop(1, n, hop, 0)

    def turn(t, carry):
        up_k, down_k, own_k = t - z, t - (n - 1 - z), t - (n - 1)

        @pl.when((up_k >= 0) & (up_k < steps))
        def _():
            pass_up(up_k)

        @pl.when((down_k >= 0) & (down_k < steps))
        def _():
            pass_down(down_k)

        @pl.when((own_k >= 0) & (own_k < steps))
        def _():
            own(own_k)

        if gather:
            forward(own_k)
            experts, units = down_out.shape[:2]
            e = t - n

            @pl.when((e >= 0) & (e < experts))
            def _():
                c = pl.ds(pl.multiple_of(e * units, units), units)
                down_out[e] = dot_tn(hidden[:, c], g_all[...]).astype(bf16)

        return carry

    lax.fori_loop(0, steps + (2 * n - 2 if gather else n - 1), turn, 0)
    if gather:
        gain_out[...] = gain_acc[...]
    else:
        C = D // n
        for s in range(n):
            c = slice(s * C, (s + 1) * C)
            pieces[s, 0:1] = jnp.sum(gain_acc[:, c], axis=0, keepdims=True)
            pieces[s, 1:2] = jnp.sum(expert_gains[:, c], axis=0, keepdims=True)
            pieces[s, 2:8] = jnp.zeros((6, C), f32)

        def piece(p):
            o = lax.rem(z + p, n)
            return pltpu.make_async_remote_copy(
                src_ref=pieces.at[o], dst_ref=landed.at[z], send_sem=piece_send.at[p - 1],
                recv_sem=piece_recv.at[z], device_id=(d, o), device_id_type=MESH,
            )

        for p in range(1, n):
            piece(p).start()
        landed[z] = pieces[z]
        for p in range(1, n):
            o = lax.rem(z + n - p, n)
            pltpu.make_async_remote_copy(
                src_ref=pieces.at[o], dst_ref=landed.at[o], send_sem=piece_send.at[p - 1],
                recv_sem=piece_recv.at[o], device_id=(d, o), device_id_type=MESH,
            ).wait_recv()
        two = landed[0]
        for s in range(1, n):
            two = two + landed[s]
        sums[d, 0:1] = two[0:1]
        sums[d, 1:3] = head_gains[...]
        sums[d, 3:4] = two[1:2]
        sums[d, 4:8] = jnp.zeros((4, C), f32)
        for p in range(1, groups):
            pltpu.make_async_remote_copy(
                src_ref=sums.at[d], dst_ref=sums.at[d], send_sem=sum_send.at[p - 1],
                recv_sem=sum_recv.at[d], device_id=alike[p - 1], device_id_type=MESH,
            ).start()
        for p in range(1, groups):
            o = lax.rem(d + groups - p, groups)
            pltpu.make_async_remote_copy(
                src_ref=sums.at[o], dst_ref=sums.at[o], send_sem=sum_send.at[p - 1],
                recv_sem=sum_recv.at[o], device_id=(o, z), device_id_type=MESH,
            ).wait_recv()
        total = sums[0]
        for s in range(1, groups):
            total = total + sums[s]
        gain_out[...] = total
        for p in range(1, n):
            piece(p).wait_send()
        for p in range(1, groups):
            pltpu.make_async_remote_copy(
                src_ref=sums.at[d], dst_ref=sums.at[d], send_sem=sum_send.at[p - 1],
                recv_sem=sum_recv.at[d], device_id=alike[p - 1], device_id_type=MESH,
            ).wait_send()

    def drain(i, carry):
        o, k = i // steps, i % steps

        @pl.when(o > z)
        def _():
            move_up(part, o, k).wait_send()

        @pl.when(o < z)
        def _():
            move_down(part, o, k).wait_send()

        if gather:

            @pl.when((z < n - 1) & (o <= z))
            def _():
                all_up(o, k).wait_send()

            @pl.when((z > 0) & (o >= z))
            def _():
                all_down(o, k).wait_send()

        return carry

    lax.fori_loop(0, n * steps, drain, 0)
    if gather:
        C = D // n
        c = pl.ds(pl.multiple_of(z * C, C), C)
        copies = []
        for o in range(n):
            own_columns = alls.at[o, :, :, c]
            copies.append(
                pltpu.make_async_copy(own_columns, columns_out.at[o], all_sem.at[n + o])
            )
            copies.append(pltpu.make_async_copy(alls.at[o], all_out.at[o], all_sem.at[o]))
        for copy in copies:
            copy.start()
        for copy in copies:
            copy.wait()


def scatter_norm(n, groups, steps, part, base, gain, more=None, other_gains=None):
    gather = more is not None
    T, D = base.shape
    R = T // steps
    C = D // n
    hbm = pl.BlockSpec(memory_space=pl.ANY)
    vmem = pl.BlockSpec(memory_space=pltpu.VMEM)
    dma = pltpu.SemaphoreType.DMA
    slots = pltpu.VMEM((n, steps, R, D), bf16)
    rows = jax.ShapeDtypeStruct((steps, R, D), f32)
    sems = dma((n, steps))
    if gather:
        addend, attended, hidden, g_all, experts = more
        units = hidden.shape[1] // experts
        more = (
            addend.reshape(steps, R, D), attended.reshape(n, steps, R, D), hidden, g_all,
        )
        own = [slots, sems, sems, sems, dma((2 * n,)), pltpu.VMEM((steps, R, D), f32), dma((1,))]
        outs = [rows, jax.ShapeDtypeStruct((n, steps, R, D), bf16)]
        outs += [jax.ShapeDtypeStruct((n, steps, R, C), bf16)]
        outs += [jax.ShapeDtypeStruct((8, D), f32)]
        outs += [jax.ShapeDtypeStruct((experts, units, D), bf16)]
    else:
        own = [
            pltpu.VMEM((n, 8, C), f32), pltpu.VMEM((n, 8, C), f32),
            pltpu.VMEM((groups, 8, C), f32), dma((n,)), dma((n,)), dma((groups,)), dma((groups,)),
        ]
        outs = [rows, jax.ShapeDtypeStruct((8, C), f32)]
    return pl.pallas_call(
        functools.partial(scatter_norm_kernel, n, groups, steps, gather),
        out_shape=outs,
        in_specs=[vmem] * 4 + [hbm, vmem, vmem] if gather else [vmem] * 5,
        out_specs=[vmem, hbm, hbm, vmem, vmem] if gather else [vmem, vmem],
        scratch_shapes=own + [slots, slots, pltpu.VMEM((8, D), f32), sems, sems, sems, sems],
        compiler_params=pltpu.CompilerParams(
            collective_id=2 if gather else 3, has_side_effects=True, vmem_limit_bytes=VMEM_LIMIT
        ),
        cost_estimate=pl.CostEstimate(
            flops=10**9, bytes_accessed=2**20, transcendentals=0
        ),
        name="scatter_norm_gather" if gather else "scatter_norm",
    )(
        part.reshape(n, steps, R, D),
        base.reshape(steps, R, D),
        gain,
        *(more if gather else other_gains),
    )


def forward_kernel(
    mixed, weight, x_ref, gain, combine, gate_w, up_w, down_w,
    attended_out, turned_out, gate_out, up_out, hidden_out, sum_out, gate_t, up_t, down_t,
    in_out, units,
):
    e = pl.program_id(1)
    last = pl.num_programs(1) - 1
    D = in_out.shape[1]
    F = hidden_out.shape[1]

    @pl.when(e == 0)
    def _():
        attended_out[...] = dot(mixed[...], weight[...])
        part = 32

        def rows(i, carry):
            r = pl.ds(pl.multiple_of(i * part, part), part)
            v = attended_out[r, :] + x_ref[r, :].astype(f32)
            factor = lax.rsqrt(jnp.sum(v * v, axis=1, keepdims=True) / D + EPSILON)
            in_out[r, :] = (v * factor * gain[1:2, :]).astype(bf16)
            return carry

        lax.fori_loop(0, in_out.shape[0] // part, rows, 0)
        turned_out[...] = in_out[...].T

    lane = lax.broadcasted_iota(jnp.int32, combine.shape, 1)
    share = jnp.sum(jnp.where(lane == e, combine[...], 0.0), axis=1, keepdims=True)
    @pl.when(pl.program_id(0) == 0)
    def _():
        gate_t[0] = gate_w[0].T
        up_t[0] = up_w[0].T
        down_t[0] = down_w[pl.ds(pl.multiple_of(e * F, F), F), :].T

    gate_part = dot(in_out[...], gate_w[0])
    up_part = dot(in_out[...], up_w[0])
    sig = jax.nn.sigmoid(gate_part)
    silu = gate_part * sig * share
    gate_out[...] = up_part * sig * (1.0 + gate_part * (1.0 - sig)) * share
    up_out[...] = silu
    hidden = (silu * up_part).astype(bf16)
    hidden_out[...] = hidden
    units[:, pl.ds(pl.multiple_of(e * F, F), F)] = hidden

    @pl.when(e == last)
    def _():
        sum_out[...] = dot(units[...], down_w[...]).astype(bf16)


def forward_pass(mixed, weight, x, gain, combine, gate_w, up_w, down_w):
    L, D = x.shape
    E, _, F = gate_w.shape
    block = min(512, L)
    rows = pl.BlockSpec((block, D), lambda i, e: (i, 0))
    held = pl.BlockSpec((block, D), lambda i, e: (i, 0), pipeline_mode=pl.Buffered(1))
    units = pl.BlockSpec((block, F), lambda i, e: (i, e))
    column = pl.BlockSpec((1, D, F), lambda i, e: (e, 0, 0))
    once = pl.Buffered(1)
    turned = pl.BlockSpec((1, F, D), lambda i, e: (jnp.where(i == 0, e, E - 1), 0, 0))
    turned_down = pl.BlockSpec((1, D, F), lambda i, e: (jnp.where(i == 0, e, E - 1), 0, 0))
    return pl.pallas_call(
        forward_kernel,
        out_shape=[
            jax.ShapeDtypeStruct((L, D), f32),
            jax.ShapeDtypeStruct((D, L), bf16),
            jax.ShapeDtypeStruct((L, E * F), f32),
            jax.ShapeDtypeStruct((L, E * F), f32),
            jax.ShapeDtypeStruct((L, E * F), bf16),
            jax.ShapeDtypeStruct((L, D), bf16),
            jax.ShapeDtypeStruct((E, F, D), bf16),
            jax.ShapeDtypeStruct((E, F, D), bf16),
            jax.ShapeDtypeStruct((E, D, F), bf16),
        ],
        grid=(L // block, E),
        in_specs=[
            held,
            pl.BlockSpec((D, D), lambda i, e: (0, 0), pipeline_mode=once),
            held,
            pl.BlockSpec((8, D), lambda i, e: (0, 0)),
            pl.BlockSpec((block, combine.shape[1]), lambda i, e: (i, 0)),
            column, column,
            pl.BlockSpec((E * F, D), lambda i, e: (0, 0), pipeline_mode=once),
        ],
        out_specs=[
            rows, pl.BlockSpec((D, block), lambda i, e: (0, i)), units, units, units, rows, turned,
            turned, turned_down,
        ],
        scratch_shapes=[pltpu.VMEM((block, D), bf16), pltpu.VMEM((block, E * F), bf16)],
        compiler_params=pltpu.CompilerParams(vmem_limit_bytes=VMEM_LIMIT),
        cost_estimate=pl.CostEstimate(
            flops=6 * L * D * E * F + 2 * L * D * D, bytes_accessed=50 * 2**20,
            transcendentals=L * E * F,
        ),
        name="forward_pass",
    )(mixed, weight, x, gain, combine, gate_w, up_w, down_w.reshape(E * F, D))


def backward_kernel(
    first, rest, gate_ref, up_ref, gate_hbm, up_hbm, down_t,
    g_out, in_out, gate_out, up_out, both, turned, load_sem,
):
    i, e = pl.program_id(0), pl.program_id(1)
    last = pl.num_programs(1) - 1
    F = gate_out.shape[1]
    half = turned.shape[0] // 2
    loads = [
        pltpu.make_async_copy(gate_hbm, turned.at[0:half], load_sem.at[0]),
        pltpu.make_async_copy(up_hbm, turned.at[half : 2 * half], load_sem.at[1]),
    ]

    @pl.when((i == 0) & (e == 0))
    def _():
        for load in loads:
            load.start()

    @pl.when(e == 0)
    def _():
        few, many = first.shape[1], rest.shape[1]
        for j in range(first.shape[0]):
            top = j * (few + many)
            g_out[top : top + few, :] = first[j]
            g_out[top + few : top + few + many, :] = rest[j]

    hidden_grad = dot(g_out[...], down_t[0])
    gate_grad = (hidden_grad * gate_ref[...]).astype(bf16)
    gate_out[...] = gate_grad
    both[:, pl.ds(pl.multiple_of(e * F, F), F)] = gate_grad
    up_grad = (hidden_grad * up_ref[...]).astype(bf16)
    up_out[...] = up_grad
    both[:, pl.ds(pl.multiple_of(half + e * F, F), F)] = up_grad

    @pl.when((i == 0) & (e == last))
    def _():
        for load in loads:
            load.wait()

    @pl.when(e == last)
    def _():
        in_out[...] = dot(both[...], turned[...]).astype(bf16)


def backward_pass(first, rest, gate_by, up_by, gate_t, up_t, down_t):
    n, few, D = first.shape
    T = few + rest.shape[1]
    L = n * T
    E, F, _ = gate_t.shape
    block = max(T, min(512, L))
    owners = block // T
    rows = pl.BlockSpec((block, D), lambda i, e: (i, 0))
    units = pl.BlockSpec((block, F), lambda i, e: (i, e))
    hbm = pl.BlockSpec(memory_space=pl.ANY)
    wide = jax.ShapeDtypeStruct((L, D), bf16)
    narrow = jax.ShapeDtypeStruct((L, E * F), bf16)
    return pl.pallas_call(
        backward_kernel,
        out_shape=[wide, wide, narrow, narrow],
        grid=(L // block, E),
        in_specs=[
            pl.BlockSpec((owners, few, D), lambda i, e: (i, 0, 0)),
            pl.BlockSpec((owners, T - few, D), lambda i, e: (i, 0, 0)),
            units, units, hbm, hbm, pl.BlockSpec((1, D, F), lambda i, e: (e, 0, 0)),
        ],
        out_specs=[rows, rows, units, units],
        scratch_shapes=[
            pltpu.VMEM((block, 2 * E * F), bf16),
            pltpu.VMEM((2 * E * F, D), bf16),
            pltpu.SemaphoreType.DMA((2,)),
        ],
        compiler_params=pltpu.CompilerParams(vmem_limit_bytes=VMEM_LIMIT),
        cost_estimate=pl.CostEstimate(
            flops=6 * L * D * E * F, bytes_accessed=40 * 2**20, transcendentals=0
        ),
        name="backward_pass",
    )(first, rest, gate_by, up_by, gate_t.reshape(E * F, D), up_t.reshape(E * F, D), down_t)


def line_sum(n, steps, part, out, landed, up_send, up_recv, down_send, down_recv):
    d, z = lax.axis_index("dp"), lax.axis_index("shard")
    upper, lower = (d, lax.rem(z + 1, n)), (d, lax.rem(z + n - 1, n))

    def move_up(src, o, k):
        return pltpu.make_async_remote_copy(
            src_ref=src.at[o, k], dst_ref=landed.at[o, k], send_sem=up_send.at[o, k],
            recv_sem=up_recv.at[o, k], device_id=upper, device_id_type=MESH,
        )

    def move_down(src, o, k):
        slot = jnp.where(o == z - 1, n, o)
        return pltpu.make_async_remote_copy(
            src_ref=src.at[o, k], dst_ref=landed.at[slot, k], send_sem=down_send.at[o, k],
            recv_sem=down_recv.at[o, k], device_id=lower, device_id_type=MESH,
        )

    def passing(move, first, owner):
        def run(k):
            def far(i, carry):
                o = owner(i)

                @pl.when((o >= 0) & (o < n))
                def _():
                    @pl.when(z == first)
                    def _():
                        move(part, o, k).start()

                    @pl.when(z != first)
                    def _():
                        move(part, o, k).wait_recv()
                        both = landed[o, k].astype(f32) + part[o, k].astype(f32)
                        landed[o, k] = both.astype(bf16)
                        move(landed, o, k).start()

                return carry

            lax.fori_loop(0, n - 1, far, 0)

        return run

    pass_up = passing(move_up, 0, lambda i: z + n - 1 - i)
    pass_down = passing(move_down, n - 1, lambda i: z - n + 1 + i)

    def own(k):
        @pl.when(z > 0)
        def _():
            move_up(part, z, k).wait_recv()

        @pl.when(z == 0)
        def _():
            landed[z, k] = jnp.zeros(part.shape[2:], bf16)

        @pl.when(z < n - 1)
        def _():
            move_down(part, z, k).wait_recv()

        @pl.when(z == n - 1)
        def _():
            landed[n, k] = jnp.zeros(part.shape[2:], bf16)

        out[k] = part[z, k].astype(f32) + landed[z, k].astype(f32) + landed[n, k].astype(f32)

    def turn(t):
        up_k, down_k, own_k = t - z, t - (n - 1 - z), t - (n - 1)

        @pl.when((up_k >= 0) & (up_k < steps))
        def _():
            pass_up(up_k)

        @pl.when((down_k >= 0) & (down_k < steps))
        def _():
            pass_down(down_k)

        @pl.when((own_k >= 0) & (own_k < steps))
        def _():
            own(own_k)

    def drain():
        def one(i, carry):
            o, k = i // steps, i % steps

            @pl.when(o > z)
            def _():
                move_up(part, o, k).wait_send()

            @pl.when(o < z)
            def _():
                move_down(part, o, k).wait_send()

            return carry

        lax.fori_loop(0, n * steps, one, 0)

    return turn, drain


def line_scratch(n, steps, R, D):
    dma = pltpu.SemaphoreType.DMA
    slots = [pltpu.VMEM((n, steps, R, D), bf16), pltpu.VMEM((n + 1, steps, R, D), bf16)]
    return slots + [dma((n, steps))] * 4 + [dma((1,))]


def expert_grads_kernel(xt, gate_grad, up_grad, gate_out, up_out):
    gate_out[0] = dot(xt[...], gate_grad[...]).astype(bf16)
    up_out[0] = dot(xt[...], up_grad[...]).astype(bf16)


def expert_grads(turned, gate_grad, up_grad, experts):
    D, L = turned.shape
    F = gate_grad.shape[1] // experts
    whole = pl.BlockSpec((D, L), lambda e: (0, 0))
    units = pl.BlockSpec((L, F), lambda e: (0, e))
    column = pl.BlockSpec((1, D, F), lambda e: (e, 0, 0))
    grad = jax.ShapeDtypeStruct((experts, D, F), bf16)
    return pl.pallas_call(
        expert_grads_kernel,
        out_shape=[grad, grad],
        grid=(experts,),
        in_specs=[whole, units, units],
        out_specs=[column, column],
        compiler_params=pltpu.CompilerParams(vmem_limit_bytes=VMEM_LIMIT),
        cost_estimate=pl.CostEstimate(
            flops=4 * L * D * experts * F, bytes_accessed=16 * 2**20, transcendentals=0
        ),
        name="expert_grads",
    )(turned, gate_grad, up_grad)


def widen_kernel(count, *refs):
    for src, dst in zip(refs[:count], refs[count:]):
        dst[...] = src[...].astype(f32)


def widen(*arrays):
    flat = [v.reshape(-1, v.shape[-1]) for v in arrays]
    steps = 8
    specs = [
        pl.BlockSpec((v.shape[0] // steps, v.shape[1]), lambda i: (i, 0)) for v in flat
    ]
    out = pl.pallas_call(
        functools.partial(widen_kernel, len(flat)),
        out_shape=[jax.ShapeDtypeStruct(v.shape, f32) for v in flat],
        grid=(steps,),
        in_specs=specs,
        out_specs=specs,
        compiler_params=pltpu.CompilerParams(vmem_limit_bytes=VMEM_LIMIT),
        cost_estimate=pl.CostEstimate(
            flops=0, bytes_accessed=sum(6 * v.size for v in flat), transcendentals=0
        ),
        name="widen",
    )(*flat)
    return tuple(v.reshape(w.shape) for v, w in zip(out, arrays))


def gather_line_kernel(n, v_hbm, out, slots, load_sem, up_sem, down_sem, recv_sem, out_sem):
    d, z, peers = others(n)
    own_load = pltpu.make_async_copy(v_hbm, slots.at[z], load_sem.at[0])
    own_load.start()
    greet(peers)

    def send_up(o):
        return pltpu.make_async_remote_copy(
            src_ref=slots.at[o], dst_ref=slots.at[o], send_sem=up_sem.at[o],
            recv_sem=recv_sem.at[o], device_id=(d, lax.rem(z + 1, n)), device_id_type=MESH,
        )

    def send_down(o):
        return pltpu.make_async_remote_copy(
            src_ref=slots.at[o], dst_ref=slots.at[o], send_sem=down_sem.at[o],
            recv_sem=recv_sem.at[o], device_id=(d, lax.rem(z + n - 1, n)), device_id_type=MESH,
        )

    own_load.wait()

    @pl.when(z < n - 1)
    def _():
        send_up(z).start()

    @pl.when(z > 0)
    def _():
        send_down(z).start()

    C = slots.shape[2]

    def save(o):
        c = pl.ds(pl.multiple_of(o * C, C), C)
        return pltpu.make_async_copy(slots.at[o], out.at[:, c], out_sem.at[o])

    save(z).start()

    def step(s, carry):
        below, above = z - s, z + s

        @pl.when(below >= 0)
        def _():
            send_up(below).wait_recv()

            @pl.when(z < n - 1)
            def _():
                send_up(below).start()

            save(below).start()

        @pl.when(above < n)
        def _():
            send_down(above).wait_recv()

            @pl.when(z > 0)
            def _():
                send_down(above).start()

            save(above).start()

        return carry

    lax.fori_loop(1, n, step, 0)

    def finish(o, carry):
        save(o).wait()

        @pl.when((z < n - 1) & (o <= z))
        def _():
            send_up(o).wait_send()

        @pl.when((z > 0) & (o >= z))
        def _():
            send_down(o).wait_send()

        return carry

    lax.fori_loop(0, n, finish, 0)


def gather_line(n, v, collective_id):
    hbm = pl.BlockSpec(memory_space=pl.ANY)
    dma = pltpu.SemaphoreType.DMA
    return pl.pallas_call(
        functools.partial(gather_line_kernel, n),
        out_shape=jax.ShapeDtypeStruct((v.shape[0], n * v.shape[1]), v.dtype),
        in_specs=[hbm],
        out_specs=hbm,
        scratch_shapes=[
            pltpu.VMEM((n,) + v.shape, v.dtype), dma((1,)), dma((n,)), dma((n,)), dma((n,)),
            dma((n,)),
        ],
        compiler_params=pltpu.CompilerParams(
            collective_id=collective_id, has_side_effects=True, vmem_limit_bytes=VMEM_LIMIT
        ),
        cost_estimate=pl.CostEstimate(flops=70 * 10**9, bytes_accessed=8 * 2**20, transcendentals=0),
        name="gather_line",
    )(v)


def per_device(
    tokens,
    out_grad,
    routes,
    gate_weights,
    prefix,
    query_weight,
    key_weight,
    value_weight,
    output_weight,
    norm_gains,
    expert_gate,
    expert_up,
    expert_down,
):
    rows, width = tokens.shape
    shards = lax.axis_size("shard")
    groups = lax.axis_size("dp")
    place = lax.axis_index("shard")
    group = lax.axis_index("dp")
    length = rows * shards
    local = width // shards
    experts = expert_gate.shape[0]
    units = expert_gate.shape[2]

    expert_ids = jnp.arange(experts, dtype=jnp.int32)
    weight_own = jnp.sum(
        jnp.where(routes[:, :, None] == expert_ids[None, None, :], gate_weights[:, :, None], 0.0),
        axis=1,
    )
    own_gains = norm_gains.astype(f32)
    small = jnp.concatenate(
        [
            jnp.pad(weight_own.T, ((0, 8 - experts), (0, 0))),
            jnp.pad(jnp.stack([own_gains[0], own_gains[3]]), ((0, 6), (0, 0))),
        ],
        axis=1,
    )
    x_all_b, normed, query_raw, key_raw, values, out_slab, combine, gains, factors = (
        gather_project(
            shards, groups, tokens, small, output_weight, query_weight, key_weight, value_weight
        )
    )
    full_output = lax.all_gather(out_slab, "dp", axis=0, tiled=True)
    x_all_b = x_all_b.reshape(length, width)
    normed = normed.reshape(length, width)
    query_raw = query_raw.reshape(length, local)
    key_raw = key_raw.reshape(length, local)
    values = values.reshape(length, local)
    cosine, sine = rotary_tables(length)
    limit = jnp.broadcast_to(prefix.reshape(1, 1), (8, 128))
    few = rows // 4
    queries, keys, mixed_own, grad_first = attention(
        shards, limit, query_raw, key_raw, values, factors, cosine, sine, own_gains, out_grad, few
    )
    mixed_all = gather_line(shards, mixed_own, 1)
    grad_rest, mixed_all = lax.optimization_barrier((out_grad[few:], mixed_all))
    grad_rest = lax.all_gather(grad_rest, "shard", axis=0)
    attended, expert_turned, gate_by, up_by, hidden, sum_part, gate_t, up_t, down_t = forward_pass(
        mixed_all, full_output, x_all_b, gains, combine, expert_gate, expert_up, expert_down
    )
    attended_own = lax.dynamic_slice_in_dim(attended, place * rows, rows, 0)
    g_all, in_part, gate_grad, up_grad = backward_pass(
        grad_first, grad_rest, gate_by, up_by, gate_t, up_t, down_t
    )
    sum_parts = sum_part.reshape(shards, 16, rows // 16, width)
    grad_gate, grad_up = expert_grads(expert_turned, gate_grad, up_grad, experts)
    in_part, grad_gate, grad_up = lax.optimization_barrier((in_part, grad_gate, grad_up))
    grad_gate, grad_up = lax.psum((grad_gate, grad_up), "dp")

    x_own = tokens.astype(f32)
    residual_own = x_own + attended_own
    residual_grad, attended_grad, own_columns, gain_grad_res, grad_down = scatter_norm(
        shards, groups, 16, in_part, tokens, gains,
        more=(out_grad, attended, hidden, g_all, experts),
    )
    residual_grad = residual_grad.reshape(rows, width)
    attended_grad = attended_grad.reshape(length, width)

    grad_output = dot_tn(mixed_all, own_columns.reshape(length, local))
    grad_output, grad_down, grad_gate, grad_up, attended_grad = lax.optimization_barrier(
        (grad_output.astype(bf16), grad_down, grad_gate, grad_up, attended_grad)
    )
    grad_output, grad_down = lax.psum((grad_output, grad_down), "dp")
    grad_query, grad_key, grad_value, normed_part, gain_grad_heads, expert_sum = attention_back(
        shards, width, limit, queries, keys, values, query_raw, key_raw, factors, cosine, sine,
        own_gains, query_weight, key_weight, value_weight, normed, sum_parts, attended_grad,
        full_output,
    )
    expert_sum = expert_sum.reshape(rows, width)
    expert_sum, grad_gate, grad_up = lax.optimization_barrier((expert_sum, grad_gate, grad_up))
    grad_gate, grad_up = widen(grad_gate, grad_up)
    (
        grad_query, grad_key, grad_value, normed_part, grad_output, grad_down, grad_gate, grad_up,
    ) = lax.optimization_barrier(
        (
            grad_query, grad_key, grad_value, normed_part, grad_output, grad_down, grad_gate,
            grad_up,
        )
    )
    grad_query, grad_key, grad_value = lax.psum((grad_query, grad_key, grad_value), "dp")
    through_norm, grad_gains = scatter_norm(
        shards, groups, 16, normed_part, tokens, gains,
        other_gains=(gain_grad_res, gain_grad_heads),
    )
    through_norm, expert_sum = lax.optimization_barrier((through_norm, expert_sum))
    grad_tokens = residual_grad + through_norm.reshape(rows, width)
    grad_gains = grad_gains[:4]
    output = residual_own + expert_sum
    root_means = jnp.stack([root_mean(attended_own), root_mean(expert_sum), root_mean(output)])
    grad_down, grad_output = widen(grad_down, grad_output)
    grad_query, grad_key, grad_value = widen(grad_query, grad_key, grad_value)

    return (
        output.astype(bf16),
        grad_tokens,
        root_means,
        grad_query,
        grad_key,
        grad_value,
        grad_output,
        grad_gains,
        grad_gate,
        grad_up,
        grad_down,
    )


def solution(mesh):
    placed = (
        P(("dp", "shard"), None),
        P(("dp", "shard"), None),
        P(("dp", "shard"), None),
        P(("dp", "shard"), None),
        P("dp"),
        P(None, "shard"),
        P(None, "shard"),
        P(None, "shard"),
        P(None, "shard"),
        P(None, "shard"),
        P(None, None, "shard"),
        P(None, None, "shard"),
        P(None, "shard", None),
    )
    return jax.shard_map(
        per_device,
        mesh=mesh,
        in_specs=placed,
        out_specs=(
            P(("dp", "shard"), None),
            P(("dp", "shard"), None),
            P(None, ("dp", "shard")),
            P(None, "shard"),
            P(None, "shard"),
            P(None, "shard"),
            P(None, "shard"),
            P(None, "shard"),
            P(None, None, "shard"),
            P(None, None, "shard"),
            P(None, "shard", None),
        ),
        check_vma=False,
    )
```

```python
import functools

import jax
import jax.numpy as jnp
import numpy as np
from jax import lax
from jax.experimental import pallas as pl
from jax.experimental.pallas import tpu as pltpu
from jax.sharding import PartitionSpec as P

HEAD_DIM = 128
EPSILON = 1e-05
ROPE_BASE = 10000.0
MASKED = -1e30
VMEM_LIMIT = 60 * 2**20

f32 = jnp.float32
bf16 = jnp.bfloat16


def rotary_tables(row_count):
    half_dim = HEAD_DIM // 2
    inverse = ROPE_BASE ** (-np.arange(half_dim) / half_dim)
    angles = np.arange(row_count)[:, None] * inverse.astype(np.float32).astype(np.float64)[None, :]
    angles = angles.astype(np.float32).astype(np.float64)
    cosine, sine = np.cos(angles), np.sin(angles)
    return (
        jnp.asarray(np.concatenate([cosine, cosine], 1), f32),
        jnp.asarray(np.concatenate([-sine, sine], 1), f32),
    )


def row_factor(values):
    return lax.rsqrt(jnp.mean(values * values, axis=-1, keepdims=True) + EPSILON)


def norm_back(grad_unit, unit_rows, factor):
    return factor * (
        grad_unit - unit_rows * jnp.mean(grad_unit * unit_rows, axis=-1, keepdims=True)
    )


def root_mean(values):
    return jnp.sqrt(jnp.mean(values * values, axis=-1))


def dot(a, b):
    return jnp.dot(a, b, preferred_element_type=f32)


def dot_nt(a, b):
    return lax.dot_general(a, b, (((1,), (1,)), ((), ())), preferred_element_type=f32)


def dot_tn(a, b):
    return lax.dot_general(a, b, (((0,), (0,)), ((), ())), preferred_element_type=f32)


MESH = pl.DeviceIdType.MESH


def greet(peers):
    barrier = pltpu.get_barrier_semaphore()
    for peer in peers:
        pl.semaphore_signal(barrier, inc=1, device_id=peer, device_id_type=MESH)
    pl.semaphore_wait(barrier, len(peers))


def others(n):
    d, z = lax.axis_index("dp"), lax.axis_index("shard")
    return d, z, [(d, lax.rem(z + p, n)) for p in range(1, n)]


def line_gather(n, slots, up_sem, down_sem, recv_sem):
    d, z = lax.axis_index("dp"), lax.axis_index("shard")

    def send_up(o):
        return pltpu.make_async_remote_copy(
            src_ref=slots.at[o], dst_ref=slots.at[o], send_sem=up_sem.at[o],
            recv_sem=recv_sem.at[o], device_id=(d, lax.rem(z + 1, n)), device_id_type=MESH,
        )

    def send_down(o):
        return pltpu.make_async_remote_copy(
            src_ref=slots.at[o], dst_ref=slots.at[o], send_sem=down_sem.at[o],
            recv_sem=recv_sem.at[o], device_id=(d, lax.rem(z + n - 1, n)), device_id_type=MESH,
        )

    def begin():
        @pl.when(z < n - 1)
        def _():
            send_up(z).start()

        @pl.when(z > 0)
        def _():
            send_down(z).start()

    def hop(s, landed):
        below, above = z - s, z + s

        @pl.when((s > 0) & (below >= 0))
        def _():
            send_up(below).wait_recv()

            @pl.when(z < n - 1)
            def _():
                send_up(below).start()

            landed(below)

        @pl.when((s > 0) & (above < n))
        def _():
            send_down(above).wait_recv()

            @pl.when(z > 0)
            def _():
                send_down(above).start()

            landed(above)

    def drain():
        def one(o, carry):
            @pl.when((z < n - 1) & (o <= z))
            def _():
                send_up(o).wait_send()

            @pl.when((z > 0) & (o >= z))
            def _():
                send_down(o).wait_send()

            return carry

        lax.fori_loop(0, n, one, 0)

    return begin, hop, drain


def gather_project_kernel(
    n, x_hbm, small_ref, slab_hbm, wq_hbm, wk_hbm, wv_hbm,
    x_out, normed_out, q_out, k_out, v_out, slab_out, combine_out, gains_out, sq_out,
    slabs, xs, nb, qb, kb, vb, wq, wk, wv, sq_all, small_all,
    load_sem, out_sem, up_sem, down_sem, recv_sem, small_send, small_recv, sq_send, sq_recv,
    slab_up, slab_down, slab_recv, slab_sem,
):
    T, D = xs.shape[1:]
    C = qb.shape[2]
    d, z, peers = others(n)
    S = slabs.shape[1]
    slab_rows = pl.ds(pl.multiple_of(d * S, S), S)
    slab_load = pltpu.make_async_copy(slab_hbm.at[slab_rows, :], slabs.at[z], load_sem.at[4])
    slab_load.start()
    own_load = pltpu.make_async_copy(x_hbm, xs.at[z], load_sem.at[0])
    own_load.start()
    slab_begin, slab_hop, slab_drain = line_gather(n, slabs, slab_up, slab_down, slab_recv)

    def slab_save(o):
        c = pl.ds(pl.multiple_of(o * C, C), C)
        return pltpu.make_async_copy(slabs.at[o], slab_out.at[:, c], slab_sem.at[o])

    loads = [
        pltpu.make_async_copy(src, dst, load_sem.at[i + 1])
        for i, (src, dst) in enumerate(((wq_hbm, wq), (wk_hbm, wk), (wv_hbm, wv)))
    ]
    for load in loads:
        load.start()
    greet(peers)

    def send_up(o):
        return pltpu.make_async_remote_copy(
            src_ref=xs.at[o], dst_ref=xs.at[o], send_sem=up_sem.at[o], recv_sem=recv_sem.at[o],
            device_id=(d, lax.rem(z + 1, n)), device_id_type=MESH,
        )

    def send_down(o):
        return pltpu.make_async_remote_copy(
            src_ref=xs.at[o], dst_ref=xs.at[o], send_sem=down_sem.at[o], recv_sem=recv_sem.at[o],
            device_id=(d, lax.rem(z + n - 1, n)), device_id_type=MESH,
        )

    own_load.wait()
    small_copies = []
    for p, peer in enumerate(peers):
        copy = pltpu.make_async_remote_copy(
            src_ref=small_ref, dst_ref=small_all.at[z], send_sem=small_send.at[p],
            recv_sem=small_recv.at[z], device_id=peer, device_id_type=MESH,
        )
        copy.start()
        small_copies.append(copy)

    @pl.when(z < n - 1)
    def _():
        send_up(z).start()

    @pl.when(z > 0)
    def _():
        send_down(z).start()

    small_all[z] = small_ref[...]
    for load in loads:
        load.wait()
    for p in range(1, n):
        o = lax.rem(z + n - p, n)
        pltpu.make_async_remote_copy(
            src_ref=small_ref, dst_ref=small_all.at[o], send_sem=small_send.at[p - 1],
            recv_sem=small_recv.at[o], device_id=(d, o), device_id_type=MESH,
        ).wait_recv()

    lanes = lax.broadcasted_iota(jnp.int32, (T, 128), 1)
    step_rows = 32

    def outs(o):
        return [
            pltpu.make_async_copy(src.at[o], dst.at[o], out_sem.at[i, o])
            for i, (src, dst) in enumerate(
                ((xs, x_out), (nb, normed_out), (qb, q_out), (kb, k_out), (vb, v_out))
            )
        ]

    def compute(o):
        gain = jnp.concatenate([small_all[s, 0:1, T:] for s in range(n)], axis=1)

        def norm_rows(i, carry):
            r = pl.ds(pl.multiple_of(i * step_rows, step_rows), step_rows)
            x = xs[o, r, :].astype(f32)
            factor = lax.rsqrt(jnp.sum(x * x, axis=1, keepdims=True) / D + EPSILON)
            nb[o, r, :] = (x * factor * gain).astype(bf16)
            return carry

        lax.fori_loop(0, T // step_rows, norm_rows, 0)
        q = jnp.dot(nb[o], wq[...], preferred_element_type=f32)
        qb[o] = q
        q_sum = jnp.sum(q * q, axis=1, keepdims=True)
        k = jnp.dot(nb[o], wk[...], preferred_element_type=f32)
        kb[o] = k
        k_sum = jnp.sum(k * k, axis=1, keepdims=True)
        vb[o] = jnp.dot(nb[o], wv[...], preferred_element_type=f32).astype(bf16)
        both = jnp.where(lanes == 0, q_sum, jnp.where(lanes == 1, k_sum, 0.0))
        sq_all[z, o] = both.T[0:8]
        for copy in outs(o):
            copy.start()

    def step(s, carry):
        below, above = z - s, z + s

        @pl.when((s > 0) & (below >= 0))
        def _():
            send_up(below).wait_recv()

            @pl.when(z < n - 1)
            def _():
                send_up(below).start()

        @pl.when((s > 0) & (above < n))
        def _():
            send_down(above).wait_recv()

            @pl.when(z > 0)
            def _():
                send_down(above).start()

        @pl.when(s == n - 1)
        def _():
            slab_load.wait()
            slab_begin()
            slab_save(z).start()

        def side(j, inner):
            o = z - s + 2 * s * j

            @pl.when((o >= 0) & (o < n) & ((s > 0) | (j == 0)))
            def _():
                compute(o)

            return inner

        lax.fori_loop(0, 2, side, 0)
        return carry

    lax.fori_loop(0, n, step, 0)

    sq_copies = []
    for p, peer in enumerate(peers):
        copy = pltpu.make_async_remote_copy(
            src_ref=sq_all.at[z], dst_ref=sq_all.at[z], send_sem=sq_send.at[p],
            recv_sem=sq_recv.at[z], device_id=peer, device_id_type=MESH,
        )
        copy.start()
        sq_copies.append(copy)

    def slab_hops(s, carry):
        slab_hop(s, lambda o: slab_save(o).start())
        return carry

    lax.fori_loop(1, n, slab_hops, 0)

    def spread(o, carry):
        r = pl.ds(pl.multiple_of(o * T, T), T)
        tall = jnp.concatenate([small_all[o, :, 0:T], jnp.zeros((120, T), f32)], axis=0)
        combine_out[r, :] = tall.T
        return carry

    lax.fori_loop(0, n, spread, 0)
    for s in range(n):
        gains_out[:, s * C : (s + 1) * C] = small_all[s, :, T:]

    def finish(o, carry):
        for copy in outs(o):
            copy.wait()
        slab_save(o).wait()

        @pl.when((z < n - 1) & (o <= z))
        def _():
            send_up(o).wait_send()

        @pl.when((z > 0) & (o >= z))
        def _():
            send_down(o).wait_send()

        return carry

    lax.fori_loop(0, n, finish, 0)
    slab_drain()
    for p in range(1, n):
        o = lax.rem(z + n - p, n)
        pltpu.make_async_remote_copy(
            src_ref=sq_all.at[o], dst_ref=sq_all.at[o], send_sem=sq_send.at[p - 1],
            recv_sem=sq_recv.at[o], device_id=(d, o), device_id_type=MESH,
        ).wait_recv()
    def turn_factors(i, carry):
        total = sq_all[0, i]
        for s in range(1, n):
            total = total + sq_all[s, i]
        total = jnp.concatenate([total, jnp.zeros((120, T), f32)], axis=0).T
        r = pl.ds(pl.multiple_of(i * T, T), T)
        sq_out[r, :] = lax.rsqrt(total / D + EPSILON)
        return carry

    lax.fori_loop(0, n, turn_factors, 0)
    for copy in small_copies + sq_copies:
        copy.wait_send()


def gather_project(n, groups, tokens, small, wo, wq, wk, wv):
    T, D = tokens.shape
    C = wq.shape[1]
    S = D // groups
    hbm = pl.BlockSpec(memory_space=pl.ANY)
    vmem = pl.BlockSpec(memory_space=pltpu.VMEM)
    dma = pltpu.SemaphoreType.DMA
    return pl.pallas_call(
        functools.partial(gather_project_kernel, n),
        out_shape=[
            jax.ShapeDtypeStruct((n, T, D), bf16),
            jax.ShapeDtypeStruct((n, T, D), bf16),
            jax.ShapeDtypeStruct((n, T, C), f32),
            jax.ShapeDtypeStruct((n, T, C), f32),
            jax.ShapeDtypeStruct((n, T, C), bf16),
            jax.ShapeDtypeStruct((S, D), bf16),
            jax.ShapeDtypeStruct((n * T, 128), f32),
            jax.ShapeDtypeStruct((8, D), f32),
            jax.ShapeDtypeStruct((n * T, 128), f32),
        ],
        in_specs=[hbm, vmem, hbm, hbm, hbm, hbm],
        out_specs=[hbm] * 6 + [vmem] * 3,
        scratch_shapes=[
            pltpu.VMEM((n, S, C), bf16),
            pltpu.VMEM((n, T, D), bf16),
            pltpu.VMEM((n, T, D), bf16),
            pltpu.VMEM((n, T, C), f32),
            pltpu.VMEM((n, T, C), f32),
            pltpu.VMEM((n, T, C), bf16),
            pltpu.VMEM((D, C), bf16),
            pltpu.VMEM((D, C), bf16),
            pltpu.VMEM((D, C), bf16),
            pltpu.VMEM((n, n, 8, T), f32),
            pltpu.VMEM((n,) + small.shape, f32),
            dma((5,)),
            dma((5, n)),
            dma((n,)),
            dma((n,)),
            dma((n,)),
            dma((n,)),
            dma((n,)),
            dma((n,)),
            dma((n,)),
            dma((n,)),
            dma((n,)),
            dma((n,)),
            dma((n,)),
        ],
        compiler_params=pltpu.CompilerParams(
            collective_id=0, has_side_effects=True, vmem_limit_bytes=VMEM_LIMIT
        ),
        cost_estimate=pl.CostEstimate(flops=80 * 10**9, bytes_accessed=32 * 2**20, transcendentals=0),
        name="gather_project",
    )(tokens, small, wo, wq, wk, wv)


def rope(v, cosine, sine):
    return v * cosine + pltpu.roll(v, HEAD_DIM // 2, 1) * sine


def key_span(i, block, length):
    return min(length, max((i + 1) * block, length // 2))


def block_scores(q, k, i, block, limit):
    s = dot_nt(q, k) * (HEAD_DIM**-0.5)
    row = lax.broadcasted_iota(jnp.int32, s.shape, 0) + i * block
    col = lax.broadcasted_iota(jnp.int32, s.shape, 1)
    return jnp.where((col <= row) | (col < limit), s, MASKED)


def attention_kernel(
    n, limit_ref, q_raw, k_raw, v_ref, factors, cosine, sine, gains, grad_hbm,
    q_out, k_out, mixed, first_out, slots, load_sem, up_sem, down_sem, recv_sem, out_sem,
):
    length = q_raw.shape[0]
    block = 256
    limit = limit_ref[0:1, 0:1]
    h, heads = pl.program_id(0), pl.num_programs(0)
    begin, hop, drain = line_gather(n, slots, up_sem, down_sem, recv_sem)
    z = lax.axis_index("shard")

    def save(o):
        return pltpu.make_async_copy(slots.at[o], first_out.at[o], out_sem.at[o])

    few = slots.shape[1]

    @pl.when(h == 0)
    def _():
        load = pltpu.make_async_copy(grad_hbm.at[0:few], slots.at[z], load_sem.at[0])
        load.start()
        _, _, peers = others(n)
        greet(peers)
        load.wait()
        begin()
        save(z).start()

    def turn(raw, out, column, gain):
        def part(i, carry):
            r = pl.ds(pl.multiple_of(i * block, block), block)
            v = raw[r, :] * factors[r, column : column + 1] * gain
            out[r, :] = rope(v, cosine[r, :], sine[r, :]).astype(bf16)
            return carry

        lax.fori_loop(0, length // block, part, 0)

    turn(q_raw, q_out, 0, gains[1:2, :])
    turn(k_raw, k_out, 1, gains[2:3, :])
    for i in range(length // block):
        span = key_span(i, block, length)
        r = pl.ds(i * block, block)
        s = block_scores(q_out[r, :], k_out[0:span, :], i, block, limit)
        e = jnp.exp(s - jnp.max(s, axis=1, keepdims=True))
        total = jnp.sum(e, axis=1, keepdims=True)
        mixed[r, :] = (dot(e.astype(bf16), v_ref[0:span, :]) / total).astype(bf16)

    def hops(s, carry):
        hop(s, lambda o: save(o).start())
        return carry

    lax.fori_loop(1 + h * (n - 1) // heads, 1 + (h + 1) * (n - 1) // heads, hops, 0)

    @pl.when(h == heads - 1)
    def _():
        drain()

        def finish(o, carry):
            save(o).wait()
            return carry

        lax.fori_loop(0, n, finish, 0)


def attention(n, limit, q_raw, k_raw, values, factors, cosine, sine, gains, grad, few):
    length, local = q_raw.shape
    heads = local // HEAD_DIM
    head = pl.BlockSpec((length, HEAD_DIM), lambda h: (0, h))
    whole = lambda a: pl.BlockSpec(a.shape, lambda h: (0, 0))
    hbm = pl.BlockSpec(memory_space=pl.ANY)
    out = jax.ShapeDtypeStruct((length, local), bf16)
    dma = pltpu.SemaphoreType.DMA
    return pl.pallas_call(
        functools.partial(attention_kernel, n),
        out_shape=[out] * 3
        + [jax.ShapeDtypeStruct((n, few, grad.shape[1]), bf16)],
        grid=(heads,),
        in_specs=[
            whole(limit), head, head, head, whole(factors), whole(cosine), whole(sine),
            pl.BlockSpec((gains.shape[0], HEAD_DIM), lambda h: (0, h)), hbm,
        ],
        out_specs=[head] * 3 + [hbm],
        scratch_shapes=[pltpu.VMEM((n, few, grad.shape[1]), bf16), dma((1,))] + [dma((n,))] * 4,
        compiler_params=pltpu.CompilerParams(
            collective_id=7, has_side_effects=True, vmem_limit_bytes=VMEM_LIMIT
        ),
        cost_estimate=pl.CostEstimate(
            flops=20 * 10**9, bytes_accessed=16 * 2**20, transcendentals=0
        ),
        name="attention",
    )(limit, q_raw, k_raw, values, factors, cosine, sine, gains, grad)


def attention_back_kernel(
    n, steps, width, limit_ref, q_ref, k_ref, v_ref, q_raw, k_raw, factors, cosine, sine,
    gains, wq, wk, wv, normed_hbm, sum_hbm, grad_hbm, output_hbm, gq_out, gk_out, gv_out, normed_out, gain_out, own_sum,
    g_ref, output, dq_acc, dk_acc, k_acc, v_acc, q_grad, k_grad, v_grad, columns, turned, staged,
    inner_all, inner_send, inner_recv, column_sem, staged_sem, grad_sem, part, *line,
):
    length, local = q_ref.shape
    strips = width // local
    heads = local // HEAD_DIM
    block = 256
    blocks = length // block
    scale = HEAD_DIM**-0.5
    load_sem = line[-1]
    turn, drain = line_sum(n, steps, part, own_sum, *line[:-1])
    d, z, peers = others(n)
    load = pltpu.make_async_copy(sum_hbm, part, load_sem.at[0])
    load.start()

    def grad_rows(i):
        r = pl.ds(pl.multiple_of(i * block, block), block)
        return pltpu.make_async_copy(
            grad_hbm.at[r, :], staged.at[lax.rem(i, 2)], grad_sem.at[lax.rem(i, 2)]
        )

    own_rows = pl.ds(pl.multiple_of(z * local, local), local)
    output_load = pltpu.make_async_copy(output_hbm.at[own_rows, :], output, grad_sem.at[2])
    output_load.start()
    grad_rows(0).start()
    greet(peers)

    def strip(b):
        c = pl.ds(pl.multiple_of(b * local, local), local)
        return pltpu.make_async_copy(
            normed_hbm.at[:, c], columns.at[lax.rem(b, 2)], column_sem.at[lax.rem(b, 2)]
        )

    strip(0).start()
    load.wait()
    turns = steps + n - 1
    in_heads, in_parts = 8 * turns // 19, 4 * turns // 19
    slots = -(-in_heads // heads)
    past = 1 + heads * slots
    in_strips = turns - past - in_parts - 2

    def take(first, count, i, of):
        def one(t, carry):
            turn(first + t)
            return carry

        lax.fori_loop(i * count // of, (i + 1) * count // of, one, 0)
    limit = limit_ref[0:1, 0:1]
    lanes = lax.broadcasted_iota(jnp.int32, (block, 128), 1)

    def clear(i, carry):
        inner_all[z, i] = jnp.zeros((8, block), f32)
        return carry

    lax.fori_loop(0, blocks, clear, 0)

    turn(0)
    output_load.wait()

    def mixed_rows(i, carry):
        r = pl.ds(pl.multiple_of(i * block, block), block)
        grad_rows(i).wait()

        @pl.when(i + 1 < blocks)
        def _():
            grad_rows(i + 1).start()

        g_ref[r, :] = dot_nt(staged[lax.rem(i, 2)], output[...]).astype(bf16)
        return carry

    lax.fori_loop(0, blocks, mixed_rows, 0)

    def head(h, carry):
        c = pl.ds(pl.multiple_of(h * HEAD_DIM, HEAD_DIM), HEAD_DIM)
        k_acc[...] = jnp.zeros_like(k_acc)
        v_acc[...] = jnp.zeros_like(v_acc)
        for i in range(blocks):
            for j in range(i * slots // blocks, (i + 1) * slots // blocks):
                turn(1 + h * slots + j)
            span = key_span(i, block, length)
            r = pl.ds(i * block, block)
            q, g, k, v = q_ref[r, c], g_ref[r, c], k_ref[0:span, c], v_ref[0:span, c]
            s = block_scores(q, k, i, block, limit)
            e = jnp.exp(s - jnp.max(s, axis=1, keepdims=True))
            p = e * (1.0 / jnp.sum(e, axis=1, keepdims=True))
            t = p * dot_nt(g, v)
            ds = (t - p * jnp.sum(t, axis=1, keepdims=True)).astype(bf16)
            dq_acc[r, c] = dot(ds, k) * scale
            k_acc[0:span, :] += dot_tn(ds, q) * scale
            v_acc[0:span, :] += dot_tn(p.astype(bf16), g)
        v_grad[:, c] = v_acc[...].astype(bf16)
        gain_q, gain_k = gains[1:2, c], gains[2:3, c]

        def back(i, carry):
            gq, gk = carry
            r = pl.ds(pl.multiple_of(i * block, block), block)
            cos, sin = cosine[r, :], sine[r, :]
            dq = rope(dq_acc[r, c], cos, -sin)
            dk = rope(k_acc[r, :], cos, -sin)
            uq = q_raw[r, c] * factors[r, 0:1]
            uk = k_raw[r, c] * factors[r, 1:2]
            gq = gq + jnp.sum(dq * uq, axis=0, keepdims=True)
            gk = gk + jnp.sum(dk * uk, axis=0, keepdims=True)
            dq = dq * gain_q
            dk = dk * gain_k
            dq_acc[r, c] = dq
            dk_acc[r, c] = dk
            inner_q = jnp.sum(dq * uq, axis=1, keepdims=True)
            inner_k = jnp.sum(dk * uk, axis=1, keepdims=True)
            both = jnp.where(lanes == 0, inner_q, jnp.where(lanes == 1, inner_k, 0.0))
            inner_all[z, i] += both.T[0:8]
            return gq, gk

        zero = jnp.zeros((1, HEAD_DIM), f32)
        gq, gk = lax.fori_loop(0, blocks, back, (zero, zero))
        gain_out[0:1, c] = gq
        gain_out[1:2, c] = gk
        return carry

    lax.fori_loop(0, heads, head, 0)

    copies = []
    for p, peer in enumerate(peers):
        copy = pltpu.make_async_remote_copy(
            src_ref=inner_all.at[z], dst_ref=inner_all.at[z], send_sem=inner_send.at[p],
            recv_sem=inner_recv.at[z], device_id=peer, device_id_type=MESH,
        )
        copy.start()
        copies.append(copy)
    turn(past)
    for p in range(1, n):
        o = lax.rem(z + n - p, n)
        pltpu.make_async_remote_copy(
            src_ref=inner_all.at[o], dst_ref=inner_all.at[o], send_sem=inner_send.at[p - 1],
            recv_sem=inner_recv.at[o], device_id=(d, o), device_id_type=MESH,
        ).wait_recv()

    def raw(i, carry):
        r = pl.ds(pl.multiple_of(i * block, block), block)
        total = inner_all[0, i]
        for s in range(1, n):
            total = total + inner_all[s, i]
        total = jnp.concatenate([total, jnp.zeros((120, block), f32)], axis=0).T
        fq, fk = factors[r, 0:1], factors[r, 1:2]
        mean_q, mean_k = total[:, 0:1] / width, total[:, 1:2] / width
        q_grad[r, :] = (fq * (dq_acc[r, :] - q_raw[r, :] * (fq * mean_q))).astype(bf16)
        k_grad[r, :] = (fk * (dk_acc[r, :] - k_raw[r, :] * (fk * mean_k))).astype(bf16)
        return carry

    lax.fori_loop(0, blocks, raw, 0)
    turn(past + 1)

    def save(i):
        r = pl.ds(pl.multiple_of(i * block, block), block)
        return pltpu.make_async_copy(
            staged.at[lax.rem(i, 2)], normed_out.at[r, :], staged_sem.at[lax.rem(i, 2)]
        )

    def rows_back(i, carry):
        r = pl.ds(pl.multiple_of(i * block, block), block)

        @pl.when(i >= 2)
        def _():
            save(i - 2).wait()

        staged[lax.rem(i, 2)] = (
            dot_nt(q_grad[r, :], wq[...])
            + dot_nt(k_grad[r, :], wk[...])
            + dot_nt(v_grad[r, :], wv[...])
        ).astype(bf16)
        save(i).start()
        take(past + 2, in_parts, i, blocks)
        return carry

    lax.fori_loop(0, blocks, rows_back, 0)

    def strip_grads(b, carry):
        strip(b).wait()

        @pl.when(b + 1 < strips)
        def _():
            strip(b + 1).start()

        turned[...] = columns[lax.rem(b, 2)].T
        c = pl.ds(pl.multiple_of(b * local, local), local)
        gq_out[c, :] = dot(turned[...], q_grad[...]).astype(bf16)
        gk_out[c, :] = dot(turned[...], k_grad[...]).astype(bf16)
        gv_out[c, :] = dot(turned[...], v_grad[...]).astype(bf16)
        take(past + 2 + in_parts, in_strips, b, strips)
        return carry

    lax.fori_loop(0, strips, strip_grads, 0)
    drain()
    for i in range(max(blocks - 2, 0), blocks):
        save(i).wait()
    for copy in copies:
        copy.wait_send()


def attention_back(
    n, width, limit, q, k, v, q_raw, k_raw, factors, cosine, sine, gains, wq, wk, wv, normed,
    sum_parts, attended_grad, full_output,
):
    length, local = q.shape
    _, steps, R, D = sum_parts.shape
    hbm = pl.BlockSpec(memory_space=pl.ANY)
    vmem = pl.BlockSpec(memory_space=pltpu.VMEM)
    dma = pltpu.SemaphoreType.DMA
    weight = jax.ShapeDtypeStruct((D, local), bf16)
    raw = pltpu.VMEM((length, local), bf16)
    return pl.pallas_call(
        functools.partial(attention_back_kernel, n, steps, width),
        out_shape=[
            weight, weight, weight, jax.ShapeDtypeStruct((length, D), bf16),
            jax.ShapeDtypeStruct((2, local), f32),
            jax.ShapeDtypeStruct((steps, R, D), f32),
        ],
        in_specs=[vmem] * 13 + [hbm] * 4,
        out_specs=[vmem, vmem, vmem, hbm, vmem, vmem],
        scratch_shapes=[
            raw,
            pltpu.VMEM((local, D), bf16),
            pltpu.VMEM((length, local), f32),
            pltpu.VMEM((length, local), f32),
            pltpu.VMEM((length, HEAD_DIM), f32),
            pltpu.VMEM((length, HEAD_DIM), f32),
            raw,
            raw,
            raw,
            pltpu.VMEM((2, length, local), bf16),
            pltpu.VMEM((local, length), bf16),
            pltpu.VMEM((2, 256, D), bf16),
            pltpu.VMEM((n, length // 256, 8, 256), f32),
            dma((n,)),
            dma((n,)),
            dma((2,)),
            dma((2,)),
            dma((3,)),
        ]
        + line_scratch(n, steps, R, D),
        compiler_params=pltpu.CompilerParams(
            collective_id=6, has_side_effects=True, vmem_limit_bytes=VMEM_LIMIT
        ),
        cost_estimate=pl.CostEstimate(
            flops=2 * 10**9, bytes_accessed=2**20, transcendentals=0
        ),
        name="attention_back",
    )(
        limit, q, k, v, q_raw, k_raw, factors, cosine, sine, gains, wq, wk, wv, normed, sum_parts,
        attended_grad, full_output,
    )


def scatter_norm_kernel(n, groups, steps, gather, *refs):
    part_hbm, base, gain = refs[:3]
    part, part_sem = refs[-2:]
    refs = refs[3:-2]
    steps_first = 2
    part_loads = [
        pltpu.make_async_copy(part_hbm.at[:, c], part.at[:, c], part_sem.at[i])
        for i, c in enumerate((slice(0, steps_first), slice(steps_first, steps)))
    ]
    for part_load in part_loads:
        part_load.start()
    if gather:
        addend, attended_hbm, hidden_hbm, g_hbm = refs[:4]
        out, all_out, columns_out, gain_out, down_out = refs[4:9]
        alls, ag_up, ag_down, ag_recv, all_sem, attended, load_sem = refs[9:16]
        hidden, g_all, down, down_sem = refs[16:20]
        refs = refs[20:]
        later_loads = [
            pltpu.make_async_copy(hidden_hbm, hidden, load_sem.at[1]),
            pltpu.make_async_copy(g_hbm, g_all, load_sem.at[2]),
        ]

        def down_save(e):
            return pltpu.make_async_copy(down.at[e], down_out.at[e], down_sem.at[e])
    else:
        expert_gains, head_gains, out, gain_out = refs[:4]
        pieces, landed, sums, piece_send, piece_recv, sum_send, sum_recv = refs[4:11]
        refs = refs[11:]
    from_below, from_above, gain_acc, up_send, up_recv, down_send, down_recv = refs
    R, D = part.shape[2:]
    d, z, peers = others(n)
    upper, lower = (d, lax.rem(z + 1, n)), (d, lax.rem(z + n - 1, n))
    alike = [] if gather else [(lax.rem(d + p, groups), z) for p in range(1, groups)]
    if gather:
        load = pltpu.make_async_copy(attended_hbm.at[z], attended, load_sem.at[0])
        load.start()
    greet(peers + alike)
    if gather:
        load.wait()
        for later_load in later_loads:
            later_load.start()
    part_loads[0].wait()
    gain_acc[...] = jnp.zeros_like(gain_acc)

    def move_up(src, o, k):
        return pltpu.make_async_remote_copy(
            src_ref=src.at[o, k], dst_ref=from_below.at[o, k], send_sem=up_send.at[o, k],
            recv_sem=up_recv.at[o, k], device_id=upper, device_id_type=MESH,
        )

    def move_down(src, o, k):
        return pltpu.make_async_remote_copy(
            src_ref=src.at[o, k], dst_ref=from_above.at[o, k], send_sem=down_send.at[o, k],
            recv_sem=down_recv.at[o, k], device_id=lower, device_id_type=MESH,
        )

    def all_up(o, k):
        return pltpu.make_async_remote_copy(
            src_ref=alls.at[o, k], dst_ref=alls.at[o, k], send_sem=ag_up.at[o, k],
            recv_sem=ag_recv.at[o, k], device_id=upper, device_id_type=MESH,
        )

    def all_down(o, k):
        return pltpu.make_async_remote_copy(
            src_ref=alls.at[o, k], dst_ref=alls.at[o, k], send_sem=ag_down.at[o, k],
            recv_sem=ag_recv.at[o, k], device_id=lower, device_id_type=MESH,
        )

    def pass_up(k):
        def far(i, carry):
            o = z + n - 1 - i

            @pl.when(o < n)
            def _():
                @pl.when(z == 0)
                def _():
                    move_up(part, o, k).start()

                @pl.when(z > 0)
                def _():
                    move_up(part, o, k).wait_recv()
                    both = from_below[o, k].astype(f32) + part[o, k].astype(f32)
                    from_below[o, k] = both.astype(bf16)
                    move_up(from_below, o, k).start()

            return carry

        lax.fori_loop(0, n - 1, far, 0)

    def pass_down(k):
        def far(i, carry):
            o = z - n + 1 + i

            @pl.when(o >= 0)
            def _():
                @pl.when(z == n - 1)
                def _():
                    move_down(part, o, k).start()

                @pl.when(z < n - 1)
                def _():
                    move_down(part, o, k).wait_recv()
                    both = from_above[o, k].astype(f32) + part[o, k].astype(f32)
                    from_above[o, k] = both.astype(bf16)
                    move_down(from_above, o, k).start()

            return carry

        lax.fori_loop(0, n - 1, far, 0)

    def own(k):
        @pl.when(z > 0)
        def _():
            move_up(part, z, k).wait_recv()

        @pl.when(z == 0)
        def _():
            from_below[z, k] = jnp.zeros((R, D), bf16)

        @pl.when(z < n - 1)
        def _():
            move_down(part, z, k).wait_recv()

        @pl.when(z == n - 1)
        def _():
            from_above[z, k] = jnp.zeros((R, D), bf16)

        total = (
            part[z, k].astype(f32) + from_below[z, k].astype(f32) + from_above[z, k].astype(f32)
        )
        rows = base[k].astype(f32)
        if gather:
            rows = rows + attended[k]
        factor = lax.rsqrt(jnp.sum(rows * rows, axis=1, keepdims=True) / D + EPSILON)
        unit = rows * factor
        along = total * unit
        gain_acc[...] += jnp.sum(along.reshape(R // 8, 8, D), axis=0)
        weights = gain[1:2, :] if gather else gain[0:1, :]
        weighted = along * weights
        mean = jnp.sum(weighted, axis=1, keepdims=True) / D
        result = factor * (total * weights - unit * mean)
        if gather:
            result = result + addend[k].astype(f32)
        out[k] = result
        if gather:
            alls[z, k] = result.astype(bf16)

            @pl.when(z < n - 1)
            def _():
                all_up(z, k).start()

            @pl.when(z > 0)
            def _():
                all_down(z, k).start()

    def forward(own_k):
        def hop(s, carry):
            below, above, k = z - s, z + s, own_k - s
            live = (k >= 0) & (k < steps)

            @pl.when(live & (below >= 0))
            def _():
                all_up(below, k).wait_recv()

                @pl.when(z < n - 1)
                def _():
                    all_up(below, k).start()

            @pl.when(live & (above < n))
            def _():
                all_down(above, k).wait_recv()

                @pl.when(z > 0)
                def _():
                    all_down(above, k).start()

            return carry

        lax.fori_loop(1, n, hop, 0)

    def turn(t, carry):
        up_k, down_k, own_k = t - z, t - (n - 1 - z), t - (n - 1)

        @pl.when(t == steps_first)
        def _():
            part_loads[1].wait()

        @pl.when((up_k >= 0) & (up_k < steps))
        def _():
            pass_up(up_k)

        @pl.when((down_k >= 0) & (down_k < steps))
        def _():
            pass_down(down_k)

        @pl.when((own_k >= 0) & (own_k < steps))
        def _():
            own(own_k)

        if gather:
            forward(own_k)
            experts, units = down.shape[:2]
            e = t - n

            @pl.when(e == 0)
            def _():
                for later_load in later_loads:
                    later_load.wait()

            @pl.when((e >= 0) & (e < experts))
            def _():
                c = pl.ds(pl.multiple_of(e * units, units), units)
                down[e] = dot_tn(hidden[:, c], g_all[...]).astype(bf16)
                down_save(e).start()

        return carry

    lax.fori_loop(0, steps + (2 * n - 2 if gather else n - 1), turn, 0)
    if gather:
        gain_out[...] = gain_acc[...]
    else:
        C = D // n
        for s in range(n):
            c = slice(s * C, (s + 1) * C)
            pieces[s, 0:1] = jnp.sum(gain_acc[:, c], axis=0, keepdims=True)
            pieces[s, 1:2] = jnp.sum(expert_gains[:, c], axis=0, keepdims=True)
            pieces[s, 2:8] = jnp.zeros((6, C), f32)

        def piece(p):
            o = lax.rem(z + p, n)
            return pltpu.make_async_remote_copy(
                src_ref=pieces.at[o], dst_ref=landed.at[z], send_sem=piece_send.at[p - 1],
                recv_sem=piece_recv.at[z], device_id=(d, o), device_id_type=MESH,
            )

        for p in range(1, n):
            piece(p).start()
        landed[z] = pieces[z]
        for p in range(1, n):
            o = lax.rem(z + n - p, n)
            pltpu.make_async_remote_copy(
                src_ref=pieces.at[o], dst_ref=landed.at[o], send_sem=piece_send.at[p - 1],
                recv_sem=piece_recv.at[o], device_id=(d, o), device_id_type=MESH,
            ).wait_recv()
        two = landed[0]
        for s in range(1, n):
            two = two + landed[s]
        sums[d, 0:1] = two[0:1]
        sums[d, 1:3] = head_gains[...]
        sums[d, 3:4] = two[1:2]
        sums[d, 4:8] = jnp.zeros((4, C), f32)
        for p in range(1, groups):
            pltpu.make_async_remote_copy(
                src_ref=sums.at[d], dst_ref=sums.at[d], send_sem=sum_send.at[p - 1],
                recv_sem=sum_recv.at[d], device_id=alike[p - 1], device_id_type=MESH,
            ).start()
        for p in range(1, groups):
            o = lax.rem(d + groups - p, groups)
            pltpu.make_async_remote_copy(
                src_ref=sums.at[o], dst_ref=sums.at[o], send_sem=sum_send.at[p - 1],
                recv_sem=sum_recv.at[o], device_id=(o, z), device_id_type=MESH,
            ).wait_recv()
        total = sums[0]
        for s in range(1, groups):
            total = total + sums[s]
        gain_out[...] = total
        for p in range(1, n):
            piece(p).wait_send()
        for p in range(1, groups):
            pltpu.make_async_remote_copy(
                src_ref=sums.at[d], dst_ref=sums.at[d], send_sem=sum_send.at[p - 1],
                recv_sem=sum_recv.at[d], device_id=alike[p - 1], device_id_type=MESH,
            ).wait_send()

    def drain(i, carry):
        o, k = i // steps, i % steps

        @pl.when(o > z)
        def _():
            move_up(part, o, k).wait_send()

        @pl.when(o < z)
        def _():
            move_down(part, o, k).wait_send()

        if gather:

            @pl.when((z < n - 1) & (o <= z))
            def _():
                all_up(o, k).wait_send()

            @pl.when((z > 0) & (o >= z))
            def _():
                all_down(o, k).wait_send()

        return carry

    lax.fori_loop(0, n * steps, drain, 0)
    if gather:
        C = D // n
        c = pl.ds(pl.multiple_of(z * C, C), C)
        copies = []
        for o in range(n):
            own_columns = alls.at[o, :, :, c]
            copies.append(
                pltpu.make_async_copy(own_columns, columns_out.at[o], all_sem.at[n + o])
            )
            copies.append(pltpu.make_async_copy(alls.at[o], all_out.at[o], all_sem.at[o]))
        for copy in copies:
            copy.start()
        for e in range(down.shape[0]):
            down_save(e).wait()
        for copy in copies:
            copy.wait()


def scatter_norm(n, groups, steps, part, base, gain, more=None, other_gains=None):
    gather = more is not None
    T, D = base.shape
    R = T // steps
    C = D // n
    hbm = pl.BlockSpec(memory_space=pl.ANY)
    vmem = pl.BlockSpec(memory_space=pltpu.VMEM)
    dma = pltpu.SemaphoreType.DMA
    slots = pltpu.VMEM((n, steps, R, D), bf16)
    rows = jax.ShapeDtypeStruct((steps, R, D), f32)
    sems = dma((n, steps))
    if gather:
        addend, attended, hidden, g_all, experts = more
        units = hidden.shape[1] // experts
        more = (
            addend.reshape(steps, R, D), attended.reshape(n, steps, R, D), hidden, g_all,
        )
        own = [slots, sems, sems, sems, dma((2 * n,)), pltpu.VMEM((steps, R, D), f32), dma((3,))]
        own += [pltpu.VMEM(hidden.shape, bf16), pltpu.VMEM(g_all.shape, bf16)]
        own += [pltpu.VMEM((experts, units, D), bf16), dma((experts,))]
        outs = [rows, jax.ShapeDtypeStruct((n, steps, R, D), bf16)]
        outs += [jax.ShapeDtypeStruct((n, steps, R, C), bf16)]
        outs += [jax.ShapeDtypeStruct((8, D), f32)]
        outs += [jax.ShapeDtypeStruct((experts, units, D), bf16)]
    else:
        own = [
            pltpu.VMEM((n, 8, C), f32), pltpu.VMEM((n, 8, C), f32),
            pltpu.VMEM((groups, 8, C), f32), dma((n,)), dma((n,)), dma((groups,)), dma((groups,)),
        ]
        outs = [rows, jax.ShapeDtypeStruct((8, C), f32)]
    return pl.pallas_call(
        functools.partial(scatter_norm_kernel, n, groups, steps, gather),
        out_shape=outs,
        in_specs=[hbm] + ([vmem] * 3 + [hbm] * 3 if gather else [vmem] * 4),
        out_specs=[vmem, hbm, hbm, vmem, hbm] if gather else [vmem, vmem],
        scratch_shapes=own
        + [slots, slots, pltpu.VMEM((8, D), f32), sems, sems, sems, sems, slots, dma((2,))],
        compiler_params=pltpu.CompilerParams(
            collective_id=2 if gather else 3, has_side_effects=True, vmem_limit_bytes=VMEM_LIMIT
        ),
        cost_estimate=pl.CostEstimate(
            flops=10**9, bytes_accessed=2**20, transcendentals=0
        ),
        name="scatter_norm_gather" if gather else "scatter_norm",
    )(
        part.reshape(n, steps, R, D),
        base.reshape(steps, R, D),
        gain,
        *(more if gather else other_gains),
    )


def forward_kernel(
    mixed, weight, x_ref, gain, combine, gate_w, up_w, down_w,
    attended_out, turned_out, gate_out, up_out, hidden_out, sum_out, gate_t, up_t, down_t,
    in_out, units,
):
    e = pl.program_id(1)
    last = pl.num_programs(1) - 1
    D = in_out.shape[1]
    F = hidden_out.shape[1]

    @pl.when(e == 0)
    def _():
        attended_out[...] = dot(mixed[...], weight[...])
        part = 32

        def rows(i, carry):
            r = pl.ds(pl.multiple_of(i * part, part), part)
            v = attended_out[r, :] + x_ref[r, :].astype(f32)
            factor = lax.rsqrt(jnp.sum(v * v, axis=1, keepdims=True) / D + EPSILON)
            in_out[r, :] = (v * factor * gain[1:2, :]).astype(bf16)
            return carry

        lax.fori_loop(0, in_out.shape[0] // part, rows, 0)
        turned_out[...] = in_out[...].T

    lane = lax.broadcasted_iota(jnp.int32, combine.shape, 1)
    share = jnp.sum(jnp.where(lane == e, combine[...], 0.0), axis=1, keepdims=True)
    @pl.when(pl.program_id(0) == 0)
    def _():
        gate_t[0] = gate_w[0].T
        up_t[0] = up_w[0].T
        down_t[0] = down_w[pl.ds(pl.multiple_of(e * F, F), F), :].T

    gate_part = dot(in_out[...], gate_w[0])
    up_part = dot(in_out[...], up_w[0])
    sig = jax.nn.sigmoid(gate_part)
    silu = gate_part * sig * share
    gate_out[...] = up_part * sig * (1.0 + gate_part * (1.0 - sig)) * share
    up_out[...] = silu
    hidden = (silu * up_part).astype(bf16)
    hidden_out[...] = hidden
    units[:, pl.ds(pl.multiple_of(e * F, F), F)] = hidden

    @pl.when(e == last)
    def _():
        sum_out[...] = dot(units[...], down_w[...]).astype(bf16)


def forward_pass(mixed, weight, x, gain, combine, gate_w, up_w, down_w):
    L, D = x.shape
    E, _, F = gate_w.shape
    block = min(512, L)
    rows = pl.BlockSpec((block, D), lambda i, e: (i, 0))
    held = pl.BlockSpec((block, D), lambda i, e: (i, 0), pipeline_mode=pl.Buffered(1))
    units = pl.BlockSpec((block, F), lambda i, e: (i, e))
    column = pl.BlockSpec((1, D, F), lambda i, e: (e, 0, 0))
    once = pl.Buffered(1)
    turned = pl.BlockSpec((1, F, D), lambda i, e: (jnp.where(i == 0, e, E - 1), 0, 0))
    turned_down = pl.BlockSpec((1, D, F), lambda i, e: (jnp.where(i == 0, e, E - 1), 0, 0))
    return pl.pallas_call(
        forward_kernel,
        out_shape=[
            jax.ShapeDtypeStruct((L, D), f32),
            jax.ShapeDtypeStruct((D, L), bf16),
            jax.ShapeDtypeStruct((L, E * F), f32),
            jax.ShapeDtypeStruct((L, E * F), f32),
            jax.ShapeDtypeStruct((L, E * F), bf16),
            jax.ShapeDtypeStruct((L, D), bf16),
            jax.ShapeDtypeStruct((E, F, D), bf16),
            jax.ShapeDtypeStruct((E, F, D), bf16),
            jax.ShapeDtypeStruct((E, D, F), bf16),
        ],
        grid=(L // block, E),
        in_specs=[
            held,
            pl.BlockSpec((D, D), lambda i, e: (0, 0), pipeline_mode=once),
            held,
            pl.BlockSpec((8, D), lambda i, e: (0, 0)),
            pl.BlockSpec((block, combine.shape[1]), lambda i, e: (i, 0)),
            column, column,
            pl.BlockSpec((E * F, D), lambda i, e: (0, 0), pipeline_mode=once),
        ],
        out_specs=[
            rows, pl.BlockSpec((D, block), lambda i, e: (0, i)), units, units, units, rows, turned,
            turned, turned_down,
        ],
        scratch_shapes=[pltpu.VMEM((block, D), bf16), pltpu.VMEM((block, E * F), bf16)],
        compiler_params=pltpu.CompilerParams(vmem_limit_bytes=VMEM_LIMIT),
        cost_estimate=pl.CostEstimate(
            flops=6 * L * D * E * F + 2 * L * D * D, bytes_accessed=50 * 2**20,
            transcendentals=L * E * F,
        ),
        name="forward_pass",
    )(mixed, weight, x, gain, combine, gate_w, up_w, down_w.reshape(E * F, D))


def backward_kernel(
    first, rest, gate_ref, up_ref, gate_hbm, up_hbm, down_t,
    g_out, in_out, gate_out, up_out, both, turned, load_sem,
):
    i, e = pl.program_id(0), pl.program_id(1)
    last = pl.num_programs(1) - 1
    F = gate_out.shape[1]
    half = turned.shape[0] // 2
    loads = [
        pltpu.make_async_copy(gate_hbm, turned.at[0:half], load_sem.at[0]),
        pltpu.make_async_copy(up_hbm, turned.at[half : 2 * half], load_sem.at[1]),
    ]

    @pl.when((i == 0) & (e == 0))
    def _():
        for load in loads:
            load.start()

    @pl.when(e == 0)
    def _():
        few, many = first.shape[1], rest.shape[1]
        for j in range(first.shape[0]):
            top = j * (few + many)
            g_out[top : top + few, :] = first[j]
            g_out[top + few : top + few + many, :] = rest[j]

    hidden_grad = dot(g_out[...], down_t[0])
    gate_grad = (hidden_grad * gate_ref[...]).astype(bf16)
    gate_out[...] = gate_grad
    both[:, pl.ds(pl.multiple_of(e * F, F), F)] = gate_grad
    up_grad = (hidden_grad * up_ref[...]).astype(bf16)
    up_out[...] = up_grad
    both[:, pl.ds(pl.multiple_of(half + e * F, F), F)] = up_grad

    @pl.when((i == 0) & (e == last))
    def _():
        for load in loads:
            load.wait()

    @pl.when(e == last)
    def _():
        in_out[...] = dot(both[...], turned[...]).astype(bf16)


def backward_pass(first, rest, gate_by, up_by, gate_t, up_t, down_t):
    n, few, D = first.shape
    T = few + rest.shape[1]
    L = n * T
    E, F, _ = gate_t.shape
    block = max(T, min(512, L))
    owners = block // T
    rows = pl.BlockSpec((block, D), lambda i, e: (i, 0))
    units = pl.BlockSpec((block, F), lambda i, e: (i, e))
    hbm = pl.BlockSpec(memory_space=pl.ANY)
    wide = jax.ShapeDtypeStruct((L, D), bf16)
    narrow = jax.ShapeDtypeStruct((L, E * F), bf16)
    return pl.pallas_call(
        backward_kernel,
        out_shape=[wide, wide, narrow, narrow],
        grid=(L // block, E),
        in_specs=[
            pl.BlockSpec((owners, few, D), lambda i, e: (i, 0, 0)),
            pl.BlockSpec((owners, T - few, D), lambda i, e: (i, 0, 0)),
            units, units, hbm, hbm, pl.BlockSpec((1, D, F), lambda i, e: (e, 0, 0)),
        ],
        out_specs=[rows, rows, units, units],
        scratch_shapes=[
            pltpu.VMEM((block, 2 * E * F), bf16),
            pltpu.VMEM((2 * E * F, D), bf16),
            pltpu.SemaphoreType.DMA((2,)),
        ],
        compiler_params=pltpu.CompilerParams(vmem_limit_bytes=VMEM_LIMIT),
        cost_estimate=pl.CostEstimate(
            flops=6 * L * D * E * F, bytes_accessed=40 * 2**20, transcendentals=0
        ),
        name="backward_pass",
    )(first, rest, gate_by, up_by, gate_t.reshape(E * F, D), up_t.reshape(E * F, D), down_t)


def line_sum(n, steps, part, out, landed, up_send, up_recv, down_send, down_recv):
    d, z = lax.axis_index("dp"), lax.axis_index("shard")
    upper, lower = (d, lax.rem(z + 1, n)), (d, lax.rem(z + n - 1, n))

    def move_up(src, o, k):
        return pltpu.make_async_remote_copy(
            src_ref=src.at[o, k], dst_ref=landed.at[o, k], send_sem=up_send.at[o, k],
            recv_sem=up_recv.at[o, k], device_id=upper, device_id_type=MESH,
        )

    def move_down(src, o, k):
        slot = jnp.where(o == z - 1, n, o)
        return pltpu.make_async_remote_copy(
            src_ref=src.at[o, k], dst_ref=landed.at[slot, k], send_sem=down_send.at[o, k],
            recv_sem=down_recv.at[o, k], device_id=lower, device_id_type=MESH,
        )

    def passing(move, first, owner):
        def run(k):
            def far(i, carry):
                o = owner(i)

                @pl.when((o >= 0) & (o < n))
                def _():
                    @pl.when(z == first)
                    def _():
                        move(part, o, k).start()

                    @pl.when(z != first)
                    def _():
                        move(part, o, k).wait_recv()
                        both = landed[o, k].astype(f32) + part[o, k].astype(f32)
                        landed[o, k] = both.astype(bf16)
                        move(landed, o, k).start()

                return carry

            lax.fori_loop(0, n - 1, far, 0)

        return run

    pass_up = passing(move_up, 0, lambda i: z + n - 1 - i)
    pass_down = passing(move_down, n - 1, lambda i: z - n + 1 + i)

    def own(k):
        @pl.when(z > 0)
        def _():
            move_up(part, z, k).wait_recv()

        @pl.when(z == 0)
        def _():
            landed[z, k] = jnp.zeros(part.shape[2:], bf16)

        @pl.when(z < n - 1)
        def _():
            move_down(part, z, k).wait_recv()

        @pl.when(z == n - 1)
        def _():
            landed[n, k] = jnp.zeros(part.shape[2:], bf16)

        out[k] = part[z, k].astype(f32) + landed[z, k].astype(f32) + landed[n, k].astype(f32)

    def turn(t):
        up_k, down_k, own_k = t - z, t - (n - 1 - z), t - (n - 1)

        @pl.when((up_k >= 0) & (up_k < steps))
        def _():
            pass_up(up_k)

        @pl.when((down_k >= 0) & (down_k < steps))
        def _():
            pass_down(down_k)

        @pl.when((own_k >= 0) & (own_k < steps))
        def _():
            own(own_k)

    def drain():
        def one(i, carry):
            o, k = i // steps, i % steps

            @pl.when(o > z)
            def _():
                move_up(part, o, k).wait_send()

            @pl.when(o < z)
            def _():
                move_down(part, o, k).wait_send()

            return carry

        lax.fori_loop(0, n * steps, one, 0)

    return turn, drain


def line_scratch(n, steps, R, D):
    dma = pltpu.SemaphoreType.DMA
    slots = [pltpu.VMEM((n, steps, R, D), bf16), pltpu.VMEM((n + 1, steps, R, D), bf16)]
    return slots + [dma((n, steps))] * 4 + [dma((1,))]


def expert_grads_kernel(xt, gate_grad, up_grad, gate_out, up_out):
    gate_out[0] = dot(xt[...], gate_grad[...]).astype(bf16)
    up_out[0] = dot(xt[...], up_grad[...]).astype(bf16)


def expert_grads(turned, gate_grad, up_grad, experts):
    D, L = turned.shape
    F = gate_grad.shape[1] // experts
    whole = pl.BlockSpec((D, L), lambda e: (0, 0))
    units = pl.BlockSpec((L, F), lambda e: (0, e))
    column = pl.BlockSpec((1, D, F), lambda e: (e, 0, 0))
    grad = jax.ShapeDtypeStruct((experts, D, F), bf16)
    return pl.pallas_call(
        expert_grads_kernel,
        out_shape=[grad, grad],
        grid=(experts,),
        in_specs=[whole, units, units],
        out_specs=[column, column],
        compiler_params=pltpu.CompilerParams(vmem_limit_bytes=VMEM_LIMIT),
        cost_estimate=pl.CostEstimate(
            flops=4 * L * D * experts * F, bytes_accessed=16 * 2**20, transcendentals=0
        ),
        name="expert_grads",
    )(turned, gate_grad, up_grad)


def widen_kernel(count, *refs):
    for src, dst in zip(refs[:count], refs[count:]):
        dst[...] = src[...].astype(f32)


def widen(*arrays):
    flat = [v.reshape(-1, v.shape[-1]) for v in arrays]
    steps = 8
    specs = [
        pl.BlockSpec((v.shape[0] // steps, v.shape[1]), lambda i: (i, 0)) for v in flat
    ]
    out = pl.pallas_call(
        functools.partial(widen_kernel, len(flat)),
        out_shape=[jax.ShapeDtypeStruct(v.shape, f32) for v in flat],
        grid=(steps,),
        in_specs=specs,
        out_specs=specs,
        compiler_params=pltpu.CompilerParams(vmem_limit_bytes=VMEM_LIMIT),
        cost_estimate=pl.CostEstimate(
            flops=0, bytes_accessed=sum(6 * v.size for v in flat), transcendentals=0
        ),
        name="widen",
    )(*flat)
    return tuple(v.reshape(w.shape) for v, w in zip(out, arrays))


def gather_line_kernel(n, v_hbm, out, slots, load_sem, up_sem, down_sem, recv_sem, out_sem):
    d, z, peers = others(n)
    own_load = pltpu.make_async_copy(v_hbm, slots.at[z], load_sem.at[0])
    own_load.start()
    greet(peers)

    def send_up(o):
        return pltpu.make_async_remote_copy(
            src_ref=slots.at[o], dst_ref=slots.at[o], send_sem=up_sem.at[o],
            recv_sem=recv_sem.at[o], device_id=(d, lax.rem(z + 1, n)), device_id_type=MESH,
        )

    def send_down(o):
        return pltpu.make_async_remote_copy(
            src_ref=slots.at[o], dst_ref=slots.at[o], send_sem=down_sem.at[o],
            recv_sem=recv_sem.at[o], device_id=(d, lax.rem(z + n - 1, n)), device_id_type=MESH,
        )

    own_load.wait()

    @pl.when(z < n - 1)
    def _():
        send_up(z).start()

    @pl.when(z > 0)
    def _():
        send_down(z).start()

    C = slots.shape[2]

    def save(o):
        c = pl.ds(pl.multiple_of(o * C, C), C)
        return pltpu.make_async_copy(slots.at[o], out.at[:, c], out_sem.at[o])

    save(z).start()

    def step(s, carry):
        below, above = z - s, z + s

        @pl.when(below >= 0)
        def _():
            send_up(below).wait_recv()

            @pl.when(z < n - 1)
            def _():
                send_up(below).start()

            save(below).start()

        @pl.when(above < n)
        def _():
            send_down(above).wait_recv()

            @pl.when(z > 0)
            def _():
                send_down(above).start()

            save(above).start()

        return carry

    lax.fori_loop(1, n, step, 0)

    def finish(o, carry):
        save(o).wait()

        @pl.when((z < n - 1) & (o <= z))
        def _():
            send_up(o).wait_send()

        @pl.when((z > 0) & (o >= z))
        def _():
            send_down(o).wait_send()

        return carry

    lax.fori_loop(0, n, finish, 0)


def gather_line(n, v, collective_id):
    hbm = pl.BlockSpec(memory_space=pl.ANY)
    dma = pltpu.SemaphoreType.DMA
    return pl.pallas_call(
        functools.partial(gather_line_kernel, n),
        out_shape=jax.ShapeDtypeStruct((v.shape[0], n * v.shape[1]), v.dtype),
        in_specs=[hbm],
        out_specs=hbm,
        scratch_shapes=[
            pltpu.VMEM((n,) + v.shape, v.dtype), dma((1,)), dma((n,)), dma((n,)), dma((n,)),
            dma((n,)),
        ],
        compiler_params=pltpu.CompilerParams(
            collective_id=collective_id, has_side_effects=True, vmem_limit_bytes=VMEM_LIMIT
        ),
        cost_estimate=pl.CostEstimate(flops=70 * 10**9, bytes_accessed=8 * 2**20, transcendentals=0),
        name="gather_line",
    )(v)


def per_device(
    tokens,
    out_grad,
    routes,
    gate_weights,
    prefix,
    query_weight,
    key_weight,
    value_weight,
    output_weight,
    norm_gains,
    expert_gate,
    expert_up,
    expert_down,
):
    rows, width = tokens.shape
    shards = lax.axis_size("shard")
    groups = lax.axis_size("dp")
    place = lax.axis_index("shard")
    group = lax.axis_index("dp")
    length = rows * shards
    local = width // shards
    experts = expert_gate.shape[0]
    units = expert_gate.shape[2]

    expert_ids = jnp.arange(experts, dtype=jnp.int32)
    weight_own = jnp.sum(
        jnp.where(routes[:, :, None] == expert_ids[None, None, :], gate_weights[:, :, None], 0.0),
        axis=1,
    )
    own_gains = norm_gains.astype(f32)
    small = jnp.concatenate(
        [
            jnp.pad(weight_own.T, ((0, 8 - experts), (0, 0))),
            jnp.pad(jnp.stack([own_gains[0], own_gains[3]]), ((0, 6), (0, 0))),
        ],
        axis=1,
    )
    x_all_b, normed, query_raw, key_raw, values, out_slab, combine, gains, factors = (
        gather_project(
            shards, groups, tokens, small, output_weight, query_weight, key_weight, value_weight
        )
    )
    full_output = lax.all_gather(out_slab, "dp", axis=0, tiled=True)
    x_all_b = x_all_b.reshape(length, width)
    normed = normed.reshape(length, width)
    query_raw = query_raw.reshape(length, local)
    key_raw = key_raw.reshape(length, local)
    values = values.reshape(length, local)
    cosine, sine = rotary_tables(length)
    limit = jnp.broadcast_to(prefix.reshape(1, 1), (8, 128))
    few = rows // 4
    queries, keys, mixed_own, grad_first = attention(
        shards, limit, query_raw, key_raw, values, factors, cosine, sine, own_gains, out_grad, few
    )
    mixed_all = gather_line(shards, mixed_own, 1)
    grad_rest, mixed_all = lax.optimization_barrier((out_grad[few:], mixed_all))
    grad_rest = lax.all_gather(grad_rest, "shard", axis=0)
    attended, expert_turned, gate_by, up_by, hidden, sum_part, gate_t, up_t, down_t = forward_pass(
        mixed_all, full_output, x_all_b, gains, combine, expert_gate, expert_up, expert_down
    )
    attended_own = lax.dynamic_slice_in_dim(attended, place * rows, rows, 0)
    g_all, in_part, gate_grad, up_grad = backward_pass(
        grad_first, grad_rest, gate_by, up_by, gate_t, up_t, down_t
    )
    sum_parts = sum_part.reshape(shards, 16, rows // 16, width)
    grad_gate, grad_up = expert_grads(expert_turned, gate_grad, up_grad, experts)
    in_part, grad_gate, grad_up = lax.optimization_barrier((in_part, grad_gate, grad_up))
    grad_gate, grad_up = lax.psum((grad_gate, grad_up), "dp")

    x_own = tokens.astype(f32)
    residual_own = x_own + attended_own
    residual_grad, attended_grad, own_columns, gain_grad_res, grad_down = scatter_norm(
        shards, groups, 16, in_part, tokens, gains,
        more=(out_grad, attended, hidden, g_all, experts),
    )
    residual_grad = residual_grad.reshape(rows, width)
    attended_grad = attended_grad.reshape(length, width)

    grad_output = dot_tn(mixed_all, own_columns.reshape(length, local))
    grad_output, grad_down, grad_gate, grad_up, attended_grad = lax.optimization_barrier(
        (grad_output.astype(bf16), grad_down, grad_gate, grad_up, attended_grad)
    )
    grad_output, grad_down = lax.psum((grad_output, grad_down), "dp")
    grad_query, grad_key, grad_value, normed_part, gain_grad_heads, expert_sum = attention_back(
        shards, width, limit, queries, keys, values, query_raw, key_raw, factors, cosine, sine,
        own_gains, query_weight, key_weight, value_weight, normed, sum_parts, attended_grad,
        full_output,
    )
    expert_sum = expert_sum.reshape(rows, width)
    expert_sum, grad_gate, grad_up = lax.optimization_barrier((expert_sum, grad_gate, grad_up))
    grad_gate, grad_up = widen(grad_gate, grad_up)
    (
        grad_query, grad_key, grad_value, normed_part, grad_output, grad_down, grad_gate, grad_up,
    ) = lax.optimization_barrier(
        (
            grad_query, grad_key, grad_value, normed_part, grad_output, grad_down, grad_gate,
            grad_up,
        )
    )
    grad_query, grad_key, grad_value = lax.psum((grad_query, grad_key, grad_value), "dp")
    through_norm, grad_gains = scatter_norm(
        shards, groups, 16, normed_part, tokens, gains,
        other_gains=(gain_grad_res, gain_grad_heads),
    )
    through_norm, expert_sum = lax.optimization_barrier((through_norm, expert_sum))
    grad_tokens = residual_grad + through_norm.reshape(rows, width)
    grad_gains = grad_gains[:4]
    output = residual_own + expert_sum
    root_means = jnp.stack([root_mean(attended_own), root_mean(expert_sum), root_mean(output)])
    grad_down, grad_output = widen(grad_down, grad_output)
    grad_query, grad_key, grad_value = widen(grad_query, grad_key, grad_value)

    return (
        output.astype(bf16),
        grad_tokens,
        root_means,
        grad_query,
        grad_key,
        grad_value,
        grad_output,
        grad_gains,
        grad_gate,
        grad_up,
        grad_down,
    )


def solution(mesh):
    placed = (
        P(("dp", "shard"), None),
        P(("dp", "shard"), None),
        P(("dp", "shard"), None),
        P(("dp", "shard"), None),
        P("dp"),
        P(None, "shard"),
        P(None, "shard"),
        P(None, "shard"),
        P(None, "shard"),
        P(None, "shard"),
        P(None, None, "shard"),
        P(None, None, "shard"),
        P(None, "shard", None),
    )
    return jax.shard_map(
        per_device,
        mesh=mesh,
        in_specs=placed,
        out_specs=(
            P(("dp", "shard"), None),
            P(("dp", "shard"), None),
            P(None, ("dp", "shard")),
            P(None, "shard"),
            P(None, "shard"),
            P(None, "shard"),
            P(None, "shard"),
            P(None, "shard"),
            P(None, None, "shard"),
            P(None, None, "shard"),
            P(None, "shard", None),
        ),
        check_vma=False,
    )
```

```python
import functools

import jax
import jax.numpy as jnp
import numpy as np
from jax import lax
from jax.experimental import pallas as pl
from jax.experimental.pallas import tpu as pltpu
from jax.sharding import PartitionSpec as P

HEAD_DIM = 128
EPSILON = 1e-05
ROPE_BASE = 10000.0
MASKED = -1e30
VMEM_LIMIT = 60 * 2**20

f32 = jnp.float32
bf16 = jnp.bfloat16


def rotary_tables(row_count):
    half_dim = HEAD_DIM // 2
    inverse = ROPE_BASE ** (-np.arange(half_dim) / half_dim)
    angles = np.arange(row_count)[:, None] * inverse.astype(np.float32).astype(np.float64)[None, :]
    angles = angles.astype(np.float32).astype(np.float64)
    cosine, sine = np.cos(angles), np.sin(angles)
    return (
        jnp.asarray(np.concatenate([cosine, cosine], 1), f32),
        jnp.asarray(np.concatenate([-sine, sine], 1), f32),
    )


def row_factor(values):
    return lax.rsqrt(jnp.mean(values * values, axis=-1, keepdims=True) + EPSILON)


def norm_back(grad_unit, unit_rows, factor):
    return factor * (
        grad_unit - unit_rows * jnp.mean(grad_unit * unit_rows, axis=-1, keepdims=True)
    )


def root_mean(values):
    return jnp.sqrt(jnp.mean(values * values, axis=-1))


def dot(a, b):
    return jnp.dot(a, b, preferred_element_type=f32)


def dot_nt(a, b):
    return lax.dot_general(a, b, (((1,), (1,)), ((), ())), preferred_element_type=f32)


def dot_tn(a, b):
    return lax.dot_general(a, b, (((0,), (0,)), ((), ())), preferred_element_type=f32)


MESH = pl.DeviceIdType.MESH


def greet(peers):
    barrier = pltpu.get_barrier_semaphore()
    for peer in peers:
        pl.semaphore_signal(barrier, inc=1, device_id=peer, device_id_type=MESH)
    pl.semaphore_wait(barrier, len(peers))


def others(n):
    d, z = lax.axis_index("dp"), lax.axis_index("shard")
    return d, z, [(d, lax.rem(z + p, n)) for p in range(1, n)]


def line_gather(n, slots, up_sem, down_sem, recv_sem):
    d, z = lax.axis_index("dp"), lax.axis_index("shard")

    def send_up(o):
        return pltpu.make_async_remote_copy(
            src_ref=slots.at[o], dst_ref=slots.at[o], send_sem=up_sem.at[o],
            recv_sem=recv_sem.at[o], device_id=(d, lax.rem(z + 1, n)), device_id_type=MESH,
        )

    def send_down(o):
        return pltpu.make_async_remote_copy(
            src_ref=slots.at[o], dst_ref=slots.at[o], send_sem=down_sem.at[o],
            recv_sem=recv_sem.at[o], device_id=(d, lax.rem(z + n - 1, n)), device_id_type=MESH,
        )

    def begin():
        @pl.when(z < n - 1)
        def _():
            send_up(z).start()

        @pl.when(z > 0)
        def _():
            send_down(z).start()

    def hop(s, landed):
        below, above = z - s, z + s

        @pl.when((s > 0) & (below >= 0))
        def _():
            send_up(below).wait_recv()

            @pl.when(z < n - 1)
            def _():
                send_up(below).start()

            landed(below)

        @pl.when((s > 0) & (above < n))
        def _():
            send_down(above).wait_recv()

            @pl.when(z > 0)
            def _():
                send_down(above).start()

            landed(above)

    def drain():
        def one(o, carry):
            @pl.when((z < n - 1) & (o <= z))
            def _():
                send_up(o).wait_send()

            @pl.when((z > 0) & (o >= z))
            def _():
                send_down(o).wait_send()

            return carry

        lax.fori_loop(0, n, one, 0)

    return begin, hop, drain


def gather_project_kernel(
    n, x_hbm, small_ref, slab_hbm, wq_hbm, wk_hbm, wv_hbm,
    x_out, normed_out, q_out, k_out, v_out, slab_out, combine_out, gains_out, sq_out,
    slabs, xs, nb, qb, kb, vb, wq, wk, wv, sq_all, small_all,
    load_sem, out_sem, up_sem, down_sem, recv_sem, small_send, small_recv, sq_send, sq_recv,
    slab_up, slab_down, slab_recv, slab_sem,
):
    T, D = xs.shape[1:]
    C = qb.shape[2]
    d, z, peers = others(n)
    S = slabs.shape[1]
    slab_rows = pl.ds(pl.multiple_of(d * S, S), S)
    slab_load = pltpu.make_async_copy(slab_hbm.at[slab_rows, :], slabs.at[z], load_sem.at[4])
    slab_load.start()
    own_load = pltpu.make_async_copy(x_hbm, xs.at[z], load_sem.at[0])
    own_load.start()
    slab_begin, slab_hop, slab_drain = line_gather(n, slabs, slab_up, slab_down, slab_recv)

    def slab_save(o):
        c = pl.ds(pl.multiple_of(o * C, C), C)
        return pltpu.make_async_copy(slabs.at[o], slab_out.at[:, c], slab_sem.at[o])

    loads = [
        pltpu.make_async_copy(src, dst, load_sem.at[i + 1])
        for i, (src, dst) in enumerate(((wq_hbm, wq), (wk_hbm, wk), (wv_hbm, wv)))
    ]
    for load in loads:
        load.start()
    greet(peers)

    def send_up(o):
        return pltpu.make_async_remote_copy(
            src_ref=xs.at[o], dst_ref=xs.at[o], send_sem=up_sem.at[o], recv_sem=recv_sem.at[o],
            device_id=(d, lax.rem(z + 1, n)), device_id_type=MESH,
        )

    def send_down(o):
        return pltpu.make_async_remote_copy(
            src_ref=xs.at[o], dst_ref=xs.at[o], send_sem=down_sem.at[o], recv_sem=recv_sem.at[o],
            device_id=(d, lax.rem(z + n - 1, n)), device_id_type=MESH,
        )

    own_load.wait()
    small_copies = []
    for p, peer in enumerate(peers):
        copy = pltpu.make_async_remote_copy(
            src_ref=small_ref, dst_ref=small_all.at[z], send_sem=small_send.at[p],
            recv_sem=small_recv.at[z], device_id=peer, device_id_type=MESH,
        )
        copy.start()
        small_copies.append(copy)

    @pl.when(z < n - 1)
    def _():
        send_up(z).start()

    @pl.when(z > 0)
    def _():
        send_down(z).start()

    small_all[z] = small_ref[...]
    for load in loads:
        load.wait()
    for p in range(1, n):
        o = lax.rem(z + n - p, n)
        pltpu.make_async_remote_copy(
            src_ref=small_ref, dst_ref=small_all.at[o], send_sem=small_send.at[p - 1],
            recv_sem=small_recv.at[o], device_id=(d, o), device_id_type=MESH,
        ).wait_recv()

    lanes = lax.broadcasted_iota(jnp.int32, (T, 128), 1)
    step_rows = 32

    def outs(o):
        return [
            pltpu.make_async_copy(src.at[o], dst.at[o], out_sem.at[i, o])
            for i, (src, dst) in enumerate(
                ((xs, x_out), (nb, normed_out), (qb, q_out), (kb, k_out), (vb, v_out))
            )
        ]

    def compute(o):
        gain = jnp.concatenate([small_all[s, 0:1, T:] for s in range(n)], axis=1)

        def norm_rows(i, carry):
            r = pl.ds(pl.multiple_of(i * step_rows, step_rows), step_rows)
            x = xs[o, r, :].astype(f32)
            factor = lax.rsqrt(jnp.sum(x * x, axis=1, keepdims=True) / D + EPSILON)
            nb[o, r, :] = (x * factor * gain).astype(bf16)
            return carry

        lax.fori_loop(0, T // step_rows, norm_rows, 0)
        q = jnp.dot(nb[o], wq[...], preferred_element_type=f32)
        qb[o] = q
        q_sum = jnp.sum(q * q, axis=1, keepdims=True)
        k = jnp.dot(nb[o], wk[...], preferred_element_type=f32)
        kb[o] = k
        k_sum = jnp.sum(k * k, axis=1, keepdims=True)
        vb[o] = jnp.dot(nb[o], wv[...], preferred_element_type=f32).astype(bf16)
        both = jnp.where(lanes == 0, q_sum, jnp.where(lanes == 1, k_sum, 0.0))
        sq_all[z, o] = both.T[0:8]
        for copy in outs(o):
            copy.start()

    def step(s, carry):
        below, above = z - s, z + s

        @pl.when((s > 0) & (below >= 0))
        def _():
            send_up(below).wait_recv()

            @pl.when(z < n - 1)
            def _():
                send_up(below).start()

        @pl.when((s > 0) & (above < n))
        def _():
            send_down(above).wait_recv()

            @pl.when(z > 0)
            def _():
                send_down(above).start()

        @pl.when(s == n - 2)
        def _():
            slab_load.wait()
            slab_begin()
            slab_save(z).start()

        @pl.when(s == n - 1)
        def _():
            slab_hop(1, lambda o: slab_save(o).start())

        def side(j, inner):
            o = z - s + 2 * s * j

            @pl.when((o >= 0) & (o < n) & ((s > 0) | (j == 0)))
            def _():
                compute(o)

            return inner

        lax.fori_loop(0, 2, side, 0)
        return carry

    lax.fori_loop(0, n, step, 0)

    sq_copies = []
    for p, peer in enumerate(peers):
        copy = pltpu.make_async_remote_copy(
            src_ref=sq_all.at[z], dst_ref=sq_all.at[z], send_sem=sq_send.at[p],
            recv_sem=sq_recv.at[z], device_id=peer, device_id_type=MESH,
        )
        copy.start()
        sq_copies.append(copy)

    def slab_hops(s, carry):
        slab_hop(s, lambda o: slab_save(o).start())
        return carry

    lax.fori_loop(2, n - 1, slab_hops, 0)

    def spread(o, carry):
        r = pl.ds(pl.multiple_of(o * T, T), T)
        tall = jnp.concatenate([small_all[o, :, 0:T], jnp.zeros((120, T), f32)], axis=0)
        combine_out[r, :] = tall.T
        return carry

    lax.fori_loop(0, n, spread, 0)
    for s in range(n):
        gains_out[:, s * C : (s + 1) * C] = small_all[s, :, T:]

    for p in range(1, n):
        o = lax.rem(z + n - p, n)
        pltpu.make_async_remote_copy(
            src_ref=sq_all.at[o], dst_ref=sq_all.at[o], send_sem=sq_send.at[p - 1],
            recv_sem=sq_recv.at[o], device_id=(d, o), device_id_type=MESH,
        ).wait_recv()
    def turn_factors(i, carry):
        total = sq_all[0, i]
        for s in range(1, n):
            total = total + sq_all[s, i]
        total = jnp.concatenate([total, jnp.zeros((120, T), f32)], axis=0).T
        r = pl.ds(pl.multiple_of(i * T, T), T)
        sq_out[r, :] = lax.rsqrt(total / D + EPSILON)
        return carry

    lax.fori_loop(0, n, turn_factors, 0)
    lax.fori_loop(max(2, n - 1), n, slab_hops, 0)

    def finish(o, carry):
        for copy in outs(o):
            copy.wait()
        slab_save(o).wait()

        @pl.when((z < n - 1) & (o <= z))
        def _():
            send_up(o).wait_send()

        @pl.when((z > 0) & (o >= z))
        def _():
            send_down(o).wait_send()

        return carry

    lax.fori_loop(0, n, finish, 0)
    slab_drain()
    for copy in small_copies + sq_copies:
        copy.wait_send()


def gather_project(n, groups, tokens, small, wo, wq, wk, wv):
    T, D = tokens.shape
    C = wq.shape[1]
    S = D // groups
    hbm = pl.BlockSpec(memory_space=pl.ANY)
    vmem = pl.BlockSpec(memory_space=pltpu.VMEM)
    dma = pltpu.SemaphoreType.DMA
    return pl.pallas_call(
        functools.partial(gather_project_kernel, n),
        out_shape=[
            jax.ShapeDtypeStruct((n, T, D), bf16),
            jax.ShapeDtypeStruct((n, T, D), bf16),
            jax.ShapeDtypeStruct((n, T, C), f32),
            jax.ShapeDtypeStruct((n, T, C), f32),
            jax.ShapeDtypeStruct((n, T, C), bf16),
            jax.ShapeDtypeStruct((S, D), bf16),
            jax.ShapeDtypeStruct((n * T, 128), f32),
            jax.ShapeDtypeStruct((8, D), f32),
            jax.ShapeDtypeStruct((n * T, 128), f32),
        ],
        in_specs=[hbm, vmem, hbm, hbm, hbm, hbm],
        out_specs=[hbm] * 6 + [vmem] * 3,
        scratch_shapes=[
            pltpu.VMEM((n, S, C), bf16),
            pltpu.VMEM((n, T, D), bf16),
            pltpu.VMEM((n, T, D), bf16),
            pltpu.VMEM((n, T, C), f32),
            pltpu.VMEM((n, T, C), f32),
            pltpu.VMEM((n, T, C), bf16),
            pltpu.VMEM((D, C), bf16),
            pltpu.VMEM((D, C), bf16),
            pltpu.VMEM((D, C), bf16),
            pltpu.VMEM((n, n, 8, T), f32),
            pltpu.VMEM((n,) + small.shape, f32),
            dma((5,)),
            dma((5, n)),
            dma((n,)),
            dma((n,)),
            dma((n,)),
            dma((n,)),
            dma((n,)),
            dma((n,)),
            dma((n,)),
            dma((n,)),
            dma((n,)),
            dma((n,)),
            dma((n,)),
        ],
        compiler_params=pltpu.CompilerParams(
            collective_id=0, has_side_effects=True, vmem_limit_bytes=VMEM_LIMIT
        ),
        cost_estimate=pl.CostEstimate(flops=80 * 10**9, bytes_accessed=32 * 2**20, transcendentals=0),
        name="gather_project",
    )(tokens, small, wo, wq, wk, wv)


def rope(v, cosine, sine):
    return v * cosine + pltpu.roll(v, HEAD_DIM // 2, 1) * sine


def key_span(i, block, length):
    return min(length, max((i + 1) * block, length // 2))


def block_scores(q, k, i, block, limit):
    s = dot_nt(q, k) * (HEAD_DIM**-0.5)
    row = lax.broadcasted_iota(jnp.int32, s.shape, 0) + i * block
    col = lax.broadcasted_iota(jnp.int32, s.shape, 1)
    return jnp.where((col <= row) | (col < limit), s, MASKED)


def attention_kernel(
    n, limit_ref, q_raw, k_raw, v_ref, factors, cosine, sine, gains, grad_hbm,
    q_out, k_out, mixed, first_out, slots, load_sem, up_sem, down_sem, recv_sem, out_sem,
):
    length = q_raw.shape[0]
    block = 256
    limit = limit_ref[0:1, 0:1]
    h, heads = pl.program_id(0), pl.num_programs(0)
    begin, hop, drain = line_gather(n, slots, up_sem, down_sem, recv_sem)
    z = lax.axis_index("shard")

    def save(o):
        return pltpu.make_async_copy(slots.at[o], first_out.at[o], out_sem.at[o])

    few = slots.shape[1]

    @pl.when(h == 0)
    def _():
        load = pltpu.make_async_copy(grad_hbm.at[0:few], slots.at[z], load_sem.at[0])
        load.start()
        _, _, peers = others(n)
        greet(peers)
        load.wait()
        begin()
        save(z).start()

    def turn(raw, out, column, gain):
        def part(i, carry):
            r = pl.ds(pl.multiple_of(i * block, block), block)
            v = raw[r, :] * factors[r, column : column + 1] * gain
            out[r, :] = rope(v, cosine[r, :], sine[r, :]).astype(bf16)
            return carry

        lax.fori_loop(0, length // block, part, 0)

    turn(q_raw, q_out, 0, gains[1:2, :])
    turn(k_raw, k_out, 1, gains[2:3, :])
    for i in range(length // block):
        span = key_span(i, block, length)
        r = pl.ds(i * block, block)
        s = block_scores(q_out[r, :], k_out[0:span, :], i, block, limit)
        e = jnp.exp(s - jnp.max(s, axis=1, keepdims=True))
        total = jnp.sum(e, axis=1, keepdims=True)
        mixed[r, :] = (dot(e.astype(bf16), v_ref[0:span, :]) / total).astype(bf16)

    def hops(s, carry):
        hop(s, lambda o: save(o).start())
        return carry

    lax.fori_loop(1 + h * (n - 1) // heads, 1 + (h + 1) * (n - 1) // heads, hops, 0)

    @pl.when(h == heads - 1)
    def _():
        drain()

        def finish(o, carry):
            save(o).wait()
            return carry

        lax.fori_loop(0, n, finish, 0)


def attention(n, limit, q_raw, k_raw, values, factors, cosine, sine, gains, grad, few):
    length, local = q_raw.shape
    heads = local // HEAD_DIM
    head = pl.BlockSpec((length, HEAD_DIM), lambda h: (0, h))
    whole = lambda a: pl.BlockSpec(a.shape, lambda h: (0, 0))
    hbm = pl.BlockSpec(memory_space=pl.ANY)
    out = jax.ShapeDtypeStruct((length, local), bf16)
    dma = pltpu.SemaphoreType.DMA
    return pl.pallas_call(
        functools.partial(attention_kernel, n),
        out_shape=[out] * 3
        + [jax.ShapeDtypeStruct((n, few, grad.shape[1]), bf16)],
        grid=(heads,),
        in_specs=[
            whole(limit), head, head, head, whole(factors), whole(cosine), whole(sine),
            pl.BlockSpec((gains.shape[0], HEAD_DIM), lambda h: (0, h)), hbm,
        ],
        out_specs=[head] * 3 + [hbm],
        scratch_shapes=[pltpu.VMEM((n, few, grad.shape[1]), bf16), dma((1,))] + [dma((n,))] * 4,
        compiler_params=pltpu.CompilerParams(
            collective_id=7, has_side_effects=True, vmem_limit_bytes=VMEM_LIMIT
        ),
        cost_estimate=pl.CostEstimate(
            flops=20 * 10**9, bytes_accessed=16 * 2**20, transcendentals=0
        ),
        name="attention",
    )(limit, q_raw, k_raw, values, factors, cosine, sine, gains, grad)


def attention_back_kernel(
    n, steps, width, limit_ref, q_ref, k_ref, v_ref, q_raw, k_raw, factors, cosine, sine,
    gains, wq, wk, wv, normed_hbm, sum_hbm, grad_hbm, output_hbm, gq_out, gk_out, gv_out, normed_out, gain_out, own_sum,
    g_ref, output, dq_acc, dk_acc, k_acc, v_acc, q_grad, k_grad, v_grad, columns, turned, staged,
    inner_all, inner_send, inner_recv, column_sem, staged_sem, grad_sem, part, *line,
):
    length, local = q_ref.shape
    strips = width // local
    heads = local // HEAD_DIM
    block = 256
    blocks = length // block
    scale = HEAD_DIM**-0.5
    load_sem = line[-1]
    turn, drain = line_sum(n, steps, part, own_sum, *line[:-1])
    d, z, peers = others(n)
    load = pltpu.make_async_copy(sum_hbm, part, load_sem.at[0])
    load.start()

    def grad_rows(i):
        r = pl.ds(pl.multiple_of(i * block, block), block)
        return pltpu.make_async_copy(
            grad_hbm.at[r, :], staged.at[lax.rem(i, 2)], grad_sem.at[lax.rem(i, 2)]
        )

    own_rows = pl.ds(pl.multiple_of(z * local, local), local)
    output_load = pltpu.make_async_copy(output_hbm.at[own_rows, :], output, grad_sem.at[2])
    output_load.start()
    grad_rows(0).start()
    greet(peers)

    def strip(b):
        c = pl.ds(pl.multiple_of(b * local, local), local)
        return pltpu.make_async_copy(
            normed_hbm.at[:, c], columns.at[lax.rem(b, 2)], column_sem.at[lax.rem(b, 2)]
        )

    strip(0).start()
    load.wait()
    turns = steps + n - 1
    in_heads, in_parts = 8 * turns // 19, 4 * turns // 19
    slots = -(-in_heads // heads)
    past = 1 + heads * slots
    in_strips = turns - past - in_parts - 2

    def take(first, count, i, of):
        def one(t, carry):
            turn(first + t)
            return carry

        lax.fori_loop(i * count // of, (i + 1) * count // of, one, 0)
    limit = limit_ref[0:1, 0:1]
    lanes = lax.broadcasted_iota(jnp.int32, (block, 128), 1)

    def clear(i, carry):
        inner_all[z, i] = jnp.zeros((8, block), f32)
        return carry

    lax.fori_loop(0, blocks, clear, 0)

    turn(0)
    output_load.wait()

    def mixed_rows(i, carry):
        r = pl.ds(pl.multiple_of(i * block, block), block)
        grad_rows(i).wait()

        @pl.when(i + 1 < blocks)
        def _():
            grad_rows(i + 1).start()

        g_ref[r, :] = dot_nt(staged[lax.rem(i, 2)], output[...]).astype(bf16)
        return carry

    lax.fori_loop(0, blocks, mixed_rows, 0)

    def head(h, carry):
        c = pl.ds(pl.multiple_of(h * HEAD_DIM, HEAD_DIM), HEAD_DIM)
        k_acc[...] = jnp.zeros_like(k_acc)
        v_acc[...] = jnp.zeros_like(v_acc)
        for i in range(blocks):
            for j in range(i * slots // blocks, (i + 1) * slots // blocks):
                turn(1 + h * slots + j)
            span = key_span(i, block, length)
            r = pl.ds(i * block, block)
            q, g, k, v = q_ref[r, c], g_ref[r, c], k_ref[0:span, c], v_ref[0:span, c]
            s = block_scores(q, k, i, block, limit)
            e = jnp.exp(s - jnp.max(s, axis=1, keepdims=True))
            p = e * (1.0 / jnp.sum(e, axis=1, keepdims=True))
            t = p * dot_nt(g, v)
            ds = (t - p * jnp.sum(t, axis=1, keepdims=True)).astype(bf16)
            dq_acc[r, c] = dot(ds, k) * scale
            k_acc[0:span, :] += dot_tn(ds, q) * scale
            v_acc[0:span, :] += dot_tn(p.astype(bf16), g)
        v_grad[:, c] = v_acc[...].astype(bf16)
        gain_q, gain_k = gains[1:2, c], gains[2:3, c]

        def back(i, carry):
            gq, gk = carry
            r = pl.ds(pl.multiple_of(i * block, block), block)
            cos, sin = cosine[r, :], sine[r, :]
            dq = rope(dq_acc[r, c], cos, -sin)
            dk = rope(k_acc[r, :], cos, -sin)
            uq = q_raw[r, c] * factors[r, 0:1]
            uk = k_raw[r, c] * factors[r, 1:2]
            gq = gq + jnp.sum(dq * uq, axis=0, keepdims=True)
            gk = gk + jnp.sum(dk * uk, axis=0, keepdims=True)
            dq = dq * gain_q
            dk = dk * gain_k
            dq_acc[r, c] = dq
            dk_acc[r, c] = dk
            inner_q = jnp.sum(dq * uq, axis=1, keepdims=True)
            inner_k = jnp.sum(dk * uk, axis=1, keepdims=True)
            both = jnp.where(lanes == 0, inner_q, jnp.where(lanes == 1, inner_k, 0.0))
            inner_all[z, i] += both.T[0:8]
            return gq, gk

        zero = jnp.zeros((1, HEAD_DIM), f32)
        gq, gk = lax.fori_loop(0, blocks, back, (zero, zero))
        gain_out[0:1, c] = gq
        gain_out[1:2, c] = gk
        return carry

    lax.fori_loop(0, heads, head, 0)

    copies = []
    for p, peer in enumerate(peers):
        copy = pltpu.make_async_remote_copy(
            src_ref=inner_all.at[z], dst_ref=inner_all.at[z], send_sem=inner_send.at[p],
            recv_sem=inner_recv.at[z], device_id=peer, device_id_type=MESH,
        )
        copy.start()
        copies.append(copy)
    turn(past)
    for p in range(1, n):
        o = lax.rem(z + n - p, n)
        pltpu.make_async_remote_copy(
            src_ref=inner_all.at[o], dst_ref=inner_all.at[o], send_sem=inner_send.at[p - 1],
            recv_sem=inner_recv.at[o], device_id=(d, o), device_id_type=MESH,
        ).wait_recv()

    def raw(i, carry):
        r = pl.ds(pl.multiple_of(i * block, block), block)
        total = inner_all[0, i]
        for s in range(1, n):
            total = total + inner_all[s, i]
        total = jnp.concatenate([total, jnp.zeros((120, block), f32)], axis=0).T
        fq, fk = factors[r, 0:1], factors[r, 1:2]
        mean_q, mean_k = total[:, 0:1] / width, total[:, 1:2] / width
        q_grad[r, :] = (fq * (dq_acc[r, :] - q_raw[r, :] * (fq * mean_q))).astype(bf16)
        k_grad[r, :] = (fk * (dk_acc[r, :] - k_raw[r, :] * (fk * mean_k))).astype(bf16)
        return carry

    lax.fori_loop(0, blocks, raw, 0)
    turn(past + 1)

    def save(i):
        r = pl.ds(pl.multiple_of(i * block, block), block)
        return pltpu.make_async_copy(
            staged.at[lax.rem(i, 2)], normed_out.at[r, :], staged_sem.at[lax.rem(i, 2)]
        )

    def rows_back(i, carry):
        r = pl.ds(pl.multiple_of(i * block, block), block)

        @pl.when(i >= 2)
        def _():
            save(i - 2).wait()

        staged[lax.rem(i, 2)] = (
            dot_nt(q_grad[r, :], wq[...])
            + dot_nt(k_grad[r, :], wk[...])
            + dot_nt(v_grad[r, :], wv[...])
        ).astype(bf16)
        save(i).start()
        take(past + 2, in_parts, i, blocks)
        return carry

    lax.fori_loop(0, blocks, rows_back, 0)

    def strip_grads(b, carry):
        strip(b).wait()

        @pl.when(b + 1 < strips)
        def _():
            strip(b + 1).start()

        turned[...] = columns[lax.rem(b, 2)].T
        c = pl.ds(pl.multiple_of(b * local, local), local)
        gq_out[c, :] = dot(turned[...], q_grad[...]).astype(bf16)
        gk_out[c, :] = dot(turned[...], k_grad[...]).astype(bf16)
        gv_out[c, :] = dot(turned[...], v_grad[...]).astype(bf16)
        take(past + 2 + in_parts, in_strips, b, strips)
        return carry

    lax.fori_loop(0, strips, strip_grads, 0)
    drain()
    for i in range(max(blocks - 2, 0), blocks):
        save(i).wait()
    for copy in copies:
        copy.wait_send()


def attention_back(
    n, width, limit, q, k, v, q_raw, k_raw, factors, cosine, sine, gains, wq, wk, wv, normed,
    sum_parts, attended_grad, full_output,
):
    length, local = q.shape
    _, steps, R, D = sum_parts.shape
    hbm = pl.BlockSpec(memory_space=pl.ANY)
    vmem = pl.BlockSpec(memory_space=pltpu.VMEM)
    dma = pltpu.SemaphoreType.DMA
    weight = jax.ShapeDtypeStruct((D, local), bf16)
    raw = pltpu.VMEM((length, local), bf16)
    return pl.pallas_call(
        functools.partial(attention_back_kernel, n, steps, width),
        out_shape=[
            weight, weight, weight, jax.ShapeDtypeStruct((length, D), bf16),
            jax.ShapeDtypeStruct((2, local), f32),
            jax.ShapeDtypeStruct((steps, R, D), f32),
        ],
        in_specs=[vmem] * 13 + [hbm] * 4,
        out_specs=[vmem, vmem, vmem, hbm, vmem, vmem],
        scratch_shapes=[
            raw,
            pltpu.VMEM((local, D), bf16),
            pltpu.VMEM((length, local), f32),
            pltpu.VMEM((length, local), f32),
            pltpu.VMEM((length, HEAD_DIM), f32),
            pltpu.VMEM((length, HEAD_DIM), f32),
            raw,
            raw,
            raw,
            pltpu.VMEM((2, length, local), bf16),
            pltpu.VMEM((local, length), bf16),
            pltpu.VMEM((2, 256, D), bf16),
            pltpu.VMEM((n, length // 256, 8, 256), f32),
            dma((n,)),
            dma((n,)),
            dma((2,)),
            dma((2,)),
            dma((3,)),
        ]
        + line_scratch(n, steps, R, D),
        compiler_params=pltpu.CompilerParams(
            collective_id=6, has_side_effects=True, vmem_limit_bytes=VMEM_LIMIT
        ),
        cost_estimate=pl.CostEstimate(
            flops=2 * 10**9, bytes_accessed=2**20, transcendentals=0
        ),
        name="attention_back",
    )(
        limit, q, k, v, q_raw, k_raw, factors, cosine, sine, gains, wq, wk, wv, normed, sum_parts,
        attended_grad, full_output,
    )


def scatter_norm_kernel(n, groups, steps, gather, *refs):
    part_hbm, base, gain = refs[:3]
    part, part_sem = refs[-2:]
    refs = refs[3:-2]
    steps_first = 2
    part_loads = [
        pltpu.make_async_copy(part_hbm.at[:, c], part.at[:, c], part_sem.at[i])
        for i, c in enumerate((slice(0, steps_first), slice(steps_first, steps)))
    ]
    for part_load in part_loads:
        part_load.start()
    if gather:
        addend, attended_hbm, hidden_hbm, g_hbm = refs[:4]
        out, all_out, columns_out, gain_out, down_out = refs[4:9]
        alls, ag_up, ag_down, ag_recv, all_sem, attended, load_sem = refs[9:16]
        hidden, g_all, down, down_sem = refs[16:20]
        refs = refs[20:]
        later_loads = [
            pltpu.make_async_copy(hidden_hbm, hidden, load_sem.at[1]),
            pltpu.make_async_copy(g_hbm, g_all, load_sem.at[2]),
        ]

        def down_save(e):
            return pltpu.make_async_copy(down.at[e], down_out.at[e], down_sem.at[e])
    else:
        expert_gains, head_gains, out, gain_out = refs[:4]
        pieces, landed, sums, piece_send, piece_recv, sum_send, sum_recv = refs[4:11]
        refs = refs[11:]
    from_below, from_above, gain_acc, up_send, up_recv, down_send, down_recv = refs
    R, D = part.shape[2:]
    d, z, peers = others(n)
    upper, lower = (d, lax.rem(z + 1, n)), (d, lax.rem(z + n - 1, n))
    alike = [] if gather else [(lax.rem(d + p, groups), z) for p in range(1, groups)]
    if gather:
        load = pltpu.make_async_copy(attended_hbm.at[z], attended, load_sem.at[0])
        load.start()
    greet(peers + alike)
    if gather:
        load.wait()
        for later_load in later_loads:
            later_load.start()
    part_loads[0].wait()
    gain_acc[...] = jnp.zeros_like(gain_acc)

    def move_up(src, o, k):
        return pltpu.make_async_remote_copy(
            src_ref=src.at[o, k], dst_ref=from_below.at[o, k], send_sem=up_send.at[o, k],
            recv_sem=up_recv.at[o, k], device_id=upper, device_id_type=MESH,
        )

    def move_down(src, o, k):
        return pltpu.make_async_remote_copy(
            src_ref=src.at[o, k], dst_ref=from_above.at[o, k], send_sem=down_send.at[o, k],
            recv_sem=down_recv.at[o, k], device_id=lower, device_id_type=MESH,
        )

    def all_up(o, k):
        return pltpu.make_async_remote_copy(
            src_ref=alls.at[o, k], dst_ref=alls.at[o, k], send_sem=ag_up.at[o, k],
            recv_sem=ag_recv.at[o, k], device_id=upper, device_id_type=MESH,
        )

    def all_down(o, k):
        return pltpu.make_async_remote_copy(
            src_ref=alls.at[o, k], dst_ref=alls.at[o, k], send_sem=ag_down.at[o, k],
            recv_sem=ag_recv.at[o, k], device_id=lower, device_id_type=MESH,
        )

    def pass_up(k):
        def far(i, carry):
            o = z + n - 1 - i

            @pl.when(o < n)
            def _():
                @pl.when(z == 0)
                def _():
                    move_up(part, o, k).start()

                @pl.when(z > 0)
                def _():
                    move_up(part, o, k).wait_recv()
                    both = from_below[o, k].astype(f32) + part[o, k].astype(f32)
                    from_below[o, k] = both.astype(bf16)
                    move_up(from_below, o, k).start()

            return carry

        lax.fori_loop(0, n - 1, far, 0)

    def pass_down(k):
        def far(i, carry):
            o = z - n + 1 + i

            @pl.when(o >= 0)
            def _():
                @pl.when(z == n - 1)
                def _():
                    move_down(part, o, k).start()

                @pl.when(z < n - 1)
                def _():
                    move_down(part, o, k).wait_recv()
                    both = from_above[o, k].astype(f32) + part[o, k].astype(f32)
                    from_above[o, k] = both.astype(bf16)
                    move_down(from_above, o, k).start()

            return carry

        lax.fori_loop(0, n - 1, far, 0)

    def own(k):
        @pl.when(z > 0)
        def _():
            move_up(part, z, k).wait_recv()

        @pl.when(z == 0)
        def _():
            from_below[z, k] = jnp.zeros((R, D), bf16)

        @pl.when(z < n - 1)
        def _():
            move_down(part, z, k).wait_recv()

        @pl.when(z == n - 1)
        def _():
            from_above[z, k] = jnp.zeros((R, D), bf16)

        total = (
            part[z, k].astype(f32) + from_below[z, k].astype(f32) + from_above[z, k].astype(f32)
        )
        rows = base[k].astype(f32)
        if gather:
            rows = rows + attended[k]
        factor = lax.rsqrt(jnp.sum(rows * rows, axis=1, keepdims=True) / D + EPSILON)
        unit = rows * factor
        along = total * unit
        gain_acc[...] += jnp.sum(along.reshape(R // 8, 8, D), axis=0)
        weights = gain[1:2, :] if gather else gain[0:1, :]
        weighted = along * weights
        mean = jnp.sum(weighted, axis=1, keepdims=True) / D
        result = factor * (total * weights - unit * mean)
        if gather:
            result = result + addend[k].astype(f32)
        out[k] = result
        if gather:
            alls[z, k] = result.astype(bf16)

            @pl.when(z < n - 1)
            def _():
                all_up(z, k).start()

            @pl.when(z > 0)
            def _():
                all_down(z, k).start()

    def forward(own_k):
        def hop(s, carry):
            below, above, k = z - s, z + s, own_k - s
            live = (k >= 0) & (k < steps)

            @pl.when(live & (below >= 0))
            def _():
                all_up(below, k).wait_recv()

                @pl.when(z < n - 1)
                def _():
                    all_up(below, k).start()

            @pl.when(live & (above < n))
            def _():
                all_down(above, k).wait_recv()

                @pl.when(z > 0)
                def _():
                    all_down(above, k).start()

            return carry

        lax.fori_loop(1, n, hop, 0)

    def turn(t, carry):
        up_k, down_k, own_k = t - z, t - (n - 1 - z), t - (n - 1)

        @pl.when(t == steps_first)
        def _():
            part_loads[1].wait()

        @pl.when((up_k >= 0) & (up_k < steps))
        def _():
            pass_up(up_k)

        @pl.when((down_k >= 0) & (down_k < steps))
        def _():
            pass_down(down_k)

        @pl.when((own_k >= 0) & (own_k < steps))
        def _():
            own(own_k)

        if gather:
            forward(own_k)
            experts, units = down.shape[:2]
            e = t - n

            @pl.when(e == 0)
            def _():
                for later_load in later_loads:
                    later_load.wait()

            @pl.when((e >= 0) & (e < experts))
            def _():
                c = pl.ds(pl.multiple_of(e * units, units), units)
                down[e] = dot_tn(hidden[:, c], g_all[...]).astype(bf16)
                down_save(e).start()

        return carry

    lax.fori_loop(0, steps + (2 * n - 2 if gather else n - 1), turn, 0)
    if gather:
        gain_out[...] = gain_acc[...]
    else:
        C = D // n
        for s in range(n):
            c = slice(s * C, (s + 1) * C)
            pieces[s, 0:1] = jnp.sum(gain_acc[:, c], axis=0, keepdims=True)
            pieces[s, 1:2] = jnp.sum(expert_gains[:, c], axis=0, keepdims=True)
            pieces[s, 2:8] = jnp.zeros((6, C), f32)

        def piece(p):
            o = lax.rem(z + p, n)
            return pltpu.make_async_remote_copy(
                src_ref=pieces.at[o], dst_ref=landed.at[z], send_sem=piece_send.at[p - 1],
                recv_sem=piece_recv.at[z], device_id=(d, o), device_id_type=MESH,
            )

        for p in range(1, n):
            piece(p).start()
        landed[z] = pieces[z]
        for p in range(1, n):
            o = lax.rem(z + n - p, n)
            pltpu.make_async_remote_copy(
                src_ref=pieces.at[o], dst_ref=landed.at[o], send_sem=piece_send.at[p - 1],
                recv_sem=piece_recv.at[o], device_id=(d, o), device_id_type=MESH,
            ).wait_recv()
        two = landed[0]
        for s in range(1, n):
            two = two + landed[s]
        sums[d, 0:1] = two[0:1]
        sums[d, 1:3] = head_gains[...]
        sums[d, 3:4] = two[1:2]
        sums[d, 4:8] = jnp.zeros((4, C), f32)
        for p in range(1, groups):
            pltpu.make_async_remote_copy(
                src_ref=sums.at[d], dst_ref=sums.at[d], send_sem=sum_send.at[p - 1],
                recv_sem=sum_recv.at[d], device_id=alike[p - 1], device_id_type=MESH,
            ).start()
        for p in range(1, groups):
            o = lax.rem(d + groups - p, groups)
            pltpu.make_async_remote_copy(
                src_ref=sums.at[o], dst_ref=sums.at[o], send_sem=sum_send.at[p - 1],
                recv_sem=sum_recv.at[o], device_id=(o, z), device_id_type=MESH,
            ).wait_recv()
        total = sums[0]
        for s in range(1, groups):
            total = total + sums[s]
        gain_out[...] = total
        for p in range(1, n):
            piece(p).wait_send()
        for p in range(1, groups):
            pltpu.make_async_remote_copy(
                src_ref=sums.at[d], dst_ref=sums.at[d], send_sem=sum_send.at[p - 1],
                recv_sem=sum_recv.at[d], device_id=alike[p - 1], device_id_type=MESH,
            ).wait_send()

    def drain(i, carry):
        o, k = i // steps, i % steps

        @pl.when(o > z)
        def _():
            move_up(part, o, k).wait_send()

        @pl.when(o < z)
        def _():
            move_down(part, o, k).wait_send()

        if gather:

            @pl.when((z < n - 1) & (o <= z))
            def _():
                all_up(o, k).wait_send()

            @pl.when((z > 0) & (o >= z))
            def _():
                all_down(o, k).wait_send()

        return carry

    lax.fori_loop(0, n * steps, drain, 0)
    if gather:
        C = D // n
        c = pl.ds(pl.multiple_of(z * C, C), C)
        copies = []
        for o in range(n):
            own_columns = alls.at[o, :, :, c]
            copies.append(
                pltpu.make_async_copy(own_columns, columns_out.at[o], all_sem.at[n + o])
            )
            copies.append(pltpu.make_async_copy(alls.at[o], all_out.at[o], all_sem.at[o]))
        for copy in copies:
            copy.start()
        for e in range(down.shape[0]):
            down_save(e).wait()
        for copy in copies:
            copy.wait()


def scatter_norm(n, groups, steps, part, base, gain, more=None, other_gains=None):
    gather = more is not None
    T, D = base.shape
    R = T // steps
    C = D // n
    hbm = pl.BlockSpec(memory_space=pl.ANY)
    vmem = pl.BlockSpec(memory_space=pltpu.VMEM)
    dma = pltpu.SemaphoreType.DMA
    slots = pltpu.VMEM((n, steps, R, D), bf16)
    rows = jax.ShapeDtypeStruct((steps, R, D), f32)
    sems = dma((n, steps))
    if gather:
        addend, attended, hidden, g_all, experts = more
        units = hidden.shape[1] // experts
        more = (
            addend.reshape(steps, R, D), attended.reshape(n, steps, R, D), hidden, g_all,
        )
        own = [slots, sems, sems, sems, dma((2 * n,)), pltpu.VMEM((steps, R, D), f32), dma((3,))]
        own += [pltpu.VMEM(hidden.shape, bf16), pltpu.VMEM(g_all.shape, bf16)]
        own += [pltpu.VMEM((experts, units, D), bf16), dma((experts,))]
        outs = [rows, jax.ShapeDtypeStruct((n, steps, R, D), bf16)]
        outs += [jax.ShapeDtypeStruct((n, steps, R, C), bf16)]
        outs += [jax.ShapeDtypeStruct((8, D), f32)]
        outs += [jax.ShapeDtypeStruct((experts, units, D), bf16)]
    else:
        own = [
            pltpu.VMEM((n, 8, C), f32), pltpu.VMEM((n, 8, C), f32),
            pltpu.VMEM((groups, 8, C), f32), dma((n,)), dma((n,)), dma((groups,)), dma((groups,)),
        ]
        outs = [rows, jax.ShapeDtypeStruct((8, C), f32)]
    return pl.pallas_call(
        functools.partial(scatter_norm_kernel, n, groups, steps, gather),
        out_shape=outs,
        in_specs=[hbm] + ([vmem] * 3 + [hbm] * 3 if gather else [vmem] * 4),
        out_specs=[vmem, hbm, hbm, vmem, hbm] if gather else [vmem, vmem],
        scratch_shapes=own
        + [slots, slots, pltpu.VMEM((8, D), f32), sems, sems, sems, sems, slots, dma((2,))],
        compiler_params=pltpu.CompilerParams(
            collective_id=2 if gather else 3, has_side_effects=True, vmem_limit_bytes=VMEM_LIMIT
        ),
        cost_estimate=pl.CostEstimate(
            flops=10**9, bytes_accessed=2**20, transcendentals=0
        ),
        name="scatter_norm_gather" if gather else "scatter_norm",
    )(
        part.reshape(n, steps, R, D),
        base.reshape(steps, R, D),
        gain,
        *(more if gather else other_gains),
    )


def forward_kernel(
    mixed, weight, x_ref, gain, combine, gate_w, up_w, down_w,
    attended_out, turned_out, gate_out, up_out, hidden_out, sum_out, gate_t, up_t, down_t,
    in_out, units,
):
    e = pl.program_id(1)
    last = pl.num_programs(1) - 1
    D = in_out.shape[1]
    F = hidden_out.shape[1]

    @pl.when(e == 0)
    def _():
        attended_out[...] = dot(mixed[...], weight[...])
        part = 32

        def rows(i, carry):
            r = pl.ds(pl.multiple_of(i * part, part), part)
            v = attended_out[r, :] + x_ref[r, :].astype(f32)
            factor = lax.rsqrt(jnp.sum(v * v, axis=1, keepdims=True) / D + EPSILON)
            in_out[r, :] = (v * factor * gain[1:2, :]).astype(bf16)
            return carry

        lax.fori_loop(0, in_out.shape[0] // part, rows, 0)
        turned_out[...] = in_out[...].T

    lane = lax.broadcasted_iota(jnp.int32, combine.shape, 1)
    share = jnp.sum(jnp.where(lane == e, combine[...], 0.0), axis=1, keepdims=True)
    @pl.when(pl.program_id(0) == 0)
    def _():
        gate_t[0] = gate_w[0].T
        up_t[0] = up_w[0].T
        down_t[0] = down_w[pl.ds(pl.multiple_of(e * F, F), F), :].T

    gate_part = dot(in_out[...], gate_w[0])
    up_part = dot(in_out[...], up_w[0])
    sig = jax.nn.sigmoid(gate_part)
    silu = gate_part * sig * share
    gate_out[...] = up_part * sig * (1.0 + gate_part * (1.0 - sig)) * share
    up_out[...] = silu
    hidden = (silu * up_part).astype(bf16)
    hidden_out[...] = hidden
    units[:, pl.ds(pl.multiple_of(e * F, F), F)] = hidden

    @pl.when(e == last)
    def _():
        sum_out[...] = dot(units[...], down_w[...]).astype(bf16)


def forward_pass(mixed, weight, x, gain, combine, gate_w, up_w, down_w):
    L, D = x.shape
    E, _, F = gate_w.shape
    block = min(512, L)
    rows = pl.BlockSpec((block, D), lambda i, e: (i, 0))
    held = pl.BlockSpec((block, D), lambda i, e: (i, 0), pipeline_mode=pl.Buffered(1))
    units = pl.BlockSpec((block, F), lambda i, e: (i, e))
    column = pl.BlockSpec((1, D, F), lambda i, e: (e, 0, 0))
    once = pl.Buffered(1)
    turned = pl.BlockSpec((1, F, D), lambda i, e: (jnp.where(i == 0, e, E - 1), 0, 0))
    turned_down = pl.BlockSpec((1, D, F), lambda i, e: (jnp.where(i == 0, e, E - 1), 0, 0))
    return pl.pallas_call(
        forward_kernel,
        out_shape=[
            jax.ShapeDtypeStruct((L, D), f32),
            jax.ShapeDtypeStruct((D, L), bf16),
            jax.ShapeDtypeStruct((L, E * F), f32),
            jax.ShapeDtypeStruct((L, E * F), f32),
            jax.ShapeDtypeStruct((L, E * F), bf16),
            jax.ShapeDtypeStruct((L, D), bf16),
            jax.ShapeDtypeStruct((E, F, D), bf16),
            jax.ShapeDtypeStruct((E, F, D), bf16),
            jax.ShapeDtypeStruct((E, D, F), bf16),
        ],
        grid=(L // block, E),
        in_specs=[
            held,
            pl.BlockSpec((D, D), lambda i, e: (0, 0), pipeline_mode=once),
            held,
            pl.BlockSpec((8, D), lambda i, e: (0, 0)),
            pl.BlockSpec((block, combine.shape[1]), lambda i, e: (i, 0)),
            column, column,
            pl.BlockSpec((E * F, D), lambda i, e: (0, 0), pipeline_mode=once),
        ],
        out_specs=[
            rows, pl.BlockSpec((D, block), lambda i, e: (0, i)), units, units, units, rows, turned,
            turned, turned_down,
        ],
        scratch_shapes=[pltpu.VMEM((block, D), bf16), pltpu.VMEM((block, E * F), bf16)],
        compiler_params=pltpu.CompilerParams(vmem_limit_bytes=VMEM_LIMIT),
        cost_estimate=pl.CostEstimate(
            flops=6 * L * D * E * F + 2 * L * D * D, bytes_accessed=50 * 2**20,
            transcendentals=L * E * F,
        ),
        name="forward_pass",
    )(mixed, weight, x, gain, combine, gate_w, up_w, down_w.reshape(E * F, D))


def backward_kernel(
    first, rest, gate_ref, up_ref, gate_hbm, up_hbm, down_t,
    g_out, in_out, gate_out, up_out, both, turned, load_sem,
):
    i, e = pl.program_id(0), pl.program_id(1)
    last = pl.num_programs(1) - 1
    F = gate_out.shape[1]
    half = turned.shape[0] // 2
    loads = [
        pltpu.make_async_copy(gate_hbm, turned.at[0:half], load_sem.at[0]),
        pltpu.make_async_copy(up_hbm, turned.at[half : 2 * half], load_sem.at[1]),
    ]

    @pl.when((i == 0) & (e == 0))
    def _():
        for load in loads:
            load.start()

    @pl.when(e == 0)
    def _():
        few, many = first.shape[1], rest.shape[1]
        for j in range(first.shape[0]):
            top = j * (few + many)
            g_out[top : top + few, :] = first[j]
            g_out[top + few : top + few + many, :] = rest[j]

    hidden_grad = dot(g_out[...], down_t[0])
    gate_grad = (hidden_grad * gate_ref[...]).astype(bf16)
    gate_out[...] = gate_grad
    both[:, pl.ds(pl.multiple_of(e * F, F), F)] = gate_grad
    up_grad = (hidden_grad * up_ref[...]).astype(bf16)
    up_out[...] = up_grad
    both[:, pl.ds(pl.multiple_of(half + e * F, F), F)] = up_grad

    @pl.when((i == 0) & (e == last))
    def _():
        for load in loads:
            load.wait()

    @pl.when(e == last)
    def _():
        in_out[...] = dot(both[...], turned[...]).astype(bf16)


def backward_pass(first, rest, gate_by, up_by, gate_t, up_t, down_t):
    n, few, D = first.shape
    T = few + rest.shape[1]
    L = n * T
    E, F, _ = gate_t.shape
    block = max(T, min(512, L))
    owners = block // T
    rows = pl.BlockSpec((block, D), lambda i, e: (i, 0))
    units = pl.BlockSpec((block, F), lambda i, e: (i, e))
    hbm = pl.BlockSpec(memory_space=pl.ANY)
    wide = jax.ShapeDtypeStruct((L, D), bf16)
    narrow = jax.ShapeDtypeStruct((L, E * F), bf16)
    return pl.pallas_call(
        backward_kernel,
        out_shape=[wide, wide, narrow, narrow],
        grid=(L // block, E),
        in_specs=[
            pl.BlockSpec((owners, few, D), lambda i, e: (i, 0, 0)),
            pl.BlockSpec((owners, T - few, D), lambda i, e: (i, 0, 0)),
            units, units, hbm, hbm, pl.BlockSpec((1, D, F), lambda i, e: (e, 0, 0)),
        ],
        out_specs=[rows, rows, units, units],
        scratch_shapes=[
            pltpu.VMEM((block, 2 * E * F), bf16),
            pltpu.VMEM((2 * E * F, D), bf16),
            pltpu.SemaphoreType.DMA((2,)),
        ],
        compiler_params=pltpu.CompilerParams(vmem_limit_bytes=VMEM_LIMIT),
        cost_estimate=pl.CostEstimate(
            flops=6 * L * D * E * F, bytes_accessed=40 * 2**20, transcendentals=0
        ),
        name="backward_pass",
    )(first, rest, gate_by, up_by, gate_t.reshape(E * F, D), up_t.reshape(E * F, D), down_t)


def line_sum(n, steps, part, out, landed, up_send, up_recv, down_send, down_recv):
    d, z = lax.axis_index("dp"), lax.axis_index("shard")
    upper, lower = (d, lax.rem(z + 1, n)), (d, lax.rem(z + n - 1, n))

    def move_up(src, o, k):
        return pltpu.make_async_remote_copy(
            src_ref=src.at[o, k], dst_ref=landed.at[o, k], send_sem=up_send.at[o, k],
            recv_sem=up_recv.at[o, k], device_id=upper, device_id_type=MESH,
        )

    def move_down(src, o, k):
        slot = jnp.where(o == z - 1, n, o)
        return pltpu.make_async_remote_copy(
            src_ref=src.at[o, k], dst_ref=landed.at[slot, k], send_sem=down_send.at[o, k],
            recv_sem=down_recv.at[o, k], device_id=lower, device_id_type=MESH,
        )

    def passing(move, first, owner):
        def run(k):
            def far(i, carry):
                o = owner(i)

                @pl.when((o >= 0) & (o < n))
                def _():
                    @pl.when(z == first)
                    def _():
                        move(part, o, k).start()

                    @pl.when(z != first)
                    def _():
                        move(part, o, k).wait_recv()
                        both = landed[o, k].astype(f32) + part[o, k].astype(f32)
                        landed[o, k] = both.astype(bf16)
                        move(landed, o, k).start()

                return carry

            lax.fori_loop(0, n - 1, far, 0)

        return run

    pass_up = passing(move_up, 0, lambda i: z + n - 1 - i)
    pass_down = passing(move_down, n - 1, lambda i: z - n + 1 + i)

    def own(k):
        @pl.when(z > 0)
        def _():
            move_up(part, z, k).wait_recv()

        @pl.when(z == 0)
        def _():
            landed[z, k] = jnp.zeros(part.shape[2:], bf16)

        @pl.when(z < n - 1)
        def _():
            move_down(part, z, k).wait_recv()

        @pl.when(z == n - 1)
        def _():
            landed[n, k] = jnp.zeros(part.shape[2:], bf16)

        out[k] = part[z, k].astype(f32) + landed[z, k].astype(f32) + landed[n, k].astype(f32)

    def turn(t):
        up_k, down_k, own_k = t - z, t - (n - 1 - z), t - (n - 1)

        @pl.when((up_k >= 0) & (up_k < steps))
        def _():
            pass_up(up_k)

        @pl.when((down_k >= 0) & (down_k < steps))
        def _():
            pass_down(down_k)

        @pl.when((own_k >= 0) & (own_k < steps))
        def _():
            own(own_k)

    def drain():
        def one(i, carry):
            o, k = i // steps, i % steps

            @pl.when(o > z)
            def _():
                move_up(part, o, k).wait_send()

            @pl.when(o < z)
            def _():
                move_down(part, o, k).wait_send()

            return carry

        lax.fori_loop(0, n * steps, one, 0)

    return turn, drain


def line_scratch(n, steps, R, D):
    dma = pltpu.SemaphoreType.DMA
    slots = [pltpu.VMEM((n, steps, R, D), bf16), pltpu.VMEM((n + 1, steps, R, D), bf16)]
    return slots + [dma((n, steps))] * 4 + [dma((1,))]


def expert_grads_kernel(xt, gate_grad, up_grad, gate_out, up_out):
    gate_out[0] = dot(xt[...], gate_grad[...]).astype(bf16)
    up_out[0] = dot(xt[...], up_grad[...]).astype(bf16)


def expert_grads(turned, gate_grad, up_grad, experts):
    D, L = turned.shape
    F = gate_grad.shape[1] // experts
    whole = pl.BlockSpec((D, L), lambda e: (0, 0))
    units = pl.BlockSpec((L, F), lambda e: (0, e))
    column = pl.BlockSpec((1, D, F), lambda e: (e, 0, 0))
    grad = jax.ShapeDtypeStruct((experts, D, F), bf16)
    return pl.pallas_call(
        expert_grads_kernel,
        out_shape=[grad, grad],
        grid=(experts,),
        in_specs=[whole, units, units],
        out_specs=[column, column],
        compiler_params=pltpu.CompilerParams(vmem_limit_bytes=VMEM_LIMIT),
        cost_estimate=pl.CostEstimate(
            flops=4 * L * D * experts * F, bytes_accessed=16 * 2**20, transcendentals=0
        ),
        name="expert_grads",
    )(turned, gate_grad, up_grad)


def widen_kernel(count, *refs):
    for src, dst in zip(refs[:count], refs[count:]):
        dst[...] = src[...].astype(f32)


def widen(*arrays):
    flat = [v.reshape(-1, v.shape[-1]) for v in arrays]
    steps = 4
    specs = [
        pl.BlockSpec((v.shape[0] // steps, v.shape[1]), lambda i: (i, 0)) for v in flat
    ]
    out = pl.pallas_call(
        functools.partial(widen_kernel, len(flat)),
        out_shape=[jax.ShapeDtypeStruct(v.shape, f32) for v in flat],
        grid=(steps,),
        in_specs=specs,
        out_specs=specs,
        compiler_params=pltpu.CompilerParams(vmem_limit_bytes=VMEM_LIMIT),
        cost_estimate=pl.CostEstimate(
            flops=0, bytes_accessed=sum(6 * v.size for v in flat), transcendentals=0
        ),
        name="widen",
    )(*flat)
    return tuple(v.reshape(w.shape) for v, w in zip(out, arrays))


def gather_line_kernel(n, v_hbm, out, slots, load_sem, up_sem, down_sem, recv_sem, out_sem):
    d, z, peers = others(n)
    own_load = pltpu.make_async_copy(v_hbm, slots.at[z], load_sem.at[0])
    own_load.start()
    greet(peers)

    def send_up(o):
        return pltpu.make_async_remote_copy(
            src_ref=slots.at[o], dst_ref=slots.at[o], send_sem=up_sem.at[o],
            recv_sem=recv_sem.at[o], device_id=(d, lax.rem(z + 1, n)), device_id_type=MESH,
        )

    def send_down(o):
        return pltpu.make_async_remote_copy(
            src_ref=slots.at[o], dst_ref=slots.at[o], send_sem=down_sem.at[o],
            recv_sem=recv_sem.at[o], device_id=(d, lax.rem(z + n - 1, n)), device_id_type=MESH,
        )

    own_load.wait()

    @pl.when(z < n - 1)
    def _():
        send_up(z).start()

    @pl.when(z > 0)
    def _():
        send_down(z).start()

    C = slots.shape[2]

    def save(o):
        c = pl.ds(pl.multiple_of(o * C, C), C)
        return pltpu.make_async_copy(slots.at[o], out.at[:, c], out_sem.at[o])

    save(z).start()

    def step(s, carry):
        below, above = z - s, z + s

        @pl.when(below >= 0)
        def _():
            send_up(below).wait_recv()

            @pl.when(z < n - 1)
            def _():
                send_up(below).start()

            save(below).start()

        @pl.when(above < n)
        def _():
            send_down(above).wait_recv()

            @pl.when(z > 0)
            def _():
                send_down(above).start()

            save(above).start()

        return carry

    lax.fori_loop(1, n, step, 0)

    def finish(o, carry):
        save(o).wait()

        @pl.when((z < n - 1) & (o <= z))
        def _():
            send_up(o).wait_send()

        @pl.when((z > 0) & (o >= z))
        def _():
            send_down(o).wait_send()

        return carry

    lax.fori_loop(0, n, finish, 0)


def gather_line(n, v, collective_id):
    hbm = pl.BlockSpec(memory_space=pl.ANY)
    dma = pltpu.SemaphoreType.DMA
    return pl.pallas_call(
        functools.partial(gather_line_kernel, n),
        out_shape=jax.ShapeDtypeStruct((v.shape[0], n * v.shape[1]), v.dtype),
        in_specs=[hbm],
        out_specs=hbm,
        scratch_shapes=[
            pltpu.VMEM((n,) + v.shape, v.dtype), dma((1,)), dma((n,)), dma((n,)), dma((n,)),
            dma((n,)),
        ],
        compiler_params=pltpu.CompilerParams(
            collective_id=collective_id, has_side_effects=True, vmem_limit_bytes=VMEM_LIMIT
        ),
        cost_estimate=pl.CostEstimate(flops=70 * 10**9, bytes_accessed=8 * 2**20, transcendentals=0),
        name="gather_line",
    )(v)


def per_device(
    tokens,
    out_grad,
    routes,
    gate_weights,
    prefix,
    query_weight,
    key_weight,
    value_weight,
    output_weight,
    norm_gains,
    expert_gate,
    expert_up,
    expert_down,
):
    rows, width = tokens.shape
    shards = lax.axis_size("shard")
    groups = lax.axis_size("dp")
    place = lax.axis_index("shard")
    group = lax.axis_index("dp")
    length = rows * shards
    local = width // shards
    experts = expert_gate.shape[0]
    units = expert_gate.shape[2]

    expert_ids = jnp.arange(experts, dtype=jnp.int32)
    weight_own = jnp.sum(
        jnp.where(routes[:, :, None] == expert_ids[None, None, :], gate_weights[:, :, None], 0.0),
        axis=1,
    )
    own_gains = norm_gains.astype(f32)
    small = jnp.concatenate(
        [
            jnp.pad(weight_own.T, ((0, 8 - experts), (0, 0))),
            jnp.pad(jnp.stack([own_gains[0], own_gains[3]]), ((0, 6), (0, 0))),
        ],
        axis=1,
    )
    x_all_b, normed, query_raw, key_raw, values, out_slab, combine, gains, factors = (
        gather_project(
            shards, groups, tokens, small, output_weight, query_weight, key_weight, value_weight
        )
    )
    full_output = lax.all_gather(out_slab, "dp", axis=0, tiled=True)
    x_all_b = x_all_b.reshape(length, width)
    normed = normed.reshape(length, width)
    query_raw = query_raw.reshape(length, local)
    key_raw = key_raw.reshape(length, local)
    values = values.reshape(length, local)
    cosine, sine = rotary_tables(length)
    limit = jnp.broadcast_to(prefix.reshape(1, 1), (8, 128))
    few = rows // 4
    queries, keys, mixed_own, grad_first = attention(
        shards, limit, query_raw, key_raw, values, factors, cosine, sine, own_gains, out_grad, few
    )
    mixed_all = gather_line(shards, mixed_own, 1)
    grad_rest, mixed_all = lax.optimization_barrier((out_grad[few:], mixed_all))
    grad_rest = lax.all_gather(grad_rest, "shard", axis=0)
    attended, expert_turned, gate_by, up_by, hidden, sum_part, gate_t, up_t, down_t = forward_pass(
        mixed_all, full_output, x_all_b, gains, combine, expert_gate, expert_up, expert_down
    )
    attended_own = lax.dynamic_slice_in_dim(attended, place * rows, rows, 0)
    g_all, in_part, gate_grad, up_grad = backward_pass(
        grad_first, grad_rest, gate_by, up_by, gate_t, up_t, down_t
    )
    sum_parts = sum_part.reshape(shards, 16, rows // 16, width)
    grad_gate, grad_up = expert_grads(expert_turned, gate_grad, up_grad, experts)
    in_part, grad_gate, grad_up = lax.optimization_barrier((in_part, grad_gate, grad_up))
    grad_gate, grad_up = lax.psum((grad_gate, grad_up), "dp")

    x_own = tokens.astype(f32)
    residual_own = x_own + attended_own
    residual_grad, attended_grad, own_columns, gain_grad_res, grad_down = scatter_norm(
        shards, groups, 16, in_part, tokens, gains,
        more=(out_grad, attended, hidden, g_all, experts),
    )
    residual_grad = residual_grad.reshape(rows, width)
    attended_grad = attended_grad.reshape(length, width)

    grad_output = dot_tn(mixed_all, own_columns.reshape(length, local))
    grad_output, grad_down, grad_gate, grad_up, attended_grad = lax.optimization_barrier(
        (grad_output.astype(bf16), grad_down, grad_gate, grad_up, attended_grad)
    )
    grad_output, grad_down = lax.psum((grad_output, grad_down), "dp")
    grad_query, grad_key, grad_value, normed_part, gain_grad_heads, expert_sum = attention_back(
        shards, width, limit, queries, keys, values, query_raw, key_raw, factors, cosine, sine,
        own_gains, query_weight, key_weight, value_weight, normed, sum_parts, attended_grad,
        full_output,
    )
    expert_sum = expert_sum.reshape(rows, width)
    expert_sum, grad_gate, grad_up = lax.optimization_barrier((expert_sum, grad_gate, grad_up))
    grad_gate, grad_up = widen(grad_gate, grad_up)
    (
        grad_query, grad_key, grad_value, normed_part, grad_output, grad_down, grad_gate, grad_up,
    ) = lax.optimization_barrier(
        (
            grad_query, grad_key, grad_value, normed_part, grad_output, grad_down, grad_gate,
            grad_up,
        )
    )
    grad_query, grad_key, grad_value = lax.psum((grad_query, grad_key, grad_value), "dp")
    through_norm, grad_gains = scatter_norm(
        shards, groups, 16, normed_part, tokens, gains,
        other_gains=(gain_grad_res, gain_grad_heads),
    )
    through_norm, expert_sum = lax.optimization_barrier((through_norm, expert_sum))
    grad_tokens = residual_grad + through_norm.reshape(rows, width)
    grad_gains = grad_gains[:4]
    output = residual_own + expert_sum
    root_means = jnp.stack([root_mean(attended_own), root_mean(expert_sum), root_mean(output)])
    grad_down, grad_output = widen(grad_down, grad_output)
    grad_query, grad_key, grad_value = widen(grad_query, grad_key, grad_value)

    return (
        output.astype(bf16),
        grad_tokens,
        root_means,
        grad_query,
        grad_key,
        grad_value,
        grad_output,
        grad_gains,
        grad_gate,
        grad_up,
        grad_down,
    )


def solution(mesh):
    placed = (
        P(("dp", "shard"), None),
        P(("dp", "shard"), None),
        P(("dp", "shard"), None),
        P(("dp", "shard"), None),
        P("dp"),
        P(None, "shard"),
        P(None, "shard"),
        P(None, "shard"),
        P(None, "shard"),
        P(None, "shard"),
        P(None, None, "shard"),
        P(None, None, "shard"),
        P(None, "shard", None),
    )
    return jax.shard_map(
        per_device,
        mesh=mesh,
        in_specs=placed,
        out_specs=(
            P(("dp", "shard"), None),
            P(("dp", "shard"), None),
            P(None, ("dp", "shard")),
            P(None, "shard"),
            P(None, "shard"),
            P(None, "shard"),
            P(None, "shard"),
            P(None, "shard"),
            P(None, None, "shard"),
            P(None, None, "shard"),
            P(None, "shard", None),
        ),
        check_vma=False,
    )
```

```python
import functools

import jax
import jax.numpy as jnp
import numpy as np
from jax import lax
from jax.experimental import pallas as pl
from jax.experimental.pallas import tpu as pltpu
from jax.sharding import PartitionSpec as P

HEAD_DIM = 128
EPSILON = 1e-05
ROPE_BASE = 10000.0
MASKED = -1e30
VMEM_LIMIT = 60 * 2**20

f32 = jnp.float32
bf16 = jnp.bfloat16


def rotary_tables(row_count):
    half_dim = HEAD_DIM // 2
    inverse = ROPE_BASE ** (-np.arange(half_dim) / half_dim)
    angles = np.arange(row_count)[:, None] * inverse.astype(np.float32).astype(np.float64)[None, :]
    angles = angles.astype(np.float32).astype(np.float64)
    cosine, sine = np.cos(angles), np.sin(angles)
    return (
        jnp.asarray(np.concatenate([cosine, cosine], 1), f32),
        jnp.asarray(np.concatenate([-sine, sine], 1), f32),
    )


def row_factor(values):
    return lax.rsqrt(jnp.mean(values * values, axis=-1, keepdims=True) + EPSILON)


def norm_back(grad_unit, unit_rows, factor):
    return factor * (
        grad_unit - unit_rows * jnp.mean(grad_unit * unit_rows, axis=-1, keepdims=True)
    )


def root_mean(values):
    return jnp.sqrt(jnp.mean(values * values, axis=-1))


def dot(a, b):
    return jnp.dot(a, b, preferred_element_type=f32)


def dot_nt(a, b):
    return lax.dot_general(a, b, (((1,), (1,)), ((), ())), preferred_element_type=f32)


def dot_tn(a, b):
    return lax.dot_general(a, b, (((0,), (0,)), ((), ())), preferred_element_type=f32)


MESH = pl.DeviceIdType.MESH


def greet(peers):
    barrier = pltpu.get_barrier_semaphore()
    for peer in peers:
        pl.semaphore_signal(barrier, inc=1, device_id=peer, device_id_type=MESH)
    pl.semaphore_wait(barrier, len(peers))


def others(n):
    d, z = lax.axis_index("dp"), lax.axis_index("shard")
    return d, z, [(d, lax.rem(z + p, n)) for p in range(1, n)]


def line_gather(n, slots, up_sem, down_sem, recv_sem):
    d, z = lax.axis_index("dp"), lax.axis_index("shard")

    def send_up(o):
        return pltpu.make_async_remote_copy(
            src_ref=slots.at[o], dst_ref=slots.at[o], send_sem=up_sem.at[o],
            recv_sem=recv_sem.at[o], device_id=(d, lax.rem(z + 1, n)), device_id_type=MESH,
        )

    def send_down(o):
        return pltpu.make_async_remote_copy(
            src_ref=slots.at[o], dst_ref=slots.at[o], send_sem=down_sem.at[o],
            recv_sem=recv_sem.at[o], device_id=(d, lax.rem(z + n - 1, n)), device_id_type=MESH,
        )

    def begin():
        @pl.when(z < n - 1)
        def _():
            send_up(z).start()

        @pl.when(z > 0)
        def _():
            send_down(z).start()

    def hop(s, landed):
        below, above = z - s, z + s

        @pl.when((s > 0) & (below >= 0))
        def _():
            send_up(below).wait_recv()

            @pl.when(z < n - 1)
            def _():
                send_up(below).start()

            landed(below)

        @pl.when((s > 0) & (above < n))
        def _():
            send_down(above).wait_recv()

            @pl.when(z > 0)
            def _():
                send_down(above).start()

            landed(above)

    def drain():
        def one(o, carry):
            @pl.when((z < n - 1) & (o <= z))
            def _():
                send_up(o).wait_send()

            @pl.when((z > 0) & (o >= z))
            def _():
                send_down(o).wait_send()

            return carry

        lax.fori_loop(0, n, one, 0)

    return begin, hop, drain


def gather_project_kernel(
    n, x_hbm, small_ref, slab_hbm, wq_hbm, wk_hbm, wv_hbm,
    x_out, normed_out, q_out, k_out, v_out, slab_out, combine_out, gains_out, sq_out,
    slabs, xs, nb, qb, kb, vb, wq, wk, wv, sq_all, small_all,
    load_sem, out_sem, up_sem, down_sem, recv_sem, small_send, small_recv, sq_send, sq_recv,
    slab_up, slab_down, slab_recv, slab_sem,
):
    T, D = xs.shape[1:]
    C = qb.shape[2]
    d, z, peers = others(n)
    S = slabs.shape[1]
    slab_rows = pl.ds(pl.multiple_of(d * S, S), S)
    slab_load = pltpu.make_async_copy(slab_hbm.at[slab_rows, :], slabs.at[z], load_sem.at[4])
    slab_load.start()
    own_load = pltpu.make_async_copy(x_hbm, xs.at[z], load_sem.at[0])
    own_load.start()
    slab_begin, slab_hop, slab_drain = line_gather(n, slabs, slab_up, slab_down, slab_recv)

    def slab_save(o):
        c = pl.ds(pl.multiple_of(o * C, C), C)
        return pltpu.make_async_copy(slabs.at[o], slab_out.at[:, c], slab_sem.at[o])

    loads = [
        pltpu.make_async_copy(src, dst, load_sem.at[i + 1])
        for i, (src, dst) in enumerate(((wq_hbm, wq), (wk_hbm, wk), (wv_hbm, wv)))
    ]
    for load in loads:
        load.start()
    greet(peers)

    def send_up(o):
        return pltpu.make_async_remote_copy(
            src_ref=xs.at[o], dst_ref=xs.at[o], send_sem=up_sem.at[o], recv_sem=recv_sem.at[o],
            device_id=(d, lax.rem(z + 1, n)), device_id_type=MESH,
        )

    def send_down(o):
        return pltpu.make_async_remote_copy(
            src_ref=xs.at[o], dst_ref=xs.at[o], send_sem=down_sem.at[o], recv_sem=recv_sem.at[o],
            device_id=(d, lax.rem(z + n - 1, n)), device_id_type=MESH,
        )

    own_load.wait()
    small_copies = []
    for p, peer in enumerate(peers):
        copy = pltpu.make_async_remote_copy(
            src_ref=small_ref, dst_ref=small_all.at[z], send_sem=small_send.at[p],
            recv_sem=small_recv.at[z], device_id=peer, device_id_type=MESH,
        )
        copy.start()
        small_copies.append(copy)

    @pl.when(z < n - 1)
    def _():
        send_up(z).start()

    @pl.when(z > 0)
    def _():
        send_down(z).start()

    small_all[z] = small_ref[...]
    for load in loads:
        load.wait()
    for p in range(1, n):
        o = lax.rem(z + n - p, n)
        pltpu.make_async_remote_copy(
            src_ref=small_ref, dst_ref=small_all.at[o], send_sem=small_send.at[p - 1],
            recv_sem=small_recv.at[o], device_id=(d, o), device_id_type=MESH,
        ).wait_recv()

    lanes = lax.broadcasted_iota(jnp.int32, (T, 128), 1)
    step_rows = 32

    def outs(o):
        return [
            pltpu.make_async_copy(src.at[o], dst.at[o], out_sem.at[i, o])
            for i, (src, dst) in enumerate(
                ((xs, x_out), (nb, normed_out), (qb, q_out), (kb, k_out), (vb, v_out))
            )
        ]

    def compute(o):
        gain = jnp.concatenate([small_all[s, 0:1, T:] for s in range(n)], axis=1)

        def norm_rows(i, carry):
            r = pl.ds(pl.multiple_of(i * step_rows, step_rows), step_rows)
            x = xs[o, r, :].astype(f32)
            factor = lax.rsqrt(jnp.sum(x * x, axis=1, keepdims=True) / D + EPSILON)
            nb[o, r, :] = (x * factor * gain).astype(bf16)
            return carry

        lax.fori_loop(0, T // step_rows, norm_rows, 0)
        q = jnp.dot(nb[o], wq[...], preferred_element_type=f32)
        qb[o] = q
        q_sum = jnp.sum(q * q, axis=1, keepdims=True)
        k = jnp.dot(nb[o], wk[...], preferred_element_type=f32)
        kb[o] = k
        k_sum = jnp.sum(k * k, axis=1, keepdims=True)
        vb[o] = jnp.dot(nb[o], wv[...], preferred_element_type=f32).astype(bf16)
        both = jnp.where(lanes == 0, q_sum, jnp.where(lanes == 1, k_sum, 0.0))
        sq_all[z, o] = both.T[0:8]
        for copy in outs(o):
            copy.start()

    def step(s, carry):
        below, above = z - s, z + s

        @pl.when((s > 0) & (below >= 0))
        def _():
            send_up(below).wait_recv()

            @pl.when(z < n - 1)
            def _():
                send_up(below).start()

        @pl.when((s > 0) & (above < n))
        def _():
            send_down(above).wait_recv()

            @pl.when(z > 0)
            def _():
                send_down(above).start()

        @pl.when(s == n - 2)
        def _():
            slab_load.wait()
            slab_begin()
            slab_save(z).start()

        @pl.when(s == n - 1)
        def _():
            slab_hop(1, lambda o: slab_save(o).start())

        def side(j, inner):
            o = z - s + 2 * s * j

            @pl.when((o >= 0) & (o < n) & ((s > 0) | (j == 0)))
            def _():
                compute(o)

            return inner

        lax.fori_loop(0, 2, side, 0)
        return carry

    lax.fori_loop(0, n, step, 0)

    sq_copies = []
    for p, peer in enumerate(peers):
        copy = pltpu.make_async_remote_copy(
            src_ref=sq_all.at[z], dst_ref=sq_all.at[z], send_sem=sq_send.at[p],
            recv_sem=sq_recv.at[z], device_id=peer, device_id_type=MESH,
        )
        copy.start()
        sq_copies.append(copy)

    def slab_hops(s, carry):
        slab_hop(s, lambda o: slab_save(o).start())
        return carry

    lax.fori_loop(2, n - 1, slab_hops, 0)

    def spread(o, carry):
        r = pl.ds(pl.multiple_of(o * T, T), T)
        tall = jnp.concatenate([small_all[o, :, 0:T], jnp.zeros((120, T), f32)], axis=0)
        combine_out[r, :] = tall.T
        return carry

    lax.fori_loop(0, n, spread, 0)
    for s in range(n):
        gains_out[:, s * C : (s + 1) * C] = small_all[s, :, T:]

    for p in range(1, n):
        o = lax.rem(z + n - p, n)
        pltpu.make_async_remote_copy(
            src_ref=sq_all.at[o], dst_ref=sq_all.at[o], send_sem=sq_send.at[p - 1],
            recv_sem=sq_recv.at[o], device_id=(d, o), device_id_type=MESH,
        ).wait_recv()
    def turn_factors(i, carry):
        total = sq_all[0, i]
        for s in range(1, n):
            total = total + sq_all[s, i]
        total = jnp.concatenate([total, jnp.zeros((120, T), f32)], axis=0).T
        r = pl.ds(pl.multiple_of(i * T, T), T)
        sq_out[r, :] = lax.rsqrt(total / D + EPSILON)
        return carry

    lax.fori_loop(0, n, turn_factors, 0)
    lax.fori_loop(max(2, n - 1), n, slab_hops, 0)

    def finish(o, carry):
        for copy in outs(o):
            copy.wait()
        slab_save(o).wait()

        @pl.when((z < n - 1) & (o <= z))
        def _():
            send_up(o).wait_send()

        @pl.when((z > 0) & (o >= z))
        def _():
            send_down(o).wait_send()

        return carry

    lax.fori_loop(0, n, finish, 0)
    slab_drain()
    for copy in small_copies + sq_copies:
        copy.wait_send()


def gather_project(n, groups, tokens, small, wo, wq, wk, wv):
    T, D = tokens.shape
    C = wq.shape[1]
    S = D // groups
    hbm = pl.BlockSpec(memory_space=pl.ANY)
    vmem = pl.BlockSpec(memory_space=pltpu.VMEM)
    dma = pltpu.SemaphoreType.DMA
    return pl.pallas_call(
        functools.partial(gather_project_kernel, n),
        out_shape=[
            jax.ShapeDtypeStruct((n, T, D), bf16),
            jax.ShapeDtypeStruct((n, T, D), bf16),
            jax.ShapeDtypeStruct((n, T, C), f32),
            jax.ShapeDtypeStruct((n, T, C), f32),
            jax.ShapeDtypeStruct((n, T, C), bf16),
            jax.ShapeDtypeStruct((S, D), bf16),
            jax.ShapeDtypeStruct((n * T, 128), f32),
            jax.ShapeDtypeStruct((8, D), f32),
            jax.ShapeDtypeStruct((n * T, 128), f32),
        ],
        in_specs=[hbm, vmem, hbm, hbm, hbm, hbm],
        out_specs=[hbm] * 6 + [vmem] * 3,
        scratch_shapes=[
            pltpu.VMEM((n, S, C), bf16),
            pltpu.VMEM((n, T, D), bf16),
            pltpu.VMEM((n, T, D), bf16),
            pltpu.VMEM((n, T, C), f32),
            pltpu.VMEM((n, T, C), f32),
            pltpu.VMEM((n, T, C), bf16),
            pltpu.VMEM((D, C), bf16),
            pltpu.VMEM((D, C), bf16),
            pltpu.VMEM((D, C), bf16),
            pltpu.VMEM((n, n, 8, T), f32),
            pltpu.VMEM((n,) + small.shape, f32),
            dma((5,)),
            dma((5, n)),
            dma((n,)),
            dma((n,)),
            dma((n,)),
            dma((n,)),
            dma((n,)),
            dma((n,)),
            dma((n,)),
            dma((n,)),
            dma((n,)),
            dma((n,)),
            dma((n,)),
        ],
        compiler_params=pltpu.CompilerParams(
            collective_id=0, has_side_effects=True, vmem_limit_bytes=VMEM_LIMIT
        ),
        cost_estimate=pl.CostEstimate(flops=80 * 10**9, bytes_accessed=32 * 2**20, transcendentals=0),
        name="gather_project",
    )(tokens, small, wo, wq, wk, wv)


def rope(v, cosine, sine):
    return v * cosine + pltpu.roll(v, HEAD_DIM // 2, 1) * sine


def key_span(i, block, length):
    return min(length, max((i + 1) * block, length // 2))


def block_scores(q, k, i, block, limit):
    s = dot_nt(q, k) * (HEAD_DIM**-0.5)
    row = lax.broadcasted_iota(jnp.int32, s.shape, 0) + i * block
    col = lax.broadcasted_iota(jnp.int32, s.shape, 1)
    return jnp.where((col <= row) | (col < limit), s, MASKED)


def attention_kernel(
    n, limit_ref, q_raw, k_raw, v_ref, factors, cosine, sine, gains, grad_hbm,
    q_out, k_out, mixed, first_out, slots, load_sem, up_sem, down_sem, recv_sem, out_sem,
):
    length = q_raw.shape[0]
    block = 256
    limit = limit_ref[0:1, 0:1]
    h, heads = pl.program_id(0), pl.num_programs(0)
    begin, hop, drain = line_gather(n, slots, up_sem, down_sem, recv_sem)
    z = lax.axis_index("shard")

    def save(o):
        return pltpu.make_async_copy(slots.at[o], first_out.at[o], out_sem.at[o])

    few = slots.shape[1]

    @pl.when(h == 0)
    def _():
        load = pltpu.make_async_copy(grad_hbm.at[0:few], slots.at[z], load_sem.at[0])
        load.start()
        _, _, peers = others(n)
        greet(peers)
        load.wait()
        begin()
        save(z).start()

    def turn(raw, out, column, gain):
        def part(i, carry):
            r = pl.ds(pl.multiple_of(i * block, block), block)
            v = raw[r, :] * factors[r, column : column + 1] * gain
            out[r, :] = rope(v, cosine[r, :], sine[r, :]).astype(bf16)
            return carry

        lax.fori_loop(0, length // block, part, 0)

    turn(q_raw, q_out, 0, gains[1:2, :])
    turn(k_raw, k_out, 1, gains[2:3, :])
    for i in range(length // block):
        span = key_span(i, block, length)
        r = pl.ds(i * block, block)
        s = block_scores(q_out[r, :], k_out[0:span, :], i, block, limit)
        e = jnp.exp(s - jnp.max(s, axis=1, keepdims=True))
        total = jnp.sum(e, axis=1, keepdims=True)
        mixed[r, :] = (dot(e.astype(bf16), v_ref[0:span, :]) / total).astype(bf16)

    def hops(s, carry):
        hop(s, lambda o: save(o).start())
        return carry

    lax.fori_loop(1 + h * (n - 1) // heads, 1 + (h + 1) * (n - 1) // heads, hops, 0)

    @pl.when(h == heads - 1)
    def _():
        drain()

        def finish(o, carry):
            save(o).wait()
            return carry

        lax.fori_loop(0, n, finish, 0)


def attention(n, limit, q_raw, k_raw, values, factors, cosine, sine, gains, grad, few):
    length, local = q_raw.shape
    heads = local // HEAD_DIM
    head = pl.BlockSpec((length, HEAD_DIM), lambda h: (0, h))
    whole = lambda a: pl.BlockSpec(a.shape, lambda h: (0, 0))
    hbm = pl.BlockSpec(memory_space=pl.ANY)
    out = jax.ShapeDtypeStruct((length, local), bf16)
    dma = pltpu.SemaphoreType.DMA
    return pl.pallas_call(
        functools.partial(attention_kernel, n),
        out_shape=[out] * 3
        + [jax.ShapeDtypeStruct((n, few, grad.shape[1]), bf16)],
        grid=(heads,),
        in_specs=[
            whole(limit), head, head, head, whole(factors), whole(cosine), whole(sine),
            pl.BlockSpec((gains.shape[0], HEAD_DIM), lambda h: (0, h)), hbm,
        ],
        out_specs=[head] * 3 + [hbm],
        scratch_shapes=[pltpu.VMEM((n, few, grad.shape[1]), bf16), dma((1,))] + [dma((n,))] * 4,
        compiler_params=pltpu.CompilerParams(
            collective_id=7, has_side_effects=True, vmem_limit_bytes=VMEM_LIMIT
        ),
        cost_estimate=pl.CostEstimate(
            flops=20 * 10**9, bytes_accessed=16 * 2**20, transcendentals=0
        ),
        name="attention",
    )(limit, q_raw, k_raw, values, factors, cosine, sine, gains, grad)


def attention_back_kernel(
    n, steps, width, limit_ref, q_ref, k_ref, v_ref, q_raw, k_raw, factors, cosine, sine,
    gains, wq, wk, wv, normed_hbm, sum_hbm, grad_hbm, output_hbm, gq_out, gk_out, gv_out, normed_out, gain_out, own_sum,
    g_ref, output, dq_acc, dk_acc, k_acc, v_acc, q_grad, k_grad, v_grad, columns, turned, staged,
    inner_all, inner_send, inner_recv, column_sem, staged_sem, grad_sem, part, *line,
):
    length, local = q_ref.shape
    strips = width // local
    heads = local // HEAD_DIM
    block = 256
    blocks = length // block
    scale = HEAD_DIM**-0.5
    load_sem = line[-1]
    turn, drain = line_sum(n, steps, part, own_sum, *line[:-1])
    d, z, peers = others(n)
    load = pltpu.make_async_copy(sum_hbm, part, load_sem.at[0])
    load.start()

    def grad_rows(i):
        r = pl.ds(pl.multiple_of(i * block, block), block)
        return pltpu.make_async_copy(
            grad_hbm.at[r, :], staged.at[lax.rem(i, 2)], grad_sem.at[lax.rem(i, 2)]
        )

    own_rows = pl.ds(pl.multiple_of(z * local, local), local)
    output_load = pltpu.make_async_copy(output_hbm.at[own_rows, :], output, grad_sem.at[2])
    output_load.start()
    grad_rows(0).start()
    greet(peers)

    def strip(b):
        c = pl.ds(pl.multiple_of(b * local, local), local)
        return pltpu.make_async_copy(
            normed_hbm.at[:, c], columns.at[lax.rem(b, 2)], column_sem.at[lax.rem(b, 2)]
        )

    strip(0).start()
    load.wait()
    turns = steps + n - 1
    in_heads, in_parts = 8 * turns // 19, 4 * turns // 19
    slots = -(-in_heads // heads)
    past = 1 + heads * slots
    in_strips = turns - past - in_parts - 2

    def take(first, count, i, of):
        def one(t, carry):
            turn(first + t)
            return carry

        lax.fori_loop(i * count // of, (i + 1) * count // of, one, 0)
    limit = limit_ref[0:1, 0:1]
    lanes = lax.broadcasted_iota(jnp.int32, (block, 128), 1)

    def clear(i, carry):
        inner_all[z, i] = jnp.zeros((8, block), f32)
        return carry

    lax.fori_loop(0, blocks, clear, 0)

    turn(0)
    output_load.wait()

    def mixed_rows(i, carry):
        r = pl.ds(pl.multiple_of(i * block, block), block)
        grad_rows(i).wait()

        @pl.when(i + 1 < blocks)
        def _():
            grad_rows(i + 1).start()

        g_ref[r, :] = dot_nt(staged[lax.rem(i, 2)], output[...]).astype(bf16)
        return carry

    lax.fori_loop(0, blocks, mixed_rows, 0)

    def head(h, carry):
        c = pl.ds(pl.multiple_of(h * HEAD_DIM, HEAD_DIM), HEAD_DIM)
        k_acc[...] = jnp.zeros_like(k_acc)
        v_acc[...] = jnp.zeros_like(v_acc)
        for i in range(blocks):
            for j in range(i * slots // blocks, (i + 1) * slots // blocks):
                turn(1 + h * slots + j)
            span = key_span(i, block, length)
            r = pl.ds(i * block, block)
            q, g, k, v = q_ref[r, c], g_ref[r, c], k_ref[0:span, c], v_ref[0:span, c]
            s = block_scores(q, k, i, block, limit)
            e = jnp.exp(s - jnp.max(s, axis=1, keepdims=True))
            p = e * (1.0 / jnp.sum(e, axis=1, keepdims=True))
            t = p * dot_nt(g, v)
            ds = (t - p * jnp.sum(t, axis=1, keepdims=True)).astype(bf16)
            dq_acc[r, c] = dot(ds, k) * scale
            k_acc[0:span, :] += dot_tn(ds, q) * scale
            v_acc[0:span, :] += dot_tn(p.astype(bf16), g)
        v_grad[:, c] = v_acc[...].astype(bf16)
        gain_q, gain_k = gains[1:2, c], gains[2:3, c]

        def back(i, carry):
            gq, gk = carry
            r = pl.ds(pl.multiple_of(i * block, block), block)
            cos, sin = cosine[r, :], sine[r, :]
            dq = rope(dq_acc[r, c], cos, -sin)
            dk = rope(k_acc[r, :], cos, -sin)
            uq = q_raw[r, c] * factors[r, 0:1]
            uk = k_raw[r, c] * factors[r, 1:2]
            gq = gq + jnp.sum(dq * uq, axis=0, keepdims=True)
            gk = gk + jnp.sum(dk * uk, axis=0, keepdims=True)
            dq = dq * gain_q
            dk = dk * gain_k
            dq_acc[r, c] = dq
            dk_acc[r, c] = dk
            inner_q = jnp.sum(dq * uq, axis=1, keepdims=True)
            inner_k = jnp.sum(dk * uk, axis=1, keepdims=True)
            both = jnp.where(lanes == 0, inner_q, jnp.where(lanes == 1, inner_k, 0.0))
            inner_all[z, i] += both.T[0:8]
            return gq, gk

        zero = jnp.zeros((1, HEAD_DIM), f32)
        gq, gk = lax.fori_loop(0, blocks, back, (zero, zero))
        gain_out[0:1, c] = gq
        gain_out[1:2, c] = gk
        return carry

    lax.fori_loop(0, heads, head, 0)

    copies = []
    for p, peer in enumerate(peers):
        copy = pltpu.make_async_remote_copy(
            src_ref=inner_all.at[z], dst_ref=inner_all.at[z], send_sem=inner_send.at[p],
            recv_sem=inner_recv.at[z], device_id=peer, device_id_type=MESH,
        )
        copy.start()
        copies.append(copy)
    turn(past)
    for p in range(1, n):
        o = lax.rem(z + n - p, n)
        pltpu.make_async_remote_copy(
            src_ref=inner_all.at[o], dst_ref=inner_all.at[o], send_sem=inner_send.at[p - 1],
            recv_sem=inner_recv.at[o], device_id=(d, o), device_id_type=MESH,
        ).wait_recv()

    def raw(i, carry):
        r = pl.ds(pl.multiple_of(i * block, block), block)
        total = inner_all[0, i]
        for s in range(1, n):
            total = total + inner_all[s, i]
        total = jnp.concatenate([total, jnp.zeros((120, block), f32)], axis=0).T
        fq, fk = factors[r, 0:1], factors[r, 1:2]
        mean_q, mean_k = total[:, 0:1] / width, total[:, 1:2] / width
        q_grad[r, :] = (fq * (dq_acc[r, :] - q_raw[r, :] * (fq * mean_q))).astype(bf16)
        k_grad[r, :] = (fk * (dk_acc[r, :] - k_raw[r, :] * (fk * mean_k))).astype(bf16)
        return carry

    lax.fori_loop(0, blocks, raw, 0)
    turn(past + 1)

    def save(i):
        r = pl.ds(pl.multiple_of(i * block, block), block)
        return pltpu.make_async_copy(
            staged.at[lax.rem(i, 2)], normed_out.at[r, :], staged_sem.at[lax.rem(i, 2)]
        )

    def rows_back(i, carry):
        r = pl.ds(pl.multiple_of(i * block, block), block)

        @pl.when(i >= 2)
        def _():
            save(i - 2).wait()

        staged[lax.rem(i, 2)] = (
            dot_nt(q_grad[r, :], wq[...])
            + dot_nt(k_grad[r, :], wk[...])
            + dot_nt(v_grad[r, :], wv[...])
        ).astype(bf16)
        save(i).start()
        take(past + 2, in_parts, i, blocks)
        return carry

    lax.fori_loop(0, blocks, rows_back, 0)

    def strip_grads(b, carry):
        strip(b).wait()

        @pl.when(b + 1 < strips)
        def _():
            strip(b + 1).start()

        turned[...] = columns[lax.rem(b, 2)].T
        c = pl.ds(pl.multiple_of(b * local, local), local)
        gq_out[c, :] = dot(turned[...], q_grad[...]).astype(bf16)
        gk_out[c, :] = dot(turned[...], k_grad[...]).astype(bf16)
        gv_out[c, :] = dot(turned[...], v_grad[...]).astype(bf16)
        take(past + 2 + in_parts, in_strips, b, strips)
        return carry

    lax.fori_loop(0, strips, strip_grads, 0)
    drain()
    for i in range(max(blocks - 2, 0), blocks):
        save(i).wait()
    for copy in copies:
        copy.wait_send()


def attention_back(
    n, width, limit, q, k, v, q_raw, k_raw, factors, cosine, sine, gains, wq, wk, wv, normed,
    sum_parts, attended_grad, full_output,
):
    length, local = q.shape
    _, steps, R, D = sum_parts.shape
    hbm = pl.BlockSpec(memory_space=pl.ANY)
    vmem = pl.BlockSpec(memory_space=pltpu.VMEM)
    dma = pltpu.SemaphoreType.DMA
    weight = jax.ShapeDtypeStruct((D, local), bf16)
    raw = pltpu.VMEM((length, local), bf16)
    return pl.pallas_call(
        functools.partial(attention_back_kernel, n, steps, width),
        out_shape=[
            weight, weight, weight, jax.ShapeDtypeStruct((length, D), bf16),
            jax.ShapeDtypeStruct((2, local), f32),
            jax.ShapeDtypeStruct((steps, R, D), f32),
        ],
        in_specs=[vmem] * 13 + [hbm] * 4,
        out_specs=[vmem, vmem, vmem, hbm, vmem, vmem],
        scratch_shapes=[
            raw,
            pltpu.VMEM((local, D), bf16),
            pltpu.VMEM((length, local), f32),
            pltpu.VMEM((length, local), f32),
            pltpu.VMEM((length, HEAD_DIM), f32),
            pltpu.VMEM((length, HEAD_DIM), f32),
            raw,
            raw,
            raw,
            pltpu.VMEM((2, length, local), bf16),
            pltpu.VMEM((local, length), bf16),
            pltpu.VMEM((2, 256, D), bf16),
            pltpu.VMEM((n, length // 256, 8, 256), f32),
            dma((n,)),
            dma((n,)),
            dma((2,)),
            dma((2,)),
            dma((3,)),
        ]
        + line_scratch(n, steps, R, D),
        compiler_params=pltpu.CompilerParams(
            collective_id=6, has_side_effects=True, vmem_limit_bytes=VMEM_LIMIT
        ),
        cost_estimate=pl.CostEstimate(
            flops=2 * 10**9, bytes_accessed=2**20, transcendentals=0
        ),
        name="attention_back",
    )(
        limit, q, k, v, q_raw, k_raw, factors, cosine, sine, gains, wq, wk, wv, normed, sum_parts,
        attended_grad, full_output,
    )


def scatter_norm_kernel(n, groups, steps, gather, *refs):
    part_hbm, base, gain = refs[:3]
    part, part_sem = refs[-2:]
    refs = refs[3:-2]
    steps_first = 2
    part_loads = [
        pltpu.make_async_copy(part_hbm.at[:, c], part.at[:, c], part_sem.at[i])
        for i, c in enumerate((slice(0, steps_first), slice(steps_first, steps)))
    ]
    for part_load in part_loads:
        part_load.start()
    if gather:
        addend, attended_hbm, hidden_hbm, g_hbm = refs[:4]
        out, all_out, columns_out, gain_out, down_out = refs[4:9]
        alls, ag_up, ag_down, ag_recv, all_sem, attended, load_sem = refs[9:16]
        hidden, g_all, down, down_sem = refs[16:20]
        refs = refs[20:]
        later_loads = [
            pltpu.make_async_copy(hidden_hbm, hidden, load_sem.at[1]),
            pltpu.make_async_copy(g_hbm, g_all, load_sem.at[2]),
        ]

        def down_save(e):
            return pltpu.make_async_copy(down.at[e], down_out.at[e], down_sem.at[e])
    else:
        expert_gains, head_gains, out, gain_out = refs[:4]
        pieces, landed, sums, piece_send, piece_recv, sum_send, sum_recv = refs[4:11]
        refs = refs[11:]
    from_below, from_above, gain_acc, up_send, up_recv, down_send, down_recv = refs
    R, D = part.shape[2:]
    d, z, peers = others(n)
    upper, lower = (d, lax.rem(z + 1, n)), (d, lax.rem(z + n - 1, n))
    alike = [] if gather else [(lax.rem(d + p, groups), z) for p in range(1, groups)]
    if gather:
        load = pltpu.make_async_copy(attended_hbm.at[z], attended, load_sem.at[0])
        load.start()
    greet(peers + alike)
    if gather:
        load.wait()
        for later_load in later_loads:
            later_load.start()
    part_loads[0].wait()
    gain_acc[...] = jnp.zeros_like(gain_acc)

    def move_up(src, o, k):
        return pltpu.make_async_remote_copy(
            src_ref=src.at[o, k], dst_ref=from_below.at[o, k], send_sem=up_send.at[o, k],
            recv_sem=up_recv.at[o, k], device_id=upper, device_id_type=MESH,
        )

    def move_down(src, o, k):
        return pltpu.make_async_remote_copy(
            src_ref=src.at[o, k], dst_ref=from_above.at[o, k], send_sem=down_send.at[o, k],
            recv_sem=down_recv.at[o, k], device_id=lower, device_id_type=MESH,
        )

    def all_up(o, k):
        return pltpu.make_async_remote_copy(
            src_ref=alls.at[o, k], dst_ref=alls.at[o, k], send_sem=ag_up.at[o, k],
            recv_sem=ag_recv.at[o, k], device_id=upper, device_id_type=MESH,
        )

    def all_down(o, k):
        return pltpu.make_async_remote_copy(
            src_ref=alls.at[o, k], dst_ref=alls.at[o, k], send_sem=ag_down.at[o, k],
            recv_sem=ag_recv.at[o, k], device_id=lower, device_id_type=MESH,
        )

    def pass_up(k):
        def far(i, carry):
            o = z + n - 1 - i

            @pl.when(o < n)
            def _():
                @pl.when(z == 0)
                def _():
                    move_up(part, o, k).start()

                @pl.when(z > 0)
                def _():
                    move_up(part, o, k).wait_recv()
                    both = from_below[o, k].astype(f32) + part[o, k].astype(f32)
                    from_below[o, k] = both.astype(bf16)
                    move_up(from_below, o, k).start()

            return carry

        lax.fori_loop(0, n - 1, far, 0)

    def pass_down(k):
        def far(i, carry):
            o = z - n + 1 + i

            @pl.when(o >= 0)
            def _():
                @pl.when(z == n - 1)
                def _():
                    move_down(part, o, k).start()

                @pl.when(z < n - 1)
                def _():
                    move_down(part, o, k).wait_recv()
                    both = from_above[o, k].astype(f32) + part[o, k].astype(f32)
                    from_above[o, k] = both.astype(bf16)
                    move_down(from_above, o, k).start()

            return carry

        lax.fori_loop(0, n - 1, far, 0)

    def own(k):
        @pl.when(z > 0)
        def _():
            move_up(part, z, k).wait_recv()

        @pl.when(z == 0)
        def _():
            from_below[z, k] = jnp.zeros((R, D), bf16)

        @pl.when(z < n - 1)
        def _():
            move_down(part, z, k).wait_recv()

        @pl.when(z == n - 1)
        def _():
            from_above[z, k] = jnp.zeros((R, D), bf16)

        total = (
            part[z, k].astype(f32) + from_below[z, k].astype(f32) + from_above[z, k].astype(f32)
        )
        rows = base[k].astype(f32)
        if gather:
            rows = rows + attended[k]
        factor = lax.rsqrt(jnp.sum(rows * rows, axis=1, keepdims=True) / D + EPSILON)
        unit = rows * factor
        along = total * unit
        gain_acc[...] += jnp.sum(along.reshape(R // 8, 8, D), axis=0)
        weights = gain[1:2, :] if gather else gain[0:1, :]
        weighted = along * weights
        mean = jnp.sum(weighted, axis=1, keepdims=True) / D
        result = factor * (total * weights - unit * mean)
        if gather:
            result = result + addend[k].astype(f32)
        out[k] = result
        if gather:
            alls[z, k] = result.astype(bf16)

            @pl.when(z < n - 1)
            def _():
                all_up(z, k).start()

            @pl.when(z > 0)
            def _():
                all_down(z, k).start()

    def forward(own_k):
        def hop(s, carry):
            below, above, k = z - s, z + s, own_k - s
            live = (k >= 0) & (k < steps)

            @pl.when(live & (below >= 0))
            def _():
                all_up(below, k).wait_recv()

                @pl.when(z < n - 1)
                def _():
                    all_up(below, k).start()

            @pl.when(live & (above < n))
            def _():
                all_down(above, k).wait_recv()

                @pl.when(z > 0)
                def _():
                    all_down(above, k).start()

            return carry

        lax.fori_loop(1, n, hop, 0)

    def turn(t, carry):
        up_k, down_k, own_k = t - z, t - (n - 1 - z), t - (n - 1)

        @pl.when(t == steps_first)
        def _():
            part_loads[1].wait()

        @pl.when((up_k >= 0) & (up_k < steps))
        def _():
            pass_up(up_k)

        @pl.when((down_k >= 0) & (down_k < steps))
        def _():
            pass_down(down_k)

        @pl.when((own_k >= 0) & (own_k < steps))
        def _():
            own(own_k)

        if gather:
            forward(own_k)
            experts, units = down.shape[:2]
            e = t - n

            @pl.when(e == 0)
            def _():
                for later_load in later_loads:
                    later_load.wait()

            @pl.when((e >= 0) & (e < experts))
            def _():
                c = pl.ds(pl.multiple_of(e * units, units), units)
                down[e] = dot_tn(hidden[:, c], g_all[...]).astype(bf16)
                down_save(e).start()

        return carry

    lax.fori_loop(0, steps + (2 * n - 2 if gather else n - 1), turn, 0)
    if gather:
        gain_out[...] = gain_acc[...]
    else:
        C = D // n
        for s in range(n):
            c = slice(s * C, (s + 1) * C)
            pieces[s, 0:1] = jnp.sum(gain_acc[:, c], axis=0, keepdims=True)
            pieces[s, 1:2] = jnp.sum(expert_gains[:, c], axis=0, keepdims=True)
            pieces[s, 2:8] = jnp.zeros((6, C), f32)

        def piece(p):
            o = lax.rem(z + p, n)
            return pltpu.make_async_remote_copy(
                src_ref=pieces.at[o], dst_ref=landed.at[z], send_sem=piece_send.at[p - 1],
                recv_sem=piece_recv.at[z], device_id=(d, o), device_id_type=MESH,
            )

        for p in range(1, n):
            piece(p).start()
        landed[z] = pieces[z]
        for p in range(1, n):
            o = lax.rem(z + n - p, n)
            pltpu.make_async_remote_copy(
                src_ref=pieces.at[o], dst_ref=landed.at[o], send_sem=piece_send.at[p - 1],
                recv_sem=piece_recv.at[o], device_id=(d, o), device_id_type=MESH,
            ).wait_recv()
        two = landed[0]
        for s in range(1, n):
            two = two + landed[s]
        sums[d, 0:1] = two[0:1]
        sums[d, 1:3] = head_gains[...]
        sums[d, 3:4] = two[1:2]
        sums[d, 4:8] = jnp.zeros((4, C), f32)
        for p in range(1, groups):
            pltpu.make_async_remote_copy(
                src_ref=sums.at[d], dst_ref=sums.at[d], send_sem=sum_send.at[p - 1],
                recv_sem=sum_recv.at[d], device_id=alike[p - 1], device_id_type=MESH,
            ).start()
        for p in range(1, groups):
            o = lax.rem(d + groups - p, groups)
            pltpu.make_async_remote_copy(
                src_ref=sums.at[o], dst_ref=sums.at[o], send_sem=sum_send.at[p - 1],
                recv_sem=sum_recv.at[o], device_id=(o, z), device_id_type=MESH,
            ).wait_recv()
        total = sums[0]
        for s in range(1, groups):
            total = total + sums[s]
        gain_out[...] = total
        for p in range(1, n):
            piece(p).wait_send()
        for p in range(1, groups):
            pltpu.make_async_remote_copy(
                src_ref=sums.at[d], dst_ref=sums.at[d], send_sem=sum_send.at[p - 1],
                recv_sem=sum_recv.at[d], device_id=alike[p - 1], device_id_type=MESH,
            ).wait_send()

    def drain(i, carry):
        o, k = i // steps, i % steps

        @pl.when(o > z)
        def _():
            move_up(part, o, k).wait_send()

        @pl.when(o < z)
        def _():
            move_down(part, o, k).wait_send()

        if gather:

            @pl.when((z < n - 1) & (o <= z))
            def _():
                all_up(o, k).wait_send()

            @pl.when((z > 0) & (o >= z))
            def _():
                all_down(o, k).wait_send()

        return carry

    lax.fori_loop(0, n * steps, drain, 0)
    if gather:
        C = D // n
        c = pl.ds(pl.multiple_of(z * C, C), C)
        copies = []
        for o in range(n):
            own_columns = alls.at[o, :, :, c]
            copies.append(
                pltpu.make_async_copy(own_columns, columns_out.at[o], all_sem.at[n + o])
            )
            copies.append(pltpu.make_async_copy(alls.at[o], all_out.at[o], all_sem.at[o]))
        for copy in copies:
            copy.start()
        for e in range(down.shape[0]):
            down_save(e).wait()
        for copy in copies:
            copy.wait()


def scatter_norm(n, groups, steps, part, base, gain, more=None, other_gains=None):
    gather = more is not None
    T, D = base.shape
    R = T // steps
    C = D // n
    hbm = pl.BlockSpec(memory_space=pl.ANY)
    vmem = pl.BlockSpec(memory_space=pltpu.VMEM)
    dma = pltpu.SemaphoreType.DMA
    slots = pltpu.VMEM((n, steps, R, D), bf16)
    rows = jax.ShapeDtypeStruct((steps, R, D), f32)
    sems = dma((n, steps))
    if gather:
        addend, attended, hidden, g_all, experts = more
        units = hidden.shape[1] // experts
        more = (
            addend.reshape(steps, R, D), attended.reshape(n, steps, R, D), hidden, g_all,
        )
        own = [slots, sems, sems, sems, dma((2 * n,)), pltpu.VMEM((steps, R, D), f32), dma((3,))]
        own += [pltpu.VMEM(hidden.shape, bf16), pltpu.VMEM(g_all.shape, bf16)]
        own += [pltpu.VMEM((experts, units, D), bf16), dma((experts,))]
        outs = [rows, jax.ShapeDtypeStruct((n, steps, R, D), bf16)]
        outs += [jax.ShapeDtypeStruct((n, steps, R, C), bf16)]
        outs += [jax.ShapeDtypeStruct((8, D), f32)]
        outs += [jax.ShapeDtypeStruct((experts, units, D), bf16)]
    else:
        own = [
            pltpu.VMEM((n, 8, C), f32), pltpu.VMEM((n, 8, C), f32),
            pltpu.VMEM((groups, 8, C), f32), dma((n,)), dma((n,)), dma((groups,)), dma((groups,)),
        ]
        outs = [rows, jax.ShapeDtypeStruct((8, C), f32)]
    return pl.pallas_call(
        functools.partial(scatter_norm_kernel, n, groups, steps, gather),
        out_shape=outs,
        in_specs=[hbm] + ([vmem] * 3 + [hbm] * 3 if gather else [vmem] * 4),
        out_specs=[vmem, hbm, hbm, vmem, hbm] if gather else [vmem, vmem],
        scratch_shapes=own
        + [slots, slots, pltpu.VMEM((8, D), f32), sems, sems, sems, sems, slots, dma((2,))],
        compiler_params=pltpu.CompilerParams(
            collective_id=2 if gather else 3, has_side_effects=True, vmem_limit_bytes=VMEM_LIMIT
        ),
        cost_estimate=pl.CostEstimate(
            flops=10**9, bytes_accessed=2**20, transcendentals=0
        ),
        name="scatter_norm_gather" if gather else "scatter_norm",
    )(
        part.reshape(n, steps, R, D),
        base.reshape(steps, R, D),
        gain,
        *(more if gather else other_gains),
    )


def forward_kernel(
    mixed, weight, x_ref, gain, combine, gate_w, up_w, down_w,
    attended_out, turned_out, gate_out, up_out, hidden_out, sum_out, gate_t, up_t, down_t,
    in_out, units,
):
    e = pl.program_id(1)
    last = pl.num_programs(1) - 1
    D = in_out.shape[1]
    F = hidden_out.shape[1]

    @pl.when(e == 0)
    def _():
        attended_out[...] = dot(mixed[...], weight[...])
        part = 32

        def rows(i, carry):
            r = pl.ds(pl.multiple_of(i * part, part), part)
            v = attended_out[r, :] + x_ref[r, :].astype(f32)
            factor = lax.rsqrt(jnp.sum(v * v, axis=1, keepdims=True) / D + EPSILON)
            in_out[r, :] = (v * factor * gain[1:2, :]).astype(bf16)
            return carry

        lax.fori_loop(0, in_out.shape[0] // part, rows, 0)
        turned_out[...] = in_out[...].T

    lane = lax.broadcasted_iota(jnp.int32, combine.shape, 1)
    share = jnp.sum(jnp.where(lane == e, combine[...], 0.0), axis=1, keepdims=True)
    @pl.when(pl.program_id(0) == 0)
    def _():
        gate_t[0] = gate_w[0].T
        up_t[0] = up_w[0].T
        down_t[0] = down_w[pl.ds(pl.multiple_of(e * F, F), F), :].T

    gate_part = dot(in_out[...], gate_w[0])
    up_part = dot(in_out[...], up_w[0])
    sig = jax.nn.sigmoid(gate_part)
    silu = gate_part * sig * share
    gate_out[...] = up_part * sig * (1.0 + gate_part * (1.0 - sig)) * share
    up_out[...] = silu
    hidden = (silu * up_part).astype(bf16)
    hidden_out[...] = hidden
    units[:, pl.ds(pl.multiple_of(e * F, F), F)] = hidden

    @pl.when(e == last)
    def _():
        sum_out[...] = dot(units[...], down_w[...]).astype(bf16)


def forward_pass(mixed, weight, x, gain, combine, gate_w, up_w, down_w):
    L, D = x.shape
    E, _, F = gate_w.shape
    block = min(512, L)
    rows = pl.BlockSpec((block, D), lambda i, e: (i, 0))
    held = pl.BlockSpec((block, D), lambda i, e: (i, 0), pipeline_mode=pl.Buffered(1))
    units = pl.BlockSpec((block, F), lambda i, e: (i, e))
    column = pl.BlockSpec((1, D, F), lambda i, e: (e, 0, 0))
    once = pl.Buffered(1)
    turned = pl.BlockSpec((1, F, D), lambda i, e: (jnp.where(i == 0, e, E - 1), 0, 0))
    turned_down = pl.BlockSpec((1, D, F), lambda i, e: (jnp.where(i == 0, e, E - 1), 0, 0))
    return pl.pallas_call(
        forward_kernel,
        out_shape=[
            jax.ShapeDtypeStruct((L, D), f32),
            jax.ShapeDtypeStruct((D, L), bf16),
            jax.ShapeDtypeStruct((L, E * F), f32),
            jax.ShapeDtypeStruct((L, E * F), f32),
            jax.ShapeDtypeStruct((L, E * F), bf16),
            jax.ShapeDtypeStruct((L, D), bf16),
            jax.ShapeDtypeStruct((E, F, D), bf16),
            jax.ShapeDtypeStruct((E, F, D), bf16),
            jax.ShapeDtypeStruct((E, D, F), bf16),
        ],
        grid=(L // block, E),
        in_specs=[
            held,
            pl.BlockSpec((D, D), lambda i, e: (0, 0), pipeline_mode=once),
            held,
            pl.BlockSpec((8, D), lambda i, e: (0, 0)),
            pl.BlockSpec((block, combine.shape[1]), lambda i, e: (i, 0)),
            column, column,
            pl.BlockSpec((E * F, D), lambda i, e: (0, 0), pipeline_mode=once),
        ],
        out_specs=[
            rows, pl.BlockSpec((D, block), lambda i, e: (0, i)), units, units, units, rows, turned,
            turned, turned_down,
        ],
        scratch_shapes=[pltpu.VMEM((block, D), bf16), pltpu.VMEM((block, E * F), bf16)],
        compiler_params=pltpu.CompilerParams(vmem_limit_bytes=VMEM_LIMIT),
        cost_estimate=pl.CostEstimate(
            flops=6 * L * D * E * F + 2 * L * D * D, bytes_accessed=50 * 2**20,
            transcendentals=L * E * F,
        ),
        name="forward_pass",
    )(mixed, weight, x, gain, combine, gate_w, up_w, down_w.reshape(E * F, D))


def backward_kernel(
    first, rest, gate_ref, up_ref, gate_hbm, up_hbm, down_t,
    g_out, in_out, gate_out, up_out, both, turned, load_sem,
):
    i, e = pl.program_id(0), pl.program_id(1)
    last = pl.num_programs(1) - 1
    F = gate_out.shape[1]
    half = turned.shape[0] // 2
    loads = [
        pltpu.make_async_copy(gate_hbm, turned.at[0:half], load_sem.at[0]),
        pltpu.make_async_copy(up_hbm, turned.at[half : 2 * half], load_sem.at[1]),
    ]

    @pl.when((i == 0) & (e == 0))
    def _():
        for load in loads:
            load.start()

    @pl.when(e == 0)
    def _():
        few, many = first.shape[1], rest.shape[1]
        for j in range(first.shape[0]):
            top = j * (few + many)
            g_out[top : top + few, :] = first[j]
            g_out[top + few : top + few + many, :] = rest[j]

    hidden_grad = dot(g_out[...], down_t[0])
    gate_grad = (hidden_grad * gate_ref[...]).astype(bf16)
    gate_out[...] = gate_grad
    both[:, pl.ds(pl.multiple_of(e * F, F), F)] = gate_grad
    up_grad = (hidden_grad * up_ref[...]).astype(bf16)
    up_out[...] = up_grad
    both[:, pl.ds(pl.multiple_of(half + e * F, F), F)] = up_grad

    @pl.when((i == 0) & (e == last))
    def _():
        for load in loads:
            load.wait()

    @pl.when(e == last)
    def _():
        in_out[...] = dot(both[...], turned[...]).astype(bf16)


def backward_pass(first, rest, gate_by, up_by, gate_t, up_t, down_t):
    n, few, D = first.shape
    T = few + rest.shape[1]
    L = n * T
    E, F, _ = gate_t.shape
    block = max(T, min(1024, L))
    owners = block // T
    rows = pl.BlockSpec((block, D), lambda i, e: (i, 0))
    units = pl.BlockSpec((block, F), lambda i, e: (i, e))
    hbm = pl.BlockSpec(memory_space=pl.ANY)
    wide = jax.ShapeDtypeStruct((L, D), bf16)
    narrow = jax.ShapeDtypeStruct((L, E * F), bf16)
    return pl.pallas_call(
        backward_kernel,
        out_shape=[wide, wide, narrow, narrow],
        grid=(L // block, E),
        in_specs=[
            pl.BlockSpec((owners, few, D), lambda i, e: (i, 0, 0)),
            pl.BlockSpec((owners, T - few, D), lambda i, e: (i, 0, 0)),
            units, units, hbm, hbm, pl.BlockSpec((1, D, F), lambda i, e: (e, 0, 0)),
        ],
        out_specs=[rows, rows, units, units],
        scratch_shapes=[
            pltpu.VMEM((block, 2 * E * F), bf16),
            pltpu.VMEM((2 * E * F, D), bf16),
            pltpu.SemaphoreType.DMA((2,)),
        ],
        compiler_params=pltpu.CompilerParams(vmem_limit_bytes=VMEM_LIMIT),
        cost_estimate=pl.CostEstimate(
            flops=6 * L * D * E * F, bytes_accessed=40 * 2**20, transcendentals=0
        ),
        name="backward_pass",
    )(first, rest, gate_by, up_by, gate_t.reshape(E * F, D), up_t.reshape(E * F, D), down_t)


def line_sum(n, steps, part, out, landed, up_send, up_recv, down_send, down_recv):
    d, z = lax.axis_index("dp"), lax.axis_index("shard")
    upper, lower = (d, lax.rem(z + 1, n)), (d, lax.rem(z + n - 1, n))

    def move_up(src, o, k):
        return pltpu.make_async_remote_copy(
            src_ref=src.at[o, k], dst_ref=landed.at[o, k], send_sem=up_send.at[o, k],
            recv_sem=up_recv.at[o, k], device_id=upper, device_id_type=MESH,
        )

    def move_down(src, o, k):
        slot = jnp.where(o == z - 1, n, o)
        return pltpu.make_async_remote_copy(
            src_ref=src.at[o, k], dst_ref=landed.at[slot, k], send_sem=down_send.at[o, k],
            recv_sem=down_recv.at[o, k], device_id=lower, device_id_type=MESH,
        )

    def passing(move, first, owner):
        def run(k):
            def far(i, carry):
                o = owner(i)

                @pl.when((o >= 0) & (o < n))
                def _():
                    @pl.when(z == first)
                    def _():
                        move(part, o, k).start()

                    @pl.when(z != first)
                    def _():
                        move(part, o, k).wait_recv()
                        both = landed[o, k].astype(f32) + part[o, k].astype(f32)
                        landed[o, k] = both.astype(bf16)
                        move(landed, o, k).start()

                return carry

            lax.fori_loop(0, n - 1, far, 0)

        return run

    pass_up = passing(move_up, 0, lambda i: z + n - 1 - i)
    pass_down = passing(move_down, n - 1, lambda i: z - n + 1 + i)

    def own(k):
        @pl.when(z > 0)
        def _():
            move_up(part, z, k).wait_recv()

        @pl.when(z == 0)
        def _():
            landed[z, k] = jnp.zeros(part.shape[2:], bf16)

        @pl.when(z < n - 1)
        def _():
            move_down(part, z, k).wait_recv()

        @pl.when(z == n - 1)
        def _():
            landed[n, k] = jnp.zeros(part.shape[2:], bf16)

        out[k] = part[z, k].astype(f32) + landed[z, k].astype(f32) + landed[n, k].astype(f32)

    def turn(t):
        up_k, down_k, own_k = t - z, t - (n - 1 - z), t - (n - 1)

        @pl.when((up_k >= 0) & (up_k < steps))
        def _():
            pass_up(up_k)

        @pl.when((down_k >= 0) & (down_k < steps))
        def _():
            pass_down(down_k)

        @pl.when((own_k >= 0) & (own_k < steps))
        def _():
            own(own_k)

    def drain():
        def one(i, carry):
            o, k = i // steps, i % steps

            @pl.when(o > z)
            def _():
                move_up(part, o, k).wait_send()

            @pl.when(o < z)
            def _():
                move_down(part, o, k).wait_send()

            return carry

        lax.fori_loop(0, n * steps, one, 0)

    return turn, drain


def line_scratch(n, steps, R, D):
    dma = pltpu.SemaphoreType.DMA
    slots = [pltpu.VMEM((n, steps, R, D), bf16), pltpu.VMEM((n + 1, steps, R, D), bf16)]
    return slots + [dma((n, steps))] * 4 + [dma((1,))]


def expert_grads_kernel(xt, gate_grad, up_grad, gate_out, up_out):
    gate_out[0] = dot(xt[...], gate_grad[...]).astype(bf16)
    up_out[0] = dot(xt[...], up_grad[...]).astype(bf16)


def expert_grads(turned, gate_grad, up_grad, experts):
    D, L = turned.shape
    F = gate_grad.shape[1] // experts
    whole = pl.BlockSpec((D, L), lambda e: (0, 0))
    units = pl.BlockSpec((L, F), lambda e: (0, e))
    column = pl.BlockSpec((1, D, F), lambda e: (e, 0, 0))
    grad = jax.ShapeDtypeStruct((experts, D, F), bf16)
    return pl.pallas_call(
        expert_grads_kernel,
        out_shape=[grad, grad],
        grid=(experts,),
        in_specs=[whole, units, units],
        out_specs=[column, column],
        compiler_params=pltpu.CompilerParams(vmem_limit_bytes=VMEM_LIMIT),
        cost_estimate=pl.CostEstimate(
            flops=4 * L * D * experts * F, bytes_accessed=16 * 2**20, transcendentals=0
        ),
        name="expert_grads",
    )(turned, gate_grad, up_grad)


def widen_kernel(count, *refs):
    for src, dst in zip(refs[:count], refs[count:]):
        dst[...] = src[...].astype(f32)


def widen(*arrays):
    flat = [v.reshape(-1, v.shape[-1]) for v in arrays]
    steps = 4
    specs = [
        pl.BlockSpec((v.shape[0] // steps, v.shape[1]), lambda i: (i, 0)) for v in flat
    ]
    out = pl.pallas_call(
        functools.partial(widen_kernel, len(flat)),
        out_shape=[jax.ShapeDtypeStruct(v.shape, f32) for v in flat],
        grid=(steps,),
        in_specs=specs,
        out_specs=specs,
        compiler_params=pltpu.CompilerParams(vmem_limit_bytes=VMEM_LIMIT),
        cost_estimate=pl.CostEstimate(
            flops=0, bytes_accessed=sum(6 * v.size for v in flat), transcendentals=0
        ),
        name="widen",
    )(*flat)
    return tuple(v.reshape(w.shape) for v, w in zip(out, arrays))


def gather_line_kernel(n, v_hbm, out, slots, load_sem, up_sem, down_sem, recv_sem, out_sem):
    d, z, peers = others(n)
    own_load = pltpu.make_async_copy(v_hbm, slots.at[z], load_sem.at[0])
    own_load.start()
    greet(peers)

    def send_up(o):
        return pltpu.make_async_remote_copy(
            src_ref=slots.at[o], dst_ref=slots.at[o], send_sem=up_sem.at[o],
            recv_sem=recv_sem.at[o], device_id=(d, lax.rem(z + 1, n)), device_id_type=MESH,
        )

    def send_down(o):
        return pltpu.make_async_remote_copy(
            src_ref=slots.at[o], dst_ref=slots.at[o], send_sem=down_sem.at[o],
            recv_sem=recv_sem.at[o], device_id=(d, lax.rem(z + n - 1, n)), device_id_type=MESH,
        )

    own_load.wait()

    @pl.when(z < n - 1)
    def _():
        send_up(z).start()

    @pl.when(z > 0)
    def _():
        send_down(z).start()

    C = slots.shape[2]

    def save(o):
        c = pl.ds(pl.multiple_of(o * C, C), C)
        return pltpu.make_async_copy(slots.at[o], out.at[:, c], out_sem.at[o])

    save(z).start()

    def step(s, carry):
        below, above = z - s, z + s

        @pl.when(below >= 0)
        def _():
            send_up(below).wait_recv()

            @pl.when(z < n - 1)
            def _():
                send_up(below).start()

            save(below).start()

        @pl.when(above < n)
        def _():
            send_down(above).wait_recv()

            @pl.when(z > 0)
            def _():
                send_down(above).start()

            save(above).start()

        return carry

    lax.fori_loop(1, n, step, 0)

    def finish(o, carry):
        save(o).wait()

        @pl.when((z < n - 1) & (o <= z))
        def _():
            send_up(o).wait_send()

        @pl.when((z > 0) & (o >= z))
        def _():
            send_down(o).wait_send()

        return carry

    lax.fori_loop(0, n, finish, 0)


def gather_line(n, v, collective_id):
    hbm = pl.BlockSpec(memory_space=pl.ANY)
    dma = pltpu.SemaphoreType.DMA
    return pl.pallas_call(
        functools.partial(gather_line_kernel, n),
        out_shape=jax.ShapeDtypeStruct((v.shape[0], n * v.shape[1]), v.dtype),
        in_specs=[hbm],
        out_specs=hbm,
        scratch_shapes=[
            pltpu.VMEM((n,) + v.shape, v.dtype), dma((1,)), dma((n,)), dma((n,)), dma((n,)),
            dma((n,)),
        ],
        compiler_params=pltpu.CompilerParams(
            collective_id=collective_id, has_side_effects=True, vmem_limit_bytes=VMEM_LIMIT
        ),
        cost_estimate=pl.CostEstimate(flops=70 * 10**9, bytes_accessed=8 * 2**20, transcendentals=0),
        name="gather_line",
    )(v)


def per_device(
    tokens,
    out_grad,
    routes,
    gate_weights,
    prefix,
    query_weight,
    key_weight,
    value_weight,
    output_weight,
    norm_gains,
    expert_gate,
    expert_up,
    expert_down,
):
    rows, width = tokens.shape
    shards = lax.axis_size("shard")
    groups = lax.axis_size("dp")
    place = lax.axis_index("shard")
    group = lax.axis_index("dp")
    length = rows * shards
    local = width // shards
    experts = expert_gate.shape[0]
    units = expert_gate.shape[2]

    expert_ids = jnp.arange(experts, dtype=jnp.int32)
    weight_own = jnp.sum(
        jnp.where(routes[:, :, None] == expert_ids[None, None, :], gate_weights[:, :, None], 0.0),
        axis=1,
    )
    own_gains = norm_gains.astype(f32)
    small = jnp.concatenate(
        [
            jnp.pad(weight_own.T, ((0, 8 - experts), (0, 0))),
            jnp.pad(jnp.stack([own_gains[0], own_gains[3]]), ((0, 6), (0, 0))),
        ],
        axis=1,
    )
    x_all_b, normed, query_raw, key_raw, values, out_slab, combine, gains, factors = (
        gather_project(
            shards, groups, tokens, small, output_weight, query_weight, key_weight, value_weight
        )
    )
    full_output = lax.all_gather(out_slab, "dp", axis=0, tiled=True)
    x_all_b = x_all_b.reshape(length, width)
    normed = normed.reshape(length, width)
    query_raw = query_raw.reshape(length, local)
    key_raw = key_raw.reshape(length, local)
    values = values.reshape(length, local)
    cosine, sine = rotary_tables(length)
    limit = jnp.broadcast_to(prefix.reshape(1, 1), (8, 128))
    few = rows // 4
    queries, keys, mixed_own, grad_first = attention(
        shards, limit, query_raw, key_raw, values, factors, cosine, sine, own_gains, out_grad, few
    )
    mixed_all = gather_line(shards, mixed_own, 1)
    grad_rest, mixed_all = lax.optimization_barrier((out_grad[few:], mixed_all))
    grad_rest = lax.all_gather(grad_rest, "shard", axis=0)
    attended, expert_turned, gate_by, up_by, hidden, sum_part, gate_t, up_t, down_t = forward_pass(
        mixed_all, full_output, x_all_b, gains, combine, expert_gate, expert_up, expert_down
    )
    attended_own = lax.dynamic_slice_in_dim(attended, place * rows, rows, 0)
    g_all, in_part, gate_grad, up_grad = backward_pass(
        grad_first, grad_rest, gate_by, up_by, gate_t, up_t, down_t
    )
    sum_parts = sum_part.reshape(shards, 16, rows // 16, width)
    grad_gate, grad_up = expert_grads(expert_turned, gate_grad, up_grad, experts)
    in_part, grad_gate, grad_up = lax.optimization_barrier((in_part, grad_gate, grad_up))
    grad_gate, grad_up = lax.psum((grad_gate, grad_up), "dp")

    x_own = tokens.astype(f32)
    residual_own = x_own + attended_own
    residual_grad, attended_grad, own_columns, gain_grad_res, grad_down = scatter_norm(
        shards, groups, 16, in_part, tokens, gains,
        more=(out_grad, attended, hidden, g_all, experts),
    )
    residual_grad = residual_grad.reshape(rows, width)
    attended_grad = attended_grad.reshape(length, width)

    grad_output = dot_tn(mixed_all, own_columns.reshape(length, local))
    grad_output, grad_down, grad_gate, grad_up, attended_grad = lax.optimization_barrier(
        (grad_output.astype(bf16), grad_down, grad_gate, grad_up, attended_grad)
    )
    grad_output, grad_down = lax.psum((grad_output, grad_down), "dp")
    grad_query, grad_key, grad_value, normed_part, gain_grad_heads, expert_sum = attention_back(
        shards, width, limit, queries, keys, values, query_raw, key_raw, factors, cosine, sine,
        own_gains, query_weight, key_weight, value_weight, normed, sum_parts, attended_grad,
        full_output,
    )
    expert_sum = expert_sum.reshape(rows, width)
    expert_sum, grad_gate, grad_up = lax.optimization_barrier((expert_sum, grad_gate, grad_up))
    grad_gate, grad_up = widen(grad_gate, grad_up)
    (
        grad_query, grad_key, grad_value, normed_part, grad_output, grad_down, grad_gate, grad_up,
    ) = lax.optimization_barrier(
        (
            grad_query, grad_key, grad_value, normed_part, grad_output, grad_down, grad_gate,
            grad_up,
        )
    )
    grad_query, grad_key, grad_value = lax.psum((grad_query, grad_key, grad_value), "dp")
    through_norm, grad_gains = scatter_norm(
        shards, groups, 16, normed_part, tokens, gains,
        other_gains=(gain_grad_res, gain_grad_heads),
    )
    through_norm, expert_sum = lax.optimization_barrier((through_norm, expert_sum))
    grad_tokens = residual_grad + through_norm.reshape(rows, width)
    grad_gains = grad_gains[:4]
    output = residual_own + expert_sum
    root_means = jnp.stack([root_mean(attended_own), root_mean(expert_sum), root_mean(output)])
    grad_down, grad_output = widen(grad_down, grad_output)
    grad_query, grad_key, grad_value = widen(grad_query, grad_key, grad_value)

    return (
        output.astype(bf16),
        grad_tokens,
        root_means,
        grad_query,
        grad_key,
        grad_value,
        grad_output,
        grad_gains,
        grad_gate,
        grad_up,
        grad_down,
    )


def solution(mesh):
    placed = (
        P(("dp", "shard"), None),
        P(("dp", "shard"), None),
        P(("dp", "shard"), None),
        P(("dp", "shard"), None),
        P("dp"),
        P(None, "shard"),
        P(None, "shard"),
        P(None, "shard"),
        P(None, "shard"),
        P(None, "shard"),
        P(None, None, "shard"),
        P(None, None, "shard"),
        P(None, "shard", None),
    )
    return jax.shard_map(
        per_device,
        mesh=mesh,
        in_specs=placed,
        out_specs=(
            P(("dp", "shard"), None),
            P(("dp", "shard"), None),
            P(None, ("dp", "shard")),
            P(None, "shard"),
            P(None, "shard"),
            P(None, "shard"),
            P(None, "shard"),
            P(None, "shard"),
            P(None, None, "shard"),
            P(None, None, "shard"),
            P(None, "shard", None),
        ),
        check_vma=False,
    )
```
